32 devices in a mesh: cp: 8 (over y, x, core), tp: 4 (over z).
Axes of the slice: x: 2, y: 2, z: 4, core: 2. Of those that a mesh axis runs over, the one named last changes fastest.
Arguments:
- layer_input: bfloat16 [4096, 2048], P('cp'), may hold values from -6 to 6
- seq_lengths: int32 [3], replicated, may hold values from 1024 to 2048, as said below
- active_until: int32 [3], replicated, may hold values from 896 to 2048, as said below
- ln_gains: float32 [2, 2048], replicated, may hold values from 0.1 to 1.9
- ln_shifts: float32 [2, 2048], replicated, may hold values from -1.75 to 1.75
- query_key_value_weight: bfloat16 [2048, 3, 2048], P(None, None, 'tp'), may hold values from -0.125 to 0.125
- b_qv: float32 [2, 2048], P(None, 'tp'), may hold values from -0.625 to 0.625
- w_out: bfloat16 [2048, 2048], P('tp'), may hold values from -1.5 to 1.5
- b_outs: float32 [2, 2048], replicated, may hold values from -1.75 to 1.75
- w_up: bfloat16 [2048, 8192], P(None, 'tp'), may hold values from -0.125 to 0.125
- b_up: float32 [8192], P('tp'), may hold values from -3 to 3
- w_down: bfloat16 [8192, 2048], P('tp'), may hold values from -0.0625 to 0.0625
- d_out: bfloat16 [4096, 2048], P('cp'), may hold values from -6 to 6
Outputs:
- out: float32 [4096, 2048], P('cp')
- g_x: float32 [4096, 2048], P('cp')
- g_ln_gains: float32 [2, 2048], replicated
- g_ln_shifts: float32 [2, 2048], replicated
- g_qkv: float32 [2048, 3, 2048], P('cp', None, 'tp')
- g_bqv: float32 [2, 2048], P(None, 'tp')
- g_out: float32 [2048, 2048], P('tp', 'cp')
- g_bouts: float32 [2, 2048], replicated
- g_up: float32 [2048, 8192], P('cp', 'tp')
- g_bup: float32 [8192], P('tp')
- g_down: float32 [8192, 2048], P('tp', 'cp')
The draws below stay inside these ranges and needn't reach their ends.
Inputs may be any that keep to these rules, and one draw needn't show every extreme that they name: `seq_lengths`: two sequences have 2048 // 2 tokens and all others 2048, in an order drawn from the seed; the lengths sum to 4096. `active_until`: entry s lies between the length of sequence s minus an eighth of it (rounded down) and that length.
All inputs are finite; a program needn't handle non-finite values.
Results may differ from the reference program's by a relative error of at most 0.02.
Values may be sent and summed in bfloat16 or wider, within the bound.
A program may use at most 192 MiB of HBM per device.

```python
import math
import jax
import jax.numpy as jnp
from jax import lax

D = 2048
HEADS = 32
HD = 64
FF = 8192
LONG = 2048
TOKENS = 4096


def sequence_draw(key):
    base = jax.random.fold_in(key, 11)
    pick_key, cut_key = jax.random.split(base, 2)
    count = TOKENS // LONG + 1
    index = jnp.arange(count)
    table = jnp.where(index < count - 2, LONG, LONG // 2).astype(jnp.int32)
    spare = jax.random.randint(cut_key, (count,), 0, 1 << 20)
    cut = (spare % (table // 8 + 1)).astype(jnp.int32)
    cut = jnp.where(index == 0, 0, cut)
    cut = jnp.where(index == count - 1, table // 8, cut)
    order = jax.random.permutation(pick_key, count)
    lengths = table[order].astype(jnp.int32)
    until = (table - cut)[order].astype(jnp.int32)
    return (lengths, until)


def draw_seq_lengths(key, part):
    return sequence_draw(key)[0]


def draw_active_until(key, part):
    return sequence_draw(key)[1]


def steps_of(stream_key, shape, cuts, smallest, largest):
    factor_of, own = 1.0, jax.random.fold_in(stream_key, 6)
    for dim, shards_of in cuts:
        draws = jnp.exp(jax.random.uniform(jax.random.fold_in(own, dim), (shards_of,), jnp.float32, smallest / len(cuts), largest / len(cuts)))
        factor_of = factor_of * jnp.repeat(draws, shape[dim] // shards_of).reshape([-1 if axis == dim else 1 for axis in range(len(shape))])
    return factor_of


def noise(stream_key, dims, width, most, cuts=(), kind=jnp.bfloat16):
    loudness = steps_of(stream_key, dims, cuts, -0.22, 0.18) if cuts else 1.0
    result = jax.random.normal(stream_key, dims, jnp.float32) * width * loudness
    return jnp.minimum(jnp.maximum(result, -most), most).astype(kind)


def setup_inputs(seed: int = 0) -> dict:
    streams_of = jax.random.split(jax.random.key(seed), 14)
    return {
        "layer_input": noise(streams_of[0], (TOKENS, D), 1.0, 6.0, ((0, 8),)),
        "seq_lengths": draw_seq_lengths(jax.random.fold_in(streams_of[13], 71), 0),
        "active_until": draw_active_until(jax.random.fold_in(streams_of[13], 71), 0),
        "ln_gains": jnp.clip(1.0 + 0.18 * jax.random.normal(streams_of[3], (2, D), jnp.float32), 0.1, 1.9),
        "ln_shifts": noise(streams_of[4], (2, D), 0.3, 1.75, (), jnp.float32),
        "query_key_value_weight": noise(streams_of[5], (D, 3, D), D ** -0.5, 0.125, ((2, 4),)),
        "b_qv": noise(streams_of[6], (2, D), 0.1, 0.625, ((1, 4),), jnp.float32),
        "w_out": noise(streams_of[7], (D, D), 16 ** -0.5, 1.5, ((0, 4),)),
        "b_outs": noise(streams_of[8], (2, D), 0.3, 1.75, (), jnp.float32),
        "w_up": noise(streams_of[9], (D, FF), D ** -0.5, 0.125, ((1, 4),)),
        "b_up": noise(streams_of[10], (FF,), 0.5, 3.0, ((0, 4),), jnp.float32),
        "w_down": noise(streams_of[11], (FF, D), FF ** -0.5, 0.0625, ((0, 4),)),
        "d_out": noise(streams_of[12], (TOKENS, D), 1.0, 6.0, ((0, 8),)),
    }


@jax.custom_vjp
def low(v):
    return lax.optimization_barrier(v.astype(jnp.bfloat16)).astype(jnp.float32)

@jax.custom_vjp
def low_back(v):
    return v

def low_keep(v):
    return (low(v), None)

def low_pass(kept, grad):
    return (grad,)

def back_keep(v):
    return (v, None)

def back_low(kept, grad):
    return (low(grad),)
low.defvjp(low_keep, low_pass)
low_back.defvjp(back_keep, back_low)
EPS = 1e-05
NEG = -1e+30
HIGHEST_PRECISE = lax.Precision.HIGHEST

def layer_norm(v, gain, shift):
    mean = lax.optimization_barrier(jnp.mean(v, axis=-1, keepdims=True))
    centred = v - mean
    var = lax.optimization_barrier(jnp.mean(centred * centred, axis=-1, keepdims=True))
    return centred * lax.rsqrt(var + EPS) * gain + shift

def row_info(seq_lengths, active_until, first, count):
    ends = jnp.cumsum(seq_lengths).astype(jnp.int32)
    starts = (ends - seq_lengths).astype(jnp.int32)
    rows = (first + jnp.arange(count)).astype(jnp.int32)
    inside = (rows[:, None] >= starts[None, :]) & (rows[:, None] < ends[None, :])
    numbers = jnp.arange(seq_lengths.shape[0]).astype(jnp.int32)
    segment = (lax.optimization_barrier(jnp.sum(jnp.where(inside, numbers[None, :] + 1, 0), axis=1)) - 1).astype(jnp.int32)
    position = (rows - lax.optimization_barrier(jnp.sum(jnp.where(inside, starts[None, :], 0), axis=1))).astype(jnp.int32)
    limit = lax.optimization_barrier(jnp.sum(jnp.where(inside, active_until[None, :], 0), axis=1)).astype(jnp.int32)
    active = (position < limit).astype(jnp.float32)
    return (rows, segment, active)

def attention(queries, keys, values, rows, segment):
    count = queries.shape[0]
    block = math.gcd(count, 512)
    scale = HD ** (-0.5)
    keys_h = keys.reshape(count, HEADS, HD)
    values_h = values.reshape(count, HEADS, HD)

    def one_block(args):
        query_block, query_rows, query_seg = args
        scores = jnp.einsum('qhd,khd->hqk', query_block.reshape(block, HEADS, HD), keys_h, precision=HIGHEST_PRECISE) * scale
        scores = low_back(scores)
        allowed = (rows[None, :] <= query_rows[:, None]) & (segment[None, :] == query_seg[:, None])
        masked = jnp.where(allowed[None], scores, NEG)
        top = lax.optimization_barrier(jnp.max(masked, axis=-1, keepdims=True))
        expd = jnp.where(allowed[None], jnp.exp(masked - top), 0.0)
        probs = expd / lax.optimization_barrier(jnp.sum(expd, axis=-1, keepdims=True))
        probs_low = low(probs)
        mixed = jnp.einsum('hqk,khd->qhd', probs_low, values_h, precision=HIGHEST_PRECISE)
        return mixed.reshape(block, HEADS * HD)
    blocks = lax.map(jax.checkpoint(one_block), (queries.reshape(count // block, block, HEADS * HD), rows.reshape(count // block, block), segment.reshape(count // block, block)))
    return blocks.reshape(count, HEADS * HD)

def forward(layer_input, ln_gains, ln_shifts, query_key_value_weight, b_qv, w_out, b_outs, w_up, b_up, w_down, rows, segment, active):
    gate = active[:, None]
    first_norm_output = low(layer_norm(layer_input, ln_gains[0], ln_shifts[0]))
    projected_rows = jnp.einsum('oa,amh->omh', first_norm_output, query_key_value_weight, precision=HIGHEST_PRECISE)
    queries = low(low_back(projected_rows[:, 0] + b_qv[0]))
    keys = low(low_back(projected_rows[:, 1]))
    values = low(low_back(projected_rows[:, 2] + b_qv[1]))
    attended = low(low_back(attention(queries, keys, values, rows, segment)))
    attn_branch = low_back(jnp.dot(attended, w_out, precision=HIGHEST_PRECISE) + b_outs[0])
    hidden_state = layer_input + gate * attn_branch
    norm2 = low(layer_norm(hidden_state, ln_gains[1], ln_shifts[1]))
    pre = low_back(jnp.dot(norm2, w_up, precision=HIGHEST_PRECISE) + b_up)
    act = low(jax.nn.gelu(pre, approximate=True))
    ffn_branch = low_back(jnp.dot(act, w_down, precision=HIGHEST_PRECISE) + b_outs[1])
    return hidden_state + gate * ffn_branch

def reference(layer_input, seq_lengths, active_until, ln_gains, ln_shifts, query_key_value_weight, b_qv, w_out, b_outs, w_up, b_up, w_down, d_out):
    rows, segment, active = row_info(seq_lengths, active_until, 0, layer_input.shape[0])

    def run(input_value, gains, shifts, qkv, bqv, wout, bouts, wup, bup, wdown):
        return forward(input_value, gains, shifts, qkv, bqv, wout, bouts, wup, bup, wdown, rows, segment, active)
    out, pull = jax.vjp(run, layer_input.astype(jnp.float32), ln_gains, ln_shifts, query_key_value_weight.astype(jnp.float32), b_qv, w_out.astype(jnp.float32), b_outs, w_up.astype(jnp.float32), b_up, w_down.astype(jnp.float32))
    grads = pull(d_out.astype(jnp.float32))
    return (out, grads[0], grads[1], grads[2], grads[3], grads[4], grads[5], grads[6], grads[7], grads[8], grads[9])
```

```python
import functools

import jax
import jax.numpy as jnp
from jax import lax
from jax.experimental import pallas as pl
from jax.experimental.pallas import tpu as pltpu
from jax.sharding import PartitionSpec as P

HD = 64
LONG = 2048
EPS = 1e-05
NEG = -1e30
MESH = pl.DeviceIdType.MESH
F32 = jnp.float32
BF16 = jnp.bfloat16
ANY = pl.BlockSpec(memory_space=pl.ANY)
IN_VMEM = pl.BlockSpec(memory_space=pltpu.VMEM)
IN_SMEM = pl.BlockSpec(memory_space=pltpu.SMEM)
SUB = 32
CHUNK = 256


def dot(a, b):
    return jnp.dot(a, b, preferred_element_type=F32)


def dot_nt(a, b):
    return lax.dot_general(a, b, (((1,), (1,)), ((), ())), preferred_element_type=F32)


def dot_tn(a, b):
    return lax.dot_general(a, b, (((0,), (0,)), ((), ())), preferred_element_type=F32)


def rows_of(index, size):
    return pl.ds(pl.multiple_of(index * size, size), size)


def place():
    cp = lax.axis_index("cp")
    tp = lax.axis_index("tp")
    return cp, tp, lax.rem(cp, 2), lax.div(cp, 2)


def greet(cp, tp, others):
    barrier = pltpu.get_barrier_semaphore()
    edge = (tp == 0) | (tp == 3)
    for other in [*others, (cp, line_near(tp))]:
        pl.semaphore_signal(barrier, inc=1, device_id=other, device_id_type=MESH)

    @pl.when(jnp.logical_not(edge))
    def _():
        pl.semaphore_signal(barrier, inc=1, device_id=(cp, 3 - tp), device_id_type=MESH)

    pl.semaphore_wait(barrier, len(others) + jnp.where(edge, 1, 2))


def line_near(tp):
    return jnp.where(tp == 0, 1, jnp.where(tp == 1, 0, jnp.where(tp == 2, 3, 2)))


class LineSum:
    def __init__(self, part, slot_a, slot_b, total, send, recv):
        self.cp, self.tp, _, _ = place()
        self.edge = (self.tp == 0) | (self.tp == 3)
        self.refs = (part, slot_a, slot_b, total)
        self.send, self.recv = send, recv

    def copy(self, kind, s):
        part, slot_a, slot_b, total = self.refs
        src, dst = ((part, slot_a), (part, slot_b), (total, total))[kind]
        other = (self.cp, 3 - self.tp if kind == 1 else line_near(self.tp))
        rows = rows_of(s, SUB)
        return pltpu.make_async_remote_copy(
            src_ref=src.at[rows],
            dst_ref=dst.at[rows],
            send_sem=self.send.at[kind, s],
            recv_sem=self.recv.at[kind, s],
            device_id=other,
            device_id_type=MESH,
        )

    def push(self, s):
        @pl.when(self.edge)
        def _():
            self.copy(0, s).start()

    def relay_in(self, s):
        part, slot_a, _, _ = self.refs

        @pl.when(jnp.logical_not(self.edge))
        def _():
            rows = rows_of(s, SUB)
            self.copy(0, s).wait_recv()
            part[rows] = (part[rows].astype(F32) + slot_a[rows].astype(F32)).astype(BF16)
            self.copy(1, s).start()

    def relay_out(self, s):
        part, _, slot_b, total = self.refs

        @pl.when(jnp.logical_not(self.edge))
        def _():
            rows = rows_of(s, SUB)
            self.copy(1, s).wait_recv()
            total[rows] = (part[rows].astype(F32) + slot_b[rows].astype(F32)).astype(BF16)
            self.copy(2, s).start()

    def get(self, s):
        @pl.when(self.edge)
        def _():
            self.copy(2, s).wait_recv()

    def drain(self, s):
        @pl.when(self.edge)
        def _():
            self.copy(0, s).wait_send()

        @pl.when(jnp.logical_not(self.edge))
        def _():
            self.copy(1, s).wait_send()
            self.copy(2, s).wait_send()

    def run(self, first, last):
        def step(s, carry):
            @pl.when(s < last)
            def _():
                self.relay_in(s)

            @pl.when(s > first)
            def _():
                self.relay_out(s - 1)
                self.get(s - 1)

            return carry

        lax.fori_loop(first, last + 1, step, 0)

    def drain_all(self, count):
        def step(s, carry):
            self.drain(s)
            return carry

        lax.fori_loop(0, count, step, 0)


def line_scratch(rows, width, with_part=True):
    count = rows // SUB
    return [pltpu.VMEM((rows, width), BF16)] * 4 + [
        pltpu.SemaphoreType.DMA((3, count)),
        pltpu.SemaphoreType.DMA((3, count)),
    ]


def band_info(lengths_ref, until_ref, first):
    start = jnp.int32(0)
    begin = jnp.int32(0)
    until = jnp.int32(0)
    for i in range(lengths_ref.shape[0]):
        length = lengths_ref[i]
        inside = (first >= start) & (first < start + length)
        begin = jnp.where(inside, start, begin)
        until = jnp.where(inside, until_ref[i], until)
        start = start + length
    return begin, until + begin - first


def loop(count, body):
    def step(i, carry):
        body(i)
        return carry

    lax.fori_loop(0, count, step, 0)


def attend_kernel(
    x_hbm, lengths_ref, until_ref, gains, shifts, wqkv_hbm, bqv, wout_hbm,
    sum_hbm, norm_hbm, q_hbm, kv_hbm, att_hbm, att_t_hbm, lse_out,
    x_v, norm_v, w_v, wout_v, q_v, kv, q_t, v_t, s_v, p_v, att_t, att_v,
    part, slot_a, slot_b, total, ar_send, ar_recv, kv_send, kv_recv, load_sem, store_sem,
):
    cp, tp, core, chip = place()
    bands = lax.axis_size("cp")
    chips = bands // 2
    rows, depth = x_v.shape
    width = q_v.shape[1]
    heads = width // HD
    near = (cp + 1 - 2 * core, tp)
    after = (lax.rem(cp + 2, bands), tp)
    before = (lax.rem(cp + bands - 2, bands), tp)
    loads = [
        pltpu.make_async_copy(x_hbm, x_v, load_sem.at[0]),
        pltpu.make_async_copy(wqkv_hbm.at[1], w_v.at[1], load_sem.at[1]),
        pltpu.make_async_copy(wqkv_hbm.at[2], w_v.at[2], load_sem.at[2]),
        pltpu.make_async_copy(wqkv_hbm.at[0], w_v.at[0], load_sem.at[3]),
        pltpu.make_async_copy(wout_hbm, wout_v, load_sem.at[4]),
    ]
    for item in loads:
        item.start()
    greet(cp, tp, [near, after, before])
    begin, _ = band_info(lengths_ref, until_ref, cp * rows)
    has_before = begin < chip * 2 * rows
    loads[0].wait()

    @functools.partial(loop, rows // 64)
    def _(i):
        part_rows = rows_of(i, 64)
        v = x_v[part_rows].astype(F32)
        mean = jnp.mean(v, axis=-1, keepdims=True)
        centred = v - mean
        var = jnp.mean(centred * centred, axis=-1, keepdims=True)
        norm_v[part_rows] = (centred * lax.rsqrt(var + EPS) * gains[0:1] + shifts[0:1]).astype(BF16)

    stores = [pltpu.make_async_copy(norm_v, norm_hbm, store_sem.at[0])]
    stores[0].start()
    own = 2 + core

    for load, column in ((1, 0), (2, 1)):
        loads[load].wait()

        @functools.partial(loop, rows // CHUNK)
        def _(i):
            value = dot(norm_v[rows_of(i, CHUNK)], w_v[load])
            if column:
                value = value + bqv[1:2]
            target = pl.ds(pl.multiple_of(own * rows + i * CHUNK, CHUNK), CHUNK)
            kv[target, column * width : (column + 1) * width] = value.astype(BF16)

    def kv_copy(kind, slot, device):
        block = kv.at[rows_of(slot, rows)]
        to = kv.at[rows_of(core, rows)] if kind == 0 else block
        return pltpu.make_async_remote_copy(
            src_ref=block, dst_ref=to, send_sem=kv_send.at[kind], recv_sem=kv_recv.at[kind],
            device_id=device, device_id_type=MESH,
        )

    to_next = kv_copy(0, own, after)
    to_near = kv_copy(1, own, near)
    forward = kv_copy(2, core, near)

    @pl.when(chip < chips - 1)
    def _():
        to_next.start()

    to_near.start()

    @pl.when(chip == 0)
    def _():
        @functools.partial(loop, 2 * rows // 64)
        def _(i):
            kv[rows_of(i, 64)] = jnp.zeros((64, 2 * width), BF16)

    loads[3].wait()

    @functools.partial(loop, rows // CHUNK)
    def _(i):
        part_rows = rows_of(i, CHUNK)
        value = (dot(norm_v[part_rows], w_v[0]) + bqv[0:1]).astype(BF16)
        q_v[part_rows] = value
        turned = (value.astype(F32) * (HD ** -0.5)).T
        upper = lax.broadcasted_iota(jnp.int32, (2 * HD, CHUNK), 0) < HD
        for h in range(heads):
            both = turned[(h // 2) * 2 * HD : (h // 2 + 1) * 2 * HD]
            q_t[h, :, part_rows] = jnp.where(upper == (h % 2 == 0), both, 0.0).astype(BF16)

    stores.append(pltpu.make_async_copy(q_v, q_hbm, store_sem.at[1]))
    stores[1].start()
    to_near.wait_recv()

    def turn_values(slot):
        v_t[:, rows_of(slot, rows)] = kv[rows_of(slot, rows), width:].astype(F32).T.astype(BF16)

    turn_values(2)
    turn_values(3)

    @pl.when(chip > 0)
    def _():
        to_next.wait_recv()
        forward.start()
        forward.wait_recv()

    stores.append(pltpu.make_async_copy(kv, kv_hbm, store_sem.at[2]))
    stores[2].start()
    turn_values(0)
    turn_values(1)
    loads[4].wait()
    line = LineSum(part, slot_a, slot_b, total, ar_send, ar_recv)
    bias = jnp.where(has_before, 0.0, NEG)
    keys = 4 * rows

    for c in range(rows // CHUNK):
        columns = slice(c * CHUNK, (c + 1) * CHUNK)

        def head(h, parity, c=c, columns=columns):
            lanes = pl.ds(pl.multiple_of(lax.div(h, 2) * 2 * HD, 2 * HD), 2 * HD)
            query = q_t[h, :, columns]
            top = jnp.full((1, CHUNK), NEG, F32)
            for b in range(4):
                s = dot(kv[b * rows : (b + 1) * rows, lanes], query)
                if b < 2:
                    s = s + bias
                else:
                    key = lax.broadcasted_iota(jnp.int32, (rows, CHUNK), 0) + (b - 2) * rows
                    row = lax.broadcasted_iota(jnp.int32, (rows, CHUNK), 1) + c * CHUNK
                    s = jnp.where(key <= row + core * rows, s, NEG)
                s_v[b * rows : (b + 1) * rows] = s
                top = jnp.maximum(top, jnp.max(s, axis=0, keepdims=True))
            mass = jnp.zeros((1, CHUNK), F32)
            for b in range(4):
                p = jnp.exp(s_v[b * rows : (b + 1) * rows] - top)
                mass = mass + jnp.sum(p, axis=0, keepdims=True)
                p_v[b * rows : (b + 1) * rows] = p.astype(BF16)
            feature = pl.ds(pl.multiple_of(h * HD, HD), HD)
            att_t[feature, columns] = dot(v_t[feature], p_v[...]) / mass
            lse_out[pl.ds(h, 1), columns] = top + jnp.log(mass)

        loop(heads, lambda h: head(h, 0))
        att_v[columns] = att_t[:, columns].T.astype(BF16)

        @functools.partial(loop, depth // 512)
        def _(t):
            lanes = rows_of(t, 512)
            part[columns, lanes] = dot(att_v[columns], wout_v[:, lanes]).astype(BF16)

        loop(CHUNK // SUB, lambda s, c=c: line.push(s + c * (CHUNK // SUB)))

    stores.append(pltpu.make_async_copy(att_v, att_hbm, store_sem.at[3]))
    stores.append(pltpu.make_async_copy(att_t, att_t_hbm, store_sem.at[4]))
    stores[3].start()
    stores[4].start()
    line.run(0, rows // SUB)
    stores.append(pltpu.make_async_copy(total, sum_hbm, store_sem.at[5]))
    stores[5].start()
    line.drain_all(rows // SUB)

    @pl.when(chip < chips - 1)
    def _():
        to_next.wait_send()

    @pl.when(chip > 0)
    def _():
        forward.wait_send()

    to_near.wait_send()
    for item in stores:
        item.wait()


def attend(x, lengths, until, gains, shifts, wqkv, bqv, wout):
    rows, depth = x.shape
    width = wqkv.shape[2]
    heads = width // HD
    shape = jax.ShapeDtypeStruct
    return pl.pallas_call(
        attend_kernel,
        out_shape=(
            shape((rows, depth), BF16),
            shape((rows, depth), BF16),
            shape((rows, width), BF16),
            shape((4 * rows, 2 * width), BF16),
            shape((rows, width), BF16),
            shape((width, rows), F32),
            shape((heads, rows), F32),
        ),
        in_specs=[ANY, IN_SMEM, IN_SMEM, IN_VMEM, IN_VMEM, ANY, IN_VMEM, ANY],
        out_specs=(ANY,) * 6 + (IN_VMEM,),
        scratch_shapes=[
            pltpu.VMEM((rows, depth), BF16),
            pltpu.VMEM((rows, depth), BF16),
            pltpu.VMEM((3, depth, width), BF16),
            pltpu.VMEM((width, depth), BF16),
            pltpu.VMEM((rows, width), BF16),
            pltpu.VMEM((4 * rows, 2 * width), BF16),
            pltpu.VMEM((heads, 2 * HD, rows), BF16),
            pltpu.VMEM((width, 4 * rows), BF16),
            pltpu.VMEM((4 * rows, CHUNK), F32),
            pltpu.VMEM((4 * rows, CHUNK), BF16),
            pltpu.VMEM((width, rows), F32),
            pltpu.VMEM((rows, width), BF16),
            *line_scratch(rows, depth),
            pltpu.SemaphoreType.DMA((3,)),
            pltpu.SemaphoreType.DMA((3,)),
            pltpu.SemaphoreType.DMA((5,)),
            pltpu.SemaphoreType.DMA((6,)),
        ],
        compiler_params=pltpu.CompilerParams(collective_id=0, has_side_effects=True, vmem_limit_bytes=56 * 2**20),
        name="attend",
    )(x, lengths, until, gains, shifts, wqkv, bqv, wout)


def passed_along(value, axis, steps):
    count = lax.axis_size(axis)
    first, last = (max(0, -steps), min(count, count - steps))
    return lax.ppermute(value, axis, [(source, source + steps) for source in range(first, last)])


def layer_norm(v, gain, shift):
    mean = jnp.mean(v, axis=-1, keepdims=True)
    centred = v - mean
    var = jnp.mean(centred * centred, axis=-1, keepdims=True)
    return centred * lax.rsqrt(var + EPS) * gain + shift


def gelu_tanh(v):
    return jax.nn.gelu(v, approximate=True)


def row_info(seq_lengths, active_until, first, count):
    index = jnp.arange(seq_lengths.shape[0])
    ends = jnp.sum(jnp.where(index[None, :] <= index[:, None], seq_lengths[None, :], 0), axis=1)
    starts = ends - seq_lengths
    rows = first + jnp.arange(count)
    inside = (rows[:, None] >= starts[None, :]) & (rows[:, None] < ends[None, :])
    numbers = jnp.arange(seq_lengths.shape[0])
    segment = jnp.sum(jnp.where(inside, numbers[None, :] + 1, 0), axis=1) - 1
    position = rows - jnp.sum(jnp.where(inside, starts[None, :], 0), axis=1)
    limit = jnp.sum(jnp.where(inside, active_until[None, :], 0), axis=1)
    active = (position < limit).astype(jnp.float32)
    return (rows, segment, active)


def block_scores(query_h, key_h, query_rows, query_seg, key_rows, key_seg, scale):
    scores = jnp.einsum("qhd,khd->hqk", query_h, key_h, preferred_element_type=jnp.float32) * scale
    allowed = (
        (key_rows[None, :] <= query_rows[:, None])
        & (key_seg[None, :] == query_seg[:, None])
        & (key_seg[None, :] >= 0)
    )
    return (jnp.where(allowed[None], scores, NEG), allowed)


def shards(
    layer_input,
    seq_lengths,
    active_until,
    ln_gains,
    ln_shifts,
    query_key_value_weight,
    b_qv,
    w_out,
    b_outs,
    w_up,
    b_up,
    w_down,
    d_out,
):
    rows = layer_input.shape[0]
    width = query_key_value_weight.shape[2]
    heads = width // HD
    scale = HD ** (-0.5)
    bands = lax.axis_size("cp")
    total_rows = rows * bands
    reach = min(LONG, total_rows // 2) // rows - 1
    first = lax.axis_index("cp") * rows
    my_rows, my_seg, active = row_info(seq_lengths, active_until, first, rows)
    gate = active[:, None]
    input_full = layer_input.astype(jnp.float32)
    first_norm_output, ln1_pull = jax.vjp(layer_norm, input_full, ln_gains[0], ln_shifts[0])
    (attn_sum, first_norm_lowered, q_b, kv_all, attended_low, attended_t, lse) = attend(
        layer_input, seq_lengths, active_until, ln_gains, ln_shifts,
        jnp.transpose(query_key_value_weight, (1, 0, 2)), b_qv, w_out,
    )
    q_h = q_b.reshape(rows, heads, HD)
    core = lax.rem(lax.axis_index("cp"), 2)

    def block_of(index):
        block = lax.dynamic_slice_in_dim(kv_all, jnp.maximum(2 + core - index, 0) * rows, rows, 0)
        return (
            block[:, :width].reshape(rows, heads, HD),
            block[:, width:].reshape(rows, heads, HD),
        )

    zero_q = jnp.zeros((rows, heads, HD), jnp.float32)
    combined = attended_t.T.reshape(rows, heads, HD)
    attn = attn_sum.astype(jnp.float32) + b_outs[0]
    hidden_state = input_full + gate * attn
    norm2, ln2_pull = jax.vjp(layer_norm, hidden_state, ln_gains[1], ln_shifts[1])
    norm2_low = norm2.astype(jnp.bfloat16)
    pre = jnp.dot(norm2_low, w_up, preferred_element_type=jnp.float32) + b_up
    act, gelu_pull = jax.vjp(gelu_tanh, pre)
    act_low = act.astype(jnp.bfloat16)
    ffn = (
        lax.psum(
            jnp.dot(act_low, w_down, preferred_element_type=jnp.float32).astype(jnp.bfloat16), "tp"
        ).astype(jnp.float32)
        + b_outs[1]
    )
    out = hidden_state + gate * ffn
    grad_out = d_out.astype(jnp.float32)
    g_ffn = (gate * grad_out).astype(jnp.bfloat16)
    g_act = jnp.einsum("td,fd->tf", g_ffn, w_down, preferred_element_type=jnp.float32)
    g_pre = gelu_pull(g_act)[0].astype(jnp.bfloat16)
    down_term = jnp.einsum("tf,td->fd", act_low, g_ffn, preferred_element_type=jnp.float32)
    up_term = jnp.einsum("td,tf->df", norm2_low, g_pre, preferred_element_type=jnp.float32)
    bup_term = jnp.sum(g_pre.astype(jnp.float32), axis=0)
    g_norm2 = lax.psum(
        jnp.einsum("tf,df->td", g_pre, w_up, preferred_element_type=jnp.float32).astype(
            jnp.bfloat16
        ),
        "tp",
    ).astype(jnp.float32)
    from_norm2, gain2_term, shift2_term = ln2_pull(g_norm2)
    g_hidden = grad_out + from_norm2
    g_attn = (gate * g_hidden).astype(jnp.bfloat16)
    g_attended = jnp.einsum("td,ed->te", g_attn, w_out, preferred_element_type=jnp.float32).astype(
        jnp.bfloat16
    )
    out_term = jnp.einsum("te,td->ed", attended_low, g_attn, preferred_element_type=jnp.float32)
    bouts_term = jnp.stack(
        [jnp.sum(g_attn.astype(jnp.float32), axis=0), jnp.sum(g_ffn.astype(jnp.float32), axis=0)]
    )
    g_att_h = g_attended.reshape(rows, heads, HD)
    delta = jnp.einsum("qhd,qhd->hq", g_att_h.astype(jnp.float32), combined)
    zero_kv = jnp.zeros((rows, 2 * width), jnp.float32)

    def grad_terms(index):
        key_start = first - index * rows

        def grad_work(unused_arg):
            keys3, vals3 = block_of(index)
            key_rows, key_seg, unused = row_info(seq_lengths, active_until, key_start, rows)
            masked, allowed = block_scores(q_h, keys3, my_rows, my_seg, key_rows, key_seg, scale)
            probs = jnp.where(allowed[None], jnp.exp(masked - lse[:, :, None]), 0.0)
            g_probs = jnp.einsum("qhd,khd->hqk", g_att_h, vals3, preferred_element_type=jnp.float32)
            g_scores = (probs * (g_probs - delta[:, :, None])).astype(jnp.bfloat16)
            g_q = (
                jnp.einsum("hqk,khd->qhd", g_scores, keys3, preferred_element_type=jnp.float32)
                * scale
            )
            probs_low = probs.astype(jnp.bfloat16)
            g_k = (
                jnp.einsum("hqk,qhd->khd", g_scores, q_h, preferred_element_type=jnp.float32)
                * scale
            )
            g_v = jnp.einsum("hqk,qhd->khd", probs_low, g_att_h, preferred_element_type=jnp.float32)
            return (
                g_q,
                jnp.concatenate([g_k.reshape(rows, width), g_v.reshape(rows, width)], axis=1),
            )

        def no_terms(unused_arg):
            return (zero_q, zero_kv)

        return lax.cond(key_start >= 0, grad_work, no_terms, 0)

    last_q, last_kv = grad_terms(reach)

    def return_step(step, state):
        g_q_acc, kv_acc = state
        index = reach - 1 - step
        kv_acc = passed_along(kv_acc.astype(jnp.bfloat16), "cp", -1).astype(kv_acc.dtype)
        term_q, term_kv = grad_terms(index)
        return (g_q_acc + term_q, kv_acc + term_kv)

    g_q_sum, kv_sum = lax.fori_loop(0, reach, return_step, (last_q, last_kv))
    g_q_b = g_q_sum.reshape(rows, width).astype(jnp.bfloat16)
    g_k_b = kv_sum[:, :width].astype(jnp.bfloat16)
    g_v_b = kv_sum[:, width:].astype(jnp.bfloat16)
    projection_gradient = jnp.stack([g_q_b, g_k_b, g_v_b], axis=1)
    query_key_value_term = jnp.einsum(
        "hm,hwz->mwz", first_norm_lowered, projection_gradient, preferred_element_type=jnp.float32
    )
    bqv_term = jnp.stack(
        [jnp.sum(g_q_b.astype(jnp.float32), axis=0), jnp.sum(g_v_b.astype(jnp.float32), axis=0)]
    )
    g_norm1 = lax.psum(
        jnp.einsum(
            "wzb,gzb->wg",
            projection_gradient,
            query_key_value_weight,
            preferred_element_type=jnp.float32,
        ).astype(jnp.bfloat16),
        "tp",
    ).astype(jnp.float32)
    from_norm1, gain1_term, shift1_term = ln1_pull(g_norm1)
    g_x = g_hidden + from_norm1
    g_qkv, g_out, g_up, g_down = (
        lax.psum_scatter(
            query_key_value_term.astype(jnp.bfloat16), "cp", scatter_dimension=0, tiled=True
        ).astype(jnp.float32),
        lax.psum_scatter(
            out_term.astype(jnp.bfloat16), "cp", scatter_dimension=1, tiled=True
        ).astype(jnp.float32),
        lax.psum_scatter(
            up_term.astype(jnp.bfloat16), "cp", scatter_dimension=0, tiled=True
        ).astype(jnp.float32),
        lax.psum_scatter(
            down_term.astype(jnp.bfloat16), "cp", scatter_dimension=1, tiled=True
        ).astype(jnp.float32),
    )
    g_ln_gains, g_ln_shifts, g_bqv, g_bup, g_bouts = (
        lax.psum(jnp.stack([gain1_term, gain2_term]).astype(jnp.bfloat16), "cp").astype(
            jnp.float32
        ),
        lax.psum(jnp.stack([shift1_term, shift2_term]).astype(jnp.bfloat16), "cp").astype(
            jnp.float32
        ),
        lax.psum(bqv_term.astype(jnp.bfloat16), "cp").astype(jnp.float32),
        lax.psum(bup_term.astype(jnp.bfloat16), "cp").astype(jnp.float32),
        lax.psum(bouts_term.astype(jnp.bfloat16), "cp").astype(jnp.float32),
    )
    return (out, g_x, g_ln_gains, g_ln_shifts, g_qkv, g_bqv, g_out, g_bouts, g_up, g_bup, g_down)


def solution(mesh):
    return jax.shard_map(
        shards,
        mesh=mesh,
        in_specs=(
            P("cp", None),
            P(),
            P(),
            P(),
            P(),
            P(None, None, "tp"),
            P(None, "tp"),
            P("tp", None),
            P(),
            P(None, "tp"),
            P("tp"),
            P("tp", None),
            P("cp", None),
        ),
        out_specs=(
            P("cp", None),
            P("cp", None),
            P(),
            P(),
            P("cp", None, "tp"),
            P(None, "tp"),
            P("tp", "cp"),
            P(),
            P("cp", "tp"),
            P("tp"),
            P("tp", "cp"),
        ),
        check_vma=False,
    )
```

```python
import functools
import math

import jax
import jax.numpy as jnp
from jax import lax
from jax.experimental import pallas as pl
from jax.experimental.pallas import tpu as pltpu
from jax.sharding import PartitionSpec as P

HD = 64
LONG = 2048
EPS = 1e-05
NEG = -1e30
MESH = pl.DeviceIdType.MESH
F32 = jnp.float32
BF16 = jnp.bfloat16
ANY = pl.BlockSpec(memory_space=pl.ANY)
IN_VMEM = pl.BlockSpec(memory_space=pltpu.VMEM)
IN_SMEM = pl.BlockSpec(memory_space=pltpu.SMEM)
SUB = 32
CHUNK = 256


def dot(a, b):
    return jnp.dot(a, b, preferred_element_type=F32)


def dot_nt(a, b):
    return lax.dot_general(a, b, (((1,), (1,)), ((), ())), preferred_element_type=F32)


def dot_tn(a, b):
    return lax.dot_general(a, b, (((0,), (0,)), ((), ())), preferred_element_type=F32)


def rows_of(index, size):
    return pl.ds(pl.multiple_of(index * size, size), size)


def place():
    cp = lax.axis_index("cp")
    tp = lax.axis_index("tp")
    return cp, tp, lax.rem(cp, 2), lax.div(cp, 2)


def greet(cp, tp, others):
    barrier = pltpu.get_barrier_semaphore()
    edge = (tp == 0) | (tp == 3)
    for other in [*others, (cp, line_near(tp))]:
        pl.semaphore_signal(barrier, inc=1, device_id=other, device_id_type=MESH)

    @pl.when(jnp.logical_not(edge))
    def _():
        pl.semaphore_signal(barrier, inc=1, device_id=(cp, 3 - tp), device_id_type=MESH)

    pl.semaphore_wait(barrier, len(others) + jnp.where(edge, 1, 2))


def line_near(tp):
    return jnp.where(tp == 0, 1, jnp.where(tp == 1, 0, jnp.where(tp == 2, 3, 2)))


class LineSum:
    def __init__(self, part, slot_a, slot_b, total, send, recv):
        self.cp, self.tp, _, _ = place()
        self.edge = (self.tp == 0) | (self.tp == 3)
        self.refs = (part, slot_a, slot_b, total)
        self.send, self.recv = send, recv

    def copy(self, kind, s):
        part, slot_a, slot_b, total = self.refs
        src, dst = ((part, slot_a), (part, slot_b), (total, total))[kind]
        other = (self.cp, 3 - self.tp if kind == 1 else line_near(self.tp))
        rows = rows_of(s, SUB)
        return pltpu.make_async_remote_copy(
            src_ref=src.at[rows],
            dst_ref=dst.at[rows],
            send_sem=self.send.at[kind, s],
            recv_sem=self.recv.at[kind, s],
            device_id=other,
            device_id_type=MESH,
        )

    def push(self, s):
        @pl.when(self.edge)
        def _():
            self.copy(0, s).start()

    def relay_in(self, s):
        part, slot_a, _, _ = self.refs

        @pl.when(jnp.logical_not(self.edge))
        def _():
            rows = rows_of(s, SUB)
            self.copy(0, s).wait_recv()
            part[rows] = (part[rows].astype(F32) + slot_a[rows].astype(F32)).astype(BF16)
            self.copy(1, s).start()

    def relay_out(self, s):
        part, _, slot_b, total = self.refs

        @pl.when(jnp.logical_not(self.edge))
        def _():
            rows = rows_of(s, SUB)
            self.copy(1, s).wait_recv()
            total[rows] = (part[rows].astype(F32) + slot_b[rows].astype(F32)).astype(BF16)
            self.copy(2, s).start()

    def get(self, s):
        @pl.when(self.edge)
        def _():
            self.copy(2, s).wait_recv()

    def drain(self, s):
        @pl.when(self.edge)
        def _():
            self.copy(0, s).wait_send()

        @pl.when(jnp.logical_not(self.edge))
        def _():
            self.copy(1, s).wait_send()
            self.copy(2, s).wait_send()

    def run(self, first, last):
        def step(s, carry):
            @pl.when(s < last)
            def _():
                self.relay_in(s)

            @pl.when(s > first)
            def _():
                self.relay_out(s - 1)
                self.get(s - 1)

            return carry

        lax.fori_loop(first, last + 1, step, 0)

    def drain_all(self, count):
        def step(s, carry):
            self.drain(s)
            return carry

        lax.fori_loop(0, count, step, 0)


def line_scratch(rows, width, with_part=True):
    count = rows // SUB
    return [pltpu.VMEM((rows, width), BF16)] * 4 + [
        pltpu.SemaphoreType.DMA((3, count)),
        pltpu.SemaphoreType.DMA((3, count)),
    ]


def band_info(lengths_ref, until_ref, first):
    start = jnp.int32(0)
    begin = jnp.int32(0)
    until = jnp.int32(0)
    for i in range(lengths_ref.shape[0]):
        length = lengths_ref[i]
        inside = (first >= start) & (first < start + length)
        begin = jnp.where(inside, start, begin)
        until = jnp.where(inside, until_ref[i], until)
        start = start + length
    return begin, until + begin - first


def loop(count, body):
    def step(i, carry):
        body(i)
        return carry

    lax.fori_loop(0, count, step, 0)


def attend_kernel(
    x_hbm, lengths_ref, until_ref, gains, shifts, wqkv_hbm, bqv, wout_hbm,
    sum_hbm, norm_hbm, q_hbm, kv_hbm, att_hbm, att_t_hbm, lse_out,
    x_v, norm_v, w_v, wout_v, q_v, kv, q_t, v_t, s_v, p_v, att_t, att_v,
    part, slot_a, slot_b, total, ar_send, ar_recv, kv_send, kv_recv, load_sem, store_sem,
):
    cp, tp, core, chip = place()
    bands = lax.axis_size("cp")
    chips = bands // 2
    rows, depth = x_v.shape
    width = q_v.shape[1]
    heads = width // HD
    near = (cp + 1 - 2 * core, tp)
    after = (lax.rem(cp + 2, bands), tp)
    before = (lax.rem(cp + bands - 2, bands), tp)
    loads = [
        pltpu.make_async_copy(x_hbm, x_v, load_sem.at[0]),
        pltpu.make_async_copy(wqkv_hbm.at[1], w_v.at[1], load_sem.at[1]),
        pltpu.make_async_copy(wqkv_hbm.at[2], w_v.at[2], load_sem.at[2]),
        pltpu.make_async_copy(wqkv_hbm.at[0], w_v.at[0], load_sem.at[3]),
        pltpu.make_async_copy(wout_hbm, wout_v, load_sem.at[4]),
    ]
    for item in loads:
        item.start()
    greet(cp, tp, [near, after, before])
    begin, _ = band_info(lengths_ref, until_ref, cp * rows)
    has_before = begin < chip * 2 * rows
    loads[0].wait()

    @functools.partial(loop, rows // 64)
    def _(i):
        part_rows = rows_of(i, 64)
        v = x_v[part_rows].astype(F32)
        mean = jnp.mean(v, axis=-1, keepdims=True)
        centred = v - mean
        var = jnp.mean(centred * centred, axis=-1, keepdims=True)
        norm_v[part_rows] = (centred * lax.rsqrt(var + EPS) * gains[0:1] + shifts[0:1]).astype(BF16)

    stores = [pltpu.make_async_copy(norm_v, norm_hbm, store_sem.at[0])]
    stores[0].start()
    own = 2 + core

    for load, column in ((1, 0), (2, 1)):
        loads[load].wait()

        @functools.partial(loop, rows // CHUNK)
        def _(i):
            value = dot(norm_v[rows_of(i, CHUNK)], w_v[load])
            if column:
                value = value + bqv[1:2]
            target = pl.ds(pl.multiple_of(own * rows + i * CHUNK, CHUNK), CHUNK)
            kv[target, column * width : (column + 1) * width] = value.astype(BF16)

    def kv_copy(kind, slot, device):
        block = kv.at[rows_of(slot, rows)]
        to = kv.at[rows_of(core, rows)] if kind == 0 else block
        return pltpu.make_async_remote_copy(
            src_ref=block, dst_ref=to, send_sem=kv_send.at[kind], recv_sem=kv_recv.at[kind],
            device_id=device, device_id_type=MESH,
        )

    to_next = kv_copy(0, own, after)
    to_near = kv_copy(1, own, near)
    forward = kv_copy(2, core, near)

    @pl.when(chip < chips - 1)
    def _():
        to_next.start()

    to_near.start()

    @pl.when(chip == 0)
    def _():
        @functools.partial(loop, 2 * rows // 64)
        def _(i):
            kv[rows_of(i, 64)] = jnp.zeros((64, 2 * width), BF16)

    loads[3].wait()

    @functools.partial(loop, rows // CHUNK)
    def _(i):
        part_rows = rows_of(i, CHUNK)
        value = (dot(norm_v[part_rows], w_v[0]) + bqv[0:1]).astype(BF16)
        q_v[part_rows] = value
        turned = (value.astype(F32) * (HD ** -0.5)).T
        upper = lax.broadcasted_iota(jnp.int32, (2 * HD, CHUNK), 0) < HD
        for h in range(heads):
            both = turned[(h // 2) * 2 * HD : (h // 2 + 1) * 2 * HD]
            q_t[h, :, part_rows] = jnp.where(upper == (h % 2 == 0), both, 0.0).astype(BF16)

    stores.append(pltpu.make_async_copy(q_v, q_hbm, store_sem.at[1]))
    stores[1].start()
    to_near.wait_recv()

    def turn_values(slot):
        v_t[:, rows_of(slot, rows)] = kv[rows_of(slot, rows), width:].astype(F32).T.astype(BF16)

    turn_values(2)
    turn_values(3)

    @pl.when(chip > 0)
    def _():
        to_next.wait_recv()
        forward.start()
        forward.wait_recv()

    stores.append(pltpu.make_async_copy(kv, kv_hbm, store_sem.at[2]))
    stores[2].start()
    turn_values(0)
    turn_values(1)
    loads[4].wait()
    line = LineSum(part, slot_a, slot_b, total, ar_send, ar_recv)
    bias = jnp.where(has_before, 0.0, NEG)
    keys = 4 * rows

    for c in range(rows // CHUNK):
        columns = slice(c * CHUNK, (c + 1) * CHUNK)

        def head(h, parity, c=c, columns=columns):
            lanes = pl.ds(pl.multiple_of(lax.div(h, 2) * 2 * HD, 2 * HD), 2 * HD)
            query = q_t[h, :, columns]
            top = jnp.full((1, CHUNK), NEG, F32)
            for b in range(4):
                s = dot(kv[b * rows : (b + 1) * rows, lanes], query)
                if b < 2:
                    s = s + bias
                else:
                    key = lax.broadcasted_iota(jnp.int32, (rows, CHUNK), 0) + (b - 2) * rows
                    row = lax.broadcasted_iota(jnp.int32, (rows, CHUNK), 1) + c * CHUNK
                    s = jnp.where(key <= row + core * rows, s, NEG)
                s_v[b * rows : (b + 1) * rows] = s
                top = jnp.maximum(top, jnp.max(s, axis=0, keepdims=True))
            mass = jnp.zeros((1, CHUNK), F32)
            for b in range(4):
                p = jnp.exp(s_v[b * rows : (b + 1) * rows] - top)
                mass = mass + jnp.sum(p, axis=0, keepdims=True)
                p_v[b * rows : (b + 1) * rows] = p.astype(BF16)
            feature = pl.ds(pl.multiple_of(h * HD, HD), HD)
            att_t[feature, columns] = dot(v_t[feature], p_v[...]) / mass
            lse_out[pl.ds(h, 1), columns] = top + jnp.log(mass)

        loop(heads, lambda h: head(h, 0))
        att_v[columns] = att_t[:, columns].T.astype(BF16)

        @functools.partial(loop, depth // 512)
        def _(t):
            lanes = rows_of(t, 512)
            part[columns, lanes] = dot(att_v[columns], wout_v[:, lanes]).astype(BF16)

        loop(CHUNK // SUB, lambda s, c=c: line.push(s + c * (CHUNK // SUB)))

    stores.append(pltpu.make_async_copy(att_v, att_hbm, store_sem.at[3]))
    stores.append(pltpu.make_async_copy(att_t, att_t_hbm, store_sem.at[4]))
    stores[3].start()
    stores[4].start()
    line.run(0, rows // SUB)
    stores.append(pltpu.make_async_copy(total, sum_hbm, store_sem.at[5]))
    stores[5].start()
    line.drain_all(rows // SUB)

    @pl.when(chip < chips - 1)
    def _():
        to_next.wait_send()

    @pl.when(chip > 0)
    def _():
        forward.wait_send()

    to_near.wait_send()
    for item in stores:
        item.wait()


def attend(x, lengths, until, gains, shifts, wqkv, bqv, wout):
    rows, depth = x.shape
    width = wqkv.shape[2]
    heads = width // HD
    shape = jax.ShapeDtypeStruct
    return pl.pallas_call(
        attend_kernel,
        out_shape=(
            shape((rows, depth), BF16),
            shape((rows, depth), BF16),
            shape((rows, width), BF16),
            shape((4 * rows, 2 * width), BF16),
            shape((rows, width), BF16),
            shape((width, rows), F32),
            shape((heads, rows), F32),
        ),
        in_specs=[ANY, IN_SMEM, IN_SMEM, IN_VMEM, IN_VMEM, ANY, IN_VMEM, ANY],
        out_specs=(ANY,) * 6 + (IN_VMEM,),
        scratch_shapes=[
            pltpu.VMEM((rows, depth), BF16),
            pltpu.VMEM((rows, depth), BF16),
            pltpu.VMEM((3, depth, width), BF16),
            pltpu.VMEM((width, depth), BF16),
            pltpu.VMEM((rows, width), BF16),
            pltpu.VMEM((4 * rows, 2 * width), BF16),
            pltpu.VMEM((heads, 2 * HD, rows), BF16),
            pltpu.VMEM((width, 4 * rows), BF16),
            pltpu.VMEM((4 * rows, CHUNK), F32),
            pltpu.VMEM((4 * rows, CHUNK), BF16),
            pltpu.VMEM((width, rows), F32),
            pltpu.VMEM((rows, width), BF16),
            *line_scratch(rows, depth),
            pltpu.SemaphoreType.DMA((3,)),
            pltpu.SemaphoreType.DMA((3,)),
            pltpu.SemaphoreType.DMA((5,)),
            pltpu.SemaphoreType.DMA((6,)),
        ],
        compiler_params=pltpu.CompilerParams(collective_id=0, has_side_effects=True, vmem_limit_bytes=56 * 2**20),
        name="attend",
    )(x, lengths, until, gains, shifts, wqkv, bqv, wout)


class Scatter:
    def __init__(self, terms, near, far, send, recv, split):
        self.cp, self.tp, self.core, self.chip = place()
        self.count = lax.axis_size("cp")
        self.depth = (self.count // 2).bit_length() - 1
        self.terms, self.near, self.far = terms, near, far
        self.send, self.recv = send, recv
        self.chunk = terms.shape[0] // self.count
        self.width = terms.shape[1]
        self.parts = [p for p in ((0, 0, split), (1, split, self.width)) if p[2] > p[1]]
        self.block = max(self.chunk, 128)

    def partners(self):
        others = [(self.cp + 1 - 2 * self.core, self.tp)]
        for bit in range(self.depth):
            others.append((self.cp + 2 * self.step(bit), self.tp))
        return others

    def step(self, bit):
        return (1 - 2 * self.bit(bit)) * (1 << bit)

    def bit(self, bit):
        return lax.rem(lax.div(self.chip, 1 << bit), 2)

    def fill(self, k, pick):
        if self.block == self.chunk:
            half = self.count // 2
            block = 2 * lax.rem(k, half) + jnp.where(k < half, 1 - self.core, self.core)
        else:
            block = k
        rows = rows_of(block, self.block)
        for tile in range(self.width // 512):
            lanes = slice(tile * 512, (tile + 1) * 512)
            left, right = pick(tile, rows)
            self.terms[rows, lanes] = dot_tn(left, right).astype(BF16)

    def blocks(self):
        return self.terms.shape[0] // self.block

    def near_copy(self, t):
        return pltpu.make_async_remote_copy(
            src_ref=self.terms.at[rows_of(2 * t + 1 - self.core, self.chunk)],
            dst_ref=self.near.at[rows_of(t, self.chunk)],
            send_sem=self.send.at[t],
            recv_sem=self.recv.at[t],
            device_id=(self.cp + 1 - 2 * self.core, self.tp),
            device_id_type=MESH,
        )

    def send_near(self, t):
        self.near_copy(t).start()

    def add_near(self, t):
        self.near_copy(t).wait_recv()
        base = (2 * t + self.core) * self.chunk

        @functools.partial(loop, self.chunk // 64)
        def _(i):
            mine = pl.ds(pl.multiple_of(base + i * 64, 64), 64)
            other = pl.ds(pl.multiple_of(t * self.chunk + i * 64, 64), 64)
            self.terms[mine] = (self.terms[mine].astype(F32) + self.near[other].astype(F32)).astype(BF16)

    def index(self, part, level, t, keep):
        bit = level - 1 if part == 0 else self.depth - level
        own = self.bit(bit)
        own = own if keep else 1 - own
        if part == 0:
            return lax.rem(self.chip, 1 << bit) + own * (1 << bit) + t * (2 << bit), bit
        return self.chip - lax.rem(self.chip, 2 << bit) + own * (1 << bit) + t, bit

    def pieces(self, level):
        first = self.count // 2
        for earlier in range(1, level):
            first += len(self.parts) * (1 << (self.depth - earlier))
        for part, low, high in self.parts:
            for t in range(1 << (self.depth - level)):
                yield part, slice(low, high), t, first
                first += 1

    def far_copy(self, level, part, lanes, t, sem):
        index, bit = self.index(part, level, t, False)
        return pltpu.make_async_remote_copy(
            src_ref=self.terms.at[rows_of(2 * index + self.core, self.chunk), lanes],
            dst_ref=self.far.at[pl.ds(self.place(level) + t * self.chunk, self.chunk), lanes],
            send_sem=self.send.at[sem],
            recv_sem=self.recv.at[sem],
            device_id=(self.cp + 2 * self.step(bit), self.tp),
            device_id_type=MESH,
        )

    def send_far(self, level):
        for piece in self.pieces(level):
            self.far_copy(level, *piece).start()

    def add_far(self, level):
        for part, lanes, t, sem in self.pieces(level):
            self.far_copy(level, part, lanes, t, sem).wait_recv()
            index, _ = self.index(part, level, t, True)
            base = (2 * index + self.core) * self.chunk
            there = self.place(level) + t * self.chunk

            @functools.partial(loop, self.chunk // 64)
            def _(i, base=base, lanes=lanes, there=there):
                mine = pl.ds(pl.multiple_of(base + i * 64, 64), 64)
                other = pl.ds(pl.multiple_of(there + i * 64, 64), 64)
                self.terms[mine, lanes] = (
                    self.terms[mine, lanes].astype(F32) + self.far[other, lanes].astype(F32)
                ).astype(BF16)

    def place(self, level):
        return sum(self.terms.shape[0] >> (earlier + 1) for earlier in range(1, level))

    def finish(self, write):
        level = self.depth
        mine = rows_of(self.cp, self.chunk)
        for part, lanes, t, sem in self.pieces(level):
            self.far_copy(level, part, lanes, t, sem).wait_recv()
            for tile in range(lanes.start // 512, lanes.stop // 512):
                cut = slice(tile * 512, (tile + 1) * 512)
                other = pl.ds(self.place(level), self.chunk)
                write(tile, self.terms[mine, cut].astype(F32) + self.far[other, cut].astype(F32))

    def drain(self):
        loop(self.count // 2, lambda t: self.near_copy(t).wait_send())
        for level in range(1, self.depth + 1):
            for piece in self.pieces(level):
                self.far_copy(level, *piece).wait_send()


def scatter_scratch(depth, width, split):
    count = lax.axis_size("cp")
    parts = (split > 0) + (split < width)
    sems = count // 2 + parts * (count // 2 - 1)
    return [
        pltpu.VMEM((depth // 2, width), BF16),
        pltpu.VMEM((depth // 2 - depth // count, width), BF16),
        pltpu.SemaphoreType.DMA((sems,)),
        pltpu.SemaphoreType.DMA((sems,)),
    ]


def fold(v):
    return jnp.sum(v.reshape(v.shape[0] // 8, 8, v.shape[1]), axis=0)


def gelu_parts(u):
    root = math.sqrt(2.0 / math.pi)
    square = u * u
    th = jnp.tanh(root * (u + 0.044715 * u * square))
    half = 0.5 * (1.0 + th)
    return u * half, half + 0.5 * u * (1.0 - th * th) * (root * (1.0 + 3 * 0.044715 * square))


LAG = 4
SPLIT_DOWN = 1024


def ffn_kernel(
    sum_hbm, x_hbm, d_hbm, lengths_ref, until_ref, gains, shifts, b_outs, b_up, up_hbm, down_hbm,
    norm_hbm, g_pre_hbm, ffn_hbm, g_hidden_hbm, g_attn_hbm, sums_out, down_out,
    up_v, down_v, d_v, xhat, rstd, norm_v, act_v, g_pre_v, g_ffn_v, ffn_v, g_hidden, g_attn, acc,
    part, slot_a, slot_b, total, ar_send, ar_recv, near, far, rs_send, rs_recv, load_sem, store_sem,
):
    cp, tp, core, chip = place()
    rows, depth = d_v.shape
    hidden = up_v.shape[1]
    count = rows // SUB
    loads = [
        pltpu.make_async_copy(x_hbm, g_attn, load_sem.at[0]),
        pltpu.make_async_copy(sum_hbm, ffn_v, load_sem.at[1]),
        pltpu.make_async_copy(d_hbm, d_v, load_sem.at[2]),
        pltpu.make_async_copy(up_hbm, up_v, load_sem.at[3]),
        pltpu.make_async_copy(down_hbm, down_v, load_sem.at[4]),
    ]
    for item in loads:
        item.start()
    line = LineSum(part, slot_a, slot_b, total, ar_send, ar_recv)
    scatter = Scatter(up_v, near, far, rs_send, rs_recv, SPLIT_DOWN)
    greet(cp, tp, scatter.partners())
    _, live = band_info(lengths_ref, until_ref, cp * rows)
    acc[...] = jnp.zeros_like(acc)
    for item in loads[:3]:
        item.wait()

    for c in range(rows // CHUNK):
        chunk = slice(c * CHUNK, (c + 1) * CHUNK)

        @functools.partial(loop, CHUNK // 64)
        def _(i, c=c):
            at = pl.ds(pl.multiple_of(c * CHUNK + i * 64, 64), 64)
            row = lax.broadcasted_iota(jnp.int32, (64, 1), 0) + (c * CHUNK + i * 64)
            on = row < live
            branch = ffn_v[at].astype(F32) + b_outs[0:1]
            v = g_attn[at].astype(F32) + jnp.where(on, branch, 0.0)
            mean = jnp.mean(v, axis=-1, keepdims=True)
            centred = v - mean
            scale = lax.rsqrt(jnp.mean(centred * centred, axis=-1, keepdims=True) + EPS)
            hat = centred * scale
            xhat[at] = hat
            rstd[at] = jnp.broadcast_to(scale, (64, 128))
            norm_v[at] = (hat * gains[1:2] + shifts[1:2]).astype(BF16)
            g_ffn = jnp.where(on, d_v[at].astype(F32), 0.0)
            g_ffn_v[at] = g_ffn.astype(BF16)
            acc[3] += fold(g_ffn)

        if c == 0:
            loads[3].wait()
            loads[4].wait()

        @functools.partial(loop, hidden // 512)
        def _(t, c=c, chunk=chunk):
            lanes = rows_of(t, 512)
            pre = dot(norm_v[chunk], up_v[:, lanes]) + b_up[0:1, lanes]
            g_act = dot_nt(g_ffn_v[chunk], down_v[lanes])
            act, slope = gelu_parts(pre)
            act_v[chunk, lanes] = act.astype(BF16)
            g_pre = (g_act * slope).astype(BF16)
            g_pre_v[chunk, lanes] = g_pre
            acc[4, :, lanes] += fold(g_pre.astype(F32))
            if c > 0:
                line.relay_in(t)

                @pl.when(t > 0)
                def _():
                    line.relay_out(t - 1)

        @functools.partial(loop, depth // 512)
        def _(t, chunk=chunk):
            lanes = rows_of(t, 512)
            part[chunk, lanes] = dot_nt(g_pre_v[chunk], up_v[lanes]).astype(BF16)

        loop(CHUNK // SUB, lambda s, c=c: line.push(s + c * (CHUNK // SUB)))

    stores = [
        pltpu.make_async_copy(norm_v, norm_hbm, store_sem.at[0]),
        pltpu.make_async_copy(g_pre_v, g_pre_hbm, store_sem.at[1]),
        pltpu.make_async_copy(ffn_v, ffn_hbm, store_sem.at[2]),
        pltpu.make_async_copy(g_hidden, g_hidden_hbm, store_sem.at[3]),
        pltpu.make_async_copy(g_attn, g_attn_hbm, store_sem.at[4]),
    ]
    stores[0].start()
    stores[1].start()

    def back(s):
        line.get(s)
        at = rows_of(s, SUB)
        e = total[at].astype(F32)
        hat = xhat[at]
        t = e * gains[1:2]
        along = t - jnp.mean(t, axis=-1, keepdims=True) - hat * jnp.mean(t * hat, axis=-1, keepdims=True)
        value = d_v[at].astype(F32) + along * rstd[at, 0:1]
        g_hidden[at] = value
        row = lax.broadcasted_iota(jnp.int32, (SUB, 1), 0) + s * SUB
        low = jnp.where(row < live, value, 0.0).astype(BF16)
        g_attn[at] = low
        acc[0] += fold(e * hat)
        acc[1] += fold(e)
        acc[2] += fold(low.astype(F32))

    def ahead(s):
        @pl.when(s < count)
        def _():
            line.relay_in(s)

        line.relay_out(s - 1)
        back(s - LAG)

    def term(k):
        scatter.fill(k, lambda tile, rows: (g_ffn_v[:, rows], act_v[:, tile * 512 : (tile + 1) * 512]))

    def project(k):
        chunk = rows_of(lax.div(k, depth // 512), CHUNK)
        lanes = rows_of(lax.rem(k, depth // 512), 512)
        ffn_v[chunk, lanes] = dot(act_v[chunk], down_v[:, lanes]).astype(BF16)

    blocks, half = scatter.blocks(), scatter.count // 2

    @functools.partial(loop, 4)
    def _(i):
        loop(blocks // 4, lambda j: term(i * (blocks // 4) + j))

        @pl.when((i == 1) if scatter.block == scatter.chunk else (i == 3))
        def _():
            loop(half, scatter.send_near)

        ahead(4 + i)

    @functools.partial(loop, 2)
    def _(i):
        loop(half // 2, lambda j: scatter.add_near(i * (half // 2) + j))
        ahead(8 + i)

    scatter.send_far(1)

    @functools.partial(loop, 4)
    def _(i):
        project(2 * i)
        project(2 * i + 1)
        ahead(10 + i)

    stores[2].start()
    loop(count - 13, lambda i: ahead(14 + i))
    loop(LAG - 1, lambda i: back(count - LAG + 1 + i))
    stores[3].start()
    stores[4].start()
    for level in range(1, scatter.depth):
        scatter.add_far(level)
        scatter.send_far(level + 1)

    for k in range(5):
        sums_out[k : k + 1] = jnp.sum(acc[k], axis=0, keepdims=True)

    sums_out[5:8] = jnp.zeros((3, sums_out.shape[1]), F32)

    def write(tile, value):
        down_out[tile * 512 : (tile + 1) * 512] = value.T

    scatter.finish(write)
    scatter.drain()
    line.drain_all(count)
    for item in stores:
        item.wait()


def ffn(attn_sum, x, d_out, lengths, until, gains, shifts, b_outs, b_up, w_up, w_down):
    rows, depth = x.shape
    hidden = w_up.shape[1]
    chunk = depth // lax.axis_size("cp")
    shape = jax.ShapeDtypeStruct
    return pl.pallas_call(
        ffn_kernel,
        out_shape=(
            shape((rows, depth), BF16),
            shape((rows, hidden), BF16),
            shape((rows, depth), BF16),
            shape((rows, depth), F32),
            shape((rows, depth), BF16),
            shape((8, depth), F32),
            shape((hidden, chunk), F32),
        ),
        in_specs=[ANY, ANY, ANY, IN_SMEM, IN_SMEM, IN_VMEM, IN_VMEM, IN_VMEM, IN_VMEM, ANY, ANY],
        out_specs=(ANY,) * 5 + (IN_VMEM,) * 2,
        scratch_shapes=[
            pltpu.VMEM((depth, hidden), BF16),
            pltpu.VMEM((hidden, depth), BF16),
            pltpu.VMEM((rows, depth), BF16),
            pltpu.VMEM((rows, depth), F32),
            pltpu.VMEM((rows, 128), F32),
            pltpu.VMEM((rows, depth), BF16),
            pltpu.VMEM((rows, hidden), BF16),
            pltpu.VMEM((rows, hidden), BF16),
            pltpu.VMEM((rows, depth), BF16),
            pltpu.VMEM((rows, depth), BF16),
            pltpu.VMEM((rows, depth), F32),
            pltpu.VMEM((rows, depth), BF16),
            pltpu.VMEM((5, 8, depth), F32),
            *line_scratch(rows, depth),
            *scatter_scratch(depth, hidden, SPLIT_DOWN),
            pltpu.SemaphoreType.DMA((5,)),
            pltpu.SemaphoreType.DMA((5,)),
        ],
        compiler_params=pltpu.CompilerParams(collective_id=1, has_side_effects=True, vmem_limit_bytes=62 * 2**20),
        name="ffn",
    )(attn_sum, x, d_out, lengths, until, gains, shifts, b_outs, b_up, w_up, w_down)


def passed_along(value, axis, steps):
    count = lax.axis_size(axis)
    first, last = (max(0, -steps), min(count, count - steps))
    return lax.ppermute(value, axis, [(source, source + steps) for source in range(first, last)])


def layer_norm(v, gain, shift):
    mean = jnp.mean(v, axis=-1, keepdims=True)
    centred = v - mean
    var = jnp.mean(centred * centred, axis=-1, keepdims=True)
    return centred * lax.rsqrt(var + EPS) * gain + shift


def row_info(seq_lengths, active_until, first, count):
    index = jnp.arange(seq_lengths.shape[0])
    ends = jnp.sum(jnp.where(index[None, :] <= index[:, None], seq_lengths[None, :], 0), axis=1)
    starts = ends - seq_lengths
    rows = first + jnp.arange(count)
    inside = (rows[:, None] >= starts[None, :]) & (rows[:, None] < ends[None, :])
    numbers = jnp.arange(seq_lengths.shape[0])
    segment = jnp.sum(jnp.where(inside, numbers[None, :] + 1, 0), axis=1) - 1
    position = rows - jnp.sum(jnp.where(inside, starts[None, :], 0), axis=1)
    limit = jnp.sum(jnp.where(inside, active_until[None, :], 0), axis=1)
    active = (position < limit).astype(jnp.float32)
    return (rows, segment, active)


def block_scores(query_h, key_h, query_rows, query_seg, key_rows, key_seg, scale):
    scores = jnp.einsum("qhd,khd->hqk", query_h, key_h, preferred_element_type=jnp.float32) * scale
    allowed = (
        (key_rows[None, :] <= query_rows[:, None])
        & (key_seg[None, :] == query_seg[:, None])
        & (key_seg[None, :] >= 0)
    )
    return (jnp.where(allowed[None], scores, NEG), allowed)


def shards(
    layer_input,
    seq_lengths,
    active_until,
    ln_gains,
    ln_shifts,
    query_key_value_weight,
    b_qv,
    w_out,
    b_outs,
    w_up,
    b_up,
    w_down,
    d_out,
):
    rows = layer_input.shape[0]
    width = query_key_value_weight.shape[2]
    heads = width // HD
    scale = HD ** (-0.5)
    bands = lax.axis_size("cp")
    total_rows = rows * bands
    reach = min(LONG, total_rows // 2) // rows - 1
    first = lax.axis_index("cp") * rows
    my_rows, my_seg, active = row_info(seq_lengths, active_until, first, rows)
    gate = active[:, None]
    input_full = layer_input.astype(jnp.float32)
    first_norm_output, ln1_pull = jax.vjp(layer_norm, input_full, ln_gains[0], ln_shifts[0])
    (attn_sum, first_norm_lowered, q_b, kv_all, attended_low, attended_t, lse) = attend(
        layer_input, seq_lengths, active_until, ln_gains, ln_shifts,
        jnp.transpose(query_key_value_weight, (1, 0, 2)), b_qv, w_out,
    )
    q_h = q_b.reshape(rows, heads, HD)
    core = lax.rem(lax.axis_index("cp"), 2)

    def block_of(index):
        block = lax.dynamic_slice_in_dim(kv_all, jnp.maximum(2 + core - index, 0) * rows, rows, 0)
        return (
            block[:, :width].reshape(rows, heads, HD),
            block[:, width:].reshape(rows, heads, HD),
        )

    zero_q = jnp.zeros((rows, heads, HD), jnp.float32)
    combined = attended_t.T.reshape(rows, heads, HD)
    (norm2_low, g_pre, ffn_low, g_hidden, g_attn, sums2, down_part) = ffn(
        attn_sum, layer_input, d_out, seq_lengths, active_until, ln_gains, ln_shifts, b_outs, b_up[None], w_up, w_down
    )
    hidden_state = input_full + gate * (attn_sum.astype(jnp.float32) + b_outs[0])
    out = hidden_state + gate * (lax.psum(ffn_low, "tp").astype(jnp.float32) + b_outs[1])
    up_term = jnp.einsum("td,tf->df", norm2_low, g_pre, preferred_element_type=jnp.float32)
    g_attended = jnp.einsum("td,ed->te", g_attn, w_out, preferred_element_type=jnp.float32).astype(
        jnp.bfloat16
    )
    out_term = jnp.einsum("te,td->ed", attended_low, g_attn, preferred_element_type=jnp.float32)
    g_att_h = g_attended.reshape(rows, heads, HD)
    delta = jnp.einsum("qhd,qhd->hq", g_att_h.astype(jnp.float32), combined)
    zero_kv = jnp.zeros((rows, 2 * width), jnp.float32)

    def grad_terms(index):
        key_start = first - index * rows

        def grad_work(unused_arg):
            keys3, vals3 = block_of(index)
            key_rows, key_seg, unused = row_info(seq_lengths, active_until, key_start, rows)
            masked, allowed = block_scores(q_h, keys3, my_rows, my_seg, key_rows, key_seg, scale)
            probs = jnp.where(allowed[None], jnp.exp(masked - lse[:, :, None]), 0.0)
            g_probs = jnp.einsum("qhd,khd->hqk", g_att_h, vals3, preferred_element_type=jnp.float32)
            g_scores = (probs * (g_probs - delta[:, :, None])).astype(jnp.bfloat16)
            g_q = (
                jnp.einsum("hqk,khd->qhd", g_scores, keys3, preferred_element_type=jnp.float32)
                * scale
            )
            probs_low = probs.astype(jnp.bfloat16)
            g_k = (
                jnp.einsum("hqk,qhd->khd", g_scores, q_h, preferred_element_type=jnp.float32)
                * scale
            )
            g_v = jnp.einsum("hqk,qhd->khd", probs_low, g_att_h, preferred_element_type=jnp.float32)
            return (
                g_q,
                jnp.concatenate([g_k.reshape(rows, width), g_v.reshape(rows, width)], axis=1),
            )

        def no_terms(unused_arg):
            return (zero_q, zero_kv)

        return lax.cond(key_start >= 0, grad_work, no_terms, 0)

    last_q, last_kv = grad_terms(reach)

    def return_step(step, state):
        g_q_acc, kv_acc = state
        index = reach - 1 - step
        kv_acc = passed_along(kv_acc.astype(jnp.bfloat16), "cp", -1).astype(kv_acc.dtype)
        term_q, term_kv = grad_terms(index)
        return (g_q_acc + term_q, kv_acc + term_kv)

    g_q_sum, kv_sum = lax.fori_loop(0, reach, return_step, (last_q, last_kv))
    g_q_b = g_q_sum.reshape(rows, width).astype(jnp.bfloat16)
    g_k_b = kv_sum[:, :width].astype(jnp.bfloat16)
    g_v_b = kv_sum[:, width:].astype(jnp.bfloat16)
    projection_gradient = jnp.stack([g_q_b, g_k_b, g_v_b], axis=1)
    query_key_value_term = jnp.einsum(
        "hm,hwz->mwz", first_norm_lowered, projection_gradient, preferred_element_type=jnp.float32
    )
    bqv_term = jnp.stack(
        [jnp.sum(g_q_b.astype(jnp.float32), axis=0), jnp.sum(g_v_b.astype(jnp.float32), axis=0)]
    )
    g_norm1 = lax.psum(
        jnp.einsum(
            "wzb,gzb->wg",
            projection_gradient,
            query_key_value_weight,
            preferred_element_type=jnp.float32,
        ).astype(jnp.bfloat16),
        "tp",
    ).astype(jnp.float32)
    from_norm1, gain1_term, shift1_term = ln1_pull(g_norm1)
    g_x = g_hidden + from_norm1
    g_qkv, g_out, g_up = (
        lax.psum_scatter(
            query_key_value_term.astype(jnp.bfloat16), "cp", scatter_dimension=0, tiled=True
        ).astype(jnp.float32),
        lax.psum_scatter(
            out_term.astype(jnp.bfloat16), "cp", scatter_dimension=1, tiled=True
        ).astype(jnp.float32),
        lax.psum_scatter(
            up_term.astype(jnp.bfloat16), "cp", scatter_dimension=0, tiled=True
        ).astype(jnp.float32),
    )
    g_down = down_part
    small = lax.psum(
        (sums2, gain1_term, shift1_term, bqv_term), "cp",
    )
    sums2, gain1, shift1, g_bqv = small
    g_ln_gains = jnp.stack([gain1, sums2[0]])
    g_ln_shifts = jnp.stack([shift1, sums2[1]])
    g_bouts = sums2[2:4]
    g_bup = sums2[4]
    return (out, g_x, g_ln_gains, g_ln_shifts, g_qkv, g_bqv, g_out, g_bouts, g_up, g_bup, g_down)


def solution(mesh):
    return jax.shard_map(
        shards,
        mesh=mesh,
        in_specs=(
            P("cp", None),
            P(),
            P(),
            P(),
            P(),
            P(None, None, "tp"),
            P(None, "tp"),
            P("tp", None),
            P(),
            P(None, "tp"),
            P("tp"),
            P("tp", None),
            P("cp", None),
        ),
        out_specs=(
            P("cp", None),
            P("cp", None),
            P(),
            P(),
            P("cp", None, "tp"),
            P(None, "tp"),
            P("tp", "cp"),
            P(),
            P("cp", "tp"),
            P("tp"),
            P("tp", "cp"),
        ),
        check_vma=False,
    )
```

```python
import functools
import math

import jax
import jax.numpy as jnp
from jax import lax
from jax.experimental import pallas as pl
from jax.experimental.pallas import tpu as pltpu
from jax.sharding import PartitionSpec as P

HD = 64
LONG = 2048
EPS = 1e-05
NEG = -1e30
MESH = pl.DeviceIdType.MESH
F32 = jnp.float32
BF16 = jnp.bfloat16
ANY = pl.BlockSpec(memory_space=pl.ANY)
IN_VMEM = pl.BlockSpec(memory_space=pltpu.VMEM)
IN_SMEM = pl.BlockSpec(memory_space=pltpu.SMEM)
SUB = 32
CHUNK = 256


def dot(a, b):
    return jnp.dot(a, b, preferred_element_type=F32)


def dot_nt(a, b):
    return lax.dot_general(a, b, (((1,), (1,)), ((), ())), preferred_element_type=F32)


def dot_tn(a, b):
    return lax.dot_general(a, b, (((0,), (0,)), ((), ())), preferred_element_type=F32)


def rows_of(index, size):
    return pl.ds(pl.multiple_of(index * size, size), size)


def place():
    cp = lax.axis_index("cp")
    tp = lax.axis_index("tp")
    return cp, tp, lax.rem(cp, 2), lax.div(cp, 2)


def greet(cp, tp, others):
    barrier = pltpu.get_barrier_semaphore()
    edge = (tp == 0) | (tp == 3)
    for other in [*others, (cp, line_near(tp))]:
        pl.semaphore_signal(barrier, inc=1, device_id=other, device_id_type=MESH)

    @pl.when(jnp.logical_not(edge))
    def _():
        pl.semaphore_signal(barrier, inc=1, device_id=(cp, 3 - tp), device_id_type=MESH)

    pl.semaphore_wait(barrier, len(others) + jnp.where(edge, 1, 2))


def line_near(tp):
    return jnp.where(tp == 0, 1, jnp.where(tp == 1, 0, jnp.where(tp == 2, 3, 2)))


class LineSum:
    def __init__(self, part, slot_a, slot_b, total, send, recv):
        self.cp, self.tp, _, _ = place()
        self.edge = (self.tp == 0) | (self.tp == 3)
        self.refs = (part, slot_a, slot_b, total)
        self.send, self.recv = send, recv

    def copy(self, kind, s):
        part, slot_a, slot_b, total = self.refs
        src, dst = ((part, slot_a), (part, slot_b), (total, total))[kind]
        other = (self.cp, 3 - self.tp if kind == 1 else line_near(self.tp))
        rows = rows_of(s, SUB)
        return pltpu.make_async_remote_copy(
            src_ref=src.at[rows],
            dst_ref=dst.at[rows],
            send_sem=self.send.at[kind, s],
            recv_sem=self.recv.at[kind, s],
            device_id=other,
            device_id_type=MESH,
        )

    def push(self, s):
        @pl.when(self.edge)
        def _():
            self.copy(0, s).start()

    def relay_in(self, s):
        part, slot_a, _, _ = self.refs

        @pl.when(jnp.logical_not(self.edge))
        def _():
            rows = rows_of(s, SUB)
            self.copy(0, s).wait_recv()
            part[rows] = (part[rows].astype(F32) + slot_a[rows].astype(F32)).astype(BF16)
            self.copy(1, s).start()

    def relay_out(self, s):
        part, _, slot_b, total = self.refs

        @pl.when(jnp.logical_not(self.edge))
        def _():
            rows = rows_of(s, SUB)
            self.copy(1, s).wait_recv()
            total[rows] = (part[rows].astype(F32) + slot_b[rows].astype(F32)).astype(BF16)
            self.copy(2, s).start()

    def get(self, s):
        @pl.when(self.edge)
        def _():
            self.copy(2, s).wait_recv()

    def drain(self, s):
        @pl.when(self.edge)
        def _():
            self.copy(0, s).wait_send()

        @pl.when(jnp.logical_not(self.edge))
        def _():
            self.copy(1, s).wait_send()
            self.copy(2, s).wait_send()

    def run(self, first, last):
        def step(s, carry):
            @pl.when(s < last)
            def _():
                self.relay_in(s)

            @pl.when(s > first)
            def _():
                self.relay_out(s - 1)
                self.get(s - 1)

            return carry

        lax.fori_loop(first, last + 1, step, 0)

    def drain_all(self, count):
        def step(s, carry):
            self.drain(s)
            return carry

        lax.fori_loop(0, count, step, 0)


def line_scratch(rows, width, with_part=True):
    count = rows // SUB
    return [pltpu.VMEM((rows, width), BF16)] * 4 + [
        pltpu.SemaphoreType.DMA((3, count)),
        pltpu.SemaphoreType.DMA((3, count)),
    ]


def band_info(lengths_ref, until_ref, first):
    start = jnp.int32(0)
    begin = jnp.int32(0)
    until = jnp.int32(0)
    for i in range(lengths_ref.shape[0]):
        length = lengths_ref[i]
        inside = (first >= start) & (first < start + length)
        begin = jnp.where(inside, start, begin)
        until = jnp.where(inside, until_ref[i], until)
        start = start + length
    return begin, until + begin - first


def loop(count, body):
    def step(i, carry):
        body(i)
        return carry

    lax.fori_loop(0, count, step, 0)


def attend_kernel(
    x_hbm, lengths_ref, until_ref, gains, shifts, wqkv_hbm, bqv, wout_hbm,
    sum_hbm, norm_hbm, q_hbm, kv_hbm, att_hbm, att_t_hbm, lse_out,
    x_v, norm_v, w_v, wout_v, q_v, kv, q_t, v_t, s_v, p_v, att_t, att_v,
    part, slot_a, slot_b, total, ar_send, ar_recv, kv_send, kv_recv, load_sem, store_sem,
):
    cp, tp, core, chip = place()
    bands = lax.axis_size("cp")
    chips = bands // 2
    rows, depth = x_v.shape
    width = q_v.shape[1]
    heads = width // HD
    near = (cp + 1 - 2 * core, tp)
    after = (lax.rem(cp + 2, bands), tp)
    before = (lax.rem(cp + bands - 2, bands), tp)
    loads = [
        pltpu.make_async_copy(x_hbm, x_v, load_sem.at[0]),
        pltpu.make_async_copy(wqkv_hbm.at[1], w_v.at[1], load_sem.at[1]),
        pltpu.make_async_copy(wqkv_hbm.at[2], w_v.at[2], load_sem.at[2]),
        pltpu.make_async_copy(wqkv_hbm.at[0], w_v.at[0], load_sem.at[3]),
        pltpu.make_async_copy(wout_hbm, wout_v, load_sem.at[4]),
    ]
    for item in loads:
        item.start()
    greet(cp, tp, [near, after, before])
    begin, _ = band_info(lengths_ref, until_ref, cp * rows)
    has_before = begin < chip * 2 * rows
    loads[0].wait()

    @functools.partial(loop, rows // 64)
    def _(i):
        part_rows = rows_of(i, 64)
        v = x_v[part_rows].astype(F32)
        mean = jnp.mean(v, axis=-1, keepdims=True)
        centred = v - mean
        var = jnp.mean(centred * centred, axis=-1, keepdims=True)
        norm_v[part_rows] = (centred * lax.rsqrt(var + EPS) * gains[0:1] + shifts[0:1]).astype(BF16)

    stores = [pltpu.make_async_copy(norm_v, norm_hbm, store_sem.at[0])]
    stores[0].start()
    own = 2 + core

    for load, column in ((1, 0), (2, 1)):
        loads[load].wait()

        @functools.partial(loop, rows // CHUNK)
        def _(i):
            value = dot(norm_v[rows_of(i, CHUNK)], w_v[load])
            if column:
                value = value + bqv[1:2]
            target = pl.ds(pl.multiple_of(own * rows + i * CHUNK, CHUNK), CHUNK)
            kv[target, column * width : (column + 1) * width] = value.astype(BF16)

    def kv_copy(kind, slot, device):
        block = kv.at[rows_of(slot, rows)]
        to = kv.at[rows_of(core, rows)] if kind == 0 else block
        return pltpu.make_async_remote_copy(
            src_ref=block, dst_ref=to, send_sem=kv_send.at[kind], recv_sem=kv_recv.at[kind],
            device_id=device, device_id_type=MESH,
        )

    to_next = kv_copy(0, own, after)
    to_near = kv_copy(1, own, near)
    forward = kv_copy(2, core, near)

    @pl.when(chip < chips - 1)
    def _():
        to_next.start()

    to_near.start()

    @pl.when(chip == 0)
    def _():
        @functools.partial(loop, 2 * rows // 64)
        def _(i):
            kv[rows_of(i, 64)] = jnp.zeros((64, 2 * width), BF16)

    loads[3].wait()

    @functools.partial(loop, rows // CHUNK)
    def _(i):
        part_rows = rows_of(i, CHUNK)
        value = (dot(norm_v[part_rows], w_v[0]) + bqv[0:1]).astype(BF16)
        q_v[part_rows] = value
        turned = (value.astype(F32) * (HD ** -0.5)).T
        upper = lax.broadcasted_iota(jnp.int32, (2 * HD, CHUNK), 0) < HD
        for h in range(heads):
            both = turned[(h // 2) * 2 * HD : (h // 2 + 1) * 2 * HD]
            q_t[h, :, part_rows] = jnp.where(upper == (h % 2 == 0), both, 0.0).astype(BF16)

    stores.append(pltpu.make_async_copy(q_v, q_hbm, store_sem.at[1]))
    stores[1].start()
    to_near.wait_recv()

    def turn_values(slot):
        v_t[:, rows_of(slot, rows)] = kv[rows_of(slot, rows), width:].astype(F32).T.astype(BF16)

    turn_values(2)
    turn_values(3)

    @pl.when(chip > 0)
    def _():
        to_next.wait_recv()
        forward.start()
        forward.wait_recv()

    stores.append(pltpu.make_async_copy(kv, kv_hbm, store_sem.at[2]))
    stores[2].start()
    turn_values(0)
    turn_values(1)
    loads[4].wait()
    line = LineSum(part, slot_a, slot_b, total, ar_send, ar_recv)
    bias = jnp.where(has_before, 0.0, NEG)
    keys = 4 * rows

    for c in range(rows // CHUNK):
        columns = slice(c * CHUNK, (c + 1) * CHUNK)

        def head(h, parity, c=c, columns=columns):
            lanes = pl.ds(pl.multiple_of(lax.div(h, 2) * 2 * HD, 2 * HD), 2 * HD)
            query = q_t[h, :, columns]
            top = jnp.full((1, CHUNK), NEG, F32)
            for b in range(4):
                s = dot(kv[b * rows : (b + 1) * rows, lanes], query)
                if b < 2:
                    s = s + bias
                else:
                    key = lax.broadcasted_iota(jnp.int32, (rows, CHUNK), 0) + (b - 2) * rows
                    row = lax.broadcasted_iota(jnp.int32, (rows, CHUNK), 1) + c * CHUNK
                    s = jnp.where(key <= row + core * rows, s, NEG)
                s_v[b * rows : (b + 1) * rows] = s
                top = jnp.maximum(top, jnp.max(s, axis=0, keepdims=True))
            mass = jnp.zeros((1, CHUNK), F32)
            for b in range(4):
                p = jnp.exp(s_v[b * rows : (b + 1) * rows] - top)
                mass = mass + jnp.sum(p, axis=0, keepdims=True)
                p_v[b * rows : (b + 1) * rows] = p.astype(BF16)
            feature = pl.ds(pl.multiple_of(h * HD, HD), HD)
            att_t[feature, columns] = dot(v_t[feature], p_v[...]) / mass
            lse_out[pl.ds(h, 1), columns] = top + jnp.log(mass)

        loop(heads, lambda h: head(h, 0))
        att_v[columns] = att_t[:, columns].T.astype(BF16)

        @functools.partial(loop, depth // 512)
        def _(t):
            lanes = rows_of(t, 512)
            part[columns, lanes] = dot(att_v[columns], wout_v[:, lanes]).astype(BF16)

        loop(CHUNK // SUB, lambda s, c=c: line.push(s + c * (CHUNK // SUB)))

    stores.append(pltpu.make_async_copy(att_v, att_hbm, store_sem.at[3]))
    stores.append(pltpu.make_async_copy(att_t, att_t_hbm, store_sem.at[4]))
    stores[3].start()
    stores[4].start()
    line.run(0, rows // SUB)
    stores.append(pltpu.make_async_copy(total, sum_hbm, store_sem.at[5]))
    stores[5].start()
    line.drain_all(rows // SUB)

    @pl.when(chip < chips - 1)
    def _():
        to_next.wait_send()

    @pl.when(chip > 0)
    def _():
        forward.wait_send()

    to_near.wait_send()
    for item in stores:
        item.wait()


def attend(x, lengths, until, gains, shifts, wqkv, bqv, wout):
    rows, depth = x.shape
    width = wqkv.shape[2]
    heads = width // HD
    shape = jax.ShapeDtypeStruct
    return pl.pallas_call(
        attend_kernel,
        out_shape=(
            shape((rows, depth), BF16),
            shape((rows, depth), BF16),
            shape((rows, width), BF16),
            shape((4 * rows, 2 * width), BF16),
            shape((rows, width), BF16),
            shape((width, rows), F32),
            shape((heads, rows), F32),
        ),
        in_specs=[ANY, IN_SMEM, IN_SMEM, IN_VMEM, IN_VMEM, ANY, IN_VMEM, ANY],
        out_specs=(ANY,) * 6 + (IN_VMEM,),
        scratch_shapes=[
            pltpu.VMEM((rows, depth), BF16),
            pltpu.VMEM((rows, depth), BF16),
            pltpu.VMEM((3, depth, width), BF16),
            pltpu.VMEM((width, depth), BF16),
            pltpu.VMEM((rows, width), BF16),
            pltpu.VMEM((4 * rows, 2 * width), BF16),
            pltpu.VMEM((heads, 2 * HD, rows), BF16),
            pltpu.VMEM((width, 4 * rows), BF16),
            pltpu.VMEM((4 * rows, CHUNK), F32),
            pltpu.VMEM((4 * rows, CHUNK), BF16),
            pltpu.VMEM((width, rows), F32),
            pltpu.VMEM((rows, width), BF16),
            *line_scratch(rows, depth),
            pltpu.SemaphoreType.DMA((3,)),
            pltpu.SemaphoreType.DMA((3,)),
            pltpu.SemaphoreType.DMA((5,)),
            pltpu.SemaphoreType.DMA((6,)),
        ],
        compiler_params=pltpu.CompilerParams(collective_id=0, has_side_effects=True, vmem_limit_bytes=56 * 2**20),
        name="attend",
    )(x, lengths, until, gains, shifts, wqkv, bqv, wout)


class Scatter:
    def __init__(self, terms, near, far, send, recv, split):
        self.cp, self.tp, self.core, self.chip = place()
        self.count = lax.axis_size("cp")
        self.depth = (self.count // 2).bit_length() - 1
        self.terms, self.near, self.far = terms, near, far
        self.send, self.recv = send, recv
        self.chunk = terms.shape[0] // self.count
        self.width = terms.shape[1]
        self.parts = [p for p in ((0, 0, split), (1, split, self.width)) if p[2] > p[1]]
        self.block = max(self.chunk, 128)

    def partners(self):
        others = [(self.cp + 1 - 2 * self.core, self.tp)]
        for bit in range(self.depth):
            others.append((self.cp + 2 * self.step(bit), self.tp))
        return others

    def step(self, bit):
        return (1 - 2 * self.bit(bit)) * (1 << bit)

    def bit(self, bit):
        return lax.rem(lax.div(self.chip, 1 << bit), 2)

    def fill(self, k, pick):
        if self.block == self.chunk:
            half = self.count // 2
            block = 2 * lax.rem(k, half) + jnp.where(k < half, 1 - self.core, self.core)
        else:
            block = k
        rows = rows_of(block, self.block)
        for tile in range(self.width // 512):
            lanes = slice(tile * 512, (tile + 1) * 512)
            left, right = pick(tile, rows)
            self.terms[rows, lanes] = dot_tn(left, right).astype(BF16)

    def blocks(self):
        return self.terms.shape[0] // self.block

    def near_copy(self, t):
        return pltpu.make_async_remote_copy(
            src_ref=self.terms.at[rows_of(2 * t + 1 - self.core, self.chunk)],
            dst_ref=self.near.at[rows_of(t, self.chunk)],
            send_sem=self.send.at[t],
            recv_sem=self.recv.at[t],
            device_id=(self.cp + 1 - 2 * self.core, self.tp),
            device_id_type=MESH,
        )

    def send_near(self, t):
        self.near_copy(t).start()

    def add_near(self, t):
        self.near_copy(t).wait_recv()
        base = (2 * t + self.core) * self.chunk

        @functools.partial(loop, self.chunk // 64)
        def _(i):
            mine = pl.ds(pl.multiple_of(base + i * 64, 64), 64)
            other = pl.ds(pl.multiple_of(t * self.chunk + i * 64, 64), 64)
            self.terms[mine] = (self.terms[mine].astype(F32) + self.near[other].astype(F32)).astype(BF16)

    def index(self, part, level, t, keep):
        bit = level - 1 if part == 0 else self.depth - level
        own = self.bit(bit)
        own = own if keep else 1 - own
        if part == 0:
            return lax.rem(self.chip, 1 << bit) + own * (1 << bit) + t * (2 << bit), bit
        return self.chip - lax.rem(self.chip, 2 << bit) + own * (1 << bit) + t, bit

    def pieces(self, level):
        first = self.count // 2
        for earlier in range(1, level):
            first += len(self.parts) * (1 << (self.depth - earlier))
        for part, low, high in self.parts:
            for t in range(1 << (self.depth - level)):
                yield part, slice(low, high), t, first
                first += 1

    def far_copy(self, level, part, lanes, t, sem):
        index, bit = self.index(part, level, t, False)
        return pltpu.make_async_remote_copy(
            src_ref=self.terms.at[rows_of(2 * index + self.core, self.chunk), lanes],
            dst_ref=self.far.at[pl.ds(self.place(level) + t * self.chunk, self.chunk), lanes],
            send_sem=self.send.at[sem],
            recv_sem=self.recv.at[sem],
            device_id=(self.cp + 2 * self.step(bit), self.tp),
            device_id_type=MESH,
        )

    def send_far(self, level):
        for piece in self.pieces(level):
            self.far_copy(level, *piece).start()

    def add_far(self, level):
        for part, lanes, t, sem in self.pieces(level):
            self.far_copy(level, part, lanes, t, sem).wait_recv()
            index, _ = self.index(part, level, t, True)
            base = (2 * index + self.core) * self.chunk
            there = self.place(level) + t * self.chunk

            @functools.partial(loop, self.chunk // 64)
            def _(i, base=base, lanes=lanes, there=there):
                mine = pl.ds(pl.multiple_of(base + i * 64, 64), 64)
                other = pl.ds(pl.multiple_of(there + i * 64, 64), 64)
                self.terms[mine, lanes] = (
                    self.terms[mine, lanes].astype(F32) + self.far[other, lanes].astype(F32)
                ).astype(BF16)

    def place(self, level):
        return sum(self.terms.shape[0] >> (earlier + 1) for earlier in range(1, level))

    def finish(self, write):
        level = self.depth
        mine = rows_of(self.cp, self.chunk)
        for part, lanes, t, sem in self.pieces(level):
            self.far_copy(level, part, lanes, t, sem).wait_recv()
            for tile in range(lanes.start // 512, lanes.stop // 512):
                cut = slice(tile * 512, (tile + 1) * 512)
                other = pl.ds(self.place(level), self.chunk)
                write(tile, self.terms[mine, cut].astype(F32) + self.far[other, cut].astype(F32))

    def drain(self):
        loop(self.count // 2, lambda t: self.near_copy(t).wait_send())
        for level in range(1, self.depth + 1):
            for piece in self.pieces(level):
                self.far_copy(level, *piece).wait_send()


def scatter_scratch(depth, width, split):
    count = lax.axis_size("cp")
    parts = (split > 0) + (split < width)
    sems = count // 2 + parts * (count // 2 - 1)
    return [
        pltpu.VMEM((depth // 2, width), BF16),
        pltpu.VMEM((depth // 2 - depth // count, width), BF16),
        pltpu.SemaphoreType.DMA((sems,)),
        pltpu.SemaphoreType.DMA((sems,)),
    ]


def fold(v):
    return jnp.sum(v.reshape(v.shape[0] // 8, 8, v.shape[1]), axis=0)


def gelu_parts(u):
    root = math.sqrt(2.0 / math.pi)
    square = u * u
    th = jnp.tanh(root * (u + 0.044715 * u * square))
    half = 0.5 * (1.0 + th)
    return u * half, half + 0.5 * u * (1.0 - th * th) * (root * (1.0 + 3 * 0.044715 * square))


LAG = 4
SPLIT_DOWN = 1024


def ffn_kernel(
    sum_hbm, x_hbm, d_hbm, lengths_ref, until_ref, gains, shifts, b_outs, b_up, up_hbm, down_hbm,
    norm_hbm, g_pre_hbm, ffn_hbm, g_hidden_hbm, g_attn_hbm, sums_out, down_out,
    up_v, down_v, d_v, xhat, rstd, norm_v, act_v, g_pre_v, g_ffn_v, ffn_v, g_hidden, g_attn, acc,
    part, slot_a, slot_b, total, ar_send, ar_recv, near, far, rs_send, rs_recv, load_sem, store_sem,
):
    cp, tp, core, chip = place()
    rows, depth = d_v.shape
    hidden = up_v.shape[1]
    count = rows // SUB
    loads = [
        pltpu.make_async_copy(x_hbm, g_attn, load_sem.at[0]),
        pltpu.make_async_copy(sum_hbm, ffn_v, load_sem.at[1]),
        pltpu.make_async_copy(d_hbm, d_v, load_sem.at[2]),
        pltpu.make_async_copy(up_hbm, up_v, load_sem.at[3]),
        pltpu.make_async_copy(down_hbm, down_v, load_sem.at[4]),
    ]
    for item in loads:
        item.start()
    line = LineSum(part, slot_a, slot_b, total, ar_send, ar_recv)
    scatter = Scatter(up_v, near, far, rs_send, rs_recv, SPLIT_DOWN)
    greet(cp, tp, scatter.partners())
    _, live = band_info(lengths_ref, until_ref, cp * rows)
    acc[...] = jnp.zeros_like(acc)
    for item in loads[:3]:
        item.wait()

    for c in range(rows // CHUNK):
        chunk = slice(c * CHUNK, (c + 1) * CHUNK)

        @functools.partial(loop, CHUNK // 64)
        def _(i, c=c):
            at = pl.ds(pl.multiple_of(c * CHUNK + i * 64, 64), 64)
            row = lax.broadcasted_iota(jnp.int32, (64, 1), 0) + (c * CHUNK + i * 64)
            on = row < live
            branch = ffn_v[at].astype(F32) + b_outs[0:1]
            v = g_attn[at].astype(F32) + jnp.where(on, branch, 0.0)
            mean = jnp.mean(v, axis=-1, keepdims=True)
            centred = v - mean
            scale = lax.rsqrt(jnp.mean(centred * centred, axis=-1, keepdims=True) + EPS)
            hat = centred * scale
            xhat[at] = hat
            rstd[at] = jnp.broadcast_to(scale, (64, 128))
            norm_v[at] = (hat * gains[1:2] + shifts[1:2]).astype(BF16)
            g_ffn = jnp.where(on, d_v[at].astype(F32), 0.0)
            g_ffn_v[at] = g_ffn.astype(BF16)
            acc[3] += fold(g_ffn)

        if c == 0:
            loads[3].wait()
            loads[4].wait()

        @functools.partial(loop, hidden // 512)
        def _(t, c=c, chunk=chunk):
            lanes = rows_of(t, 512)
            pre = dot(norm_v[chunk], up_v[:, lanes]) + b_up[0:1, lanes]
            g_act = dot_nt(g_ffn_v[chunk], down_v[lanes])
            act, slope = gelu_parts(pre)
            act_v[chunk, lanes] = act.astype(BF16)
            g_pre = (g_act * slope).astype(BF16)
            g_pre_v[chunk, lanes] = g_pre
            acc[4, :, lanes] += fold(g_pre.astype(F32))
            if c > 0:
                line.relay_in(t)

                @pl.when(t > 0)
                def _():
                    line.relay_out(t - 1)

        @functools.partial(loop, depth // 512)
        def _(t, chunk=chunk):
            lanes = rows_of(t, 512)
            part[chunk, lanes] = dot_nt(g_pre_v[chunk], up_v[lanes]).astype(BF16)

        loop(CHUNK // SUB, lambda s, c=c: line.push(s + c * (CHUNK // SUB)))

    stores = [
        pltpu.make_async_copy(norm_v, norm_hbm, store_sem.at[0]),
        pltpu.make_async_copy(g_pre_v, g_pre_hbm, store_sem.at[1]),
        pltpu.make_async_copy(ffn_v, ffn_hbm, store_sem.at[2]),
        pltpu.make_async_copy(g_hidden, g_hidden_hbm, store_sem.at[3]),
        pltpu.make_async_copy(g_attn, g_attn_hbm, store_sem.at[4]),
    ]
    stores[0].start()
    stores[1].start()

    def back(s):
        line.get(s)
        at = rows_of(s, SUB)
        e = total[at].astype(F32)
        hat = xhat[at]
        t = e * gains[1:2]
        along = t - jnp.mean(t, axis=-1, keepdims=True) - hat * jnp.mean(t * hat, axis=-1, keepdims=True)
        value = d_v[at].astype(F32) + along * rstd[at, 0:1]
        g_hidden[at] = value
        row = lax.broadcasted_iota(jnp.int32, (SUB, 1), 0) + s * SUB
        low = jnp.where(row < live, value, 0.0).astype(BF16)
        g_attn[at] = low
        acc[0] += fold(e * hat)
        acc[1] += fold(e)
        acc[2] += fold(low.astype(F32))

    def ahead(s):
        @pl.when(s < count)
        def _():
            line.relay_in(s)

        line.relay_out(s - 1)
        back(s - LAG)

    def term(k):
        scatter.fill(k, lambda tile, rows: (g_ffn_v[:, rows], act_v[:, tile * 512 : (tile + 1) * 512]))

    def project(k):
        chunk = rows_of(lax.div(k, depth // 512), CHUNK)
        lanes = rows_of(lax.rem(k, depth // 512), 512)
        ffn_v[chunk, lanes] = dot(act_v[chunk], down_v[:, lanes]).astype(BF16)

    blocks, half = scatter.blocks(), scatter.count // 2

    @functools.partial(loop, 4)
    def _(i):
        loop(blocks // 4, lambda j: term(i * (blocks // 4) + j))

        @pl.when((i == 1) if scatter.block == scatter.chunk else (i == 3))
        def _():
            loop(half, scatter.send_near)

        ahead(4 + i)

    @functools.partial(loop, 2)
    def _(i):
        loop(half // 2, lambda j: scatter.add_near(i * (half // 2) + j))
        ahead(8 + i)

    scatter.send_far(1)

    @functools.partial(loop, 4)
    def _(i):
        project(2 * i)
        project(2 * i + 1)
        ahead(10 + i)

    stores[2].start()
    loop(count - 13, lambda i: ahead(14 + i))
    loop(LAG - 1, lambda i: back(count - LAG + 1 + i))
    stores[3].start()
    stores[4].start()
    for level in range(1, scatter.depth):
        scatter.add_far(level)
        scatter.send_far(level + 1)

    for k in range(5):
        sums_out[k : k + 1] = jnp.sum(acc[k], axis=0, keepdims=True)

    sums_out[5:8] = jnp.zeros((3, sums_out.shape[1]), F32)

    def write(tile, value):
        down_out[tile * 512 : (tile + 1) * 512] = value.T

    scatter.finish(write)
    scatter.drain()
    line.drain_all(count)
    for item in stores:
        item.wait()


def ffn(attn_sum, x, d_out, lengths, until, gains, shifts, b_outs, b_up, w_up, w_down):
    rows, depth = x.shape
    hidden = w_up.shape[1]
    chunk = depth // lax.axis_size("cp")
    shape = jax.ShapeDtypeStruct
    return pl.pallas_call(
        ffn_kernel,
        out_shape=(
            shape((rows, depth), BF16),
            shape((rows, hidden), BF16),
            shape((rows, depth), BF16),
            shape((rows, depth), F32),
            shape((rows, depth), BF16),
            shape((8, depth), F32),
            shape((hidden, chunk), F32),
        ),
        in_specs=[ANY, ANY, ANY, IN_SMEM, IN_SMEM, IN_VMEM, IN_VMEM, IN_VMEM, IN_VMEM, ANY, ANY],
        out_specs=(ANY,) * 5 + (IN_VMEM,) * 2,
        scratch_shapes=[
            pltpu.VMEM((depth, hidden), BF16),
            pltpu.VMEM((hidden, depth), BF16),
            pltpu.VMEM((rows, depth), BF16),
            pltpu.VMEM((rows, depth), F32),
            pltpu.VMEM((rows, 128), F32),
            pltpu.VMEM((rows, depth), BF16),
            pltpu.VMEM((rows, hidden), BF16),
            pltpu.VMEM((rows, hidden), BF16),
            pltpu.VMEM((rows, depth), BF16),
            pltpu.VMEM((rows, depth), BF16),
            pltpu.VMEM((rows, depth), F32),
            pltpu.VMEM((rows, depth), BF16),
            pltpu.VMEM((5, 8, depth), F32),
            *line_scratch(rows, depth),
            *scatter_scratch(depth, hidden, SPLIT_DOWN),
            pltpu.SemaphoreType.DMA((5,)),
            pltpu.SemaphoreType.DMA((5,)),
        ],
        compiler_params=pltpu.CompilerParams(collective_id=1, has_side_effects=True, vmem_limit_bytes=62 * 2**20),
        name="ffn",
    )(attn_sum, x, d_out, lengths, until, gains, shifts, b_outs, b_up, w_up, w_down)


SPLIT_UP = 1024
SPLIT_LAST = 1024


def grad_attend_kernel(
    g_attn_hbm, wout_hbm, q_hbm, kv_hbm, att_t_hbm, lse, lengths_ref, until_ref, ffn_hbm, norm_hbm, g_pre_hbm,
    g_qkv_hbm, ffn_sum_hbm, up_out,
    g_attn_v, wout_v, q_v, kv, k_t, att_t, q_t, g_v, g_t, delta, acc, g_qkv_v,
    give_near, got_near, give_before, got_after, give_own, got_own, kv_send, kv_recv,
    norm_v, g_pre_v, terms, near, far, rs_send, rs_recv,
    part, slot_a, slot_b, total, ar_send, ar_recv, load_sem, store_sem,
):
    cp, tp, core, chip = place()
    bands = lax.axis_size("cp")
    chips = bands // 2
    rows, width = q_v.shape
    heads = width // HD
    count = rows // SUB
    sibling = (cp + 1 - 2 * core, tp)
    after = (lax.rem(cp + 2, bands), tp)
    before = (lax.rem(cp + bands - 2, bands), tp)
    loads = [
        pltpu.make_async_copy(source, target, load_sem.at[i])
        for i, (source, target) in enumerate(
            (
                (norm_hbm, norm_v),
                (g_pre_hbm, g_pre_v),
                (ffn_hbm, part),
                (g_attn_hbm, g_attn_v),
                (wout_hbm, wout_v),
                (q_hbm, q_v),
                (kv_hbm, kv),
                (att_t_hbm, att_t),
            )
        )
    ]
    for item in loads:
        item.start()
    line = LineSum(part, slot_a, slot_b, total, ar_send, ar_recv)
    scatter = Scatter(terms, near, far, rs_send, rs_recv, SPLIT_UP)
    greet(cp, tp, [*scatter.partners(), after, before])
    begin, _ = band_info(lengths_ref, until_ref, cp * rows)
    bias = jnp.where(begin < chip * 2 * rows, 0.0, NEG)
    loads[0].wait()
    loads[1].wait()
    loads[2].wait()
    loop(count, line.push)
    blocks, half = scatter.blocks(), scatter.count // 2

    def term(k):
        scatter.fill(k, lambda tile, at: (norm_v[:, at], g_pre_v[:, tile * 512 : (tile + 1) * 512]))

    loop(blocks // 2, term)
    if scatter.block == scatter.chunk:
        loop(half, scatter.send_near)
    loop(blocks - blocks // 2, lambda k: term(blocks // 2 + k))
    if scatter.block != scatter.chunk:
        loop(half, scatter.send_near)

    def relay(s):
        @pl.when(s < count)
        def _():
            line.relay_in(s)

        @pl.when(s > 0)
        def _():
            line.relay_out(s - 1)

    loop(2, relay)
    for item in loads[3:]:
        item.wait()
    scale = HD ** -0.5

    @functools.partial(loop, rows // CHUNK)
    def _(i):
        at = rows_of(i, CHUNK)
        low = dot_nt(g_attn_v[at], wout_v[...]).astype(BF16)
        g_v[at] = low
        turned = low.astype(F32).T
        turned_q = q_v[at].astype(F32).T * scale
        upper = lax.broadcasted_iota(jnp.int32, (2 * HD, CHUNK), 0) < HD
        for h in range(heads):
            both = slice((h // 2) * 2 * HD, (h // 2 + 1) * 2 * HD)
            mine = slice(h * HD, (h + 1) * HD)
            g_t[h, :, at] = jnp.where(upper == (h % 2 == 0), turned[both], 0.0).astype(BF16)
            q_t[h, :, at] = jnp.where(upper == (h % 2 == 0), turned_q[both], 0.0).astype(BF16)
            delta[h : h + 1, at] = jnp.sum(turned[mine] * att_t[mine, at], axis=0, keepdims=True)

    @functools.partial(loop, 4)
    def _(i):
        at = rows_of(i, rows)
        k_t[:, at] = kv[at, :width].astype(F32).T.astype(BF16)

    @functools.partial(loop, rows // 64)
    def _(i):
        att_t[rows_of(i, 64)] = jnp.zeros((64, rows), F32)

    @functools.partial(loop, 4 * rows // 64)
    def _(i):
        acc[rows_of(i, 64)] = jnp.zeros((64, 2 * width), F32)

    g_q_t = att_t
    relay(2)

    def head(h, bands_of):
        offset = lax.div(h, 2) * 2 * HD
        lanes = pl.ds(pl.multiple_of(offset, 2 * HD), 2 * HD)
        lanes_v = pl.ds(pl.multiple_of(offset + width, 2 * HD), 2 * HD)
        feature = pl.ds(pl.multiple_of(h * HD, HD), HD)
        low_lanes = lax.broadcasted_iota(jnp.int32, (CHUNK, 2 * HD), 1) < HD
        mine = low_lanes == (lax.rem(h, 2) == 0)
        for c in range(rows // CHUNK):
            cols = slice(c * CHUNK, (c + 1) * CHUNK)
            q_n = jnp.where(mine, q_v[cols, lanes].astype(F32), 0.0).astype(BF16)
            g_n = jnp.where(mine, g_v[cols, lanes].astype(F32), 0.0).astype(BF16)
            lse_row = lse[pl.ds(h, 1), cols]
            delta_row = delta[pl.ds(h, 1), cols]
            for b in bands_of:
                keys = slice(b * rows, (b + 1) * rows)
                s = dot(kv[keys, lanes], q_t[h, :, cols])
                if b < 2:
                    s = s + (bias - lse_row)
                else:
                    key = lax.broadcasted_iota(jnp.int32, (rows, CHUNK), 0) + (b - 2) * rows
                    row = lax.broadcasted_iota(jnp.int32, (rows, CHUNK), 1) + c * CHUNK
                    s = jnp.where(key <= row + core * rows, s - lse_row, NEG)
                p = jnp.exp(s)
                g_s = (p * (dot(kv[keys, lanes_v], g_t[h, :, cols]) - delta_row)).astype(BF16)
                acc[keys, lanes] += dot(g_s, q_n)
                acc[keys, lanes_v] += dot(p.astype(BF16), g_n)
                g_q_t[feature, cols] += dot(k_t[feature, keys], g_s)

    @functools.partial(loop, heads)
    def _(h):
        head(h, (0, 1))

        @pl.when(h == 0)
        def _():
            loop(half, scatter.add_near)
            scatter.send_far(1)

        @pl.when(lax.rem(h, 2) == 1)
        def _():
            relay(3 + lax.div(h, 2))

    def kv_copy(kind, source, target, device):
        return pltpu.make_async_remote_copy(
            src_ref=source, dst_ref=target, send_sem=kv_send.at[kind], recv_sem=kv_recv.at[kind],
            device_id=device, device_id_type=MESH,
        )

    to_near = kv_copy(0, give_near, got_near, sibling)
    to_before = kv_copy(1, give_before, got_after, before)
    to_own = kv_copy(2, give_own, got_own, sibling)

    def lower(target, slot):
        @functools.partial(loop, rows // 64)
        def _(i):
            at = pl.ds(pl.multiple_of(slot * rows + i * 64, 64), 64)
            target[rows_of(i, 64)] = acc[at].astype(BF16)

    def add_to(slot, source):
        @functools.partial(loop, rows // 64)
        def _(i):
            at = pl.ds(pl.multiple_of(slot * rows + i * 64, 64), 64)
            acc[at] += source[rows_of(i, 64)].astype(F32)

    lower(give_near, 1 - core)
    to_near.start()
    to_near.wait_recv()
    add_to(core, got_near)
    lower(give_before, core)

    @pl.when(chip > 0)
    def _():
        to_before.start()

    @functools.partial(loop, heads)
    def _(h):
        head(h, (2, 3))

        @pl.when(lax.rem(h, 2) == 1)
        def _():
            relay(7 + lax.div(h, 2))

    own = 2 + core
    lower(give_own, 3 - core)
    to_own.start()
    loop(2, lambda i: relay(11 + i))
    levels = scatter.depth
    for level in range(1, levels):
        scatter.add_far(level)
        scatter.send_far(level + 1)
    loop(4, lambda i: relay(13 + i))
    to_own.wait_recv()
    add_to(own, got_own)

    @pl.when(chip < chips - 1)
    def _():
        to_before.wait_recv()
        add_to(own, got_after)

    @functools.partial(loop, rows // 64)
    def _(i):
        at = pl.ds(pl.multiple_of(own * rows + i * 64, 64), 64)
        g_qkv_v[rows_of(i, 64), width : 2 * width] = (acc[at, :width] * scale).astype(BF16)
        g_qkv_v[rows_of(i, 64), 2 * width :] = acc[at, width:].astype(BF16)

    @functools.partial(loop, rows // CHUNK)
    def _(i):
        at = rows_of(i, CHUNK)
        g_qkv_v[at, :width] = (g_q_t[:, at].T * scale).astype(BF16)

    stores = [
        pltpu.make_async_copy(g_qkv_v, g_qkv_hbm, store_sem.at[0]),
        pltpu.make_async_copy(total, ffn_sum_hbm, store_sem.at[1]),
    ]
    stores[0].start()
    loop(count, line.get)
    stores[1].start()

    def write(tile, value):
        up_out[:, tile * 512 : (tile + 1) * 512] = value

    scatter.finish(write)
    scatter.drain()
    line.drain_all(count)
    to_near.wait_send()
    to_own.wait_send()

    @pl.when(chip > 0)
    def _():
        to_before.wait_send()

    for item in stores:
        item.wait()


def grad_attend(g_attn, wout, q, kv, att_t, lse, lengths, until, ffn_low, norm2, g_pre):
    rows, depth = g_attn.shape
    width = q.shape[1]
    heads = width // HD
    hidden = g_pre.shape[1]
    chunk = depth // lax.axis_size("cp")
    shape = jax.ShapeDtypeStruct
    return pl.pallas_call(
        grad_attend_kernel,
        out_shape=(
            shape((rows, 3 * width), BF16),
            shape((rows, depth), BF16),
            shape((chunk, hidden), F32),
        ),
        in_specs=[ANY, ANY, ANY, ANY, ANY, IN_VMEM, IN_SMEM, IN_SMEM, ANY, ANY, ANY],
        out_specs=(ANY, ANY, IN_VMEM),
        scratch_shapes=[
            pltpu.VMEM((rows, depth), BF16),
            pltpu.VMEM((width, depth), BF16),
            pltpu.VMEM((rows, width), BF16),
            pltpu.VMEM((4 * rows, 2 * width), BF16),
            pltpu.VMEM((width, 4 * rows), BF16),
            pltpu.VMEM((width, rows), F32),
            pltpu.VMEM((heads, 2 * HD, rows), BF16),
            pltpu.VMEM((rows, width), BF16),
            pltpu.VMEM((heads, 2 * HD, rows), BF16),
            pltpu.VMEM((heads, rows), F32),
            pltpu.VMEM((4 * rows, 2 * width), F32),
            pltpu.VMEM((rows, 3 * width), BF16),
            *[pltpu.VMEM((rows, 2 * width), BF16)] * 6,
            pltpu.SemaphoreType.DMA((3,)),
            pltpu.SemaphoreType.DMA((3,)),
            pltpu.VMEM((rows, depth), BF16),
            pltpu.VMEM((rows, hidden), BF16),
            pltpu.VMEM((depth, hidden), BF16),
            *scatter_scratch(depth, hidden, SPLIT_UP),
            *line_scratch(rows, depth),
            pltpu.SemaphoreType.DMA((8,)),
            pltpu.SemaphoreType.DMA((2,)),
        ],
        compiler_params=pltpu.CompilerParams(collective_id=2, has_side_effects=True, vmem_limit_bytes=63 * 2**20),
        name="grad_attend",
    )(g_attn, wout, q, kv, att_t, lse, lengths, until, ffn_low, norm2, g_pre)


def last_kernel(
    g_qkv_hbm, wqkv_hbm, x_hbm, g_hidden_hbm, norm_hbm, g_attn_hbm, att_hbm, attn_sum_hbm, ffn_sum_hbm,
    lengths_ref, until_ref, gains, b_outs, sums_in,
    g_x_hbm, out_hbm, qkv_out, w_out_out, gains_out, shifts_out, bqv_out, bouts_out, bup_out,
    g_qkv_v, w_v, x_v, g_hidden, norm_v, g_attn_v, att_v, attn_sum, ffn_sum, out_v, acc, small, small_got,
    terms, near, far, rs_send, rs_recv,
    part, slot_a, slot_b, total, ar_send, ar_recv, small_send, small_recv, load_sem, store_sem,
):
    cp, tp, core, chip = place()
    rows, depth = x_v.shape
    width = att_v.shape[1]
    count = rows // SUB
    loads = [
        pltpu.make_async_copy(source, target, load_sem.at[i])
        for i, (source, target) in enumerate(
            (
                (g_qkv_hbm, g_qkv_v),
                (wqkv_hbm, w_v),
                (norm_hbm, norm_v),
                (g_attn_hbm, g_attn_v),
                (att_hbm, att_v),
                (x_hbm, x_v),
                (g_hidden_hbm, g_hidden),
                (attn_sum_hbm, attn_sum),
                (ffn_sum_hbm, ffn_sum),
            )
        )
    ]
    for item in loads:
        item.start()
    line = LineSum(part, slot_a, slot_b, total, ar_send, ar_recv)
    scatter = Scatter(terms, near, far, rs_send, rs_recv, SPLIT_LAST)
    partners = scatter.partners()
    greet(cp, tp, partners)
    _, live = band_info(lengths_ref, until_ref, cp * rows)
    acc[...] = jnp.zeros_like(acc)
    loads[0].wait()
    loads[1].wait()

    for c in range(rows // CHUNK):
        chunk = slice(c * CHUNK, (c + 1) * CHUNK)

        @functools.partial(loop, depth // 512)
        def _(t, chunk=chunk):
            lanes = rows_of(t, 512)
            value = dot_nt(g_qkv_v[chunk, :width], w_v[0, lanes])
            value = value + dot_nt(g_qkv_v[chunk, width : 2 * width], w_v[1, lanes])
            value = value + dot_nt(g_qkv_v[chunk, 2 * width :], w_v[2, lanes])
            part[chunk, lanes] = value.astype(BF16)

        loop(CHUNK // SUB, lambda s, c=c: line.push(s + c * (CHUNK // SUB)))

    for item in loads[2:]:
        item.wait()

    def back(s):
        line.get(s)
        at = rows_of(s, SUB)
        e = total[at].astype(F32)
        v = x_v[at].astype(F32)
        centred = v - jnp.mean(v, axis=-1, keepdims=True)
        scale = lax.rsqrt(jnp.mean(centred * centred, axis=-1, keepdims=True) + EPS)
        hat = centred * scale
        t = e * gains[0:1]
        along = t - jnp.mean(t, axis=-1, keepdims=True) - hat * jnp.mean(t * hat, axis=-1, keepdims=True)
        g_hidden[at] = g_hidden[at] + along * scale
        row = lax.broadcasted_iota(jnp.int32, (SUB, 1), 0) + s * SUB
        branches = attn_sum[at].astype(F32) + b_outs[0:1] + (ffn_sum[at].astype(F32) + b_outs[1:2])
        out_v[at] = v + jnp.where(row < live, branches, 0.0)
        acc[0] += fold(e * hat)
        acc[1] += fold(e)
        pltpu.make_async_copy(g_hidden.at[at], g_x_hbm.at[at], store_sem.at[0, s]).start()
        pltpu.make_async_copy(out_v.at[at], out_hbm.at[at], store_sem.at[1, s]).start()

    behind = 2

    def ahead(s):
        @pl.when(s < count)
        def _():
            line.relay_in(s)

        @pl.when(s > 0)
        def _():
            line.relay_out(s - 1)

        @pl.when(s >= behind)
        def _():
            back(s - behind)

    def term(k):
        def pick(tile, at):
            if tile < 3:
                return norm_v[:, at], g_qkv_v[:, tile * width : (tile + 1) * width]
            return g_attn_v[:, at], att_v[...]

        scatter.fill(k, pick)

    blocks, half = scatter.blocks(), scatter.count // 2

    @functools.partial(loop, 4)
    def _(i):
        loop(blocks // 4, lambda j: term(i * (blocks // 4) + j))

        @pl.when((i == 1) if scatter.block == scatter.chunk else (i == 3))
        def _():
            loop(half, scatter.send_near)

        ahead(i)

    @functools.partial(loop, 2)
    def _(i):
        loop(half // 2, lambda j: scatter.add_near(i * (half // 2) + j))
        ahead(4 + i)

    scatter.send_far(1)
    for j in range(2):
        bias = jnp.sum(g_qkv_v[:, 2 * j * width : (2 * j + 1) * width].astype(F32), axis=0, keepdims=True)
        small[0, 7:8, j * width : (j + 1) * width] = bias
    small[0, 7:8, 2 * width :] = jnp.zeros((1, depth - 2 * width), F32)
    loop(8, lambda i: ahead(6 + i))
    for level in range(1, scatter.depth):
        scatter.add_far(level)
        scatter.send_far(level + 1)
    loop(count - 13, lambda i: ahead(14 + i))
    loop(behind - 1, lambda i: back(count + 1 - behind + i))

    small[0, 0:5] = sums_in[0:5]
    for k in range(2):
        small[0, 5 + k : 6 + k] = jnp.sum(acc[k], axis=0, keepdims=True)
    rounds = []
    for level, other in enumerate(partners):
        item = pltpu.make_async_remote_copy(
            src_ref=small.at[level], dst_ref=small_got.at[level], send_sem=small_send.at[level],
            recv_sem=small_recv.at[level], device_id=other, device_id_type=MESH,
        )
        item.start()
        item.wait_recv()
        rounds.append(item)
        small[level + 1] = small[level] + small_got[level]
    final = len(partners)
    gains_out[0:1] = small[final, 5:6]
    gains_out[1:2] = small[final, 0:1]
    shifts_out[0:1] = small[final, 6:7]
    shifts_out[1:2] = small[final, 1:2]
    bouts_out[...] = small[final, 2:4]
    bup_out[...] = small[final, 4:5]
    for j in range(2):
        bqv_out[j : j + 1] = small[final, 7:8, j * width : (j + 1) * width]

    def write(tile, value):
        if tile < 3:
            qkv_out[tile] = value
        else:
            w_out_out[...] = value.T

    scatter.finish(write)
    scatter.drain()
    line.drain_all(count)
    for item in rounds:
        item.wait_send()

    @functools.partial(loop, count)
    def _(s):
        at = rows_of(s, SUB)
        pltpu.make_async_copy(g_hidden.at[at], g_x_hbm.at[at], store_sem.at[0, s]).wait()
        pltpu.make_async_copy(out_v.at[at], out_hbm.at[at], store_sem.at[1, s]).wait()


def last(g_qkv, wqkv, x, g_hidden, norm1, g_attn, att, attn_sum, ffn_sum, lengths, until, gains, b_outs, sums):
    rows, depth = x.shape
    width = att.shape[1]
    bands = lax.axis_size("cp")
    chunk = depth // bands
    rounds = bands.bit_length() - 1
    shape = jax.ShapeDtypeStruct
    return pl.pallas_call(
        last_kernel,
        out_shape=(
            shape((rows, depth), F32),
            shape((rows, depth), F32),
            shape((3, chunk, width), F32),
            shape((width, chunk), F32),
            shape((2, depth), F32),
            shape((2, depth), F32),
            shape((2, width), F32),
            shape((2, depth), F32),
            shape((1, depth), F32),
        ),
        in_specs=[ANY] * 9 + [IN_SMEM] * 2 + [IN_VMEM] * 3,
        out_specs=(ANY,) * 2 + (IN_VMEM,) * 7,
        scratch_shapes=[
            pltpu.VMEM((rows, 3 * width), BF16),
            pltpu.VMEM((3, depth, width), BF16),
            pltpu.VMEM((rows, depth), BF16),
            pltpu.VMEM((rows, depth), F32),
            pltpu.VMEM((rows, depth), BF16),
            pltpu.VMEM((rows, depth), BF16),
            pltpu.VMEM((rows, width), BF16),
            pltpu.VMEM((rows, depth), BF16),
            pltpu.VMEM((rows, depth), BF16),
            pltpu.VMEM((rows, depth), F32),
            pltpu.VMEM((2, 8, depth), F32),
            pltpu.VMEM((rounds + 1, 8, depth), F32),
            pltpu.VMEM((rounds, 8, depth), F32),
            pltpu.VMEM((depth, depth), BF16),
            *scatter_scratch(depth, depth, SPLIT_LAST),
            *line_scratch(rows, depth),
            pltpu.SemaphoreType.DMA((rounds,)),
            pltpu.SemaphoreType.DMA((rounds,)),
            pltpu.SemaphoreType.DMA((9,)),
            pltpu.SemaphoreType.DMA((2, rows // SUB)),
        ],
        compiler_params=pltpu.CompilerParams(collective_id=3, has_side_effects=True, vmem_limit_bytes=62 * 2**20),
        name="last",
    )(g_qkv, wqkv, x, g_hidden, norm1, g_attn, att, attn_sum, ffn_sum, lengths, until, gains, b_outs, sums)


def shards(
    layer_input,
    seq_lengths,
    active_until,
    ln_gains,
    ln_shifts,
    query_key_value_weight,
    b_qv,
    w_out,
    b_outs,
    w_up,
    b_up,
    w_down,
    d_out,
):
    wqkv = jnp.transpose(query_key_value_weight, (1, 0, 2))
    attn_sum, norm1, q, kv, att, att_t, lse = attend(
        layer_input, seq_lengths, active_until, ln_gains, ln_shifts, wqkv, b_qv, w_out
    )
    norm2, g_pre, ffn_low, g_hidden, g_attn, sums, g_down = ffn(
        attn_sum, layer_input, d_out, seq_lengths, active_until, ln_gains, ln_shifts, b_outs, b_up[None], w_up, w_down
    )
    g_qkv_rows, ffn_sum, g_up = grad_attend(
        g_attn, w_out, q, kv, att_t, lse, seq_lengths, active_until, ffn_low, norm2, g_pre
    )
    g_x, out, g_qkv, g_out, g_ln_gains, g_ln_shifts, g_bqv, g_bouts, g_bup = last(
        g_qkv_rows, wqkv, layer_input, g_hidden, norm1, g_attn, att, attn_sum, ffn_sum,
        seq_lengths, active_until, ln_gains, b_outs, sums,
    )
    g_qkv = jnp.transpose(g_qkv, (1, 0, 2))
    return (out, g_x, g_ln_gains, g_ln_shifts, g_qkv, g_bqv, g_out, g_bouts, g_up, g_bup[0], g_down)


def solution(mesh):
    return jax.shard_map(
        shards,
        mesh=mesh,
        in_specs=(
            P("cp", None),
            P(),
            P(),
            P(),
            P(),
            P(None, None, "tp"),
            P(None, "tp"),
            P("tp", None),
            P(),
            P(None, "tp"),
            P("tp"),
            P("tp", None),
            P("cp", None),
        ),
        out_specs=(
            P("cp", None),
            P("cp", None),
            P(),
            P(),
            P("cp", None, "tp"),
            P(None, "tp"),
            P("tp", "cp"),
            P(),
            P("cp", "tp"),
            P("tp"),
            P("tp", "cp"),
        ),
        check_vma=False,
    )
```

```python
import functools
import math

import jax
import jax.numpy as jnp
from jax import lax
from jax.experimental import pallas as pl
from jax.experimental.pallas import tpu as pltpu
from jax.sharding import PartitionSpec as P

HD = 64
LONG = 2048
EPS = 1e-05
NEG = -1e30
MESH = pl.DeviceIdType.MESH
F32 = jnp.float32
BF16 = jnp.bfloat16
ANY = pl.BlockSpec(memory_space=pl.ANY)
IN_VMEM = pl.BlockSpec(memory_space=pltpu.VMEM)
IN_SMEM = pl.BlockSpec(memory_space=pltpu.SMEM)
SUB = 32
CHUNK = 256


def dot(a, b):
    return jnp.dot(a, b, preferred_element_type=F32)


def dot_nt(a, b):
    return lax.dot_general(a, b, (((1,), (1,)), ((), ())), preferred_element_type=F32)


def dot_tn(a, b):
    return lax.dot_general(a, b, (((0,), (0,)), ((), ())), preferred_element_type=F32)


def rows_of(index, size):
    return pl.ds(pl.multiple_of(index * size, size), size)


def place():
    cp = lax.axis_index("cp")
    tp = lax.axis_index("tp")
    return cp, tp, lax.rem(cp, 2), lax.div(cp, 2)


def greet(cp, tp, others):
    barrier = pltpu.get_barrier_semaphore()
    edge = (tp == 0) | (tp == 3)
    for other in [*others, (cp, line_near(tp))]:
        pl.semaphore_signal(barrier, inc=1, device_id=other, device_id_type=MESH)

    @pl.when(jnp.logical_not(edge))
    def _():
        pl.semaphore_signal(barrier, inc=1, device_id=(cp, 3 - tp), device_id_type=MESH)

    pl.semaphore_wait(barrier, len(others) + jnp.where(edge, 1, 2))


def line_near(tp):
    return jnp.where(tp == 0, 1, jnp.where(tp == 1, 0, jnp.where(tp == 2, 3, 2)))


class LineSum:
    def __init__(self, part, slot_a, slot_b, total, send, recv):
        self.cp, self.tp, _, _ = place()
        self.edge = (self.tp == 0) | (self.tp == 3)
        self.refs = (part, slot_a, slot_b, total)
        self.send, self.recv = send, recv
        self.count = part.shape[0] // SUB

    def copy(self, kind, s):
        part, slot_a, slot_b, total = self.refs
        src, dst = ((part, slot_a), (part, slot_b), (total, total))[kind]
        other = (self.cp, 3 - self.tp if kind == 1 else line_near(self.tp))
        rows = rows_of(s, SUB)
        return pltpu.make_async_remote_copy(
            src_ref=src.at[rows],
            dst_ref=dst.at[rows],
            send_sem=self.send.at[kind, s],
            recv_sem=self.recv.at[kind, s],
            device_id=other,
            device_id_type=MESH,
        )

    def push(self, s):
        @pl.when(self.edge)
        def _():
            self.copy(0, s).start()

    def relay_in(self, s):
        part, slot_a, _, _ = self.refs

        @pl.when(jnp.logical_not(self.edge))
        def _():
            rows = rows_of(s, SUB)
            self.copy(0, s).wait_recv()
            part[rows] = (part[rows].astype(F32) + slot_a[rows].astype(F32)).astype(BF16)
            self.copy(1, s).start()

    def relay_out(self, s):
        part, _, slot_b, total = self.refs

        @pl.when(jnp.logical_not(self.edge))
        def _():
            rows = rows_of(s, SUB)
            self.copy(1, s).wait_recv()
            total[rows] = (part[rows].astype(F32) + slot_b[rows].astype(F32)).astype(BF16)
            self.copy(2, s).start()

    def get(self, s):
        @pl.when(self.edge)
        def _():
            self.copy(2, s).wait_recv()

    def drain(self, s):
        @pl.when(self.edge)
        def _():
            self.copy(0, s).wait_send()

        @pl.when(jnp.logical_not(self.edge))
        def _():
            self.copy(1, s).wait_send()
            self.copy(2, s).wait_send()

    def tick(self, s):
        @pl.when(s < self.count)
        def _():
            self.relay_in(s)

        @pl.when(s >= 2)
        def _():
            self.relay_out(s - 2)

    def drain_all(self, count):
        def step(s, carry):
            self.drain(s)
            return carry

        lax.fori_loop(0, count, step, 0)


def line_scratch(rows, width, with_part=True):
    count = rows // SUB
    return [pltpu.VMEM((rows, width), BF16)] * 4 + [
        pltpu.SemaphoreType.DMA((3, count)),
        pltpu.SemaphoreType.DMA((3, count)),
    ]


def band_info(lengths_ref, until_ref, first):
    start = jnp.int32(0)
    begin = jnp.int32(0)
    until = jnp.int32(0)
    for i in range(lengths_ref.shape[0]):
        length = lengths_ref[i]
        inside = (first >= start) & (first < start + length)
        begin = jnp.where(inside, start, begin)
        until = jnp.where(inside, until_ref[i], until)
        start = start + length
    return begin, until + begin - first


def loop(count, body):
    def step(i, carry):
        body(i)
        return carry

    lax.fori_loop(0, count, step, 0)


class Scatter:
    def __init__(self, terms, near, far, send, recv, split):
        self.cp, self.tp, self.core, self.chip = place()
        self.count = lax.axis_size("cp")
        self.depth = (self.count // 2).bit_length() - 1
        self.terms, self.near, self.far = terms, near, far
        self.send, self.recv = send, recv
        self.chunk = terms.shape[0] // self.count
        self.width = terms.shape[1]
        self.parts = [p for p in ((0, 0, split), (1, split, self.width)) if p[2] > p[1]]
        self.block = max(self.chunk, 128)

    def partners(self):
        others = [(self.cp + 1 - 2 * self.core, self.tp)]
        for bit in range(self.depth):
            others.append((self.cp + 2 * self.step(bit), self.tp))
        return others

    def step(self, bit):
        return (1 - 2 * self.bit(bit)) * (1 << bit)

    def bit(self, bit):
        return lax.rem(lax.div(self.chip, 1 << bit), 2)

    def fill(self, k, pick):
        if self.block == self.chunk:
            half = self.count // 2
            block = 2 * lax.rem(k, half) + jnp.where(k < half, 1 - self.core, self.core)
        else:
            block = k
        rows = rows_of(block, self.block)
        for tile in range(self.width // 512):
            lanes = slice(tile * 512, (tile + 1) * 512)
            left, right = pick(tile, rows)
            self.terms[rows, lanes] = dot_tn(left, right).astype(BF16)

    def blocks(self):
        return self.terms.shape[0] // self.block

    def near_copy(self, t):
        return pltpu.make_async_remote_copy(
            src_ref=self.terms.at[rows_of(2 * t + 1 - self.core, self.chunk)],
            dst_ref=self.near.at[rows_of(t, self.chunk)],
            send_sem=self.send.at[t],
            recv_sem=self.recv.at[t],
            device_id=(self.cp + 1 - 2 * self.core, self.tp),
            device_id_type=MESH,
        )

    def send_near(self, t):
        self.near_copy(t).start()

    def add_near(self, t):
        self.near_copy(t).wait_recv()
        base = (2 * t + self.core) * self.chunk

        @functools.partial(loop, self.chunk // 64)
        def _(i):
            mine = pl.ds(pl.multiple_of(base + i * 64, 64), 64)
            other = pl.ds(pl.multiple_of(t * self.chunk + i * 64, 64), 64)
            self.terms[mine] = (self.terms[mine].astype(F32) + self.near[other].astype(F32)).astype(BF16)

    def index(self, part, level, t, keep):
        bit = level - 1 if part == 0 else self.depth - level
        own = self.bit(bit)
        own = own if keep else 1 - own
        if part == 0:
            return lax.rem(self.chip, 1 << bit) + own * (1 << bit) + t * (2 << bit), bit
        return self.chip - lax.rem(self.chip, 2 << bit) + own * (1 << bit) + t, bit

    def pieces(self, level):
        first = self.count // 2
        for earlier in range(1, level):
            first += len(self.parts) * (1 << (self.depth - earlier))
        for part, low, high in self.parts:
            for t in range(1 << (self.depth - level)):
                yield part, slice(low, high), t, first
                first += 1

    def far_copy(self, level, part, lanes, t, sem):
        index, bit = self.index(part, level, t, False)
        return pltpu.make_async_remote_copy(
            src_ref=self.terms.at[rows_of(2 * index + self.core, self.chunk), lanes],
            dst_ref=self.far.at[pl.ds(self.place(level) + t * self.chunk, self.chunk), lanes],
            send_sem=self.send.at[sem],
            recv_sem=self.recv.at[sem],
            device_id=(self.cp + 2 * self.step(bit), self.tp),
            device_id_type=MESH,
        )

    def send_far(self, level):
        for piece in self.pieces(level):
            self.far_copy(level, *piece).start()

    def add_far(self, level):
        for part, lanes, t, sem in self.pieces(level):
            self.far_copy(level, part, lanes, t, sem).wait_recv()
            index, _ = self.index(part, level, t, True)
            base = (2 * index + self.core) * self.chunk
            there = self.place(level) + t * self.chunk

            @functools.partial(loop, self.chunk // 64)
            def _(i, base=base, lanes=lanes, there=there):
                mine = pl.ds(pl.multiple_of(base + i * 64, 64), 64)
                other = pl.ds(pl.multiple_of(there + i * 64, 64), 64)
                self.terms[mine, lanes] = (
                    self.terms[mine, lanes].astype(F32) + self.far[other, lanes].astype(F32)
                ).astype(BF16)

    def place(self, level):
        return sum(self.terms.shape[0] >> (earlier + 1) for earlier in range(1, level))

    def finish(self, write):
        level = self.depth
        mine = rows_of(self.cp, self.chunk)
        for part, lanes, t, sem in self.pieces(level):
            self.far_copy(level, part, lanes, t, sem).wait_recv()
            for tile in range(lanes.start // 512, lanes.stop // 512):
                cut = slice(tile * 512, (tile + 1) * 512)
                other = pl.ds(self.place(level), self.chunk)
                write(tile, self.terms[mine, cut].astype(F32) + self.far[other, cut].astype(F32))

    def drain(self):
        loop(self.count // 2, lambda t: self.near_copy(t).wait_send())
        for level in range(1, self.depth + 1):
            for piece in self.pieces(level):
                self.far_copy(level, *piece).wait_send()


def scatter_scratch(depth, width, split):
    count = lax.axis_size("cp")
    parts = (split > 0) + (split < width)
    sems = count // 2 + parts * (count // 2 - 1)
    return [
        pltpu.VMEM((depth // 2, width), BF16),
        pltpu.VMEM((depth // 2 - depth // count, width), BF16),
        pltpu.SemaphoreType.DMA((sems,)),
        pltpu.SemaphoreType.DMA((sems,)),
    ]


def fold(v):
    return jnp.sum(v.reshape(v.shape[0] // 8, 8, v.shape[1]), axis=0)


def gelu_parts(u):
    root = math.sqrt(2.0 / math.pi)
    square = u * u
    th = jnp.tanh(root * (u + 0.044715 * u * square))
    half = 0.5 * (1.0 + th)
    return u * half, half + 0.5 * u * (1.0 - th * th) * (root * (1.0 + 3 * 0.044715 * square))


LAG = 4
SPLIT_DOWN = 1024


def front_kernel(
    x_hbm, d_hbm, lengths_ref, until_ref, gains, shifts, wqkv_hbm, bqv, wout_hbm, b_outs, b_up, up_hbm, down_hbm,
    attn_sum_hbm, norm1_hbm, q_hbm, kv_hbm, att_hbm, att_t_hbm, norm2_hbm, g_pre_hbm, ffn_hbm, g_hidden_hbm,
    g_attn_hbm, lse_out, sums_out, down_out,
    x_v, d_v, norm_v, up_v, down_v, q_v, kv, q_t, v_t, att_t, att_v, xhat, rstd, act_v, g_pre_v, acc,
    part, slot_a, total, slot_b1, slot_b2, ar_send, ar_recv, near, far, rs_send, rs_recv,
    kv_send, kv_recv, load_sem, store_sem,
):
    cp, tp, core, chip = place()
    bands = lax.axis_size("cp")
    chips = bands // 2
    rows, depth = x_v.shape
    width = q_v.shape[1]
    heads = width // HD
    hidden = act_v.shape[1]
    count = rows // SUB
    per_chunk = CHUNK // SUB
    sibling = (cp + 1 - 2 * core, tp)
    after = (lax.rem(cp + 2, bands), tp)
    before = (lax.rem(cp + bands - 2, bands), tp)
    wout_v, scores, g_hidden, g_attn, part2, ffn_v = act_v, xhat, xhat, x_v, v_t, part
    loads = [
        pltpu.make_async_copy(x_hbm, x_v, load_sem.at[0]),
        *[
            pltpu.make_async_copy(
                wqkv_hbm.at[j], up_v.at[:, j * width : (j + 1) * width], load_sem.at[i]
            )
            for i, j in ((1, 1), (2, 2), (3, 0))
        ],
        pltpu.make_async_copy(wout_hbm, wout_v, load_sem.at[4]),
        pltpu.make_async_copy(down_hbm, down_v, load_sem.at[5]),
        pltpu.make_async_copy(d_hbm, d_v, load_sem.at[6]),
        pltpu.make_async_copy(up_hbm, up_v, load_sem.at[7]),
    ]
    for item in loads[:-1]:
        item.start()
    stores = {
        name: pltpu.make_async_copy(source, target, store_sem.at[i])
        for i, (name, source, target) in enumerate(
            (
                ("norm1", norm_v, norm1_hbm),
                ("q", q_v, q_hbm),
                ("kv", kv, kv_hbm),
                ("att", att_v, att_hbm),
                ("att_t", att_t, att_t_hbm),
                ("sum0", total.at[:CHUNK], attn_sum_hbm.at[:CHUNK]),
                ("sum1", total.at[CHUNK:], attn_sum_hbm.at[CHUNK:]),
                ("norm2", norm_v, norm2_hbm),
                ("g_pre", g_pre_v, g_pre_hbm),
                ("ffn", ffn_v, ffn_hbm),
                ("g_hidden", g_hidden, g_hidden_hbm),
                ("g_attn", g_attn, g_attn_hbm),
            )
        )
    }
    line1 = LineSum(part, slot_a, slot_b1, total, ar_send.at[0], ar_recv.at[0])
    line2 = LineSum(part2, slot_a, slot_b2, total, ar_send.at[1], ar_recv.at[1])
    scatter = Scatter(up_v, near, far, rs_send, rs_recv, SPLIT_DOWN)
    greet(cp, tp, [*scatter.partners(), after, before])
    begin, live = band_info(lengths_ref, until_ref, cp * rows)
    bias = jnp.where(begin < chip * 2 * rows, 0.0, NEG)
    loads[0].wait()

    @functools.partial(loop, rows // 64)
    def _(i):
        at = rows_of(i, 64)
        v = x_v[at].astype(F32)
        mean = jnp.mean(v, axis=-1, keepdims=True)
        centred = v - mean
        var = jnp.mean(centred * centred, axis=-1, keepdims=True)
        norm_v[at] = (centred * lax.rsqrt(var + EPS) * gains[0:1] + shifts[0:1]).astype(BF16)

    stores["norm1"].start()
    own = 2 + core

    for load, column in ((1, 0), (2, 1)):
        loads[load].wait()

        @functools.partial(loop, rows // CHUNK)
        def _(i):
            value = dot(norm_v[rows_of(i, CHUNK)], up_v[:, (column + 1) * width : (column + 2) * width])
            if column:
                value = value + bqv[1:2]
            target = pl.ds(pl.multiple_of(own * rows + i * CHUNK, CHUNK), CHUNK)
            kv[target, column * width : (column + 1) * width] = value.astype(BF16)

    def kv_copy(kind, slot, device):
        block = kv.at[rows_of(slot, rows)]
        to = kv.at[rows_of(core, rows)] if kind == 0 else block
        return pltpu.make_async_remote_copy(
            src_ref=block, dst_ref=to, send_sem=kv_send.at[kind], recv_sem=kv_recv.at[kind],
            device_id=device, device_id_type=MESH,
        )

    to_next = kv_copy(0, own, after)
    to_near = kv_copy(1, own, sibling)
    forward = kv_copy(2, core, sibling)

    @pl.when(chip < chips - 1)
    def _():
        to_next.start()

    to_near.start()

    @pl.when(chip == 0)
    def _():
        @functools.partial(loop, 2 * rows // 64)
        def _(i):
            kv[rows_of(i, 64)] = jnp.zeros((64, 2 * width), BF16)

    loads[3].wait()

    @functools.partial(loop, rows // CHUNK)
    def _(i):
        at = rows_of(i, CHUNK)
        value = (dot(norm_v[at], up_v[:, :width]) + bqv[0:1]).astype(BF16)
        q_v[at] = value
        turned = (value.astype(F32) * (HD ** -0.5)).T
        upper = lax.broadcasted_iota(jnp.int32, (2 * HD, CHUNK), 0) < HD
        for h in range(heads):
            both = turned[(h // 2) * 2 * HD : (h // 2 + 1) * 2 * HD]
            q_t[h, :, at] = jnp.where(upper == (h % 2 == 0), both, 0.0).astype(BF16)

    loads[7].start()
    stores["q"].start()
    to_near.wait_recv()

    def turn_values(slot):
        v_t[:, rows_of(slot, rows)] = kv[rows_of(slot, rows), width:].astype(F32).T.astype(BF16)

    turn_values(2)
    turn_values(3)

    @pl.when(chip > 0)
    def _():
        to_next.wait_recv()
        forward.start()
        forward.wait_recv()

    stores["kv"].start()
    turn_values(0)
    turn_values(1)
    loads[4].wait()

    for c in range(rows // CHUNK):
        columns = slice(c * CHUNK, (c + 1) * CHUNK)

        def head(h, c=c, columns=columns):
            lanes = pl.ds(pl.multiple_of(lax.div(h, 2) * 2 * HD, 2 * HD), 2 * HD)
            query = q_t[h, :, columns]
            top = jnp.full((1, CHUNK), NEG, F32)
            for b in range(4):
                s = dot(kv[b * rows : (b + 1) * rows, lanes], query)
                if b < 2:
                    s = s + bias
                else:
                    key = lax.broadcasted_iota(jnp.int32, (rows, CHUNK), 0) + (b - 2) * rows
                    row = lax.broadcasted_iota(jnp.int32, (rows, CHUNK), 1) + c * CHUNK
                    s = jnp.where(key <= row + core * rows, s, NEG)
                scores[:, b * CHUNK : (b + 1) * CHUNK] = s
                top = jnp.maximum(top, jnp.max(s, axis=0, keepdims=True))
            mass = jnp.zeros((1, CHUNK), F32)
            mixed = jnp.zeros((HD, CHUNK), F32)
            feature = pl.ds(pl.multiple_of(h * HD, HD), HD)
            for b in range(4):
                p = jnp.exp(scores[:, b * CHUNK : (b + 1) * CHUNK] - top)
                mass = mass + jnp.sum(p, axis=0, keepdims=True)
                mixed = mixed + dot(v_t[feature, b * rows : (b + 1) * rows], p.astype(BF16))
            att_t[feature, columns] = mixed / mass
            lse_out[pl.ds(h, 1), columns] = top + jnp.log(mass)
            if c > 0:
                @pl.when((h >= 3) & (lax.rem(h, 2) == 1))
                def _():
                    line1.tick(lax.div(h - 3, 2))

        loop(heads, head)
        att_v[columns] = att_t[:, columns].T.astype(BF16)

        @functools.partial(loop, depth // 512)
        def _(t, columns=columns):
            lanes = rows_of(t, 512)
            part[columns, lanes] = dot(att_v[columns], wout_v[:, lanes]).astype(BF16)

        loop(per_chunk, lambda s, c=c: line1.push(s + c * per_chunk))

    stores["att"].start()
    stores["att_t"].start()
    acc[...] = jnp.zeros_like(acc)
    stores["norm1"].wait()
    loads[6].wait()

    def second_norm(s):
        line1.get(s)
        at = rows_of(s, SUB)
        row = lax.broadcasted_iota(jnp.int32, (SUB, 1), 0) + s * SUB
        on = row < live
        v = x_v[at].astype(F32) + jnp.where(on, total[at].astype(F32) + b_outs[0:1], 0.0)
        mean = jnp.mean(v, axis=-1, keepdims=True)
        centred = v - mean
        scale = lax.rsqrt(jnp.mean(centred * centred, axis=-1, keepdims=True) + EPS)
        hat = centred * scale
        xhat[at] = hat
        rstd[at] = jnp.broadcast_to(scale, (SUB, 128))
        norm_v[at] = (hat * gains[1:2] + shifts[1:2]).astype(BF16)
        acc[3] += fold(jnp.where(on, d_v[at].astype(F32), 0.0))

    def feed_forward(c, ticks):
        chunk = slice(c * CHUNK, (c + 1) * CHUNK)
        on = lax.broadcasted_iota(jnp.int32, (CHUNK, 1), 0) + c * CHUNK < live

        @functools.partial(loop, hidden // 512)
        def _(t):
            lanes = rows_of(t, 512)
            pre = dot(norm_v[chunk], up_v[:, lanes]) + b_up[0:1, lanes]
            g_act = dot_nt(d_v[chunk], down_v[lanes])
            act, slope = gelu_parts(pre)
            act_v[chunk, lanes] = jnp.where(on, act, 0.0).astype(BF16)
            g_pre = jnp.where(on, g_act * slope, 0.0).astype(BF16)
            g_pre_v[chunk, lanes] = g_pre
            acc[4, :, lanes] += fold(g_pre.astype(F32))

            @pl.when(lax.rem(t, 2) == 1)
            def _():
                ticks(lax.div(t, 2))

        @functools.partial(loop, depth // 512)
        def _(t):
            lanes = rows_of(t, 512)
            part2[chunk, lanes] = dot_nt(g_pre_v[chunk], up_v[lanes]).astype(BF16)

            @pl.when(lax.rem(t, 2) == 1)
            def _():
                ticks(2 + lax.div(t, 2))

    @functools.partial(loop, per_chunk)
    def _(i):
        line1.tick(3 + i)
        second_norm(i)

    stores["sum0"].start()
    loads[5].wait()
    loads[7].wait()
    feed_forward(0, lambda i: line1.tick(3 + per_chunk + i))
    stores["sum0"].wait()
    loop(per_chunk, line2.push)
    loop(4, lambda i: second_norm(per_chunk + i))
    for i in range(3):
        line1.tick(count - 1 + i)
        second_norm(per_chunk + 4 + i)
    second_norm(count - 1)
    stores["sum1"].start()
    stores["norm2"].start()
    line1.drain_all(count)
    feed_forward(1, line2.tick)
    stores["g_pre"].start()
    stores["sum1"].wait()
    loop(per_chunk, lambda s: line2.push(per_chunk + s))

    def back(s):
        line2.get(s)
        at = rows_of(s, SUB)
        e = total[at].astype(F32)
        hat = xhat[at]
        t = e * gains[1:2]
        along = t - jnp.mean(t, axis=-1, keepdims=True) - hat * jnp.mean(t * hat, axis=-1, keepdims=True)
        value = d_v[at].astype(F32) + along * rstd[at, 0:1]
        g_hidden[at] = value
        row = lax.broadcasted_iota(jnp.int32, (SUB, 1), 0) + s * SUB
        low = jnp.where(row < live, value, 0.0).astype(BF16)
        g_attn[at] = low
        acc[0] += fold(e * hat)
        acc[1] += fold(e)
        acc[2] += fold(low.astype(F32))

    def ahead(s):
        line2.tick(s)
        back(s - LAG)

    def term(k):
        scatter.fill(k, lambda tile, at: (d_v[:, at], act_v[:, tile * 512 : (tile + 1) * 512]))

    def project(k):
        chunk = rows_of(lax.div(k, depth // 512), CHUNK)
        lanes = rows_of(lax.rem(k, depth // 512), 512)
        ffn_v[chunk, lanes] = dot(act_v[chunk], down_v[:, lanes]).astype(BF16)

    blocks, half = scatter.blocks(), scatter.count // 2

    @functools.partial(loop, 4)
    def _(i):
        loop(blocks // 4, lambda j: term(i * (blocks // 4) + j))

        @pl.when((i == 1) if scatter.block == scatter.chunk else (i == 3))
        def _():
            loop(half, scatter.send_near)

        ahead(4 + i)

    @functools.partial(loop, 2)
    def _(i):
        loop(half // 2, lambda j: scatter.add_near(i * (half // 2) + j))
        ahead(8 + i)

    scatter.send_far(1)

    @functools.partial(loop, 4)
    def _(i):
        project(2 * i)
        project(2 * i + 1)
        ahead(10 + i)

    stores["ffn"].start()
    loop(count + 2 - 14, lambda i: ahead(14 + i))
    for level in range(1, scatter.depth):
        scatter.add_far(level)
        scatter.send_far(level + 1)
    loop(LAG - 2, lambda i: back(count - LAG + 2 + i))
    stores["g_hidden"].start()
    stores["g_attn"].start()
    for k in range(5):
        sums_out[k : k + 1] = jnp.sum(acc[k], axis=0, keepdims=True)

    sums_out[5:8] = jnp.zeros((3, sums_out.shape[1]), F32)

    def write(tile, value):
        down_out[tile * 512 : (tile + 1) * 512] = value.T

    scatter.finish(write)
    scatter.drain()
    line2.drain_all(count)

    @pl.when(chip < chips - 1)
    def _():
        to_next.wait_send()

    @pl.when(chip > 0)
    def _():
        forward.wait_send()

    to_near.wait_send()
    for name in ("q", "kv", "att", "att_t", "norm2", "g_pre", "ffn", "g_hidden", "g_attn"):
        stores[name].wait()


def front(x, d_out, lengths, until, gains, shifts, wqkv, bqv, wout, b_outs, b_up, w_up, w_down):
    rows, depth = x.shape
    width = wqkv.shape[2]
    heads = width // HD
    hidden = w_up.shape[1]
    chunk = depth // lax.axis_size("cp")
    count = rows // SUB
    shape = jax.ShapeDtypeStruct
    return pl.pallas_call(
        front_kernel,
        out_shape=(
            shape((rows, depth), BF16),
            shape((rows, depth), BF16),
            shape((rows, width), BF16),
            shape((4 * rows, 2 * width), BF16),
            shape((rows, width), BF16),
            shape((width, rows), F32),
            shape((rows, depth), BF16),
            shape((rows, hidden), BF16),
            shape((rows, depth), BF16),
            shape((rows, depth), F32),
            shape((rows, depth), BF16),
            shape((heads, rows), F32),
            shape((8, depth), F32),
            shape((hidden, chunk), F32),
        ),
        in_specs=[ANY, ANY, IN_SMEM, IN_SMEM, IN_VMEM, IN_VMEM, ANY, IN_VMEM, ANY, IN_VMEM, IN_VMEM, ANY, ANY],
        out_specs=(ANY,) * 11 + (IN_VMEM,) * 3,
        scratch_shapes=[
            pltpu.VMEM((rows, depth), BF16),
            pltpu.VMEM((rows, depth), BF16),
            pltpu.VMEM((rows, depth), BF16),
            pltpu.VMEM((depth, hidden), BF16),
            pltpu.VMEM((hidden, depth), BF16),
            pltpu.VMEM((rows, width), BF16),
            pltpu.VMEM((4 * rows, 2 * width), BF16),
            pltpu.VMEM((heads, 2 * HD, rows), BF16),
            pltpu.VMEM((width, 4 * rows), BF16),
            pltpu.VMEM((width, rows), F32),
            pltpu.VMEM((rows, width), BF16),
            pltpu.VMEM((rows, depth), F32),
            pltpu.VMEM((rows, 128), F32),
            pltpu.VMEM((rows, hidden), BF16),
            pltpu.VMEM((rows, hidden), BF16),
            pltpu.VMEM((5, 8, depth), F32),
            *[pltpu.VMEM((rows, depth), BF16)] * 5,
            pltpu.SemaphoreType.DMA((2, 3, count)),
            pltpu.SemaphoreType.DMA((2, 3, count)),
            *scatter_scratch(depth, hidden, SPLIT_DOWN),
            pltpu.SemaphoreType.DMA((3,)),
            pltpu.SemaphoreType.DMA((3,)),
            pltpu.SemaphoreType.DMA((8,)),
            pltpu.SemaphoreType.DMA((12,)),
        ],
        compiler_params=pltpu.CompilerParams(collective_id=1, has_side_effects=True, vmem_limit_bytes=63 * 2**20),
        name="front",
    )(x, d_out, lengths, until, gains, shifts, wqkv, bqv, wout, b_outs, b_up, w_up, w_down)


SPLIT_UP = 1024
SPLIT_LAST = 1024


def grad_attend_kernel(
    g_attn_hbm, wout_hbm, q_hbm, kv_hbm, att_t_hbm, lse, lengths_ref, until_ref, ffn_hbm, norm_hbm, g_pre_hbm,
    g_qkv_hbm, ffn_sum_hbm, up_out,
    g_attn_v, wout_v, q_v, kv, k_t, att_t, q_t, g_v, g_t, delta, acc, g_qkv_v,
    give_near, got_near, give_before, got_after, give_own, got_own, kv_send, kv_recv,
    norm_v, g_pre_v, terms, near, far, rs_send, rs_recv,
    part, slot_a, slot_b, total, ar_send, ar_recv, load_sem, store_sem,
):
    cp, tp, core, chip = place()
    bands = lax.axis_size("cp")
    chips = bands // 2
    rows, width = q_v.shape
    heads = width // HD
    count = rows // SUB
    sibling = (cp + 1 - 2 * core, tp)
    after = (lax.rem(cp + 2, bands), tp)
    before = (lax.rem(cp + bands - 2, bands), tp)
    loads = [
        pltpu.make_async_copy(source, target, load_sem.at[i])
        for i, (source, target) in enumerate(
            (
                (norm_hbm, norm_v),
                (g_pre_hbm, g_pre_v),
                (ffn_hbm, part),
                (g_attn_hbm, g_attn_v),
                (wout_hbm, wout_v),
                (q_hbm, q_v),
                (kv_hbm, kv),
                (att_t_hbm, att_t),
            )
        )
    ]
    for item in loads:
        item.start()
    line = LineSum(part, slot_a, slot_b, total, ar_send, ar_recv)
    scatter = Scatter(terms, near, far, rs_send, rs_recv, SPLIT_UP)
    greet(cp, tp, [*scatter.partners(), after, before])
    begin, _ = band_info(lengths_ref, until_ref, cp * rows)
    bias = jnp.where(begin < chip * 2 * rows, 0.0, NEG)
    loads[0].wait()
    loads[1].wait()
    loads[2].wait()
    loop(count, line.push)
    blocks, half = scatter.blocks(), scatter.count // 2

    def term(k):
        scatter.fill(k, lambda tile, at: (norm_v[:, at], g_pre_v[:, tile * 512 : (tile + 1) * 512]))

    loop(blocks // 2, term)
    if scatter.block == scatter.chunk:
        loop(half, scatter.send_near)
    loop(blocks - blocks // 2, lambda k: term(blocks // 2 + k))
    if scatter.block != scatter.chunk:
        loop(half, scatter.send_near)

    def relay(s):
        @pl.when(s < count)
        def _():
            line.relay_in(s)

        @pl.when(s > 0)
        def _():
            line.relay_out(s - 1)

    loop(2, relay)
    for item in loads[3:]:
        item.wait()
    scale = HD ** -0.5

    @functools.partial(loop, rows // CHUNK)
    def _(i):
        at = rows_of(i, CHUNK)
        low = dot_nt(g_attn_v[at], wout_v[...]).astype(BF16)
        g_v[at] = low
        turned = low.astype(F32).T
        turned_q = q_v[at].astype(F32).T * scale
        upper = lax.broadcasted_iota(jnp.int32, (2 * HD, CHUNK), 0) < HD
        for h in range(heads):
            both = slice((h // 2) * 2 * HD, (h // 2 + 1) * 2 * HD)
            mine = slice(h * HD, (h + 1) * HD)
            g_t[h, :, at] = jnp.where(upper == (h % 2 == 0), turned[both], 0.0).astype(BF16)
            q_t[h, :, at] = jnp.where(upper == (h % 2 == 0), turned_q[both], 0.0).astype(BF16)
            delta[h : h + 1, at] = jnp.sum(turned[mine] * att_t[mine, at], axis=0, keepdims=True)

    @functools.partial(loop, 4)
    def _(i):
        at = rows_of(i, rows)
        k_t[:, at] = kv[at, :width].astype(F32).T.astype(BF16)

    @functools.partial(loop, rows // 64)
    def _(i):
        att_t[rows_of(i, 64)] = jnp.zeros((64, rows), F32)

    @functools.partial(loop, 4 * rows // 64)
    def _(i):
        acc[rows_of(i, 64)] = jnp.zeros((64, 2 * width), F32)

    g_q_t = att_t
    relay(2)

    def head(h, bands_of):
        offset = lax.div(h, 2) * 2 * HD
        lanes = pl.ds(pl.multiple_of(offset, 2 * HD), 2 * HD)
        lanes_v = pl.ds(pl.multiple_of(offset + width, 2 * HD), 2 * HD)
        feature = pl.ds(pl.multiple_of(h * HD, HD), HD)
        low_lanes = lax.broadcasted_iota(jnp.int32, (CHUNK, 2 * HD), 1) < HD
        mine = low_lanes == (lax.rem(h, 2) == 0)
        for c in range(rows // CHUNK):
            cols = slice(c * CHUNK, (c + 1) * CHUNK)
            q_n = jnp.where(mine, q_v[cols, lanes].astype(F32), 0.0).astype(BF16)
            g_n = jnp.where(mine, g_v[cols, lanes].astype(F32), 0.0).astype(BF16)
            lse_row = lse[pl.ds(h, 1), cols]
            delta_row = delta[pl.ds(h, 1), cols]
            for b in bands_of:
                keys = slice(b * rows, (b + 1) * rows)
                s = dot(kv[keys, lanes], q_t[h, :, cols])
                if b < 2:
                    s = s + (bias - lse_row)
                else:
                    key = lax.broadcasted_iota(jnp.int32, (rows, CHUNK), 0) + (b - 2) * rows
                    row = lax.broadcasted_iota(jnp.int32, (rows, CHUNK), 1) + c * CHUNK
                    s = jnp.where(key <= row + core * rows, s - lse_row, NEG)
                p = jnp.exp(s)
                g_s = (p * (dot(kv[keys, lanes_v], g_t[h, :, cols]) - delta_row)).astype(BF16)
                acc[keys, lanes] += dot(g_s, q_n)
                acc[keys, lanes_v] += dot(p.astype(BF16), g_n)
                g_q_t[feature, cols] += dot(k_t[feature, keys], g_s)

    @functools.partial(loop, heads)
    def _(h):
        head(h, (0, 1))

        @pl.when(h == 0)
        def _():
            loop(half, scatter.add_near)
            scatter.send_far(1)

        @pl.when(lax.rem(h, 2) == 1)
        def _():
            relay(3 + lax.div(h, 2))

    def kv_copy(kind, source, target, device):
        return pltpu.make_async_remote_copy(
            src_ref=source, dst_ref=target, send_sem=kv_send.at[kind], recv_sem=kv_recv.at[kind],
            device_id=device, device_id_type=MESH,
        )

    to_near = kv_copy(0, give_near, got_near, sibling)
    to_before = kv_copy(1, give_before, got_after, before)
    to_own = kv_copy(2, give_own, got_own, sibling)

    def lower(target, slot):
        @functools.partial(loop, rows // 64)
        def _(i):
            at = pl.ds(pl.multiple_of(slot * rows + i * 64, 64), 64)
            target[rows_of(i, 64)] = acc[at].astype(BF16)

    def add_to(slot, source):
        @functools.partial(loop, rows // 64)
        def _(i):
            at = pl.ds(pl.multiple_of(slot * rows + i * 64, 64), 64)
            acc[at] += source[rows_of(i, 64)].astype(F32)

    lower(give_near, 1 - core)
    to_near.start()
    to_near.wait_recv()
    add_to(core, got_near)
    lower(give_before, core)

    @pl.when(chip > 0)
    def _():
        to_before.start()

    @functools.partial(loop, heads)
    def _(h):
        head(h, (2, 3))

        @pl.when(lax.rem(h, 2) == 1)
        def _():
            relay(7 + lax.div(h, 2))

    own = 2 + core
    lower(give_own, 3 - core)
    to_own.start()
    loop(2, lambda i: relay(11 + i))
    levels = scatter.depth
    for level in range(1, levels):
        scatter.add_far(level)
        scatter.send_far(level + 1)
    loop(4, lambda i: relay(13 + i))
    to_own.wait_recv()
    add_to(own, got_own)

    @pl.when(chip < chips - 1)
    def _():
        to_before.wait_recv()
        add_to(own, got_after)

    @functools.partial(loop, rows // 64)
    def _(i):
        at = pl.ds(pl.multiple_of(own * rows + i * 64, 64), 64)
        g_qkv_v[rows_of(i, 64), width : 2 * width] = (acc[at, :width] * scale).astype(BF16)
        g_qkv_v[rows_of(i, 64), 2 * width :] = acc[at, width:].astype(BF16)

    @functools.partial(loop, rows // CHUNK)
    def _(i):
        at = rows_of(i, CHUNK)
        g_qkv_v[at, :width] = (g_q_t[:, at].T * scale).astype(BF16)

    stores = [
        pltpu.make_async_copy(g_qkv_v, g_qkv_hbm, store_sem.at[0]),
        pltpu.make_async_copy(total, ffn_sum_hbm, store_sem.at[1]),
    ]
    stores[0].start()
    loop(count, line.get)
    stores[1].start()

    def write(tile, value):
        up_out[:, tile * 512 : (tile + 1) * 512] = value

    scatter.finish(write)
    scatter.drain()
    line.drain_all(count)
    to_near.wait_send()
    to_own.wait_send()

    @pl.when(chip > 0)
    def _():
        to_before.wait_send()

    for item in stores:
        item.wait()


def grad_attend(g_attn, wout, q, kv, att_t, lse, lengths, until, ffn_low, norm2, g_pre):
    rows, depth = g_attn.shape
    width = q.shape[1]
    heads = width // HD
    hidden = g_pre.shape[1]
    chunk = depth // lax.axis_size("cp")
    shape = jax.ShapeDtypeStruct
    return pl.pallas_call(
        grad_attend_kernel,
        out_shape=(
            shape((rows, 3 * width), BF16),
            shape((rows, depth), BF16),
            shape((chunk, hidden), F32),
        ),
        in_specs=[ANY, ANY, ANY, ANY, ANY, IN_VMEM, IN_SMEM, IN_SMEM, ANY, ANY, ANY],
        out_specs=(ANY, ANY, IN_VMEM),
        scratch_shapes=[
            pltpu.VMEM((rows, depth), BF16),
            pltpu.VMEM((width, depth), BF16),
            pltpu.VMEM((rows, width), BF16),
            pltpu.VMEM((4 * rows, 2 * width), BF16),
            pltpu.VMEM((width, 4 * rows), BF16),
            pltpu.VMEM((width, rows), F32),
            pltpu.VMEM((heads, 2 * HD, rows), BF16),
            pltpu.VMEM((rows, width), BF16),
            pltpu.VMEM((heads, 2 * HD, rows), BF16),
            pltpu.VMEM((heads, rows), F32),
            pltpu.VMEM((4 * rows, 2 * width), F32),
            pltpu.VMEM((rows, 3 * width), BF16),
            *[pltpu.VMEM((rows, 2 * width), BF16)] * 6,
            pltpu.SemaphoreType.DMA((3,)),
            pltpu.SemaphoreType.DMA((3,)),
            pltpu.VMEM((rows, depth), BF16),
            pltpu.VMEM((rows, hidden), BF16),
            pltpu.VMEM((depth, hidden), BF16),
            *scatter_scratch(depth, hidden, SPLIT_UP),
            *line_scratch(rows, depth),
            pltpu.SemaphoreType.DMA((8,)),
            pltpu.SemaphoreType.DMA((2,)),
        ],
        compiler_params=pltpu.CompilerParams(collective_id=2, has_side_effects=True, vmem_limit_bytes=63 * 2**20),
        name="grad_attend",
    )(g_attn, wout, q, kv, att_t, lse, lengths, until, ffn_low, norm2, g_pre)


def last_kernel(
    g_qkv_hbm, wqkv_hbm, x_hbm, g_hidden_hbm, norm_hbm, g_attn_hbm, att_hbm, attn_sum_hbm, ffn_sum_hbm,
    lengths_ref, until_ref, gains, b_outs, sums_in,
    g_x_hbm, out_hbm, qkv_out, w_out_out, gains_out, shifts_out, bqv_out, bouts_out, bup_out,
    g_qkv_v, w_v, x_v, g_hidden, norm_v, g_attn_v, att_v, attn_sum, ffn_sum, out_v, acc, small, small_got,
    terms, near, far, rs_send, rs_recv,
    part, slot_a, slot_b, total, ar_send, ar_recv, small_send, small_recv, load_sem, store_sem,
):
    cp, tp, core, chip = place()
    rows, depth = x_v.shape
    width = att_v.shape[1]
    count = rows // SUB
    loads = [
        pltpu.make_async_copy(source, target, load_sem.at[i])
        for i, (source, target) in enumerate(
            (
                (g_qkv_hbm, g_qkv_v),
                (wqkv_hbm, w_v),
                (norm_hbm, norm_v),
                (g_attn_hbm, g_attn_v),
                (att_hbm, att_v),
                (x_hbm, x_v),
                (g_hidden_hbm, g_hidden),
                (attn_sum_hbm, attn_sum),
                (ffn_sum_hbm, ffn_sum),
            )
        )
    ]
    for item in loads:
        item.start()
    line = LineSum(part, slot_a, slot_b, total, ar_send, ar_recv)
    scatter = Scatter(terms, near, far, rs_send, rs_recv, SPLIT_LAST)
    partners = scatter.partners()
    greet(cp, tp, partners)
    _, live = band_info(lengths_ref, until_ref, cp * rows)
    acc[...] = jnp.zeros_like(acc)
    loads[0].wait()
    loads[1].wait()

    for c in range(rows // CHUNK):
        chunk = slice(c * CHUNK, (c + 1) * CHUNK)

        @functools.partial(loop, depth // 512)
        def _(t, chunk=chunk):
            lanes = rows_of(t, 512)
            value = dot_nt(g_qkv_v[chunk, :width], w_v[0, lanes])
            value = value + dot_nt(g_qkv_v[chunk, width : 2 * width], w_v[1, lanes])
            value = value + dot_nt(g_qkv_v[chunk, 2 * width :], w_v[2, lanes])
            part[chunk, lanes] = value.astype(BF16)

        loop(CHUNK // SUB, lambda s, c=c: line.push(s + c * (CHUNK // SUB)))

    for item in loads[2:]:
        item.wait()

    def back(s):
        line.get(s)
        at = rows_of(s, SUB)
        e = total[at].astype(F32)
        v = x_v[at].astype(F32)
        centred = v - jnp.mean(v, axis=-1, keepdims=True)
        scale = lax.rsqrt(jnp.mean(centred * centred, axis=-1, keepdims=True) + EPS)
        hat = centred * scale
        t = e * gains[0:1]
        along = t - jnp.mean(t, axis=-1, keepdims=True) - hat * jnp.mean(t * hat, axis=-1, keepdims=True)
        g_hidden[at] = g_hidden[at] + along * scale
        row = lax.broadcasted_iota(jnp.int32, (SUB, 1), 0) + s * SUB
        branches = attn_sum[at].astype(F32) + b_outs[0:1] + (ffn_sum[at].astype(F32) + b_outs[1:2])
        out_v[at] = v + jnp.where(row < live, branches, 0.0)
        acc[0] += fold(e * hat)
        acc[1] += fold(e)
        pltpu.make_async_copy(g_hidden.at[at], g_x_hbm.at[at], store_sem.at[0, s]).start()
        pltpu.make_async_copy(out_v.at[at], out_hbm.at[at], store_sem.at[1, s]).start()

    behind = 2

    def ahead(s):
        @pl.when(s < count)
        def _():
            line.relay_in(s)

        @pl.when(s > 0)
        def _():
            line.relay_out(s - 1)

        @pl.when(s >= behind)
        def _():
            back(s - behind)

    def term(k):
        def pick(tile, at):
            if tile < 3:
                return norm_v[:, at], g_qkv_v[:, tile * width : (tile + 1) * width]
            return g_attn_v[:, at], att_v[...]

        scatter.fill(k, pick)

    blocks, half = scatter.blocks(), scatter.count // 2

    @functools.partial(loop, 4)
    def _(i):
        loop(blocks // 4, lambda j: term(i * (blocks // 4) + j))

        @pl.when((i == 1) if scatter.block == scatter.chunk else (i == 3))
        def _():
            loop(half, scatter.send_near)

        ahead(i)

    @functools.partial(loop, 2)
    def _(i):
        loop(half // 2, lambda j: scatter.add_near(i * (half // 2) + j))
        ahead(4 + i)

    scatter.send_far(1)
    for j in range(2):
        bias = jnp.sum(g_qkv_v[:, 2 * j * width : (2 * j + 1) * width].astype(F32), axis=0, keepdims=True)
        small[0, 7:8, j * width : (j + 1) * width] = bias
    small[0, 7:8, 2 * width :] = jnp.zeros((1, depth - 2 * width), F32)
    loop(8, lambda i: ahead(6 + i))
    for level in range(1, scatter.depth):
        scatter.add_far(level)
        scatter.send_far(level + 1)
    loop(count - 13, lambda i: ahead(14 + i))
    loop(behind - 1, lambda i: back(count + 1 - behind + i))

    small[0, 0:5] = sums_in[0:5]
    for k in range(2):
        small[0, 5 + k : 6 + k] = jnp.sum(acc[k], axis=0, keepdims=True)
    rounds = []
    for level, other in enumerate(partners):
        item = pltpu.make_async_remote_copy(
            src_ref=small.at[level], dst_ref=small_got.at[level], send_sem=small_send.at[level],
            recv_sem=small_recv.at[level], device_id=other, device_id_type=MESH,
        )
        item.start()
        item.wait_recv()
        rounds.append(item)
        small[level + 1] = small[level] + small_got[level]
    final = len(partners)
    gains_out[0:1] = small[final, 5:6]
    gains_out[1:2] = small[final, 0:1]
    shifts_out[0:1] = small[final, 6:7]
    shifts_out[1:2] = small[final, 1:2]
    bouts_out[...] = small[final, 2:4]
    bup_out[...] = small[final, 4:5]
    for j in range(2):
        bqv_out[j : j + 1] = small[final, 7:8, j * width : (j + 1) * width]

    def write(tile, value):
        if tile < 3:
            qkv_out[tile] = value
        else:
            w_out_out[...] = value.T

    scatter.finish(write)
    scatter.drain()
    line.drain_all(count)
    for item in rounds:
        item.wait_send()

    @functools.partial(loop, count)
    def _(s):
        at = rows_of(s, SUB)
        pltpu.make_async_copy(g_hidden.at[at], g_x_hbm.at[at], store_sem.at[0, s]).wait()
        pltpu.make_async_copy(out_v.at[at], out_hbm.at[at], store_sem.at[1, s]).wait()


def last(g_qkv, wqkv, x, g_hidden, norm1, g_attn, att, attn_sum, ffn_sum, lengths, until, gains, b_outs, sums):
    rows, depth = x.shape
    width = att.shape[1]
    bands = lax.axis_size("cp")
    chunk = depth // bands
    rounds = bands.bit_length() - 1
    shape = jax.ShapeDtypeStruct
    return pl.pallas_call(
        last_kernel,
        out_shape=(
            shape((rows, depth), F32),
            shape((rows, depth), F32),
            shape((3, chunk, width), F32),
            shape((width, chunk), F32),
            shape((2, depth), F32),
            shape((2, depth), F32),
            shape((2, width), F32),
            shape((2, depth), F32),
            shape((1, depth), F32),
        ),
        in_specs=[ANY] * 9 + [IN_SMEM] * 2 + [IN_VMEM] * 3,
        out_specs=(ANY,) * 2 + (IN_VMEM,) * 7,
        scratch_shapes=[
            pltpu.VMEM((rows, 3 * width), BF16),
            pltpu.VMEM((3, depth, width), BF16),
            pltpu.VMEM((rows, depth), BF16),
            pltpu.VMEM((rows, depth), F32),
            pltpu.VMEM((rows, depth), BF16),
            pltpu.VMEM((rows, depth), BF16),
            pltpu.VMEM((rows, width), BF16),
            pltpu.VMEM((rows, depth), BF16),
            pltpu.VMEM((rows, depth), BF16),
            pltpu.VMEM((rows, depth), F32),
            pltpu.VMEM((2, 8, depth), F32),
            pltpu.VMEM((rounds + 1, 8, depth), F32),
            pltpu.VMEM((rounds, 8, depth), F32),
            pltpu.VMEM((depth, depth), BF16),
            *scatter_scratch(depth, depth, SPLIT_LAST),
            *line_scratch(rows, depth),
            pltpu.SemaphoreType.DMA((rounds,)),
            pltpu.SemaphoreType.DMA((rounds,)),
            pltpu.SemaphoreType.DMA((9,)),
            pltpu.SemaphoreType.DMA((2, rows // SUB)),
        ],
        compiler_params=pltpu.CompilerParams(collective_id=3, has_side_effects=True, vmem_limit_bytes=62 * 2**20),
        name="last",
    )(g_qkv, wqkv, x, g_hidden, norm1, g_attn, att, attn_sum, ffn_sum, lengths, until, gains, b_outs, sums)


def shards(
    layer_input,
    seq_lengths,
    active_until,
    ln_gains,
    ln_shifts,
    query_key_value_weight,
    b_qv,
    w_out,
    b_outs,
    w_up,
    b_up,
    w_down,
    d_out,
):
    wqkv = jnp.transpose(query_key_value_weight, (1, 0, 2))
    (attn_sum, norm1, q, kv, att, att_t, norm2, g_pre, ffn_low, g_hidden, g_attn, lse, sums, g_down) = front(
        layer_input, d_out, seq_lengths, active_until, ln_gains, ln_shifts, wqkv, b_qv, w_out, b_outs, b_up[None],
        w_up, w_down,
    )
    g_qkv_rows, ffn_sum, g_up = grad_attend(
        g_attn, w_out, q, kv, att_t, lse, seq_lengths, active_until, ffn_low, norm2, g_pre
    )
    g_x, out, g_qkv, g_out, g_ln_gains, g_ln_shifts, g_bqv, g_bouts, g_bup = last(
        g_qkv_rows, wqkv, layer_input, g_hidden, norm1, g_attn, att, attn_sum, ffn_sum,
        seq_lengths, active_until, ln_gains, b_outs, sums,
    )
    g_qkv = jnp.transpose(g_qkv, (1, 0, 2))
    return (out, g_x, g_ln_gains, g_ln_shifts, g_qkv, g_bqv, g_out, g_bouts, g_up, g_bup[0], g_down)


def solution(mesh):
    return jax.shard_map(
        shards,
        mesh=mesh,
        in_specs=(
            P("cp", None),
            P(),
            P(),
            P(),
            P(),
            P(None, None, "tp"),
            P(None, "tp"),
            P("tp", None),
            P(),
            P(None, "tp"),
            P("tp"),
            P("tp", None),
            P("cp", None),
        ),
        out_specs=(
            P("cp", None),
            P("cp", None),
            P(),
            P(),
            P("cp", None, "tp"),
            P(None, "tp"),
            P("tp", "cp"),
            P(),
            P("cp", "tp"),
            P("tp"),
            P("tp", "cp"),
        ),
        check_vma=False,
    )
```

```python
import functools
import math

import jax
import jax.numpy as jnp
from jax import lax
from jax.experimental import pallas as pl
from jax.experimental.pallas import tpu as pltpu
from jax.sharding import PartitionSpec as P

HD = 64
LONG = 2048
EPS = 1e-05
NEG = -1e30
MESH = pl.DeviceIdType.MESH
F32 = jnp.float32
BF16 = jnp.bfloat16
ANY = pl.BlockSpec(memory_space=pl.ANY)
IN_VMEM = pl.BlockSpec(memory_space=pltpu.VMEM)
IN_SMEM = pl.BlockSpec(memory_space=pltpu.SMEM)
SUB = 32
CHUNK = 256


def dot(a, b):
    return jnp.dot(a, b, preferred_element_type=F32)


def dot_nt(a, b):
    return lax.dot_general(a, b, (((1,), (1,)), ((), ())), preferred_element_type=F32)


def dot_tn(a, b):
    return lax.dot_general(a, b, (((0,), (0,)), ((), ())), preferred_element_type=F32)


def rows_of(index, size):
    return pl.ds(pl.multiple_of(index * size, size), size)


def place():
    cp = lax.axis_index("cp")
    tp = lax.axis_index("tp")
    return cp, tp, lax.rem(cp, 2), lax.div(cp, 2)


def greet(cp, tp, others):
    barrier = pltpu.get_barrier_semaphore()
    edge = (tp == 0) | (tp == 3)
    for other in [*others, (cp, line_near(tp))]:
        pl.semaphore_signal(barrier, inc=1, device_id=other, device_id_type=MESH)

    @pl.when(jnp.logical_not(edge))
    def _():
        pl.semaphore_signal(barrier, inc=1, device_id=(cp, 3 - tp), device_id_type=MESH)

    pl.semaphore_wait(barrier, len(others) + jnp.where(edge, 1, 2))


def line_near(tp):
    return jnp.where(tp == 0, 1, jnp.where(tp == 1, 0, jnp.where(tp == 2, 3, 2)))


class LineSum:
    def __init__(self, part, slot_a, slot_b, total, send, recv):
        self.cp, self.tp, _, _ = place()
        self.edge = (self.tp == 0) | (self.tp == 3)
        self.refs = (part, slot_a, slot_b, total)
        self.send, self.recv = send, recv
        self.count = part.shape[0] // SUB

    def copy(self, kind, s):
        part, slot_a, slot_b, total = self.refs
        src, dst = ((part, slot_a), (part, slot_b), (total, total))[kind]
        other = (self.cp, 3 - self.tp if kind == 1 else line_near(self.tp))
        rows = rows_of(s, SUB)
        return pltpu.make_async_remote_copy(
            src_ref=src.at[rows],
            dst_ref=dst.at[rows],
            send_sem=self.send.at[kind, s],
            recv_sem=self.recv.at[kind, s],
            device_id=other,
            device_id_type=MESH,
        )

    def push(self, s):
        @pl.when(self.edge)
        def _():
            self.copy(0, s).start()

    def relay_in(self, s):
        part, slot_a, _, _ = self.refs

        @pl.when(jnp.logical_not(self.edge))
        def _():
            rows = rows_of(s, SUB)
            self.copy(0, s).wait_recv()
            part[rows] = (part[rows].astype(F32) + slot_a[rows].astype(F32)).astype(BF16)
            self.copy(1, s).start()

    def relay_out(self, s):
        part, _, slot_b, total = self.refs

        @pl.when(jnp.logical_not(self.edge))
        def _():
            rows = rows_of(s, SUB)
            self.copy(1, s).wait_recv()
            total[rows] = (part[rows].astype(F32) + slot_b[rows].astype(F32)).astype(BF16)
            self.copy(2, s).start()

    def get(self, s):
        @pl.when(self.edge)
        def _():
            self.copy(2, s).wait_recv()

    def drain(self, s):
        @pl.when(self.edge)
        def _():
            self.copy(0, s).wait_send()

        @pl.when(jnp.logical_not(self.edge))
        def _():
            self.copy(1, s).wait_send()
            self.copy(2, s).wait_send()

    def tick(self, s):
        @pl.when(s < self.count)
        def _():
            self.relay_in(s)

        @pl.when(s >= 2)
        def _():
            self.relay_out(s - 2)

    def drain_all(self, count):
        def step(s, carry):
            self.drain(s)
            return carry

        lax.fori_loop(0, count, step, 0)


def line_scratch(rows, width, with_part=True):
    count = rows // SUB
    return [pltpu.VMEM((rows, width), BF16)] * 4 + [
        pltpu.SemaphoreType.DMA((3, count)),
        pltpu.SemaphoreType.DMA((3, count)),
    ]


def band_info(lengths_ref, until_ref, first):
    start = jnp.int32(0)
    begin = jnp.int32(0)
    until = jnp.int32(0)
    for i in range(lengths_ref.shape[0]):
        length = lengths_ref[i]
        inside = (first >= start) & (first < start + length)
        begin = jnp.where(inside, start, begin)
        until = jnp.where(inside, until_ref[i], until)
        start = start + length
    return begin, until + begin - first


def loop(count, body):
    def step(i, carry):
        body(i)
        return carry

    lax.fori_loop(0, count, step, 0)


class Scatter:
    def __init__(self, terms, near, far, send, recv, split):
        self.cp, self.tp, self.core, self.chip = place()
        self.count = lax.axis_size("cp")
        self.depth = (self.count // 2).bit_length() - 1
        self.terms, self.near, self.far = terms, near, far
        self.send, self.recv = send, recv
        self.chunk = terms.shape[0] // self.count
        self.width = terms.shape[1]
        self.parts = [p for p in ((0, 0, split), (1, split, self.width)) if p[2] > p[1]]
        self.block = max(self.chunk, 128)

    def partners(self):
        others = [(self.cp + 1 - 2 * self.core, self.tp)]
        for bit in range(self.depth):
            others.append((self.cp + 2 * self.step(bit), self.tp))
        return others

    def step(self, bit):
        return (1 - 2 * self.bit(bit)) * (1 << bit)

    def bit(self, bit):
        return lax.rem(lax.div(self.chip, 1 << bit), 2)

    def fill(self, k, pick):
        if self.block == self.chunk:
            half = self.count // 2
            block = 2 * lax.rem(k, half) + jnp.where(k < half, 1 - self.core, self.core)
        else:
            block = k
        rows = rows_of(block, self.block)
        for tile in range(self.width // 512):
            lanes = slice(tile * 512, (tile + 1) * 512)
            left, right = pick(tile, rows)
            self.terms[rows, lanes] = dot_tn(left, right).astype(BF16)

    def blocks(self):
        return self.terms.shape[0] // self.block

    def near_copy(self, t):
        return pltpu.make_async_remote_copy(
            src_ref=self.terms.at[rows_of(2 * t + 1 - self.core, self.chunk)],
            dst_ref=self.near.at[rows_of(t, self.chunk)],
            send_sem=self.send.at[t],
            recv_sem=self.recv.at[t],
            device_id=(self.cp + 1 - 2 * self.core, self.tp),
            device_id_type=MESH,
        )

    def send_near(self, t):
        self.near_copy(t).start()

    def add_near(self, t):
        self.near_copy(t).wait_recv()
        base = (2 * t + self.core) * self.chunk

        @functools.partial(loop, self.chunk // 64)
        def _(i):
            mine = pl.ds(pl.multiple_of(base + i * 64, 64), 64)
            other = pl.ds(pl.multiple_of(t * self.chunk + i * 64, 64), 64)
            self.terms[mine] = (self.terms[mine].astype(F32) + self.near[other].astype(F32)).astype(BF16)

    def index(self, part, level, t, keep):
        bit = level - 1 if part == 0 else self.depth - level
        own = self.bit(bit)
        own = own if keep else 1 - own
        if part == 0:
            return lax.rem(self.chip, 1 << bit) + own * (1 << bit) + t * (2 << bit), bit
        return self.chip - lax.rem(self.chip, 2 << bit) + own * (1 << bit) + t, bit

    def pieces(self, level):
        first = self.count // 2
        for earlier in range(1, level):
            first += len(self.parts) * (1 << (self.depth - earlier))
        for part, low, high in self.parts:
            for t in range(1 << (self.depth - level)):
                yield part, slice(low, high), t, first
                first += 1

    def far_copy(self, level, part, lanes, t, sem):
        index, bit = self.index(part, level, t, False)
        return pltpu.make_async_remote_copy(
            src_ref=self.terms.at[rows_of(2 * index + self.core, self.chunk), lanes],
            dst_ref=self.far.at[pl.ds(self.place(level) + t * self.chunk, self.chunk), lanes],
            send_sem=self.send.at[sem],
            recv_sem=self.recv.at[sem],
            device_id=(self.cp + 2 * self.step(bit), self.tp),
            device_id_type=MESH,
        )

    def send_far(self, level):
        for piece in self.pieces(level):
            self.far_copy(level, *piece).start()

    def add_far(self, level):
        for part, lanes, t, sem in self.pieces(level):
            self.far_copy(level, part, lanes, t, sem).wait_recv()
            index, _ = self.index(part, level, t, True)
            base = (2 * index + self.core) * self.chunk
            there = self.place(level) + t * self.chunk

            @functools.partial(loop, self.chunk // 64)
            def _(i, base=base, lanes=lanes, there=there):
                mine = pl.ds(pl.multiple_of(base + i * 64, 64), 64)
                other = pl.ds(pl.multiple_of(there + i * 64, 64), 64)
                self.terms[mine, lanes] = (
                    self.terms[mine, lanes].astype(F32) + self.far[other, lanes].astype(F32)
                ).astype(BF16)

    def place(self, level):
        return sum(self.terms.shape[0] >> (earlier + 1) for earlier in range(1, level))

    def finish(self, write):
        level = self.depth
        mine = rows_of(self.cp, self.chunk)
        for part, lanes, t, sem in self.pieces(level):
            self.far_copy(level, part, lanes, t, sem).wait_recv()
            for tile in range(lanes.start // 512, lanes.stop // 512):
                cut = slice(tile * 512, (tile + 1) * 512)
                other = pl.ds(self.place(level), self.chunk)
                write(tile, self.terms[mine, cut].astype(F32) + self.far[other, cut].astype(F32))

    def drain(self):
        loop(self.count // 2, lambda t: self.near_copy(t).wait_send())
        for level in range(1, self.depth + 1):
            for piece in self.pieces(level):
                self.far_copy(level, *piece).wait_send()


def scatter_scratch(depth, width, split):
    count = lax.axis_size("cp")
    parts = (split > 0) + (split < width)
    sems = count // 2 + parts * (count // 2 - 1)
    return [
        pltpu.VMEM((depth // 2, width), BF16),
        pltpu.VMEM((depth // 2 - depth // count, width), BF16),
        pltpu.SemaphoreType.DMA((sems,)),
        pltpu.SemaphoreType.DMA((sems,)),
    ]


def fold(v):
    return jnp.sum(v.reshape(v.shape[0] // 8, 8, v.shape[1]), axis=0)


def gelu_parts(u):
    root = math.sqrt(2.0 / math.pi)
    square = u * u
    th = jnp.tanh(root * (u + 0.044715 * u * square))
    half = 0.5 * (1.0 + th)
    return u * half, half + 0.5 * u * (1.0 - th * th) * (root * (1.0 + 3 * 0.044715 * square))


LAG = 5
SPLIT_DOWN = 1024


def front_kernel(
    x_hbm, d_hbm, lengths_ref, until_ref, gains, shifts, wqkv_hbm, bqv, wout_hbm, b_outs, b_up, up_hbm, down_hbm,
    attn_sum_hbm, norm1_hbm, q_hbm, q_next_hbm, kv_hbm, att_hbm, att_t_hbm, norm2_hbm, g_pre_hbm, ffn_hbm, g_hidden_hbm,
    g_attn_hbm, lse_out, sums_out, down_out,
    x_v, d_v, norm_v, up_v, down_v, q_v, q_next, kv, q_t, q_t_next, v_t, att_t, att_v, cross, cross_in, lse_cross, lse_in, xhat, rstd, act_v, g_pre_v, acc,
    part, slot_a, total, slot_b1, slot_b2, ar_send, ar_recv, near, far, rs_send, rs_recv,
    x_send, x_recv, load_sem, store_sem,
):
    cp, tp, core, chip = place()
    bands = lax.axis_size("cp")
    chips = bands // 2
    rows, depth = x_v.shape
    width = q_v.shape[1]
    heads = width // HD
    hidden = act_v.shape[1]
    count = rows // SUB
    per_chunk = CHUNK // SUB
    sibling = (cp + 1 - 2 * core, tp)
    after = (lax.rem(cp + 2, bands), tp)
    before = (lax.rem(cp + bands - 2, bands), tp)
    wout_v, scores, g_hidden, g_attn, part2, ffn_v = act_v, xhat, xhat, x_v, v_t, part
    loads = [
        pltpu.make_async_copy(x_hbm, x_v, load_sem.at[0]),
        *[
            pltpu.make_async_copy(
                wqkv_hbm.at[j], up_v.at[:, j * width : (j + 1) * width], load_sem.at[i]
            )
            for i, j in ((1, 0), (2, 1), (3, 2))
        ],
        pltpu.make_async_copy(wout_hbm, wout_v, load_sem.at[4]),
        pltpu.make_async_copy(down_hbm, down_v, load_sem.at[5]),
        pltpu.make_async_copy(d_hbm, d_v, load_sem.at[6]),
        pltpu.make_async_copy(up_hbm, up_v, load_sem.at[7]),
    ]
    for item in loads[:4]:
        item.start()
    stores = {
        name: pltpu.make_async_copy(source, target, store_sem.at[i])
        for i, (name, source, target) in enumerate(
            (
                ("norm1", norm_v, norm1_hbm),
                ("q", q_v, q_hbm),
                ("kv", kv, kv_hbm),
                ("q_next", q_next, q_next_hbm),
                ("att", att_v, att_hbm),
                ("att_t", att_t, att_t_hbm),
                ("sum0", total.at[:CHUNK], attn_sum_hbm.at[:CHUNK]),
                ("sum1", total.at[CHUNK:], attn_sum_hbm.at[CHUNK:]),
                ("norm2", norm_v, norm2_hbm),
                ("g_pre", g_pre_v, g_pre_hbm),
                ("ffn", ffn_v, ffn_hbm),
                ("g_hidden", g_hidden, g_hidden_hbm),
                ("g_attn", g_attn, g_attn_hbm),
            )
        )
    }
    line1 = LineSum(part, slot_a, slot_b1, total, ar_send.at[0], ar_recv.at[0])
    line2 = LineSum(part2, slot_a, slot_b2, total, ar_send.at[1], ar_recv.at[1])
    scatter = Scatter(up_v, near, far, rs_send, rs_recv, SPLIT_DOWN)
    greet(cp, tp, [*scatter.partners(), after, before])
    _, live = band_info(lengths_ref, until_ref, cp * rows)
    begin, _ = band_info(lengths_ref, until_ref, (chip + 1) * 2 * rows)
    bias = jnp.where(begin < (chip + 1) * 2 * rows, 0.0, NEG)
    loads[0].wait()

    @functools.partial(loop, rows // 64)
    def _(i):
        at = rows_of(i, 64)
        v = x_v[at].astype(F32)
        mean = jnp.mean(v, axis=-1, keepdims=True)
        centred = v - mean
        var = jnp.mean(centred * centred, axis=-1, keepdims=True)
        norm_v[at] = (centred * lax.rsqrt(var + EPS) * gains[0:1] + shifts[0:1]).astype(BF16)

    stores["norm1"].start()
    pairs = heads // 2

    def exchange(kind, p):
        lanes = slice(p * 2 * HD, (p + 1) * 2 * HD)
        source, target, device = (
            (q_v.at[:, lanes], q_next.at[:, lanes], before),
            (cross.at[lanes], cross_in.at[lanes], after),
            (lse_cross, lse_in, after),
            (kv.at[rows_of(core, rows)], kv.at[rows_of(core, rows)], sibling),
        )[kind]
        sem = (p, pairs + p, 2 * pairs, 2 * pairs + 1)[kind]
        return pltpu.make_async_remote_copy(
            src_ref=source, dst_ref=target, send_sem=x_send.at[sem], recv_sem=x_recv.at[sem],
            device_id=device, device_id_type=MESH,
        )

    queries = [exchange(0, p) for p in range(pairs)]
    gathered = [exchange(1, p) for p in range(pairs)] + [exchange(2, 0)]
    to_near = exchange(3, 0)
    has_before, has_after = chip > 0, chip < chips - 1
    loads[1].wait()

    @functools.partial(loop, rows // CHUNK)
    def _(i):
        at = rows_of(i, CHUNK)
        q_v[at] = (dot(norm_v[at], up_v[:, :width]) + bqv[0:1]).astype(BF16)

    @pl.when(has_before)
    def _():
        for item in queries:
            item.start()

    @pl.when(jnp.logical_not(has_after))
    def _():
        q_next[...] = jnp.zeros_like(q_next)

    @pl.when(jnp.logical_not(has_before))
    def _():
        cross_in[...] = jnp.zeros_like(cross_in)
        lse_in[...] = jnp.full_like(lse_in, NEG)

    for load, column in ((2, 0), (3, 1)):
        loads[load].wait()

        @functools.partial(loop, rows // CHUNK)
        def _(i):
            value = dot(norm_v[rows_of(i, CHUNK)], up_v[:, (column + 1) * width : (column + 2) * width])
            if column:
                value = value + bqv[1:2]
            target = pl.ds(pl.multiple_of(core * rows + i * CHUNK, CHUNK), CHUNK)
            kv[target, column * width : (column + 1) * width] = value.astype(BF16)

    to_near.start()
    for item in loads[4:]:
        item.start()
    stores["q"].start()

    def turned(value, h):
        upper = lax.broadcasted_iota(jnp.int32, value.shape, 0) < HD
        return jnp.where(upper == (h % 2 == 0), value, 0.0).astype(BF16)

    @functools.partial(loop, rows // CHUNK)
    def _(i):
        at = rows_of(i, CHUNK)
        value = q_v[at].astype(F32).T * (HD ** -0.5)
        for h in range(heads):
            q_t[h, :, at] = turned(value[(h // 2) * 2 * HD : (h // 2 + 1) * 2 * HD], h)

    def turn_values(slot):
        v_t[:, rows_of(slot, rows)] = kv[rows_of(slot, rows), width:].astype(F32).T.astype(BF16)

    turn_values(core)
    to_near.wait_recv()
    stores["kv"].start()
    turn_values(1 - core)

    def attend(query, lanes, feature, mask):
        top = jnp.full((1, CHUNK), NEG, F32)
        for b in range(2):
            s = mask(b, dot(kv[b * rows : (b + 1) * rows, lanes], query))
            scores[:, b * CHUNK : (b + 1) * CHUNK] = s
            top = jnp.maximum(top, jnp.max(s, axis=0, keepdims=True))
        mass = jnp.zeros((1, CHUNK), F32)
        mixed = jnp.zeros((HD, CHUNK), F32)
        for b in range(2):
            p = jnp.exp(scores[:, b * CHUNK : (b + 1) * CHUNK] - top)
            mass = mass + jnp.sum(p, axis=0, keepdims=True)
            mixed = mixed + dot(v_t[feature, b * rows : (b + 1) * rows], p.astype(BF16))
        return mixed / mass, top + jnp.log(mass)

    def cross_pair(p):
        start = p * 2 * HD
        lanes = pl.ds(start, 2 * HD)
        queries[p].wait_recv()
        value = q_next[:, lanes].astype(F32).T * (HD ** -0.5)
        for parity in range(2):
            q_t_next[parity] = turned(value, parity)

        @functools.partial(loop, 2)
        def _(parity):
            h = 2 * p + parity
            feature = pl.ds(pl.multiple_of(h * HD, HD), HD)
            for c in range(rows // CHUNK):
                columns = slice(c * CHUNK, (c + 1) * CHUNK)
                mixed, lse_row = attend(q_t_next[parity, :, columns], lanes, feature, lambda b, s: s + bias)
                cross[feature, columns] = mixed.astype(BF16)
                lse_cross[pl.ds(h, 1), columns] = lse_row

        gathered[p].start()

    @pl.when(has_after)
    def _():
        for p in range(pairs):
            cross_pair(p)
        gathered[pairs].start()

    stores["q_next"].start()
    loads[4].wait()

    for c in range(rows // CHUNK):
        columns = slice(c * CHUNK, (c + 1) * CHUNK)

        def causal(b, s, c=c):
            key = lax.broadcasted_iota(jnp.int32, (rows, CHUNK), 0) + b * rows
            row = lax.broadcasted_iota(jnp.int32, (rows, CHUNK), 1) + c * CHUNK
            return jnp.where(key <= row + core * rows, s, NEG)

        def head(h, c=c, columns=columns, causal=causal):
            lanes = pl.ds(pl.multiple_of(lax.div(h, 2) * 2 * HD, 2 * HD), 2 * HD)
            feature = pl.ds(pl.multiple_of(h * HD, HD), HD)
            mixed, lse_row = attend(q_t[h, :, columns], lanes, feature, causal)
            att_t[feature, columns] = mixed
            lse_out[pl.ds(h, 1), columns] = lse_row
            if c > 0:
                @pl.when(lax.rem(h, 2) == 1)
                def _():
                    line1.tick(lax.div(h, 2))

        loop(heads, head)
        if c == 0:
            @pl.when(has_before)
            def _():
                for item in gathered:
                    item.wait_recv()

        mine, other = lse_out[:, columns], lse_in[:, columns]
        top = jnp.maximum(mine, other)
        both = top + jnp.log(jnp.exp(mine - top) + jnp.exp(other - top))
        share, share_in = jnp.exp(mine - both), jnp.exp(other - both)
        lse_out[:, columns] = both
        for h in range(heads):
            feature = slice(h * HD, (h + 1) * HD)
            att_t[feature, columns] = (
                att_t[feature, columns] * share[h : h + 1]
                + cross_in[feature, columns].astype(F32) * share_in[h : h + 1]
            )
        att_v[columns] = att_t[:, columns].T.astype(BF16)

        @functools.partial(loop, depth // 512)
        def _(t, columns=columns):
            lanes = rows_of(t, 512)
            part[columns, lanes] = dot(att_v[columns], wout_v[:, lanes]).astype(BF16)

        loop(per_chunk, lambda s, c=c: line1.push(s + c * per_chunk))

    stores["att"].start()
    stores["att_t"].start()
    acc[...] = jnp.zeros_like(acc)
    stores["norm1"].wait()
    loads[6].wait()

    def second_norm(s):
        line1.get(s)
        at = rows_of(s, SUB)
        row = lax.broadcasted_iota(jnp.int32, (SUB, 1), 0) + s * SUB
        on = row < live
        v = x_v[at].astype(F32) + jnp.where(on, total[at].astype(F32) + b_outs[0:1], 0.0)
        mean = jnp.mean(v, axis=-1, keepdims=True)
        centred = v - mean
        scale = lax.rsqrt(jnp.mean(centred * centred, axis=-1, keepdims=True) + EPS)
        hat = centred * scale
        xhat[at] = hat
        rstd[at] = jnp.broadcast_to(scale, (SUB, 128))
        norm_v[at] = (hat * gains[1:2] + shifts[1:2]).astype(BF16)
        acc[3] += fold(jnp.where(on, d_v[at].astype(F32), 0.0))

    def feed_forward(c, ticks):
        chunk = slice(c * CHUNK, (c + 1) * CHUNK)
        on = lax.broadcasted_iota(jnp.int32, (CHUNK, 1), 0) + c * CHUNK < live

        @functools.partial(loop, hidden // 512)
        def _(t):
            lanes = rows_of(t, 512)
            pre = dot(norm_v[chunk], up_v[:, lanes]) + b_up[0:1, lanes]
            g_act = dot_nt(d_v[chunk], down_v[lanes])
            act, slope = gelu_parts(pre)
            act_v[chunk, lanes] = jnp.where(on, act, 0.0).astype(BF16)
            g_pre = jnp.where(on, g_act * slope, 0.0).astype(BF16)
            g_pre_v[chunk, lanes] = g_pre
            acc[4, :, lanes] += fold(g_pre.astype(F32))

            @pl.when(lax.rem(t, 2) == 1)
            def _():
                ticks(lax.div(t, 2))

        @functools.partial(loop, depth // 512)
        def _(t):
            lanes = rows_of(t, 512)
            part2[chunk, lanes] = dot_nt(g_pre_v[chunk], up_v[lanes]).astype(BF16)

            @pl.when(lax.rem(t, 2) == 1)
            def _():
                ticks(2 + lax.div(t, 2))

    @functools.partial(loop, per_chunk)
    def _(i):
        line1.tick(4 + i)
        second_norm(i)

    stores["sum0"].start()
    loads[5].wait()
    loads[7].wait()
    feed_forward(0, lambda i: line1.tick(4 + per_chunk + i))
    stores["sum0"].wait()
    loop(per_chunk, line2.push)
    loop(4, lambda i: second_norm(per_chunk + i))
    for i in range(2):
        line1.tick(count + i)
        line2.relay_in(i)
        second_norm(per_chunk + 4 + 2 * i)
        second_norm(per_chunk + 5 + 2 * i)
    stores["sum1"].start()
    stores["norm2"].start()
    line1.drain_all(count)
    feed_forward(1, lambda i: line2.tick(2 + i))
    stores["g_pre"].start()
    stores["sum1"].wait()
    loop(per_chunk, lambda s: line2.push(per_chunk + s))

    def back(s):
        line2.get(s)
        at = rows_of(s, SUB)
        e = total[at].astype(F32)
        hat = xhat[at]
        t = e * gains[1:2]
        along = t - jnp.mean(t, axis=-1, keepdims=True) - hat * jnp.mean(t * hat, axis=-1, keepdims=True)
        value = d_v[at].astype(F32) + along * rstd[at, 0:1]
        g_hidden[at] = value
        row = lax.broadcasted_iota(jnp.int32, (SUB, 1), 0) + s * SUB
        low = jnp.where(row < live, value, 0.0).astype(BF16)
        g_attn[at] = low
        acc[0] += fold(e * hat)
        acc[1] += fold(e)
        acc[2] += fold(low.astype(F32))

    def ahead(s):
        line2.tick(s)
        back(s - LAG)

    def term(k):
        scatter.fill(k, lambda tile, at: (d_v[:, at], act_v[:, tile * 512 : (tile + 1) * 512]))

    def project(k):
        chunk = rows_of(lax.div(k, depth // 512), CHUNK)
        lanes = rows_of(lax.rem(k, depth // 512), 512)
        ffn_v[chunk, lanes] = dot(act_v[chunk], down_v[:, lanes]).astype(BF16)

    blocks, half = scatter.blocks(), scatter.count // 2

    @functools.partial(loop, 2)
    def _(i):
        loop(blocks // 2, lambda j: term(i * (blocks // 2) + j))

        @pl.when((i == 0) if scatter.block == scatter.chunk else (i == 1))
        def _():
            loop(half, scatter.send_near)

        line2.tick(6 + i)

    line2.tick(8)
    loop(half, scatter.add_near)
    scatter.send_far(1)
    loop(4, lambda i: back(i))

    @functools.partial(loop, 4)
    def _(i):
        project(2 * i)
        project(2 * i + 1)
        ahead(9 + i)

    stores["ffn"].start()
    loop(count + 2 - 13, lambda i: ahead(13 + i))
    for level in range(1, scatter.depth):
        scatter.add_far(level)
        scatter.send_far(level + 1)
    loop(LAG - 2, lambda i: back(count - LAG + 2 + i))
    stores["g_hidden"].start()
    stores["g_attn"].start()
    for k in range(5):
        sums_out[k : k + 1] = jnp.sum(acc[k], axis=0, keepdims=True)

    sums_out[5:8] = jnp.zeros((3, sums_out.shape[1]), F32)

    def write(tile, value):
        down_out[tile * 512 : (tile + 1) * 512] = value.T

    scatter.finish(write)
    scatter.drain()
    line2.drain_all(count)

    to_near.wait_send()

    @pl.when(has_before)
    def _():
        for item in queries:
            item.wait_send()

    @pl.when(has_after)
    def _():
        for item in gathered:
            item.wait_send()

    for name in ("q", "q_next", "kv", "att", "att_t", "norm2", "g_pre", "ffn", "g_hidden", "g_attn"):
        stores[name].wait()


def front(x, d_out, lengths, until, gains, shifts, wqkv, bqv, wout, b_outs, b_up, w_up, w_down):
    rows, depth = x.shape
    width = wqkv.shape[2]
    heads = width // HD
    hidden = w_up.shape[1]
    chunk = depth // lax.axis_size("cp")
    count = rows // SUB
    shape = jax.ShapeDtypeStruct
    return pl.pallas_call(
        front_kernel,
        out_shape=(
            shape((rows, depth), BF16),
            shape((rows, depth), BF16),
            shape((rows, width), BF16),
            shape((rows, width), BF16),
            shape((2 * rows, 2 * width), BF16),
            shape((rows, width), BF16),
            shape((width, rows), F32),
            shape((rows, depth), BF16),
            shape((rows, hidden), BF16),
            shape((rows, depth), BF16),
            shape((rows, depth), F32),
            shape((rows, depth), BF16),
            shape((heads, rows), F32),
            shape((8, depth), F32),
            shape((hidden, chunk), F32),
        ),
        in_specs=[ANY, ANY, IN_SMEM, IN_SMEM, IN_VMEM, IN_VMEM, ANY, IN_VMEM, ANY, IN_VMEM, IN_VMEM, ANY, ANY],
        out_specs=(ANY,) * 12 + (IN_VMEM,) * 3,
        scratch_shapes=[
            pltpu.VMEM((rows, depth), BF16),
            pltpu.VMEM((rows, depth), BF16),
            pltpu.VMEM((rows, depth), BF16),
            pltpu.VMEM((depth, hidden), BF16),
            pltpu.VMEM((hidden, depth), BF16),
            pltpu.VMEM((rows, width), BF16),
            pltpu.VMEM((rows, width), BF16),
            pltpu.VMEM((2 * rows, 2 * width), BF16),
            pltpu.VMEM((heads, 2 * HD, rows), BF16),
            pltpu.VMEM((2, 2 * HD, rows), BF16),
            pltpu.VMEM((width, depth), BF16),
            pltpu.VMEM((width, rows), F32),
            pltpu.VMEM((rows, width), BF16),
            pltpu.VMEM((width, rows), BF16),
            pltpu.VMEM((width, rows), BF16),
            pltpu.VMEM((heads, rows), F32),
            pltpu.VMEM((heads, rows), F32),
            pltpu.VMEM((rows, depth), F32),
            pltpu.VMEM((rows, 128), F32),
            pltpu.VMEM((rows, hidden), BF16),
            pltpu.VMEM((rows, hidden), BF16),
            pltpu.VMEM((5, 8, depth), F32),
            *[pltpu.VMEM((rows, depth), BF16)] * 5,
            pltpu.SemaphoreType.DMA((2, 3, count)),
            pltpu.SemaphoreType.DMA((2, 3, count)),
            *scatter_scratch(depth, hidden, SPLIT_DOWN),
            pltpu.SemaphoreType.DMA((heads + 2,)),
            pltpu.SemaphoreType.DMA((heads + 2,)),
            pltpu.SemaphoreType.DMA((8,)),
            pltpu.SemaphoreType.DMA((13,)),
        ],
        compiler_params=pltpu.CompilerParams(collective_id=1, has_side_effects=True, vmem_limit_bytes=63 * 2**20),
        name="front",
    )(x, d_out, lengths, until, gains, shifts, wqkv, bqv, wout, b_outs, b_up, w_up, w_down)


SPLIT_UP = 1024
SPLIT_LAST = 1024


def grad_attend_kernel(
    g_attn_hbm, wout_hbm, q_hbm, q_next_hbm, kv_hbm, att_t_hbm, lse, lengths_ref, until_ref, ffn_hbm, norm_hbm, g_pre_hbm,
    g_qkv_hbm, ffn_sum_hbm, up_out,
    g_attn_v, wout_v, q_v, q_next, kv, k_t, att_t, q_t, g_v, g_next, g_t, stats, stats_next, acc, g_qkv_v,
    g_q_next, give_q, got_q, give_near, got_near, x_send, x_recv,
    norm_v, g_pre_v, terms, near, far, rs_send, rs_recv,
    part, slot_a, slot_b, total, ar_send, ar_recv, load_sem, store_sem,
):
    cp, tp, core, chip = place()
    bands = lax.axis_size("cp")
    chips = bands // 2
    rows, width = q_v.shape
    heads = width // HD
    count = rows // SUB
    sibling = (cp + 1 - 2 * core, tp)
    after = (lax.rem(cp + 2, bands), tp)
    before = (lax.rem(cp + bands - 2, bands), tp)
    loads = [
        pltpu.make_async_copy(source, target, load_sem.at[i])
        for i, (source, target) in enumerate(
            (
                (norm_hbm, norm_v),
                (g_pre_hbm, g_pre_v),
                (ffn_hbm, part),
                (g_attn_hbm, g_attn_v),
                (wout_hbm, wout_v),
                (q_hbm, q_v),
                (q_next_hbm, q_next),
                (kv_hbm, kv),
                (att_t_hbm, att_t),
            )
        )
    ]
    for item in loads[:5]:
        item.start()
    line = LineSum(part, slot_a, slot_b, total, ar_send, ar_recv)
    scatter = Scatter(terms, near, far, rs_send, rs_recv, SPLIT_UP)
    greet(cp, tp, [*scatter.partners(), after, before])
    begin, _ = band_info(lengths_ref, until_ref, (chip + 1) * 2 * rows)
    has_before, has_after = chip > 0, chip < chips - 1
    bias = jnp.where((begin < (chip + 1) * 2 * rows) & has_after, 0.0, NEG)
    loads[0].wait()
    loads[1].wait()
    loads[2].wait()
    loop(count, line.push)
    blocks, half = scatter.blocks(), scatter.count // 2

    def term(k):
        scatter.fill(k, lambda tile, at: (norm_v[:, at], g_pre_v[:, tile * 512 : (tile + 1) * 512]))

    for item in loads[5:]:
        item.start()
    loop(blocks // 2, term)
    if scatter.block == scatter.chunk:
        loop(half, scatter.send_near)
    relay = line.tick
    relay(0)
    for item in loads[3:]:
        item.wait()
    scale = HD ** -0.5

    pairs = heads // 2

    def exchange(kind, p=0):
        lanes = slice(p * 2 * HD, (p + 1) * 2 * HD)
        source, target, device = (
            (g_v, g_next, before),
            (stats, stats_next, before),
            (give_near, got_near, sibling),
            (give_q.at[lanes], got_q.at[lanes], after),
        )[kind]
        return pltpu.make_async_remote_copy(
            src_ref=source, dst_ref=target, send_sem=x_send.at[kind + p], recv_sem=x_recv.at[kind + p],
            device_id=device, device_id_type=MESH,
        )

    to_before = [exchange(0), exchange(1)]
    to_near = exchange(2)
    to_after = [exchange(3, p) for p in range(pairs)]

    def turn(source, target, factor):
        @functools.partial(loop, rows // CHUNK)
        def _(i):
            at = rows_of(i, CHUNK)
            value = source[at].astype(F32).T * factor
            upper = lax.broadcasted_iota(jnp.int32, (2 * HD, CHUNK), 0) < HD
            for h in range(heads):
                both = slice((h // 2) * 2 * HD, (h // 2 + 1) * 2 * HD)
                target[h, :, at] = jnp.where(upper == (h % 2 == 0), value[both], 0.0).astype(BF16)

    stats[:heads] = lse[...]

    @functools.partial(loop, rows // CHUNK)
    def _(i):
        at = rows_of(i, CHUNK)
        low = dot_nt(g_attn_v[at], wout_v[...]).astype(BF16)
        g_v[at] = low
        value = low.astype(F32).T
        for h in range(heads):
            mine = slice(h * HD, (h + 1) * HD)
            stats[heads + h : heads + h + 1, at] = jnp.sum(value[mine] * att_t[mine, at], axis=0, keepdims=True)

    @pl.when(has_before)
    def _():
        for item in to_before:
            item.start()

    relay(1)
    loop(blocks - blocks // 2, lambda k: term(blocks // 2 + k))
    if scatter.block != scatter.chunk:
        loop(half, scatter.send_near)

    @pl.when(jnp.logical_not(has_after))
    def _():
        g_next[...] = jnp.zeros_like(g_next)
        stats_next[...] = jnp.zeros_like(stats_next)

    @pl.when(jnp.logical_not(has_before))
    def _():
        got_q[...] = jnp.zeros_like(got_q)

    turn(g_v, g_t, 1.0)
    turn(q_v, q_t, scale)

    @functools.partial(loop, 2)
    def _(i):
        at = rows_of(i, rows)
        k_t[:, at] = kv[at, :width].astype(F32).T.astype(BF16)

    @functools.partial(loop, rows // 64)
    def _(i):
        att_t[rows_of(i, 64)] = jnp.zeros((64, rows), F32)
        g_q_next[rows_of(i, 64)] = jnp.zeros((64, rows), F32)

    @functools.partial(loop, 2 * rows // 64)
    def _(i):
        acc[rows_of(i, 64)] = jnp.zeros((64, 2 * width), F32)

    relay(2)
    loop(half, scatter.add_near)
    scatter.send_far(1)

    def head(h, q_rows, g_rows, numbers, g_q_t, mask):
        offset = lax.div(h, 2) * 2 * HD
        lanes = pl.ds(pl.multiple_of(offset, 2 * HD), 2 * HD)
        lanes_v = pl.ds(pl.multiple_of(offset + width, 2 * HD), 2 * HD)
        feature = pl.ds(pl.multiple_of(h * HD, HD), HD)
        low_lanes = lax.broadcasted_iota(jnp.int32, (CHUNK, 2 * HD), 1) < HD
        mine = low_lanes == (lax.rem(h, 2) == 0)
        for c in range(rows // CHUNK):
            cols = slice(c * CHUNK, (c + 1) * CHUNK)
            q_n = jnp.where(mine, q_rows[cols, lanes].astype(F32), 0.0).astype(BF16)
            g_n = jnp.where(mine, g_rows[cols, lanes].astype(F32), 0.0).astype(BF16)
            lse_row = numbers[pl.ds(h, 1), cols]
            delta_row = numbers[pl.ds(heads + h, 1), cols]
            for b in range(2):
                keys = slice(b * rows, (b + 1) * rows)
                s = dot(kv[keys, lanes], q_t[h, :, cols])
                p = jnp.exp(mask(b, c, s, lse_row))
                g_s = (p * (dot(kv[keys, lanes_v], g_t[h, :, cols]) - delta_row)).astype(BF16)
                acc[keys, lanes] += dot(g_s, q_n)
                acc[keys, lanes_v] += dot(p.astype(BF16), g_n)
                g_q_t[feature, cols] += dot(k_t[feature, keys], g_s)

    def causal(b, c, s, lse_row):
        key = lax.broadcasted_iota(jnp.int32, (rows, CHUNK), 0) + b * rows
        row = lax.broadcasted_iota(jnp.int32, (rows, CHUNK), 1) + c * CHUNK
        return jnp.where(key <= row + core * rows, s - lse_row, NEG)

    @functools.partial(loop, heads)
    def _(h):
        head(h, q_v, g_v, stats, att_t, causal)

        @pl.when(h < heads - 2)
        def _():
            relay(3 + h)

    @pl.when(has_after)
    def _():
        for item in to_before:
            item.wait_recv()

    turn(g_next, g_t, 1.0)
    turn(q_next, q_t, scale)
    relay(9)
    for p in range(pairs):

        @functools.partial(loop, 2)
        def _(parity, p=p):
            head(2 * p + parity, q_next, g_next, stats_next, g_q_next, lambda b, c, s, row: s + (bias - row))
            relay(10 + 2 * p + parity)

        pair = slice(p * 2 * HD, (p + 1) * 2 * HD)
        give_q[pair] = g_q_next[pair].astype(BF16)

        @pl.when(has_after)
        def _():
            to_after[p].start()

    levels = scatter.depth
    for level in range(1, levels):
        scatter.add_far(level)
        scatter.send_far(level + 1)

    @functools.partial(loop, rows // 64)
    def _(i):
        at = pl.ds(pl.multiple_of((1 - core) * rows + i * 64, 64), 64)
        give_near[rows_of(i, 64)] = acc[at].astype(BF16)

    to_near.start()
    to_near.wait_recv()

    @functools.partial(loop, rows // 64)
    def _(i):
        at = pl.ds(pl.multiple_of(core * rows + i * 64, 64), 64)
        near_at = rows_of(i, 64)
        total_at = acc[at] + got_near[near_at].astype(F32)
        g_qkv_v[near_at, width : 2 * width] = (total_at[:, :width] * scale).astype(BF16)
        g_qkv_v[near_at, 2 * width :] = total_at[:, width:].astype(BF16)

    @pl.when(has_before)
    def _():
        for item in to_after:
            item.wait_recv()

    @functools.partial(loop, rows // CHUNK)
    def _(i):
        at = rows_of(i, CHUNK)
        both = att_t[:, at] + got_q[:, at].astype(F32)
        g_qkv_v[at, :width] = (both.T * scale).astype(BF16)

    stores = [
        pltpu.make_async_copy(g_qkv_v, g_qkv_hbm, store_sem.at[0]),
        pltpu.make_async_copy(total, ffn_sum_hbm, store_sem.at[1]),
    ]
    stores[0].start()
    loop(count, line.get)
    stores[1].start()

    def write(tile, value):
        up_out[:, tile * 512 : (tile + 1) * 512] = value

    scatter.finish(write)
    scatter.drain()
    line.drain_all(count)
    to_near.wait_send()

    @pl.when(has_before)
    def _():
        for item in to_before:
            item.wait_send()

    @pl.when(has_after)
    def _():
        for item in to_after:
            item.wait_send()

    for item in stores:
        item.wait()


def grad_attend(g_attn, wout, q, q_next, kv, att_t, lse, lengths, until, ffn_low, norm2, g_pre):
    rows, depth = g_attn.shape
    width = q.shape[1]
    heads = width // HD
    hidden = g_pre.shape[1]
    chunk = depth // lax.axis_size("cp")
    shape = jax.ShapeDtypeStruct
    return pl.pallas_call(
        grad_attend_kernel,
        out_shape=(
            shape((rows, 3 * width), BF16),
            shape((rows, depth), BF16),
            shape((chunk, hidden), F32),
        ),
        in_specs=[ANY] * 6 + [IN_VMEM, IN_SMEM, IN_SMEM, ANY, ANY, ANY],
        out_specs=(ANY, ANY, IN_VMEM),
        scratch_shapes=[
            pltpu.VMEM((rows, depth), BF16),
            pltpu.VMEM((width, depth), BF16),
            pltpu.VMEM((rows, width), BF16),
            pltpu.VMEM((rows, width), BF16),
            pltpu.VMEM((2 * rows, 2 * width), BF16),
            pltpu.VMEM((width, 2 * rows), BF16),
            pltpu.VMEM((width, rows), F32),
            pltpu.VMEM((heads, 2 * HD, rows), BF16),
            pltpu.VMEM((rows, width), BF16),
            pltpu.VMEM((rows, width), BF16),
            pltpu.VMEM((heads, 2 * HD, rows), BF16),
            pltpu.VMEM((2 * heads, rows), F32),
            pltpu.VMEM((2 * heads, rows), F32),
            pltpu.VMEM((2 * rows, 2 * width), F32),
            pltpu.VMEM((rows, 3 * width), BF16),
            pltpu.VMEM((width, rows), F32),
            pltpu.VMEM((width, rows), BF16),
            pltpu.VMEM((width, rows), BF16),
            pltpu.VMEM((rows, 2 * width), BF16),
            pltpu.VMEM((rows, 2 * width), BF16),
            pltpu.SemaphoreType.DMA((3 + heads // 2,)),
            pltpu.SemaphoreType.DMA((3 + heads // 2,)),
            pltpu.VMEM((rows, depth), BF16),
            pltpu.VMEM((rows, hidden), BF16),
            pltpu.VMEM((depth, hidden), BF16),
            *scatter_scratch(depth, hidden, SPLIT_UP),
            *line_scratch(rows, depth),
            pltpu.SemaphoreType.DMA((9,)),
            pltpu.SemaphoreType.DMA((2,)),
        ],
        compiler_params=pltpu.CompilerParams(collective_id=2, has_side_effects=True, vmem_limit_bytes=63 * 2**20),
        name="grad_attend",
    )(g_attn, wout, q, q_next, kv, att_t, lse, lengths, until, ffn_low, norm2, g_pre)


def last_kernel(
    g_qkv_hbm, wqkv_hbm, x_hbm, g_hidden_hbm, norm_hbm, g_attn_hbm, att_hbm, attn_sum_hbm, ffn_sum_hbm,
    lengths_ref, until_ref, gains, b_outs, sums_in,
    g_x_hbm, out_hbm, qkv_out, w_out_out, gains_out, shifts_out, bqv_out, bouts_out, bup_out,
    g_qkv_v, w_v, x_v, g_hidden, norm_v, g_attn_v, att_v, attn_sum, ffn_sum, out_v, acc, small, small_got, late, late_got,
    terms, near, far, rs_send, rs_recv,
    part, slot_a, slot_b, total, ar_send, ar_recv, small_send, small_recv, load_sem, store_sem,
):
    cp, tp, core, chip = place()
    rows, depth = x_v.shape
    width = att_v.shape[1]
    count = rows // SUB
    loads = [
        pltpu.make_async_copy(source, target, load_sem.at[i])
        for i, (source, target) in enumerate(
            (
                (g_qkv_hbm, g_qkv_v),
                (wqkv_hbm, w_v),
                (norm_hbm, norm_v),
                (g_attn_hbm, g_attn_v),
                (att_hbm, att_v),
                (x_hbm, x_v),
                (g_hidden_hbm, g_hidden),
                (attn_sum_hbm, attn_sum),
                (ffn_sum_hbm, ffn_sum),
            )
        )
    ]
    for item in loads[:2]:
        item.start()
    line = LineSum(part, slot_a, slot_b, total, ar_send, ar_recv)
    scatter = Scatter(terms, near, far, rs_send, rs_recv, SPLIT_LAST)
    bands = lax.axis_size("cp")
    greet(cp, tp, [(lax.rem(cp + k, bands), tp) for k in range(1, bands)])
    _, live = band_info(lengths_ref, until_ref, cp * rows)
    acc[...] = jnp.zeros_like(acc)
    loads[0].wait()
    loads[1].wait()

    for c in range(rows // CHUNK):
        chunk = slice(c * CHUNK, (c + 1) * CHUNK)

        @functools.partial(loop, depth // 512)
        def _(t, chunk=chunk):
            lanes = rows_of(t, 512)
            value = dot_nt(g_qkv_v[chunk, :width], w_v[0, lanes])
            value = value + dot_nt(g_qkv_v[chunk, width : 2 * width], w_v[1, lanes])
            value = value + dot_nt(g_qkv_v[chunk, 2 * width :], w_v[2, lanes])
            part[chunk, lanes] = value.astype(BF16)

        loop(CHUNK // SUB, lambda s, c=c: line.push(s + c * (CHUNK // SUB)))
        if c == 0:
            for item in loads[2:]:
                item.start()

    def small_copy(which, sender, receiver):
        source, target = ((small, small_got), (late, late_got))[which]
        return pltpu.make_async_remote_copy(
            src_ref=source, dst_ref=target.at[sender], send_sem=small_send.at[which, receiver],
            recv_sem=small_recv.at[which, sender], device_id=(receiver, tp), device_id_type=MESH,
        )

    def give_small(which):
        loop(bands - 1, lambda k: small_copy(which, cp, lax.rem(cp + 1 + k, bands)).start())

    def take_small(which):
        source, target = ((small, small_got), (late, late_got))[which]
        target[cp] = source[...]

        @functools.partial(loop, bands - 1)
        def _(k):
            sender = lax.rem(cp + 1 + k, bands)
            small_copy(which, sender, sender).wait_recv()

        value = target[0]
        for k in range(1, bands):
            value = value + target[k]
        return value

    small[0:5] = sums_in[0:5]
    small[6:8] = jnp.zeros((2, depth), F32)
    small[5:6, 2 * width :] = jnp.zeros((1, depth - 2 * width), F32)
    for j in range(2):
        bias = jnp.sum(g_qkv_v[:, 2 * j * width : (2 * j + 1) * width].astype(F32), axis=0, keepdims=True)
        small[5:6, j * width : (j + 1) * width] = bias
    give_small(0)
    for item in loads[2:]:
        item.wait()

    def back(s):
        line.get(s)
        at = rows_of(s, SUB)
        e = total[at].astype(F32)
        v = x_v[at].astype(F32)
        centred = v - jnp.mean(v, axis=-1, keepdims=True)
        scale = lax.rsqrt(jnp.mean(centred * centred, axis=-1, keepdims=True) + EPS)
        hat = centred * scale
        t = e * gains[0:1]
        along = t - jnp.mean(t, axis=-1, keepdims=True) - hat * jnp.mean(t * hat, axis=-1, keepdims=True)
        g_hidden[at] = g_hidden[at] + along * scale
        row = lax.broadcasted_iota(jnp.int32, (SUB, 1), 0) + s * SUB
        branches = attn_sum[at].astype(F32) + b_outs[0:1] + (ffn_sum[at].astype(F32) + b_outs[1:2])
        out_v[at] = v + jnp.where(row < live, branches, 0.0)
        acc[0] += fold(e * hat)
        acc[1] += fold(e)
        pltpu.make_async_copy(g_hidden.at[at], g_x_hbm.at[at], store_sem.at[0, s]).start()
        pltpu.make_async_copy(out_v.at[at], out_hbm.at[at], store_sem.at[1, s]).start()

    behind = 4

    def ahead(s):
        line.tick(s)

        @pl.when(s >= behind)
        def _():
            back(s - behind)

    def term(k):
        def pick(tile, at):
            if tile < 3:
                return norm_v[:, at], g_qkv_v[:, tile * width : (tile + 1) * width]
            return g_attn_v[:, at], att_v[...]

        scatter.fill(k, pick)

    blocks, half = scatter.blocks(), scatter.count // 2

    @functools.partial(loop, 4)
    def _(i):
        loop(blocks // 4, lambda j: term(i * (blocks // 4) + j))

        @pl.when((i == 1) if scatter.block == scatter.chunk else (i == 3))
        def _():
            loop(half, scatter.send_near)

        ahead(i)

    @functools.partial(loop, 2)
    def _(i):
        loop(half // 2, lambda j: scatter.add_near(i * (half // 2) + j))
        ahead(4 + i)

    scatter.send_far(1)
    loop(8, lambda i: ahead(6 + i))
    for level in range(1, scatter.depth):
        scatter.add_far(level)
        scatter.send_far(level + 1)
    loop(count + 2 - 14, lambda i: ahead(14 + i))
    loop(behind - 2, lambda i: back(count + 2 - behind + i))

    for k in range(2):
        late[k : k + 1] = jnp.sum(acc[k], axis=0, keepdims=True)
    give_small(1)
    early = take_small(0)
    bouts_out[...] = early[2:4]
    bup_out[...] = early[4:5]
    for j in range(2):
        bqv_out[j : j + 1] = early[5:6, j * width : (j + 1) * width]

    def write(tile, value):
        if tile < 3:
            qkv_out[tile] = value
        else:
            w_out_out[...] = value.T

    scatter.finish(write)
    final = take_small(1)
    gains_out[0:1] = final[0:1]
    gains_out[1:2] = early[0:1]
    shifts_out[0:1] = final[1:2]
    shifts_out[1:2] = early[1:2]
    scatter.drain()
    line.drain_all(count)

    @functools.partial(loop, bands - 1)
    def _(k):
        other = lax.rem(cp + 1 + k, bands)
        small_copy(0, cp, other).wait_send()
        small_copy(1, cp, other).wait_send()

    @functools.partial(loop, count)
    def _(s):
        at = rows_of(s, SUB)
        pltpu.make_async_copy(g_hidden.at[at], g_x_hbm.at[at], store_sem.at[0, s]).wait()
        pltpu.make_async_copy(out_v.at[at], out_hbm.at[at], store_sem.at[1, s]).wait()


def last(g_qkv, wqkv, x, g_hidden, norm1, g_attn, att, attn_sum, ffn_sum, lengths, until, gains, b_outs, sums):
    rows, depth = x.shape
    width = att.shape[1]
    bands = lax.axis_size("cp")
    chunk = depth // bands
    shape = jax.ShapeDtypeStruct
    return pl.pallas_call(
        last_kernel,
        out_shape=(
            shape((rows, depth), F32),
            shape((rows, depth), F32),
            shape((3, chunk, width), F32),
            shape((width, chunk), F32),
            shape((2, depth), F32),
            shape((2, depth), F32),
            shape((2, width), F32),
            shape((2, depth), F32),
            shape((1, depth), F32),
        ),
        in_specs=[ANY] * 9 + [IN_SMEM] * 2 + [IN_VMEM] * 3,
        out_specs=(ANY,) * 2 + (IN_VMEM,) * 7,
        scratch_shapes=[
            pltpu.VMEM((rows, 3 * width), BF16),
            pltpu.VMEM((3, depth, width), BF16),
            pltpu.VMEM((rows, depth), BF16),
            pltpu.VMEM((rows, depth), F32),
            pltpu.VMEM((rows, depth), BF16),
            pltpu.VMEM((rows, depth), BF16),
            pltpu.VMEM((rows, width), BF16),
            pltpu.VMEM((rows, depth), BF16),
            pltpu.VMEM((rows, depth), BF16),
            pltpu.VMEM((rows, depth), F32),
            pltpu.VMEM((2, 8, depth), F32),
            pltpu.VMEM((8, depth), F32),
            pltpu.VMEM((bands, 8, depth), F32),
            pltpu.VMEM((2, depth), F32),
            pltpu.VMEM((bands, 2, depth), F32),
            pltpu.VMEM((depth, depth), BF16),
            *scatter_scratch(depth, depth, SPLIT_LAST),
            *line_scratch(rows, depth),
            pltpu.SemaphoreType.DMA((2, bands)),
            pltpu.SemaphoreType.DMA((2, bands)),
            pltpu.SemaphoreType.DMA((9,)),
            pltpu.SemaphoreType.DMA((2, rows // SUB)),
        ],
        compiler_params=pltpu.CompilerParams(collective_id=3, has_side_effects=True, vmem_limit_bytes=62 * 2**20),
        name="last",
    )(g_qkv, wqkv, x, g_hidden, norm1, g_attn, att, attn_sum, ffn_sum, lengths, until, gains, b_outs, sums)


def shards(
    layer_input,
    seq_lengths,
    active_until,
    ln_gains,
    ln_shifts,
    query_key_value_weight,
    b_qv,
    w_out,
    b_outs,
    w_up,
    b_up,
    w_down,
    d_out,
):
    wqkv = jnp.transpose(query_key_value_weight, (1, 0, 2))
    (attn_sum, norm1, q, q_next, kv, att, att_t, norm2, g_pre, ffn_low, g_hidden, g_attn, lse, sums, g_down) = front(
        layer_input, d_out, seq_lengths, active_until, ln_gains, ln_shifts, wqkv, b_qv, w_out, b_outs, b_up[None],
        w_up, w_down,
    )
    g_qkv_rows, ffn_sum, g_up = grad_attend(
        g_attn, w_out, q, q_next, kv, att_t, lse, seq_lengths, active_until, ffn_low, norm2, g_pre
    )
    g_x, out, g_qkv, g_out, g_ln_gains, g_ln_shifts, g_bqv, g_bouts, g_bup = last(
        g_qkv_rows, wqkv, layer_input, g_hidden, norm1, g_attn, att, attn_sum, ffn_sum,
        seq_lengths, active_until, ln_gains, b_outs, sums,
    )
    g_qkv = jnp.transpose(g_qkv, (1, 0, 2))
    return (out, g_x, g_ln_gains, g_ln_shifts, g_qkv, g_bqv, g_out, g_bouts, g_up, g_bup[0], g_down)


def solution(mesh):
    return jax.shard_map(
        shards,
        mesh=mesh,
        in_specs=(
            P("cp", None),
            P(),
            P(),
            P(),
            P(),
            P(None, None, "tp"),
            P(None, "tp"),
            P("tp", None),
            P(),
            P(None, "tp"),
            P("tp"),
            P("tp", None),
            P("cp", None),
        ),
        out_specs=(
            P("cp", None),
            P("cp", None),
            P(),
            P(),
            P("cp", None, "tp"),
            P(None, "tp"),
            P("tp", "cp"),
            P(),
            P("cp", "tp"),
            P("tp"),
            P("tp", "cp"),
        ),
        check_vma=False,
    )
```

```python
import functools
import math

import jax
import jax.numpy as jnp
from jax import lax
from jax.experimental import pallas as pl
from jax.experimental.pallas import tpu as pltpu
from jax.sharding import PartitionSpec as P

HD = 64
LONG = 2048
EPS = 1e-05
NEG = -1e30
MESH = pl.DeviceIdType.MESH
F32 = jnp.float32
BF16 = jnp.bfloat16
ANY = pl.BlockSpec(memory_space=pl.ANY)
IN_VMEM = pl.BlockSpec(memory_space=pltpu.VMEM)
IN_SMEM = pl.BlockSpec(memory_space=pltpu.SMEM)
SUB = 32
PIECE = 16
CHUNK = 256


def dot(a, b):
    return jnp.dot(a, b, preferred_element_type=F32)


def dot_nt(a, b):
    return lax.dot_general(a, b, (((1,), (1,)), ((), ())), preferred_element_type=F32)


def dot_tn(a, b):
    return lax.dot_general(a, b, (((0,), (0,)), ((), ())), preferred_element_type=F32)


def rows_of(index, size):
    return pl.ds(pl.multiple_of(index * size, size), size)


def place():
    cp = lax.axis_index("cp")
    tp = lax.axis_index("tp")
    return cp, tp, lax.rem(cp, 2), lax.div(cp, 2)


def greet(cp, tp, others):
    barrier = pltpu.get_barrier_semaphore()
    edge = (tp == 0) | (tp == 3)
    for other in [*others, (cp, line_near(tp))]:
        pl.semaphore_signal(barrier, inc=1, device_id=other, device_id_type=MESH)

    @pl.when(jnp.logical_not(edge))
    def _():
        pl.semaphore_signal(barrier, inc=1, device_id=(cp, 3 - tp), device_id_type=MESH)

    pl.semaphore_wait(barrier, len(others) + jnp.where(edge, 1, 2))


def line_near(tp):
    return jnp.where(tp == 0, 1, jnp.where(tp == 1, 0, jnp.where(tp == 2, 3, 2)))


class LineSum:
    def __init__(self, part, slot_a, slot_b, total, send, recv):
        self.cp, self.tp, _, _ = place()
        self.edge = (self.tp == 0) | (self.tp == 3)
        self.refs = (part, slot_a, slot_b, total)
        self.send, self.recv = send, recv
        self.count = part.shape[0] // SUB

    def copy(self, kind, piece):
        part, slot_a, slot_b, total = self.refs
        src, dst = ((part, slot_a), (part, slot_b), (total, total))[kind]
        other = (self.cp, 3 - self.tp if kind == 1 else line_near(self.tp))
        rows = rows_of(piece, PIECE)
        return pltpu.make_async_remote_copy(
            src_ref=src.at[rows],
            dst_ref=dst.at[rows],
            send_sem=self.send.at[kind, piece],
            recv_sem=self.recv.at[kind, piece],
            device_id=other,
            device_id_type=MESH,
        )

    def pieces(self, s):
        return [s * (SUB // PIECE) + j for j in range(SUB // PIECE)]

    def push(self, s):
        @pl.when(self.edge)
        def _():
            for piece in self.pieces(s):
                self.copy(0, piece).start()

    def relay_in(self, s):
        part, slot_a, _, _ = self.refs

        @pl.when(jnp.logical_not(self.edge))
        def _():
            for piece in self.pieces(s):
                rows = rows_of(piece, PIECE)
                self.copy(0, piece).wait_recv()
                part[rows] = (part[rows].astype(F32) + slot_a[rows].astype(F32)).astype(BF16)
                self.copy(1, piece).start()

    def relay_out(self, s):
        part, _, slot_b, total = self.refs

        @pl.when(jnp.logical_not(self.edge))
        def _():
            for piece in self.pieces(s):
                rows = rows_of(piece, PIECE)
                self.copy(1, piece).wait_recv()
                total[rows] = (part[rows].astype(F32) + slot_b[rows].astype(F32)).astype(BF16)
                self.copy(2, piece).start()

    def get(self, s):
        @pl.when(self.edge)
        def _():
            for piece in self.pieces(s):
                self.copy(2, piece).wait_recv()

    def tick(self, s):
        @pl.when(s < self.count)
        def _():
            self.relay_in(s)

        @pl.when(s >= 2)
        def _():
            self.relay_out(s - 2)

    def drain_all(self):
        @pl.when(self.edge)
        def _():
            loop(self.refs[0].shape[0] // PIECE, lambda piece: self.copy(0, piece).wait_send())

        @pl.when(jnp.logical_not(self.edge))
        def _():
            @functools.partial(loop, self.refs[0].shape[0] // PIECE)
            def _(piece):
                self.copy(1, piece).wait_send()
                self.copy(2, piece).wait_send()


def line_scratch(rows, width):
    return [pltpu.VMEM((rows, width), BF16)] * 4 + [pltpu.SemaphoreType.DMA((3, rows // PIECE))] * 2


def band_info(lengths_ref, until_ref, first):
    start = jnp.int32(0)
    begin = jnp.int32(0)
    until = jnp.int32(0)
    for i in range(lengths_ref.shape[0]):
        length = lengths_ref[i]
        inside = (first >= start) & (first < start + length)
        begin = jnp.where(inside, start, begin)
        until = jnp.where(inside, until_ref[i], until)
        start = start + length
    return begin, until + begin - first


def loop(count, body):
    def step(i, carry):
        body(i)
        return carry

    lax.fori_loop(0, count, step, 0)


class Scatter:
    def __init__(self, terms, near, far, send, recv, split):
        self.cp, self.tp, self.core, self.chip = place()
        self.count = lax.axis_size("cp")
        self.half = self.count // 2
        self.depth = self.half.bit_length() - 1
        self.terms, self.near, self.far = terms, near, far
        self.send, self.recv = send, recv
        self.chunk = terms.shape[0] // self.count
        self.width = terms.shape[1]
        self.lanes = {p: c for p, c in ((0, slice(0, split)), (1, slice(split, self.width))) if c.stop > c.start}
        self.order = list(range(self.half))[::-1]
        self.whole_blocks = self.chunk >= 128

    def partners(self):
        others = [(self.cp + 1 - 2 * self.core, self.tp)]
        for bit in range(self.depth):
            others.append((self.cp + 2 * self.flip(1 << bit), self.tp))
        return others

    def flip(self, e):
        change = 0
        for bit in range(self.depth):
            if e >> bit & 1:
                change = change + (1 - 2 * lax.rem(lax.div(self.chip, 1 << bit), 2)) * (1 << bit)
        return change

    def row(self, e, core):
        if isinstance(e, int):
            other = self.chip + self.flip(e)
        else:
            other = 0
            for bit in range(self.depth):
                mine = lax.rem(lax.div(self.chip, 1 << bit), 2)
                change = lax.rem(lax.div(e, 1 << bit), 2)
                other = other + (mine + change - 2 * mine * change) * (1 << bit)
        return (2 * other + core) * self.chunk

    def fill_block(self, first, size, pick):
        rows = pl.ds(pl.multiple_of(first, size), size)

        for tile in range(self.width // 512):
            left, right = pick(tile, rows)
            self.terms[rows, tile * 512 : (tile + 1) * 512] = dot_tn(left, right).astype(BF16)

    def fill_near(self, pick):
        if not self.whole_blocks:
            loop(self.terms.shape[0] // 128, lambda k: self.fill_block(k * 128, 128, pick))

        @functools.partial(loop, self.half)
        def _(k):
            e = self.half - 1 - k
            if self.whole_blocks:
                self.fill_block(self.row(e, 1 - self.core), self.chunk, pick)
            self.near_copy(e).start()

    def fill_own(self, pick):
        if self.whole_blocks:
            loop(self.half, lambda k: self.fill_block(self.row(self.half - 1 - k, self.core), self.chunk, pick))

    def near_copy(self, e):
        return pltpu.make_async_remote_copy(
            src_ref=self.terms.at[pl.ds(pl.multiple_of(self.row(e, 1 - self.core), self.chunk), self.chunk)],
            dst_ref=self.near.at[rows_of(e, self.chunk)],
            send_sem=self.send.at[e],
            recv_sem=self.recv.at[e],
            device_id=(self.cp + 1 - 2 * self.core, self.tp),
            device_id_type=MESH,
        )

    def add(self, e, source, first, lanes):
        base = self.row(e, self.core)

        @functools.partial(loop, self.chunk // 32)
        def _(i):
            mine = pl.ds(pl.multiple_of(base + i * 32, 32), 32)
            other = pl.ds(pl.multiple_of(first + i * 32, 32), 32)
            self.terms[mine, lanes] = (
                self.terms[mine, lanes].astype(F32) + source[other, lanes].astype(F32)
            ).astype(BF16)

    def add_near(self):
        for e in self.order:
            self.near_copy(e).wait_recv()
            self.add(e, self.near, e * self.chunk, slice(0, self.width))
            for part in self.lanes:
                if self.sent(1, part, e):
                    self.far_copy(1, part, e).start()

    def bit(self, level, part):
        return level - 1 if part == 0 else self.depth - level

    def sent(self, level, part, e):
        bit = self.bit(level, part)
        return e >> bit & 1 and (e & ((1 << bit) - 1) if part == 0 else e >> (bit + 1)) == 0

    def slot(self, level, part, e):
        bit = self.bit(level, part)
        return e >> (bit + 1) if part == 0 else e & ((1 << bit) - 1)

    def place(self, level):
        return sum(self.terms.shape[0] >> (earlier + 1) for earlier in range(1, level))

    def far_copy(self, level, part, e):
        bit = self.bit(level, part)
        sem = self.half + sum(len(self.lanes) * (self.half >> earlier) for earlier in range(1, level))
        sem += list(self.lanes).index(part) * (self.half >> level) + self.slot(level, part, e)
        first = self.place(level) + self.slot(level, part, e) * self.chunk
        return pltpu.make_async_remote_copy(
            src_ref=self.terms.at[
                pl.ds(pl.multiple_of(self.row(e, self.core), self.chunk), self.chunk), self.lanes[part]
            ],
            dst_ref=self.far.at[first : first + self.chunk, self.lanes[part]],
            send_sem=self.send.at[sem],
            recv_sem=self.recv.at[sem],
            device_id=(self.cp + 2 * self.flip(1 << bit), self.tp),
            device_id_type=MESH,
        )

    def coming(self, level, passed_on):
        for e in self.order:
            for part in self.lanes:
                if self.sent(level, part, e):
                    kept = e ^ (1 << self.bit(level, part))
                    if (level < self.depth and bool(self.sent(level + 1, part, kept))) == passed_on:
                        yield part, e, kept

    def arrive(self, level, part, e, kept):
        self.far_copy(level, part, e).wait_recv()
        self.add(kept, self.far, self.place(level) + self.slot(level, part, e) * self.chunk, self.lanes[part])

    def pass_on(self, level):
        for part, e, kept in self.coming(level, True):
            self.arrive(level, part, e, kept)
            self.far_copy(level + 1, part, kept).start()

    def keep(self, level):
        for part, e, kept in self.coming(level, False):
            self.arrive(level, part, e, kept)

    def between(self):
        for level in range(2, self.depth):
            self.pass_on(level)
            self.keep(level)

    def finish(self, write):
        level = self.depth
        mine = pl.ds(pl.multiple_of(self.row(0, self.core), self.chunk), self.chunk)
        for part, e, _ in self.coming(level, False):
            self.far_copy(level, part, e).wait_recv()
            lanes = self.lanes[part]
            for tile in range(lanes.start // 512, lanes.stop // 512):
                cut = slice(tile * 512, (tile + 1) * 512)
                other = pl.ds(self.place(level), self.chunk)
                write(tile, self.terms[mine, cut].astype(F32) + self.far[other, cut].astype(F32))

    def drain(self):
        for e in self.order:
            self.near_copy(e).wait_send()
            for part in self.lanes:
                for level in range(1, self.depth + 1):
                    if self.sent(level, part, e):
                        self.far_copy(level, part, e).wait_send()


def scatter_scratch(depth, width, split):
    count = lax.axis_size("cp")
    parts = (split > 0) + (split < width)
    sems = count // 2 + parts * (count // 2 - 1)
    return [
        pltpu.VMEM((depth // 2, width), BF16),
        pltpu.VMEM((depth // 2 - depth // count, width), BF16),
        pltpu.SemaphoreType.DMA((sems,)),
        pltpu.SemaphoreType.DMA((sems,)),
    ]


def fold(v):
    return jnp.sum(v.reshape(v.shape[0] // 8, 8, v.shape[1]), axis=0)


def gelu_parts(u):
    root = math.sqrt(2.0 / math.pi)
    square = u * u
    th = jnp.tanh(root * (u + 0.044715 * u * square))
    half = 0.5 * (1.0 + th)
    return u * half, half + 0.5 * u * (1.0 - th * th) * (root * (1.0 + 3 * 0.044715 * square))


LAG = 5
SPLIT_DOWN = 1024


def front_kernel(
    x_hbm, d_hbm, lengths_ref, until_ref, gains, shifts, wqkv_hbm, bqv, wout_hbm, b_outs, b_up, up_hbm, down_hbm,
    attn_sum_hbm, norm1_hbm, q_hbm, q_next_hbm, kv_hbm, att_hbm, att_t_hbm, norm2_hbm, g_pre_hbm, ffn_hbm, g_hidden_hbm,
    g_attn_hbm, lse_out, sums_out, down_out,
    x_v, d_v, norm_v, up_v, down_v, q_v, q_next, kv, q_t, q_t_next, v_t, att_t, att_v, cross, cross_in, lse_cross, lse_in, xhat, rstd, act_v, g_pre_v, acc,
    part, slot_a, total, slot_b1, slot_b2, ar_send, ar_recv, near, far, rs_send, rs_recv,
    x_send, x_recv, load_sem, store_sem,
):
    cp, tp, core, chip = place()
    bands = lax.axis_size("cp")
    chips = bands // 2
    rows, depth = x_v.shape
    width = q_v.shape[1]
    heads = width // HD
    hidden = act_v.shape[1]
    count = rows // SUB
    per_chunk = CHUNK // SUB
    sibling = (cp + 1 - 2 * core, tp)
    after = (lax.rem(cp + 2, bands), tp)
    before = (lax.rem(cp + bands - 2, bands), tp)
    wout_v, scores, g_hidden, g_attn, part2, ffn_v = act_v, xhat, xhat, x_v, v_t, part
    loads = [
        pltpu.make_async_copy(x_hbm, x_v, load_sem.at[0]),
        *[
            pltpu.make_async_copy(
                wqkv_hbm.at[j], up_v.at[:, j * width : (j + 1) * width], load_sem.at[i]
            )
            for i, j in ((1, 0), (2, 1), (3, 2))
        ],
        pltpu.make_async_copy(wout_hbm, wout_v, load_sem.at[4]),
        pltpu.make_async_copy(down_hbm, down_v, load_sem.at[5]),
        pltpu.make_async_copy(d_hbm, d_v, load_sem.at[6]),
        pltpu.make_async_copy(up_hbm, up_v, load_sem.at[7]),
    ]
    for item in loads[:4]:
        item.start()
    stores = {
        name: pltpu.make_async_copy(source, target, store_sem.at[i])
        for i, (name, source, target) in enumerate(
            (
                ("norm1", norm_v, norm1_hbm),
                ("q", q_v, q_hbm),
                ("kv", kv, kv_hbm),
                ("q_next", q_next, q_next_hbm),
                ("att", att_v, att_hbm),
                ("att_t", att_t, att_t_hbm),
                ("sum0", total.at[:CHUNK], attn_sum_hbm.at[:CHUNK]),
                ("sum1", total.at[CHUNK:], attn_sum_hbm.at[CHUNK:]),
                ("norm2", norm_v, norm2_hbm),
                ("g_pre", g_pre_v, g_pre_hbm),
                ("ffn", ffn_v, ffn_hbm),
                ("g_hidden", g_hidden, g_hidden_hbm),
                ("g_attn", g_attn, g_attn_hbm),
            )
        )
    }
    line1 = LineSum(part, slot_a, slot_b1, total, ar_send.at[0], ar_recv.at[0])
    line2 = LineSum(part2, slot_a, slot_b2, total, ar_send.at[1], ar_recv.at[1])
    scatter = Scatter(up_v, near, far, rs_send, rs_recv, SPLIT_DOWN)
    greet(cp, tp, [*scatter.partners(), after, before])
    _, live = band_info(lengths_ref, until_ref, cp * rows)
    begin, _ = band_info(lengths_ref, until_ref, (chip + 1) * 2 * rows)
    bias = jnp.where(begin < (chip + 1) * 2 * rows, 0.0, NEG)
    loads[0].wait()

    @functools.partial(loop, rows // 64)
    def _(i):
        at = rows_of(i, 64)
        v = x_v[at].astype(F32)
        mean = jnp.mean(v, axis=-1, keepdims=True)
        centred = v - mean
        var = jnp.mean(centred * centred, axis=-1, keepdims=True)
        norm_v[at] = (centred * lax.rsqrt(var + EPS) * gains[0:1] + shifts[0:1]).astype(BF16)

    stores["norm1"].start()
    chunks = rows // CHUNK

    def exchange(kind, c=0):
        cut = slice(c * CHUNK, (c + 1) * CHUNK)
        source, target, device = (
            (q_v.at[cut], q_next.at[cut], before),
            (cross.at[c], cross_in.at[c], after),
            (lse_cross.at[c], lse_in.at[c], after),
            (kv.at[rows_of(core, rows)], kv.at[rows_of(core, rows)], sibling),
        )[kind]
        sem = kind * chunks + c
        return pltpu.make_async_remote_copy(
            src_ref=source, dst_ref=target, send_sem=x_send.at[sem], recv_sem=x_recv.at[sem],
            device_id=device, device_id_type=MESH,
        )

    queries = [exchange(0, c) for c in range(chunks)]
    gathered = [[exchange(1, c), exchange(2, c)] for c in range(chunks)]
    to_near = exchange(3)
    has_before, has_after = chip > 0, chip < chips - 1
    loads[1].wait()

    for c in range(chunks):
        at = slice(c * CHUNK, (c + 1) * CHUNK)
        q_v[at] = (dot(norm_v[at], up_v[:, :width]) + bqv[0:1]).astype(BF16)

        @pl.when(has_before)
        def _(c=c):
            queries[c].start()

    @pl.when(jnp.logical_not(has_after))
    def _():
        q_next[...] = jnp.zeros_like(q_next)

    @pl.when(jnp.logical_not(has_before))
    def _():
        cross_in[...] = jnp.zeros_like(cross_in)
        lse_in[...] = jnp.full_like(lse_in, NEG)

    for load, column in ((2, 0), (3, 1)):
        loads[load].wait()

        @functools.partial(loop, rows // CHUNK)
        def _(i):
            value = dot(norm_v[rows_of(i, CHUNK)], up_v[:, (column + 1) * width : (column + 2) * width])
            if column:
                value = value + bqv[1:2]
            target = pl.ds(pl.multiple_of(core * rows + i * CHUNK, CHUNK), CHUNK)
            kv[target, column * width : (column + 1) * width] = value.astype(BF16)

    to_near.start()
    for item in loads[4:]:
        item.start()
    stores["q"].start()

    def turned(value, h):
        upper = lax.broadcasted_iota(jnp.int32, value.shape, 0) < HD
        return jnp.where(upper == (h % 2 == 0), value, 0.0).astype(BF16)

    @functools.partial(loop, rows // CHUNK)
    def _(i):
        at = rows_of(i, CHUNK)
        value = q_v[at].astype(F32).T * (HD ** -0.5)
        for h in range(heads):
            q_t[h, :, at] = turned(value[(h // 2) * 2 * HD : (h // 2 + 1) * 2 * HD], h)

    def turn_values(slot):
        v_t[:, rows_of(slot, rows)] = kv[rows_of(slot, rows), width:].astype(F32).T.astype(BF16)

    turn_values(core)
    to_near.wait_recv()
    stores["kv"].start()
    turn_values(1 - core)

    def attend(query, lanes, feature, mask):
        top = jnp.full((1, CHUNK), NEG, F32)
        for b in range(2):
            s = mask(b, dot(kv[b * rows : (b + 1) * rows, lanes], query))
            scores[:, b * CHUNK : (b + 1) * CHUNK] = s
            top = jnp.maximum(top, jnp.max(s, axis=0, keepdims=True))
        mass = jnp.zeros((1, CHUNK), F32)
        mixed = jnp.zeros((HD, CHUNK), F32)
        for b in range(2):
            p = jnp.exp(scores[:, b * CHUNK : (b + 1) * CHUNK] - top)
            mass = mass + jnp.sum(p, axis=0, keepdims=True)
            mixed = mixed + dot(v_t[feature, b * rows : (b + 1) * rows], p.astype(BF16))
        return mixed / mass, top + jnp.log(mass)

    def cross_chunk(c):
        columns = slice(c * CHUNK, (c + 1) * CHUNK)
        queries[c].wait_recv()
        value = q_next[columns].astype(F32).T * (HD ** -0.5)
        for h in range(heads):
            q_t_next[h] = turned(value[(h // 2) * 2 * HD : (h // 2 + 1) * 2 * HD], h)

        @functools.partial(loop, heads)
        def _(h):
            lanes = pl.ds(pl.multiple_of(lax.div(h, 2) * 2 * HD, 2 * HD), 2 * HD)
            feature = pl.ds(pl.multiple_of(h * HD, HD), HD)
            mixed, lse_row = attend(q_t_next[h], lanes, feature, lambda b, s: s + bias)
            cross[c, feature] = mixed.astype(BF16)
            lse_cross[c, pl.ds(h, 1)] = lse_row
            if c > 0:
                @pl.when(lax.rem(h, 4) == 3)
                def _():
                    line1.tick(lax.div(h, 4))

        for item in gathered[c]:
            item.start()

    loads[4].wait()

    for c in range(rows // CHUNK):
        columns = slice(c * CHUNK, (c + 1) * CHUNK)

        @pl.when(has_after)
        def _(c=c):
            cross_chunk(c)

        if c > 0:
            @pl.when(jnp.logical_not(has_after))
            def _():
                loop(2, line1.tick)

        def causal(b, s, c=c):
            key = lax.broadcasted_iota(jnp.int32, (rows, CHUNK), 0) + b * rows
            row = lax.broadcasted_iota(jnp.int32, (rows, CHUNK), 1) + c * CHUNK
            return jnp.where(key <= row + core * rows, s, NEG)

        def head(h, c=c, columns=columns, causal=causal):
            lanes = pl.ds(pl.multiple_of(lax.div(h, 2) * 2 * HD, 2 * HD), 2 * HD)
            feature = pl.ds(pl.multiple_of(h * HD, HD), HD)
            mixed, lse_row = attend(q_t[h, :, columns], lanes, feature, causal)
            att_t[feature, columns] = mixed
            lse_out[pl.ds(h, 1), columns] = lse_row
            if c > 0:
                @pl.when(lax.rem(h, 4) == 3)
                def _():
                    line1.tick(2 + lax.div(h, 4))

        loop(heads, head)

        @pl.when(has_before)
        def _(c=c):
            for item in gathered[c]:
                item.wait_recv()

        mine, other = lse_out[:, columns], lse_in[c]
        top = jnp.maximum(mine, other)
        both = top + jnp.log(jnp.exp(mine - top) + jnp.exp(other - top))
        share, share_in = jnp.exp(mine - both), jnp.exp(other - both)
        lse_out[:, columns] = both
        for h in range(heads):
            feature = slice(h * HD, (h + 1) * HD)
            att_t[feature, columns] = (
                att_t[feature, columns] * share[h : h + 1]
                + cross_in[c, feature].astype(F32) * share_in[h : h + 1]
            )
        att_v[columns] = att_t[:, columns].T.astype(BF16)

        @functools.partial(loop, depth // 512)
        def _(t, columns=columns):
            lanes = rows_of(t, 512)
            part[columns, lanes] = dot(att_v[columns], wout_v[:, lanes]).astype(BF16)

        loop(per_chunk, lambda s, c=c: line1.push(s + c * per_chunk))

    stores["q_next"].start()
    stores["att"].start()
    stores["att_t"].start()
    acc[...] = jnp.zeros_like(acc)
    stores["norm1"].wait()
    loads[6].wait()

    def second_norm(s):
        line1.get(s)
        at = rows_of(s, SUB)
        row = lax.broadcasted_iota(jnp.int32, (SUB, 1), 0) + s * SUB
        on = row < live
        v = x_v[at].astype(F32) + jnp.where(on, total[at].astype(F32) + b_outs[0:1], 0.0)
        mean = jnp.mean(v, axis=-1, keepdims=True)
        centred = v - mean
        scale = lax.rsqrt(jnp.mean(centred * centred, axis=-1, keepdims=True) + EPS)
        hat = centred * scale
        xhat[at] = hat
        rstd[at] = jnp.broadcast_to(scale, (SUB, 128))
        norm_v[at] = (hat * gains[1:2] + shifts[1:2]).astype(BF16)
        acc[3] += fold(jnp.where(on, d_v[at].astype(F32), 0.0))

    def feed_forward(c, ticks):
        chunk = slice(c * CHUNK, (c + 1) * CHUNK)
        on = lax.broadcasted_iota(jnp.int32, (CHUNK, 1), 0) + c * CHUNK < live

        @functools.partial(loop, hidden // 512)
        def _(t):
            lanes = rows_of(t, 512)
            pre = dot(norm_v[chunk], up_v[:, lanes]) + b_up[0:1, lanes]
            g_act = dot_nt(d_v[chunk], down_v[lanes])
            act, slope = gelu_parts(pre)
            act_v[chunk, lanes] = jnp.where(on, act, 0.0).astype(BF16)
            g_pre = jnp.where(on, g_act * slope, 0.0).astype(BF16)
            g_pre_v[chunk, lanes] = g_pre
            acc[4, :, lanes] += fold(g_pre.astype(F32))

            @pl.when(lax.rem(t, 2) == 1)
            def _():
                ticks(lax.div(t, 2))

        @functools.partial(loop, depth // 512)
        def _(t):
            lanes = rows_of(t, 512)
            part2[chunk, lanes] = dot_nt(g_pre_v[chunk], up_v[lanes]).astype(BF16)

            @pl.when(lax.rem(t, 2) == 1)
            def _():
                ticks(2 + lax.div(t, 2))

    @functools.partial(loop, per_chunk)
    def _(i):
        line1.tick(4 + i)
        second_norm(i)

    stores["sum0"].start()
    loads[5].wait()
    loads[7].wait()
    feed_forward(0, lambda i: line1.tick(4 + per_chunk + i))
    stores["sum0"].wait()
    loop(per_chunk, line2.push)
    loop(4, lambda i: second_norm(per_chunk + i))
    for i in range(2):
        line1.tick(count + i)
        line2.relay_in(i)
        second_norm(per_chunk + 4 + 2 * i)
        second_norm(per_chunk + 5 + 2 * i)
    stores["sum1"].start()
    stores["norm2"].start()
    line1.drain_all()
    feed_forward(1, lambda i: line2.tick(2 + i))
    stores["g_pre"].start()
    stores["sum1"].wait()
    loop(per_chunk, lambda s: line2.push(per_chunk + s))

    def back(s):
        line2.get(s)
        at = rows_of(s, SUB)
        e = total[at].astype(F32)
        hat = xhat[at]
        t = e * gains[1:2]
        along = t - jnp.mean(t, axis=-1, keepdims=True) - hat * jnp.mean(t * hat, axis=-1, keepdims=True)
        value = d_v[at].astype(F32) + along * rstd[at, 0:1]
        g_hidden[at] = value
        row = lax.broadcasted_iota(jnp.int32, (SUB, 1), 0) + s * SUB
        low = jnp.where(row < live, value, 0.0).astype(BF16)
        g_attn[at] = low
        acc[0] += fold(e * hat)
        acc[1] += fold(e)
        acc[2] += fold(low.astype(F32))

    def ahead(s):
        line2.tick(s)
        back(s - LAG)

    def pick(tile, at):
        return d_v[:, at], act_v[:, tile * 512 : (tile + 1) * 512]

    def project(k):
        chunk = rows_of(lax.div(k, depth // 512), CHUNK)
        lanes = rows_of(lax.rem(k, depth // 512), 512)
        ffn_v[chunk, lanes] = dot(act_v[chunk], down_v[:, lanes]).astype(BF16)

    scatter.fill_near(pick)
    line2.tick(6)
    scatter.fill_own(pick)
    line2.tick(7)
    scatter.add_near()
    line2.tick(8)
    loop(4, back)

    @functools.partial(loop, 4)
    def _(i):
        project(2 * i)
        project(2 * i + 1)
        ahead(9 + i)

    scatter.pass_on(1)
    stores["ffn"].start()
    loop(3, lambda i: ahead(13 + i))
    scatter.keep(1)
    scatter.between()
    loop(count + 2 - 16, lambda i: ahead(16 + i))
    loop(LAG - 2, lambda i: back(count - LAG + 2 + i))
    stores["g_hidden"].start()
    stores["g_attn"].start()
    for k in range(5):
        sums_out[k : k + 1] = jnp.sum(acc[k], axis=0, keepdims=True)

    sums_out[5:8] = jnp.zeros((3, sums_out.shape[1]), F32)

    def write(tile, value):
        down_out[tile * 512 : (tile + 1) * 512] = value.T

    scatter.finish(write)
    scatter.drain()
    line2.drain_all()

    to_near.wait_send()

    @pl.when(has_before)
    def _():
        for item in queries:
            item.wait_send()

    @pl.when(has_after)
    def _():
        for items in gathered:
            for item in items:
                item.wait_send()

    for name in ("q", "q_next", "kv", "att", "att_t", "norm2", "g_pre", "ffn", "g_hidden", "g_attn"):
        stores[name].wait()


def front(x, d_out, lengths, until, gains, shifts, wqkv, bqv, wout, b_outs, b_up, w_up, w_down):
    rows, depth = x.shape
    width = wqkv.shape[2]
    heads = width // HD
    hidden = w_up.shape[1]
    chunk = depth // lax.axis_size("cp")
    shape = jax.ShapeDtypeStruct
    return pl.pallas_call(
        front_kernel,
        out_shape=(
            shape((rows, depth), BF16),
            shape((rows, depth), BF16),
            shape((rows, width), BF16),
            shape((rows, width), BF16),
            shape((2 * rows, 2 * width), BF16),
            shape((rows, width), BF16),
            shape((width, rows), F32),
            shape((rows, depth), BF16),
            shape((rows, hidden), BF16),
            shape((rows, depth), BF16),
            shape((rows, depth), F32),
            shape((rows, depth), BF16),
            shape((heads, rows), F32),
            shape((8, depth), F32),
            shape((hidden, chunk), F32),
        ),
        in_specs=[ANY, ANY, IN_SMEM, IN_SMEM, IN_VMEM, IN_VMEM, ANY, IN_VMEM, ANY, IN_VMEM, IN_VMEM, ANY, ANY],
        out_specs=(ANY,) * 12 + (IN_VMEM,) * 3,
        scratch_shapes=[
            pltpu.VMEM((rows, depth), BF16),
            pltpu.VMEM((rows, depth), BF16),
            pltpu.VMEM((rows, depth), BF16),
            pltpu.VMEM((depth, hidden), BF16),
            pltpu.VMEM((hidden, depth), BF16),
            pltpu.VMEM((rows, width), BF16),
            pltpu.VMEM((rows, width), BF16),
            pltpu.VMEM((2 * rows, 2 * width), BF16),
            pltpu.VMEM((heads, 2 * HD, rows), BF16),
            pltpu.VMEM((heads, 2 * HD, CHUNK), BF16),
            pltpu.VMEM((width, depth), BF16),
            pltpu.VMEM((width, rows), F32),
            pltpu.VMEM((rows, width), BF16),
            pltpu.VMEM((rows // CHUNK, width, CHUNK), BF16),
            pltpu.VMEM((rows // CHUNK, width, CHUNK), BF16),
            pltpu.VMEM((rows // CHUNK, heads, CHUNK), F32),
            pltpu.VMEM((rows // CHUNK, heads, CHUNK), F32),
            pltpu.VMEM((rows, depth), F32),
            pltpu.VMEM((rows, 128), F32),
            pltpu.VMEM((rows, hidden), BF16),
            pltpu.VMEM((rows, hidden), BF16),
            pltpu.VMEM((5, 8, depth), F32),
            *[pltpu.VMEM((rows, depth), BF16)] * 5,
            *[pltpu.SemaphoreType.DMA((2, 3, rows // PIECE))] * 2,
            *scatter_scratch(depth, hidden, SPLIT_DOWN),
            pltpu.SemaphoreType.DMA((3 * (rows // CHUNK) + 1,)),
            pltpu.SemaphoreType.DMA((3 * (rows // CHUNK) + 1,)),
            pltpu.SemaphoreType.DMA((8,)),
            pltpu.SemaphoreType.DMA((13,)),
        ],
        compiler_params=pltpu.CompilerParams(collective_id=1, has_side_effects=True, vmem_limit_bytes=63 * 2**20),
        name="front",
    )(x, d_out, lengths, until, gains, shifts, wqkv, bqv, wout, b_outs, b_up, w_up, w_down)


SPLIT_UP = 1024
SPLIT_LAST = 1024


def grad_attend_kernel(
    g_attn_hbm, wout_hbm, q_hbm, q_next_hbm, kv_hbm, att_t_hbm, lse, lengths_ref, until_ref, ffn_hbm, norm_hbm, g_pre_hbm,
    g_qkv_hbm, ffn_sum_hbm, up_out,
    g_attn_v, wout_v, q_v, q_next, kv, k_t, att_t, q_t, g_v, g_next, g_t, stats, stats_next, acc, g_qkv_v,
    g_q_next, give_q, got_q, give_near, got_near, x_send, x_recv,
    norm_v, g_pre_v, terms, near, far, rs_send, rs_recv,
    part, slot_a, slot_b, total, ar_send, ar_recv, load_sem, store_sem,
):
    cp, tp, core, chip = place()
    bands = lax.axis_size("cp")
    chips = bands // 2
    rows, width = q_v.shape
    heads = width // HD
    count = rows // SUB
    sibling = (cp + 1 - 2 * core, tp)
    after = (lax.rem(cp + 2, bands), tp)
    before = (lax.rem(cp + bands - 2, bands), tp)
    loads = [
        pltpu.make_async_copy(source, target, load_sem.at[i])
        for i, (source, target) in enumerate(
            (
                (norm_hbm, norm_v),
                (g_pre_hbm, g_pre_v),
                (ffn_hbm, part),
                (g_attn_hbm, g_attn_v),
                (wout_hbm, wout_v),
                (q_hbm, q_v),
                (q_next_hbm, q_next),
                (kv_hbm, kv),
                (att_t_hbm, att_t),
            )
        )
    ]
    for item in loads[:5]:
        item.start()
    line = LineSum(part, slot_a, slot_b, total, ar_send, ar_recv)
    scatter = Scatter(terms, near, far, rs_send, rs_recv, SPLIT_UP)
    greet(cp, tp, [*scatter.partners(), after, before])
    begin, _ = band_info(lengths_ref, until_ref, (chip + 1) * 2 * rows)
    has_before, has_after = chip > 0, chip < chips - 1
    bias = jnp.where((begin < (chip + 1) * 2 * rows) & has_after, 0.0, NEG)
    loads[0].wait()
    loads[1].wait()
    loads[2].wait()
    loop(count, line.push)

    def pick(tile, at):
        return norm_v[:, at], g_pre_v[:, tile * 512 : (tile + 1) * 512]

    for item in loads[5:]:
        item.start()
    scatter.fill_near(pick)
    relay = line.tick
    relay(0)
    for item in loads[3:]:
        item.wait()
    scale = HD ** -0.5

    pairs = heads // 2

    def exchange(kind, p=0):
        lanes = slice(p * 2 * HD, (p + 1) * 2 * HD)
        source, target, device = (
            (g_v, g_next, before),
            (stats, stats_next, before),
            (give_near, got_near, sibling),
            (give_q.at[lanes], got_q.at[lanes], after),
        )[kind]
        return pltpu.make_async_remote_copy(
            src_ref=source, dst_ref=target, send_sem=x_send.at[kind + p], recv_sem=x_recv.at[kind + p],
            device_id=device, device_id_type=MESH,
        )

    to_before = [exchange(0), exchange(1)]
    to_near = exchange(2)
    to_after = [exchange(3, p) for p in range(pairs)]

    def turn(source, target, factor):
        @functools.partial(loop, rows // CHUNK)
        def _(i):
            at = rows_of(i, CHUNK)
            value = source[at].astype(F32).T * factor
            upper = lax.broadcasted_iota(jnp.int32, (2 * HD, CHUNK), 0) < HD
            for h in range(heads):
                both = slice((h // 2) * 2 * HD, (h // 2 + 1) * 2 * HD)
                target[h, :, at] = jnp.where(upper == (h % 2 == 0), value[both], 0.0).astype(BF16)

    stats[:heads] = lse[...]

    @functools.partial(loop, rows // CHUNK)
    def _(i):
        at = rows_of(i, CHUNK)
        low = dot_nt(g_attn_v[at], wout_v[...]).astype(BF16)
        g_v[at] = low
        value = low.astype(F32).T
        for h in range(heads):
            mine = slice(h * HD, (h + 1) * HD)
            stats[heads + h : heads + h + 1, at] = jnp.sum(value[mine] * att_t[mine, at], axis=0, keepdims=True)

    @pl.when(has_before)
    def _():
        for item in to_before:
            item.start()

    relay(1)
    scatter.fill_own(pick)
    scatter.add_near()

    @pl.when(jnp.logical_not(has_after))
    def _():
        g_next[...] = jnp.zeros_like(g_next)
        stats_next[...] = jnp.zeros_like(stats_next)

    @pl.when(jnp.logical_not(has_before))
    def _():
        got_q[...] = jnp.zeros_like(got_q)

    @functools.partial(loop, 2)
    def _(i):
        at = rows_of(i, rows)
        k_t[:, at] = kv[at, :width].astype(F32).T.astype(BF16)

    @functools.partial(loop, rows // 64)
    def _(i):
        att_t[rows_of(i, 64)] = jnp.zeros((64, rows), F32)
        g_q_next[rows_of(i, 64)] = jnp.zeros((64, rows), F32)

    @functools.partial(loop, 2 * rows // 64)
    def _(i):
        acc[rows_of(i, 64)] = jnp.zeros((64, 2 * width), F32)

    relay(2)

    def head(h, q_rows, g_rows, numbers, g_q_t, mask):
        offset = lax.div(h, 2) * 2 * HD
        lanes = pl.ds(pl.multiple_of(offset, 2 * HD), 2 * HD)
        lanes_v = pl.ds(pl.multiple_of(offset + width, 2 * HD), 2 * HD)
        feature = pl.ds(pl.multiple_of(h * HD, HD), HD)
        low_lanes = lax.broadcasted_iota(jnp.int32, (CHUNK, 2 * HD), 1) < HD
        mine = low_lanes == (lax.rem(h, 2) == 0)
        for c in range(rows // CHUNK):
            cols = slice(c * CHUNK, (c + 1) * CHUNK)
            q_n = jnp.where(mine, q_rows[cols, lanes].astype(F32), 0.0).astype(BF16)
            g_n = jnp.where(mine, g_rows[cols, lanes].astype(F32), 0.0).astype(BF16)
            lse_row = numbers[pl.ds(h, 1), cols]
            delta_row = numbers[pl.ds(heads + h, 1), cols]
            for b in range(2):
                keys = slice(b * rows, (b + 1) * rows)
                s = dot(kv[keys, lanes], q_t[h, :, cols])
                p = jnp.exp(mask(b, c, s, lse_row))
                g_s = (p * (dot(kv[keys, lanes_v], g_t[h, :, cols]) - delta_row)).astype(BF16)
                acc[keys, lanes] += dot(g_s, q_n)
                acc[keys, lanes_v] += dot(p.astype(BF16), g_n)
                g_q_t[feature, cols] += dot(k_t[feature, keys], g_s)

    def causal(b, c, s, lse_row):
        key = lax.broadcasted_iota(jnp.int32, (rows, CHUNK), 0) + b * rows
        row = lax.broadcasted_iota(jnp.int32, (rows, CHUNK), 1) + c * CHUNK
        return jnp.where(key <= row + core * rows, s - lse_row, NEG)

    @pl.when(has_after)
    def _():
        for item in to_before:
            item.wait_recv()

    turn(g_next, g_t, 1.0)
    turn(q_next, q_t, scale)
    relay(3)
    for p in range(pairs):

        @functools.partial(loop, 2)
        def _(parity, p=p):
            head(2 * p + parity, q_next, g_next, stats_next, g_q_next, lambda b, c, s, row: s + (bias - row))

        pair = slice(p * 2 * HD, (p + 1) * 2 * HD)
        give_q[pair] = g_q_next[pair].astype(BF16)

        @pl.when(has_after)
        def _(p=p):
            to_after[p].start()

        relay(4 + p)

    turn(g_v, g_t, 1.0)
    turn(q_v, q_t, scale)
    relay(8)

    @functools.partial(loop, heads)
    def _(h):
        head(h, q_v, g_v, stats, att_t, causal)

        @pl.when(lax.rem(h, 2) == 1)
        def _():
            relay(9 + lax.div(h, 2))

        @pl.when(h == 4)
        def _():
            scatter.pass_on(1)

    @functools.partial(loop, rows // 64)
    def _(i):
        at = pl.ds(pl.multiple_of((1 - core) * rows + i * 64, 64), 64)
        give_near[rows_of(i, 64)] = acc[at].astype(BF16)

    to_near.start()
    scatter.keep(1)
    scatter.between()
    relay(13)
    to_near.wait_recv()

    @functools.partial(loop, rows // 64)
    def _(i):
        at = pl.ds(pl.multiple_of(core * rows + i * 64, 64), 64)
        near_at = rows_of(i, 64)
        total_at = acc[at] + got_near[near_at].astype(F32)
        g_qkv_v[near_at, width : 2 * width] = (total_at[:, :width] * scale).astype(BF16)
        g_qkv_v[near_at, 2 * width :] = total_at[:, width:].astype(BF16)

    @pl.when(has_before)
    def _():
        for item in to_after:
            item.wait_recv()

    @functools.partial(loop, rows // CHUNK)
    def _(i):
        at = rows_of(i, CHUNK)
        both = att_t[:, at] + got_q[:, at].astype(F32)
        g_qkv_v[at, :width] = (both.T * scale).astype(BF16)

    loop(count + 2 - 14, lambda i: relay(14 + i))
    stores = [
        pltpu.make_async_copy(g_qkv_v, g_qkv_hbm, store_sem.at[0]),
        pltpu.make_async_copy(total, ffn_sum_hbm, store_sem.at[1]),
    ]
    stores[0].start()
    loop(count, line.get)
    stores[1].start()

    def write(tile, value):
        up_out[:, tile * 512 : (tile + 1) * 512] = value

    scatter.finish(write)
    scatter.drain()
    line.drain_all()
    to_near.wait_send()

    @pl.when(has_before)
    def _():
        for item in to_before:
            item.wait_send()

    @pl.when(has_after)
    def _():
        for item in to_after:
            item.wait_send()

    for item in stores:
        item.wait()


def grad_attend(g_attn, wout, q, q_next, kv, att_t, lse, lengths, until, ffn_low, norm2, g_pre):
    rows, depth = g_attn.shape
    width = q.shape[1]
    heads = width // HD
    hidden = g_pre.shape[1]
    chunk = depth // lax.axis_size("cp")
    shape = jax.ShapeDtypeStruct
    return pl.pallas_call(
        grad_attend_kernel,
        out_shape=(
            shape((rows, 3 * width), BF16),
            shape((rows, depth), BF16),
            shape((chunk, hidden), F32),
        ),
        in_specs=[ANY] * 6 + [IN_VMEM, IN_SMEM, IN_SMEM, ANY, ANY, ANY],
        out_specs=(ANY, ANY, IN_VMEM),
        scratch_shapes=[
            pltpu.VMEM((rows, depth), BF16),
            pltpu.VMEM((width, depth), BF16),
            pltpu.VMEM((rows, width), BF16),
            pltpu.VMEM((rows, width), BF16),
            pltpu.VMEM((2 * rows, 2 * width), BF16),
            pltpu.VMEM((width, 2 * rows), BF16),
            pltpu.VMEM((width, rows), F32),
            pltpu.VMEM((heads, 2 * HD, rows), BF16),
            pltpu.VMEM((rows, width), BF16),
            pltpu.VMEM((rows, width), BF16),
            pltpu.VMEM((heads, 2 * HD, rows), BF16),
            pltpu.VMEM((2 * heads, rows), F32),
            pltpu.VMEM((2 * heads, rows), F32),
            pltpu.VMEM((2 * rows, 2 * width), F32),
            pltpu.VMEM((rows, 3 * width), BF16),
            pltpu.VMEM((width, rows), F32),
            pltpu.VMEM((width, rows), BF16),
            pltpu.VMEM((width, rows), BF16),
            pltpu.VMEM((rows, 2 * width), BF16),
            pltpu.VMEM((rows, 2 * width), BF16),
            pltpu.SemaphoreType.DMA((3 + heads // 2,)),
            pltpu.SemaphoreType.DMA((3 + heads // 2,)),
            pltpu.VMEM((rows, depth), BF16),
            pltpu.VMEM((rows, hidden), BF16),
            pltpu.VMEM((depth, hidden), BF16),
            *scatter_scratch(depth, hidden, SPLIT_UP),
            *line_scratch(rows, depth),
            pltpu.SemaphoreType.DMA((9,)),
            pltpu.SemaphoreType.DMA((2,)),
        ],
        compiler_params=pltpu.CompilerParams(collective_id=2, has_side_effects=True, vmem_limit_bytes=63 * 2**20),
        name="grad_attend",
    )(g_attn, wout, q, q_next, kv, att_t, lse, lengths, until, ffn_low, norm2, g_pre)


def last_kernel(
    g_qkv_hbm, wqkv_hbm, x_hbm, g_hidden_hbm, norm_hbm, g_attn_hbm, att_hbm, attn_sum_hbm, ffn_sum_hbm,
    lengths_ref, until_ref, gains, b_outs, sums_in,
    g_x, out, qkv_out, w_out_out, gains_out, shifts_out, bqv_out, bouts_out, bup_out,
    g_qkv_v, w_v, x_v, norm_v, g_attn_v, att_v, attn_sum, ffn_sum, acc, small, small_got, late, late_got,
    terms, near, far, rs_send, rs_recv,
    part, slot_a, slot_b, total, ar_send, ar_recv, small_send, small_recv, load_sem,
):
    cp, tp, core, chip = place()
    rows, depth = x_v.shape
    width = att_v.shape[1]
    count = rows // SUB
    loads = [
        pltpu.make_async_copy(source, target, load_sem.at[i])
        for i, (source, target) in enumerate(
            (
                (g_qkv_hbm, g_qkv_v),
                (wqkv_hbm, w_v),
                (norm_hbm, norm_v),
                (g_attn_hbm, g_attn_v),
                (att_hbm, att_v),
                (x_hbm, x_v),
                (g_hidden_hbm, g_x),
                (attn_sum_hbm, attn_sum),
                (ffn_sum_hbm, ffn_sum),
            )
        )
    ]
    for item in loads[:2]:
        item.start()
    line = LineSum(part, slot_a, slot_b, total, ar_send, ar_recv)
    scatter = Scatter(terms, near, far, rs_send, rs_recv, SPLIT_LAST)
    bands = lax.axis_size("cp")
    greet(cp, tp, [(lax.rem(cp + k, bands), tp) for k in range(1, bands)])
    _, live = band_info(lengths_ref, until_ref, cp * rows)
    acc[...] = jnp.zeros_like(acc)
    loads[0].wait()
    loads[1].wait()

    for c in range(rows // CHUNK):
        chunk = slice(c * CHUNK, (c + 1) * CHUNK)

        @functools.partial(loop, depth // 512)
        def _(t, chunk=chunk):
            lanes = rows_of(t, 512)
            value = dot_nt(g_qkv_v[chunk, :width], w_v[0, lanes])
            value = value + dot_nt(g_qkv_v[chunk, width : 2 * width], w_v[1, lanes])
            value = value + dot_nt(g_qkv_v[chunk, 2 * width :], w_v[2, lanes])
            part[chunk, lanes] = value.astype(BF16)

        loop(CHUNK // SUB, lambda s, c=c: line.push(s + c * (CHUNK // SUB)))
        if c == 0:
            for item in loads[2:]:
                item.start()

    def small_copy(which, sender, receiver):
        source, target = ((small, small_got), (late, late_got))[which]
        return pltpu.make_async_remote_copy(
            src_ref=source, dst_ref=target.at[sender], send_sem=small_send.at[which, receiver],
            recv_sem=small_recv.at[which, sender], device_id=(receiver, tp), device_id_type=MESH,
        )

    def give_small(which):
        loop(bands - 1, lambda k: small_copy(which, cp, lax.rem(cp + 1 + k, bands)).start())

    def take_small(which):
        source, target = ((small, small_got), (late, late_got))[which]
        target[cp] = source[...]

        @functools.partial(loop, bands - 1)
        def _(k):
            sender = lax.rem(cp + 1 + k, bands)
            small_copy(which, sender, sender).wait_recv()

        value = target[0]
        for k in range(1, bands):
            value = value + target[k]
        return value

    small[0:5] = sums_in[0:5]
    small[6:8] = jnp.zeros((2, depth), F32)
    small[5:6, 2 * width :] = jnp.zeros((1, depth - 2 * width), F32)
    for j in range(2):
        bias = jnp.sum(g_qkv_v[:, 2 * j * width : (2 * j + 1) * width].astype(F32), axis=0, keepdims=True)
        small[5:6, j * width : (j + 1) * width] = bias
    give_small(0)
    for item in loads[2:]:
        item.wait()

    def back(s):
        line.get(s)
        at = rows_of(s, SUB)
        e = total[at].astype(F32)
        v = x_v[at].astype(F32)
        centred = v - jnp.mean(v, axis=-1, keepdims=True)
        scale = lax.rsqrt(jnp.mean(centred * centred, axis=-1, keepdims=True) + EPS)
        hat = centred * scale
        t = e * gains[0:1]
        along = t - jnp.mean(t, axis=-1, keepdims=True) - hat * jnp.mean(t * hat, axis=-1, keepdims=True)
        g_x[at] = g_x[at] + along * scale
        row = lax.broadcasted_iota(jnp.int32, (SUB, 1), 0) + s * SUB
        branches = attn_sum[at].astype(F32) + b_outs[0:1] + (ffn_sum[at].astype(F32) + b_outs[1:2])
        out[at] = v + jnp.where(row < live, branches, 0.0)
        acc[0] += fold(e * hat)
        acc[1] += fold(e)

    behind = 4

    def ahead(s):
        line.tick(s)

        @pl.when(s >= behind)
        def _():
            back(s - behind)

    def pick(tile, at):
        if tile < 3:
            return norm_v[:, at], g_qkv_v[:, tile * width : (tile + 1) * width]
        return g_attn_v[:, at], att_v[...]

    scatter.fill_near(pick)
    ahead(0)
    ahead(1)
    scatter.fill_own(pick)
    ahead(2)
    scatter.add_near()
    loop(9 - 3, lambda i: ahead(3 + i))
    scatter.pass_on(1)
    loop(13 - 9, lambda i: ahead(9 + i))
    scatter.keep(1)
    scatter.between()
    loop(count + 2 - 13, lambda i: ahead(13 + i))
    loop(behind - 2, lambda i: back(count + 2 - behind + i))

    for k in range(2):
        late[k : k + 1] = jnp.sum(acc[k], axis=0, keepdims=True)
    give_small(1)
    early = take_small(0)
    bouts_out[...] = early[2:4]
    bup_out[...] = early[4:5]
    for j in range(2):
        bqv_out[j : j + 1] = early[5:6, j * width : (j + 1) * width]

    def write(tile, value):
        if tile < 3:
            qkv_out[tile] = value
        else:
            w_out_out[...] = value.T

    scatter.finish(write)
    final = take_small(1)
    gains_out[0:1] = final[0:1]
    gains_out[1:2] = early[0:1]
    shifts_out[0:1] = final[1:2]
    shifts_out[1:2] = early[1:2]
    scatter.drain()
    line.drain_all()

    @functools.partial(loop, bands - 1)
    def _(k):
        other = lax.rem(cp + 1 + k, bands)
        small_copy(0, cp, other).wait_send()
        small_copy(1, cp, other).wait_send()


def last(g_qkv, wqkv, x, g_hidden, norm1, g_attn, att, attn_sum, ffn_sum, lengths, until, gains, b_outs, sums):
    rows, depth = x.shape
    width = att.shape[1]
    bands = lax.axis_size("cp")
    chunk = depth // bands
    pinned = bands <= 8
    result = pltpu.VMEM if pinned else jax.ShapeDtypeStruct
    return pl.pallas_call(
        last_kernel,
        out_shape=(
            result((rows, depth), F32),
            result((rows, depth), F32),
            result((3, chunk, width), F32),
            result((width, chunk), F32),
            result((2, depth), F32),
            result((2, depth), F32),
            result((2, width), F32),
            result((2, depth), F32),
            result((1, depth), F32),
        ),
        in_specs=[ANY] * 9 + [IN_SMEM] * 2 + [IN_VMEM] * 3,
        out_specs=(IN_VMEM,) * 9,
        scratch_shapes=[
            pltpu.VMEM((rows, 3 * width), BF16),
            pltpu.VMEM((3, depth, width), BF16),
            pltpu.VMEM((rows, depth), BF16),
            pltpu.VMEM((rows, depth), BF16),
            pltpu.VMEM((rows, depth), BF16),
            pltpu.VMEM((rows, width), BF16),
            pltpu.VMEM((rows, depth), BF16),
            pltpu.VMEM((rows, depth), BF16),
            pltpu.VMEM((2, 8, depth), F32),
            pltpu.VMEM((8, depth), F32),
            pltpu.VMEM((bands, 8, depth), F32),
            pltpu.VMEM((2, depth), F32),
            pltpu.VMEM((bands, 2, depth), F32),
            pltpu.VMEM((depth, depth), BF16),
            *scatter_scratch(depth, depth, SPLIT_LAST),
            *line_scratch(rows, depth),
            pltpu.SemaphoreType.DMA((2, bands)),
            pltpu.SemaphoreType.DMA((2, bands)),
            pltpu.SemaphoreType.DMA((9,)),
        ],
        compiler_params=pltpu.CompilerParams(collective_id=3, has_side_effects=True, vmem_limit_bytes=(48 if pinned else 62) * 2**20),
        name="last",
    )(g_qkv, wqkv, x, g_hidden, norm1, g_attn, att, attn_sum, ffn_sum, lengths, until, gains, b_outs, sums)


def shards(
    layer_input,
    seq_lengths,
    active_until,
    ln_gains,
    ln_shifts,
    query_key_value_weight,
    b_qv,
    w_out,
    b_outs,
    w_up,
    b_up,
    w_down,
    d_out,
):
    wqkv = jnp.transpose(query_key_value_weight, (1, 0, 2))
    (attn_sum, norm1, q, q_next, kv, att, att_t, norm2, g_pre, ffn_low, g_hidden, g_attn, lse, sums, g_down) = front(
        layer_input, d_out, seq_lengths, active_until, ln_gains, ln_shifts, wqkv, b_qv, w_out, b_outs, b_up[None],
        w_up, w_down,
    )
    g_qkv_rows, ffn_sum, g_up = grad_attend(
        g_attn, w_out, q, q_next, kv, att_t, lse, seq_lengths, active_until, ffn_low, norm2, g_pre
    )
    g_x, out, g_qkv, g_out, g_ln_gains, g_ln_shifts, g_bqv, g_bouts, g_bup = last(
        g_qkv_rows, wqkv, layer_input, g_hidden, norm1, g_attn, att, attn_sum, ffn_sum,
        seq_lengths, active_until, ln_gains, b_outs, sums,
    )
    g_qkv = jnp.transpose(g_qkv, (1, 0, 2))
    return (out, g_x, g_ln_gains, g_ln_shifts, g_qkv, g_bqv, g_out, g_bouts, g_up, g_bup[0], g_down)


def solution(mesh):
    return jax.shard_map(
        shards,
        mesh=mesh,
        in_specs=(
            P("cp", None),
            P(),
            P(),
            P(),
            P(),
            P(None, None, "tp"),
            P(None, "tp"),
            P("tp", None),
            P(),
            P(None, "tp"),
            P("tp"),
            P("tp", None),
            P("cp", None),
        ),
        out_specs=(
            P("cp", None),
            P("cp", None),
            P(),
            P(),
            P("cp", None, "tp"),
            P(None, "tp"),
            P("tp", "cp"),
            P(),
            P("cp", "tp"),
            P("tp"),
            P("tp", "cp"),
        ),
        check_vma=False,
    )
```

```python
import functools
import math

import jax
import jax.numpy as jnp
from jax import lax
from jax.experimental import pallas as pl
from jax.experimental.pallas import tpu as pltpu
from jax.sharding import PartitionSpec as P

HD = 64
LONG = 2048
EPS = 1e-05
NEG = -1e30
MESH = pl.DeviceIdType.MESH
F32 = jnp.float32
BF16 = jnp.bfloat16
ANY = pl.BlockSpec(memory_space=pl.ANY)
IN_VMEM = pl.BlockSpec(memory_space=pltpu.VMEM)
IN_SMEM = pl.BlockSpec(memory_space=pltpu.SMEM)
SUB = 32
PIECE = 16
CHUNK = 256


def dot(a, b):
    return jnp.dot(a, b, preferred_element_type=F32)


def dot_nt(a, b):
    return lax.dot_general(a, b, (((1,), (1,)), ((), ())), preferred_element_type=F32)


def dot_tn(a, b):
    return lax.dot_general(a, b, (((0,), (0,)), ((), ())), preferred_element_type=F32)


def rows_of(index, size):
    return pl.ds(pl.multiple_of(index * size, size), size)


def place():
    cp = lax.axis_index("cp")
    tp = lax.axis_index("tp")
    return cp, tp, lax.rem(cp, 2), lax.div(cp, 2)


def greet(cp, tp, others):
    barrier = pltpu.get_barrier_semaphore()
    edge = (tp == 0) | (tp == 3)
    for other in [*others, (cp, line_near(tp))]:
        pl.semaphore_signal(barrier, inc=1, device_id=other, device_id_type=MESH)

    @pl.when(jnp.logical_not(edge))
    def _():
        pl.semaphore_signal(barrier, inc=1, device_id=(cp, 3 - tp), device_id_type=MESH)

    pl.semaphore_wait(barrier, len(others) + jnp.where(edge, 1, 2))


def line_near(tp):
    return jnp.where(tp == 0, 1, jnp.where(tp == 1, 0, jnp.where(tp == 2, 3, 2)))


class LineSum:
    def __init__(self, part, slot_a, slot_b, total, send, recv):
        self.cp, self.tp, _, _ = place()
        self.edge = (self.tp == 0) | (self.tp == 3)
        self.refs = (part, slot_a, slot_b, total)
        self.send, self.recv = send, recv
        self.count = part.shape[0] // SUB

    def copy(self, kind, piece):
        part, slot_a, slot_b, total = self.refs
        src, dst = ((part, slot_a), (part, slot_b), (total, total))[kind]
        other = (self.cp, 3 - self.tp if kind == 1 else line_near(self.tp))
        rows = rows_of(piece, PIECE)
        return pltpu.make_async_remote_copy(
            src_ref=src.at[rows],
            dst_ref=dst.at[rows],
            send_sem=self.send.at[kind, piece],
            recv_sem=self.recv.at[kind, piece],
            device_id=other,
            device_id_type=MESH,
        )

    def pieces(self, s):
        return [s * (SUB // PIECE) + j for j in range(SUB // PIECE)]

    def push(self, s):
        @pl.when(self.edge)
        def _():
            for piece in self.pieces(s):
                self.copy(0, piece).start()

    def relay_in(self, s):
        part, slot_a, _, _ = self.refs

        @pl.when(jnp.logical_not(self.edge))
        def _():
            for piece in self.pieces(s):
                rows = rows_of(piece, PIECE)
                self.copy(0, piece).wait_recv()
                part[rows] = (part[rows].astype(F32) + slot_a[rows].astype(F32)).astype(BF16)
                self.copy(1, piece).start()

    def relay_out(self, s):
        part, _, slot_b, total = self.refs

        @pl.when(jnp.logical_not(self.edge))
        def _():
            for piece in self.pieces(s):
                rows = rows_of(piece, PIECE)
                self.copy(1, piece).wait_recv()
                total[rows] = (part[rows].astype(F32) + slot_b[rows].astype(F32)).astype(BF16)
                self.copy(2, piece).start()

    def get(self, s):
        @pl.when(self.edge)
        def _():
            for piece in self.pieces(s):
                self.copy(2, piece).wait_recv()

    def tick(self, s):
        @pl.when(s < self.count)
        def _():
            self.relay_in(s)

        @pl.when(s >= 2)
        def _():
            self.relay_out(s - 2)

    def drain_all(self):
        @pl.when(self.edge)
        def _():
            loop(self.refs[0].shape[0] // PIECE, lambda piece: self.copy(0, piece).wait_send())

        @pl.when(jnp.logical_not(self.edge))
        def _():
            @functools.partial(loop, self.refs[0].shape[0] // PIECE)
            def _(piece):
                self.copy(1, piece).wait_send()
                self.copy(2, piece).wait_send()


def line_scratch(rows, width):
    return [pltpu.VMEM((rows, width), BF16)] * 4 + [pltpu.SemaphoreType.DMA((3, rows // PIECE))] * 2


def band_info(lengths_ref, until_ref, first):
    start = jnp.int32(0)
    begin = jnp.int32(0)
    until = jnp.int32(0)
    for i in range(lengths_ref.shape[0]):
        length = lengths_ref[i]
        inside = (first >= start) & (first < start + length)
        begin = jnp.where(inside, start, begin)
        until = jnp.where(inside, until_ref[i], until)
        start = start + length
    return begin, until + begin - first


def loop(count, body):
    def step(i, carry):
        body(i)
        return carry

    lax.fori_loop(0, count, step, 0)


class Scatter:
    def __init__(self, terms, near, far, send, recv, split):
        self.cp, self.tp, self.core, self.chip = place()
        self.count = lax.axis_size("cp")
        self.half = self.count // 2
        self.depth = self.half.bit_length() - 1
        self.terms, self.near, self.far = terms, near, far
        self.send, self.recv = send, recv
        self.chunk = terms.shape[0] // self.count
        self.width = terms.shape[1]
        self.lanes = {p: c for p, c in ((0, slice(0, split)), (1, slice(split, self.width))) if c.stop > c.start}
        self.order = list(range(self.half))[::-1]
        self.whole_blocks = self.chunk >= 128

    def partners(self):
        others = [(self.cp + 1 - 2 * self.core, self.tp)]
        for bit in range(self.depth):
            others.append((self.cp + 2 * self.flip(1 << bit), self.tp))
        return others

    def flip(self, e):
        change = 0
        for bit in range(self.depth):
            if e >> bit & 1:
                change = change + (1 - 2 * lax.rem(lax.div(self.chip, 1 << bit), 2)) * (1 << bit)
        return change

    def row(self, e, core):
        if isinstance(e, int):
            other = self.chip + self.flip(e)
        else:
            other = 0
            for bit in range(self.depth):
                mine = lax.rem(lax.div(self.chip, 1 << bit), 2)
                change = lax.rem(lax.div(e, 1 << bit), 2)
                other = other + (mine + change - 2 * mine * change) * (1 << bit)
        return (2 * other + core) * self.chunk

    def fill_block(self, first, size, pick):
        rows = pl.ds(pl.multiple_of(first, size), size)

        for tile in range(self.width // 512):
            left, right = pick(tile, rows)
            self.terms[rows, tile * 512 : (tile + 1) * 512] = dot_tn(left, right).astype(BF16)

    def fill_near(self, pick):
        if not self.whole_blocks:
            loop(self.terms.shape[0] // 128, lambda k: self.fill_block(k * 128, 128, pick))

        @functools.partial(loop, self.half)
        def _(k):
            e = self.half - 1 - k
            if self.whole_blocks:
                self.fill_block(self.row(e, 1 - self.core), self.chunk, pick)
            self.near_copy(e).start()

    def fill_own(self, pick):
        if self.whole_blocks:
            loop(self.half, lambda k: self.fill_block(self.row(self.half - 1 - k, self.core), self.chunk, pick))

    def near_copy(self, e):
        return pltpu.make_async_remote_copy(
            src_ref=self.terms.at[pl.ds(pl.multiple_of(self.row(e, 1 - self.core), self.chunk), self.chunk)],
            dst_ref=self.near.at[rows_of(e, self.chunk)],
            send_sem=self.send.at[e],
            recv_sem=self.recv.at[e],
            device_id=(self.cp + 1 - 2 * self.core, self.tp),
            device_id_type=MESH,
        )

    def add(self, e, source, first, lanes):
        base = self.row(e, self.core)

        @functools.partial(loop, self.chunk // 32)
        def _(i):
            mine = pl.ds(pl.multiple_of(base + i * 32, 32), 32)
            other = pl.ds(pl.multiple_of(first + i * 32, 32), 32)
            self.terms[mine, lanes] = (
                self.terms[mine, lanes].astype(F32) + source[other, lanes].astype(F32)
            ).astype(BF16)

    def add_near(self):
        for e in self.order:
            self.near_copy(e).wait_recv()
            self.add(e, self.near, e * self.chunk, slice(0, self.width))
            for part in self.lanes:
                if self.sent(1, part, e):
                    self.far_copy(1, part, e).start()

    def bit(self, level, part):
        return level - 1 if part == 0 else self.depth - level

    def sent(self, level, part, e):
        bit = self.bit(level, part)
        return e >> bit & 1 and (e & ((1 << bit) - 1) if part == 0 else e >> (bit + 1)) == 0

    def slot(self, level, part, e):
        bit = self.bit(level, part)
        return e >> (bit + 1) if part == 0 else e & ((1 << bit) - 1)

    def place(self, level):
        return sum(self.terms.shape[0] >> (earlier + 1) for earlier in range(1, level))

    def far_copy(self, level, part, e):
        bit = self.bit(level, part)
        sem = self.half + sum(len(self.lanes) * (self.half >> earlier) for earlier in range(1, level))
        sem += list(self.lanes).index(part) * (self.half >> level) + self.slot(level, part, e)
        first = self.place(level) + self.slot(level, part, e) * self.chunk
        return pltpu.make_async_remote_copy(
            src_ref=self.terms.at[
                pl.ds(pl.multiple_of(self.row(e, self.core), self.chunk), self.chunk), self.lanes[part]
            ],
            dst_ref=self.far.at[first : first + self.chunk, self.lanes[part]],
            send_sem=self.send.at[sem],
            recv_sem=self.recv.at[sem],
            device_id=(self.cp + 2 * self.flip(1 << bit), self.tp),
            device_id_type=MESH,
        )

    def coming(self, level, passed_on):
        for e in self.order:
            for part in self.lanes:
                if self.sent(level, part, e):
                    kept = e ^ (1 << self.bit(level, part))
                    if (level < self.depth and bool(self.sent(level + 1, part, kept))) == passed_on:
                        yield part, e, kept

    def arrive(self, level, part, e, kept):
        self.far_copy(level, part, e).wait_recv()
        self.add(kept, self.far, self.place(level) + self.slot(level, part, e) * self.chunk, self.lanes[part])

    def pass_on(self, level):
        for part, e, kept in self.coming(level, True):
            self.arrive(level, part, e, kept)
            self.far_copy(level + 1, part, kept).start()

    def keep(self, level):
        for part, e, kept in self.coming(level, False):
            self.arrive(level, part, e, kept)

    def between(self):
        for level in range(2, self.depth):
            self.pass_on(level)
            self.keep(level)

    def finish(self, write):
        level = self.depth
        mine = pl.ds(pl.multiple_of(self.row(0, self.core), self.chunk), self.chunk)
        for part, e, _ in self.coming(level, False):
            self.far_copy(level, part, e).wait_recv()
            lanes = self.lanes[part]
            for tile in range(lanes.start // 512, lanes.stop // 512):
                cut = slice(tile * 512, (tile + 1) * 512)
                other = pl.ds(self.place(level), self.chunk)
                write(tile, self.terms[mine, cut].astype(F32) + self.far[other, cut].astype(F32))

    def drain(self):
        for e in self.order:
            self.near_copy(e).wait_send()
            for part in self.lanes:
                for level in range(1, self.depth + 1):
                    if self.sent(level, part, e):
                        self.far_copy(level, part, e).wait_send()


def scatter_scratch(depth, width, split):
    count = lax.axis_size("cp")
    parts = (split > 0) + (split < width)
    sems = count // 2 + parts * (count // 2 - 1)
    return [
        pltpu.VMEM((depth // 2, width), BF16),
        pltpu.VMEM((depth // 2 - depth // count, width), BF16),
        pltpu.SemaphoreType.DMA((sems,)),
        pltpu.SemaphoreType.DMA((sems,)),
    ]


def fold(v):
    return jnp.sum(v.reshape(v.shape[0] // 8, 8, v.shape[1]), axis=0)


def gelu_parts(u):
    root = math.sqrt(2.0 / math.pi)
    square = u * u
    th = jnp.tanh(root * (u + 0.044715 * u * square))
    half = 0.5 * (1.0 + th)
    return u * half, half + 0.5 * u * (1.0 - th * th) * (root * (1.0 + 3 * 0.044715 * square))


LAG = 5
SPLIT_DOWN = 1024


def front_kernel(
    x_hbm, d_hbm, lengths_ref, until_ref, gains, shifts, wqkv_hbm, bqv, wout_hbm, b_outs, b_up, up_hbm, down_hbm,
    attn_sum_hbm, norm1_hbm, q_hbm, q_next_hbm, kv_hbm, att_hbm, att_t_hbm, norm2_hbm, g_pre_hbm, ffn_hbm, g_hidden_hbm,
    g_attn_hbm, lse_out, sums_out, down_out,
    x_v, d_v, norm_v, up_v, down_v, q_v, q_next, kv, q_t, q_t_next, v_t, att_t, att_v, cross, cross_in, lse_cross, lse_in, xhat, rstd, act_v, g_pre_v, acc,
    part, slot_a, total, slot_b1, slot_b2, ar_send, ar_recv, near, far, rs_send, rs_recv,
    x_send, x_recv, load_sem, store_sem,
):
    cp, tp, core, chip = place()
    bands = lax.axis_size("cp")
    chips = bands // 2
    rows, depth = x_v.shape
    width = q_v.shape[1]
    heads = width // HD
    hidden = act_v.shape[1]
    count = rows // SUB
    per_chunk = CHUNK // SUB
    sibling = (cp + 1 - 2 * core, tp)
    after = (lax.rem(cp + 2, bands), tp)
    before = (lax.rem(cp + bands - 2, bands), tp)
    wout_v, scores, g_hidden, g_attn, part2, ffn_v = act_v, xhat, xhat, x_v, v_t, part
    loads = [
        pltpu.make_async_copy(x_hbm, x_v, load_sem.at[0]),
        *[
            pltpu.make_async_copy(
                wqkv_hbm.at[j], up_v.at[:, j * width : (j + 1) * width], load_sem.at[i]
            )
            for i, j in ((1, 0), (2, 1), (3, 2))
        ],
        pltpu.make_async_copy(wout_hbm, wout_v, load_sem.at[4]),
        pltpu.make_async_copy(down_hbm, down_v, load_sem.at[5]),
        pltpu.make_async_copy(d_hbm, d_v, load_sem.at[6]),
        pltpu.make_async_copy(up_hbm, up_v, load_sem.at[7]),
    ]
    for item in loads[:4]:
        item.start()
    stores = {
        name: pltpu.make_async_copy(source, target, store_sem.at[i])
        for i, (name, source, target) in enumerate(
            (
                ("norm1", norm_v, norm1_hbm),
                ("q", q_v, q_hbm),
                ("kv", kv, kv_hbm),
                ("q_next", q_next, q_next_hbm),
                ("att", att_v, att_hbm),
                ("att_t", att_t, att_t_hbm),
                ("sum0", total.at[:CHUNK], attn_sum_hbm.at[:CHUNK]),
                ("sum1", total.at[CHUNK:], attn_sum_hbm.at[CHUNK:]),
                ("norm2", norm_v, norm2_hbm),
                ("g_pre", g_pre_v, g_pre_hbm),
                ("ffn", ffn_v, ffn_hbm),
                ("g_hidden", g_hidden, g_hidden_hbm),
                ("g_attn", g_attn, g_attn_hbm),
            )
        )
    }
    line1 = LineSum(part, slot_a, slot_b1, total, ar_send.at[0], ar_recv.at[0])
    line2 = LineSum(part2, slot_a, slot_b2, total, ar_send.at[1], ar_recv.at[1])
    scatter = Scatter(up_v, near, far, rs_send, rs_recv, SPLIT_DOWN)
    greet(cp, tp, [*scatter.partners(), after, before])
    _, live = band_info(lengths_ref, until_ref, cp * rows)
    begin, _ = band_info(lengths_ref, until_ref, (chip + 1) * 2 * rows)
    bias = jnp.where(begin < (chip + 1) * 2 * rows, 0.0, NEG)
    loads[0].wait()

    @functools.partial(loop, rows // 64)
    def _(i):
        at = rows_of(i, 64)
        v = x_v[at].astype(F32)
        mean = jnp.mean(v, axis=-1, keepdims=True)
        centred = v - mean
        var = jnp.mean(centred * centred, axis=-1, keepdims=True)
        norm_v[at] = (centred * lax.rsqrt(var + EPS) * gains[0:1] + shifts[0:1]).astype(BF16)

    stores["norm1"].start()
    chunks = rows // CHUNK

    def exchange(kind, c=0):
        cut = slice(c * CHUNK, (c + 1) * CHUNK)
        source, target, device = (
            (q_v.at[cut], q_next.at[cut], before),
            (cross.at[c], cross_in.at[c], after),
            (lse_cross.at[c], lse_in.at[c], after),
            (kv.at[rows_of(core, rows)], kv.at[rows_of(core, rows)], sibling),
        )[kind]
        sem = kind * chunks + c
        return pltpu.make_async_remote_copy(
            src_ref=source, dst_ref=target, send_sem=x_send.at[sem], recv_sem=x_recv.at[sem],
            device_id=device, device_id_type=MESH,
        )

    queries = [exchange(0, c) for c in range(chunks)]
    gathered = [[exchange(1, c), exchange(2, c)] for c in range(chunks)]
    to_near = exchange(3)
    has_before, has_after = chip > 0, chip < chips - 1
    loads[1].wait()

    for c in range(chunks):
        at = slice(c * CHUNK, (c + 1) * CHUNK)
        q_v[at] = (dot(norm_v[at], up_v[:, :width]) + bqv[0:1]).astype(BF16)

        @pl.when(has_before)
        def _(c=c):
            queries[c].start()

    @pl.when(jnp.logical_not(has_after))
    def _():
        q_next[...] = jnp.zeros_like(q_next)

    @pl.when(jnp.logical_not(has_before))
    def _():
        cross_in[...] = jnp.zeros_like(cross_in)
        lse_in[...] = jnp.full_like(lse_in, NEG)

    for load, column in ((2, 0), (3, 1)):
        loads[load].wait()

        @functools.partial(loop, rows // CHUNK)
        def _(i):
            value = dot(norm_v[rows_of(i, CHUNK)], up_v[:, (column + 1) * width : (column + 2) * width])
            if column:
                value = value + bqv[1:2]
            target = pl.ds(pl.multiple_of(core * rows + i * CHUNK, CHUNK), CHUNK)
            kv[target, column * width : (column + 1) * width] = value.astype(BF16)

    to_near.start()
    for item in loads[4:]:
        item.start()
    stores["q"].start()

    def turned(value, h):
        upper = lax.broadcasted_iota(jnp.int32, value.shape, 0) < HD
        return jnp.where(upper == (h % 2 == 0), value, 0.0).astype(BF16)

    @functools.partial(loop, rows // CHUNK)
    def _(i):
        at = rows_of(i, CHUNK)
        value = q_v[at].astype(F32).T * (HD ** -0.5)
        for h in range(heads):
            q_t[h, :, at] = turned(value[(h // 2) * 2 * HD : (h // 2 + 1) * 2 * HD], h)

    def turn_values(slot):
        v_t[:, rows_of(slot, rows)] = kv[rows_of(slot, rows), width:].astype(F32).T.astype(BF16)

    turn_values(core)
    to_near.wait_recv()
    stores["kv"].start()
    turn_values(1 - core)

    def attend(query, lanes, feature, mask):
        top = jnp.full((1, CHUNK), NEG, F32)
        for b in range(2):
            s = mask(b, dot(kv[b * rows : (b + 1) * rows, lanes], query))
            scores[:, b * CHUNK : (b + 1) * CHUNK] = s
            top = jnp.maximum(top, jnp.max(s, axis=0, keepdims=True))
        mass = jnp.zeros((1, CHUNK), F32)
        mixed = jnp.zeros((HD, CHUNK), F32)
        for b in range(2):
            p = jnp.exp(scores[:, b * CHUNK : (b + 1) * CHUNK] - top)
            mass = mass + jnp.sum(p, axis=0, keepdims=True)
            mixed = mixed + dot(v_t[feature, b * rows : (b + 1) * rows], p.astype(BF16))
        return mixed / mass, top + jnp.log(mass)

    def cross_chunk(c):
        columns = slice(c * CHUNK, (c + 1) * CHUNK)
        queries[c].wait_recv()
        value = q_next[columns].astype(F32).T * (HD ** -0.5)
        for h in range(heads):
            q_t_next[h] = turned(value[(h // 2) * 2 * HD : (h // 2 + 1) * 2 * HD], h)

        @functools.partial(loop, heads)
        def _(h):
            lanes = pl.ds(pl.multiple_of(lax.div(h, 2) * 2 * HD, 2 * HD), 2 * HD)
            feature = pl.ds(pl.multiple_of(h * HD, HD), HD)
            mixed, lse_row = attend(q_t_next[h], lanes, feature, lambda b, s: s + bias)
            cross[c, feature] = mixed.astype(BF16)
            lse_cross[c, pl.ds(h, 1)] = lse_row
            if c > 0:
                @pl.when(lax.rem(h, 4) == 3)
                def _():
                    line1.tick(lax.div(h, 4))

        for item in gathered[c]:
            item.start()

    loads[4].wait()

    for c in range(rows // CHUNK):
        columns = slice(c * CHUNK, (c + 1) * CHUNK)

        @pl.when(has_after)
        def _(c=c):
            cross_chunk(c)

        if c > 0:
            @pl.when(jnp.logical_not(has_after))
            def _():
                loop(2, line1.tick)

        def causal(b, s, c=c):
            key = lax.broadcasted_iota(jnp.int32, (rows, CHUNK), 0) + b * rows
            row = lax.broadcasted_iota(jnp.int32, (rows, CHUNK), 1) + c * CHUNK
            return jnp.where(key <= row + core * rows, s, NEG)

        def head(h, c=c, columns=columns, causal=causal):
            lanes = pl.ds(pl.multiple_of(lax.div(h, 2) * 2 * HD, 2 * HD), 2 * HD)
            feature = pl.ds(pl.multiple_of(h * HD, HD), HD)
            mixed, lse_row = attend(q_t[h, :, columns], lanes, feature, causal)
            att_t[feature, columns] = mixed
            lse_out[pl.ds(h, 1), columns] = lse_row
            if c > 0:
                @pl.when(lax.rem(h, 4) == 3)
                def _():
                    line1.tick(2 + lax.div(h, 4))

        loop(heads, head)

        @pl.when(has_before)
        def _(c=c):
            for item in gathered[c]:
                item.wait_recv()

        mine, other = lse_out[:, columns], lse_in[c]
        top = jnp.maximum(mine, other)
        both = top + jnp.log(jnp.exp(mine - top) + jnp.exp(other - top))
        share, share_in = jnp.exp(mine - both), jnp.exp(other - both)
        lse_out[:, columns] = both
        for h in range(heads):
            feature = slice(h * HD, (h + 1) * HD)
            att_t[feature, columns] = (
                att_t[feature, columns] * share[h : h + 1]
                + cross_in[c, feature].astype(F32) * share_in[h : h + 1]
            )
        att_v[columns] = att_t[:, columns].T.astype(BF16)

        @functools.partial(loop, depth // 512)
        def _(t, columns=columns):
            lanes = rows_of(t, 512)
            part[columns, lanes] = dot(att_v[columns], wout_v[:, lanes]).astype(BF16)

        loop(per_chunk, lambda s, c=c: line1.push(s + c * per_chunk))

    stores["q_next"].start()
    stores["att"].start()
    stores["att_t"].start()
    acc[...] = jnp.zeros_like(acc)
    stores["norm1"].wait()
    loads[6].wait()

    def second_norm(s):
        line1.get(s)
        at = rows_of(s, SUB)
        row = lax.broadcasted_iota(jnp.int32, (SUB, 1), 0) + s * SUB
        on = row < live
        v = x_v[at].astype(F32) + jnp.where(on, total[at].astype(F32) + b_outs[0:1], 0.0)
        mean = jnp.mean(v, axis=-1, keepdims=True)
        centred = v - mean
        scale = lax.rsqrt(jnp.mean(centred * centred, axis=-1, keepdims=True) + EPS)
        hat = centred * scale
        xhat[at] = hat
        rstd[at] = jnp.broadcast_to(scale, (SUB, 128))
        norm_v[at] = (hat * gains[1:2] + shifts[1:2]).astype(BF16)
        acc[3] += fold(jnp.where(on, d_v[at].astype(F32), 0.0))

    def feed_forward(c, ticks):
        chunk = slice(c * CHUNK, (c + 1) * CHUNK)
        on = lax.broadcasted_iota(jnp.int32, (CHUNK, 1), 0) + c * CHUNK < live

        @functools.partial(loop, hidden // 512)
        def _(t):
            lanes = rows_of(t, 512)
            pre = dot(norm_v[chunk], up_v[:, lanes]) + b_up[0:1, lanes]
            g_act = dot_nt(d_v[chunk], down_v[lanes])
            act, slope = gelu_parts(pre)
            act_v[chunk, lanes] = jnp.where(on, act, 0.0).astype(BF16)
            g_pre = jnp.where(on, g_act * slope, 0.0).astype(BF16)
            g_pre_v[chunk, lanes] = g_pre
            acc[4, :, lanes] += fold(g_pre.astype(F32))

            @pl.when(lax.rem(t, 2) == 1)
            def _():
                ticks(lax.div(t, 2))

        @functools.partial(loop, depth // 512)
        def _(t):
            lanes = rows_of(t, 512)
            part2[chunk, lanes] = dot_nt(g_pre_v[chunk], up_v[lanes]).astype(BF16)

            @pl.when(lax.rem(t, 2) == 1)
            def _():
                ticks(2 + lax.div(t, 2))

    @functools.partial(loop, per_chunk)
    def _(i):
        line1.tick(4 + i)
        second_norm(i)

    stores["sum0"].start()
    loads[5].wait()
    loads[7].wait()
    feed_forward(0, lambda i: line1.tick(4 + per_chunk + i))
    stores["sum0"].wait()
    loop(per_chunk, line2.push)
    loop(4, lambda i: second_norm(per_chunk + i))
    for i in range(2):
        line1.tick(count + i)
        line2.relay_in(i)
        second_norm(per_chunk + 4 + 2 * i)
        second_norm(per_chunk + 5 + 2 * i)
    stores["sum1"].start()
    stores["norm2"].start()
    line1.drain_all()
    feed_forward(1, lambda i: line2.tick(2 + i))
    stores["g_pre"].start()
    stores["sum1"].wait()
    loop(per_chunk, lambda s: line2.push(per_chunk + s))

    def back(s):
        line2.get(s)
        at = rows_of(s, SUB)
        e = total[at].astype(F32)
        hat = xhat[at]
        t = e * gains[1:2]
        along = t - jnp.mean(t, axis=-1, keepdims=True) - hat * jnp.mean(t * hat, axis=-1, keepdims=True)
        value = d_v[at].astype(F32) + along * rstd[at, 0:1]
        g_hidden[at] = value
        row = lax.broadcasted_iota(jnp.int32, (SUB, 1), 0) + s * SUB
        low = jnp.where(row < live, value, 0.0).astype(BF16)
        g_attn[at] = low
        acc[0] += fold(e * hat)
        acc[1] += fold(e)
        acc[2] += fold(low.astype(F32))

    def ahead(s):
        line2.tick(s)
        back(s - LAG)

    def pick(tile, at):
        return d_v[:, at], act_v[:, tile * 512 : (tile + 1) * 512]

    def project(k):
        chunk = rows_of(lax.div(k, depth // 512), CHUNK)
        lanes = rows_of(lax.rem(k, depth // 512), 512)
        ffn_v[chunk, lanes] = dot(act_v[chunk], down_v[:, lanes]).astype(BF16)

    scatter.fill_near(pick)
    line2.tick(6)
    scatter.fill_own(pick)
    line2.tick(7)
    scatter.add_near()
    line2.tick(8)
    loop(4, back)

    @functools.partial(loop, 4)
    def _(i):
        project(2 * i)
        project(2 * i + 1)
        ahead(9 + i)

    scatter.pass_on(1)
    stores["ffn"].start()
    loop(3, lambda i: ahead(13 + i))
    scatter.keep(1)
    scatter.between()
    loop(count + 2 - 16, lambda i: ahead(16 + i))
    loop(LAG - 2, lambda i: back(count - LAG + 2 + i))
    stores["g_hidden"].start()
    stores["g_attn"].start()
    for k in range(5):
        sums_out[k : k + 1] = jnp.sum(acc[k], axis=0, keepdims=True)

    sums_out[5:8] = jnp.zeros((3, sums_out.shape[1]), F32)

    def write(tile, value):
        down_out[tile * 512 : (tile + 1) * 512] = value.T

    scatter.finish(write)
    scatter.drain()
    line2.drain_all()

    to_near.wait_send()

    @pl.when(has_before)
    def _():
        for item in queries:
            item.wait_send()

    @pl.when(has_after)
    def _():
        for items in gathered:
            for item in items:
                item.wait_send()

    for name in ("q", "q_next", "kv", "att", "att_t", "norm2", "g_pre", "ffn", "g_hidden", "g_attn"):
        stores[name].wait()


def front(x, d_out, lengths, until, gains, shifts, wqkv, bqv, wout, b_outs, b_up, w_up, w_down):
    rows, depth = x.shape
    width = wqkv.shape[2]
    heads = width // HD
    hidden = w_up.shape[1]
    chunk = depth // lax.axis_size("cp")
    shape = jax.ShapeDtypeStruct
    return pl.pallas_call(
        front_kernel,
        out_shape=(
            shape((rows, depth), BF16),
            shape((rows, depth), BF16),
            shape((rows, width), BF16),
            shape((rows, width), BF16),
            shape((2 * rows, 2 * width), BF16),
            shape((rows, width), BF16),
            shape((width, rows), F32),
            shape((rows, depth), BF16),
            shape((rows, hidden), BF16),
            shape((rows, depth), BF16),
            shape((rows, depth), F32),
            shape((rows, depth), BF16),
            shape((heads, rows), F32),
            shape((8, depth), F32),
            shape((hidden, chunk), F32),
        ),
        in_specs=[ANY, ANY, IN_SMEM, IN_SMEM, IN_VMEM, IN_VMEM, ANY, IN_VMEM, ANY, IN_VMEM, IN_VMEM, ANY, ANY],
        out_specs=(ANY,) * 12 + (IN_VMEM,) * 3,
        scratch_shapes=[
            pltpu.VMEM((rows, depth), BF16),
            pltpu.VMEM((rows, depth), BF16),
            pltpu.VMEM((rows, depth), BF16),
            pltpu.VMEM((depth, hidden), BF16),
            pltpu.VMEM((hidden, depth), BF16),
            pltpu.VMEM((rows, width), BF16),
            pltpu.VMEM((rows, width), BF16),
            pltpu.VMEM((2 * rows, 2 * width), BF16),
            pltpu.VMEM((heads, 2 * HD, rows), BF16),
            pltpu.VMEM((heads, 2 * HD, CHUNK), BF16),
            pltpu.VMEM((width, depth), BF16),
            pltpu.VMEM((width, rows), F32),
            pltpu.VMEM((rows, width), BF16),
            pltpu.VMEM((rows // CHUNK, width, CHUNK), BF16),
            pltpu.VMEM((rows // CHUNK, width, CHUNK), BF16),
            pltpu.VMEM((rows // CHUNK, heads, CHUNK), F32),
            pltpu.VMEM((rows // CHUNK, heads, CHUNK), F32),
            pltpu.VMEM((rows, depth), F32),
            pltpu.VMEM((rows, 128), F32),
            pltpu.VMEM((rows, hidden), BF16),
            pltpu.VMEM((rows, hidden), BF16),
            pltpu.VMEM((5, 8, depth), F32),
            *[pltpu.VMEM((rows, depth), BF16)] * 5,
            *[pltpu.SemaphoreType.DMA((2, 3, rows // PIECE))] * 2,
            *scatter_scratch(depth, hidden, SPLIT_DOWN),
            pltpu.SemaphoreType.DMA((3 * (rows // CHUNK) + 1,)),
            pltpu.SemaphoreType.DMA((3 * (rows // CHUNK) + 1,)),
            pltpu.SemaphoreType.DMA((8,)),
            pltpu.SemaphoreType.DMA((13,)),
        ],
        compiler_params=pltpu.CompilerParams(collective_id=1, has_side_effects=True, vmem_limit_bytes=63 * 2**20),
        name="front",
    )(x, d_out, lengths, until, gains, shifts, wqkv, bqv, wout, b_outs, b_up, w_up, w_down)


SPLIT_UP = 1024
SPLIT_LAST = 1024


def grad_attend_kernel(
    g_attn_hbm, wout_hbm, q_hbm, q_next_hbm, kv_hbm, att_t_hbm, lse, lengths_ref, until_ref, ffn_hbm, norm_hbm, g_pre_hbm,
    g_qkv_hbm, ffn_sum_hbm, up_out,
    g_attn_v, wout_v, q_v, q_next, kv, k_t, att_t, q_t, g_v, g_next, g_t, stats, stats_next, acc, g_qkv_v,
    g_q_next, give_q, got_q, give_near, got_near, x_send, x_recv,
    norm_v, g_pre_v, terms, near, far, rs_send, rs_recv,
    part, slot_a, slot_b, total, ar_send, ar_recv, load_sem, store_sem,
):
    cp, tp, core, chip = place()
    bands = lax.axis_size("cp")
    chips = bands // 2
    rows, width = q_v.shape
    heads = width // HD
    count = rows // SUB
    sibling = (cp + 1 - 2 * core, tp)
    after = (lax.rem(cp + 2, bands), tp)
    before = (lax.rem(cp + bands - 2, bands), tp)
    loads = [
        pltpu.make_async_copy(source, target, load_sem.at[i])
        for i, (source, target) in enumerate(
            (
                (norm_hbm, norm_v),
                (g_pre_hbm, g_pre_v),
                (ffn_hbm, part),
                (g_attn_hbm, g_attn_v),
                (wout_hbm, wout_v),
                (q_hbm, q_v),
                (q_next_hbm, q_next),
                (kv_hbm, kv),
                (att_t_hbm, att_t),
            )
        )
    ]
    for item in loads[:5]:
        item.start()
    line = LineSum(part, slot_a, slot_b, total, ar_send, ar_recv)
    scatter = Scatter(terms, near, far, rs_send, rs_recv, SPLIT_UP)
    greet(cp, tp, [*scatter.partners(), after, before])
    begin, _ = band_info(lengths_ref, until_ref, (chip + 1) * 2 * rows)
    has_before, has_after = chip > 0, chip < chips - 1
    bias = jnp.where((begin < (chip + 1) * 2 * rows) & has_after, 0.0, NEG)
    loads[0].wait()
    loads[1].wait()
    loads[2].wait()
    loop(count, line.push)

    def pick(tile, at):
        return norm_v[:, at], g_pre_v[:, tile * 512 : (tile + 1) * 512]

    for item in loads[5:]:
        item.start()
    scatter.fill_near(pick)
    relay = line.tick
    relay(0)
    for item in loads[3:]:
        item.wait()
    scale = HD ** -0.5

    pairs = heads // 2

    def exchange(kind, p=0):
        lanes = slice(p * 2 * HD, (p + 1) * 2 * HD)
        source, target, device = (
            (g_v, g_next, before),
            (stats, stats_next, before),
            (give_near, got_near, sibling),
            (give_q.at[lanes], got_q.at[lanes], after),
        )[kind]
        return pltpu.make_async_remote_copy(
            src_ref=source, dst_ref=target, send_sem=x_send.at[kind + p], recv_sem=x_recv.at[kind + p],
            device_id=device, device_id_type=MESH,
        )

    to_before = [exchange(0), exchange(1)]
    to_near = exchange(2)
    to_after = [exchange(3, p) for p in range(pairs)]

    def turn(source, target, factor):
        @functools.partial(loop, rows // CHUNK)
        def _(i):
            at = rows_of(i, CHUNK)
            value = source[at].astype(F32).T * factor
            upper = lax.broadcasted_iota(jnp.int32, (2 * HD, CHUNK), 0) < HD
            for h in range(heads):
                both = slice((h // 2) * 2 * HD, (h // 2 + 1) * 2 * HD)
                target[h, :, at] = jnp.where(upper == (h % 2 == 0), value[both], 0.0).astype(BF16)

    stats[:heads] = lse[...]

    @functools.partial(loop, rows // CHUNK)
    def _(i):
        at = rows_of(i, CHUNK)
        low = dot_nt(g_attn_v[at], wout_v[...]).astype(BF16)
        g_v[at] = low
        value = low.astype(F32).T
        for h in range(heads):
            mine = slice(h * HD, (h + 1) * HD)
            stats[heads + h : heads + h + 1, at] = jnp.sum(value[mine] * att_t[mine, at], axis=0, keepdims=True)

    @pl.when(has_before)
    def _():
        for item in to_before:
            item.start()

    relay(1)
    scatter.fill_own(pick)
    scatter.add_near()

    @pl.when(jnp.logical_not(has_after))
    def _():
        g_next[...] = jnp.zeros_like(g_next)
        stats_next[...] = jnp.zeros_like(stats_next)

    @pl.when(jnp.logical_not(has_before))
    def _():
        got_q[...] = jnp.zeros_like(got_q)

    @functools.partial(loop, 2)
    def _(i):
        at = rows_of(i, rows)
        k_t[:, at] = kv[at, :width].astype(F32).T.astype(BF16)

    @functools.partial(loop, rows // 64)
    def _(i):
        att_t[rows_of(i, 64)] = jnp.zeros((64, rows), F32)
        g_q_next[rows_of(i, 64)] = jnp.zeros((64, rows), F32)

    @functools.partial(loop, 2 * rows // 64)
    def _(i):
        acc[rows_of(i, 64)] = jnp.zeros((64, 2 * width), F32)

    relay(2)

    def head(h, q_rows, g_rows, numbers, g_q_t, mask):
        offset = lax.div(h, 2) * 2 * HD
        lanes = pl.ds(pl.multiple_of(offset, 2 * HD), 2 * HD)
        lanes_v = pl.ds(pl.multiple_of(offset + width, 2 * HD), 2 * HD)
        feature = pl.ds(pl.multiple_of(h * HD, HD), HD)
        low_lanes = lax.broadcasted_iota(jnp.int32, (CHUNK, 2 * HD), 1) < HD
        mine = low_lanes == (lax.rem(h, 2) == 0)
        for c in range(rows // CHUNK):
            cols = slice(c * CHUNK, (c + 1) * CHUNK)
            q_n = jnp.where(mine, q_rows[cols, lanes].astype(F32), 0.0).astype(BF16)
            g_n = jnp.where(mine, g_rows[cols, lanes].astype(F32), 0.0).astype(BF16)
            lse_row = numbers[pl.ds(h, 1), cols]
            delta_row = numbers[pl.ds(heads + h, 1), cols]
            for b in range(2):
                keys = slice(b * rows, (b + 1) * rows)
                s = dot(kv[keys, lanes], q_t[h, :, cols])
                p = jnp.exp(mask(b, c, s, lse_row))
                g_s = (p * (dot(kv[keys, lanes_v], g_t[h, :, cols]) - delta_row)).astype(BF16)
                acc[keys, lanes] += dot(g_s, q_n)
                acc[keys, lanes_v] += dot(p.astype(BF16), g_n)
                g_q_t[feature, cols] += dot(k_t[feature, keys], g_s)

    def causal(b, c, s, lse_row):
        key = lax.broadcasted_iota(jnp.int32, (rows, CHUNK), 0) + b * rows
        row = lax.broadcasted_iota(jnp.int32, (rows, CHUNK), 1) + c * CHUNK
        return jnp.where(key <= row + core * rows, s - lse_row, NEG)

    @pl.when(has_after)
    def _():
        for item in to_before:
            item.wait_recv()

    turn(g_next, g_t, 1.0)
    turn(q_next, q_t, scale)
    relay(3)
    for p in range(pairs):

        @functools.partial(loop, 2)
        def _(parity, p=p):
            head(2 * p + parity, q_next, g_next, stats_next, g_q_next, lambda b, c, s, row: s + (bias - row))

        pair = slice(p * 2 * HD, (p + 1) * 2 * HD)
        give_q[pair] = g_q_next[pair].astype(BF16)

        @pl.when(has_after)
        def _(p=p):
            to_after[p].start()

        relay(4 + p)

    turn(g_v, g_t, 1.0)
    turn(q_v, q_t, scale)
    relay(8)

    @functools.partial(loop, heads)
    def _(h):
        head(h, q_v, g_v, stats, att_t, causal)

        @pl.when(lax.rem(h, 2) == 1)
        def _():
            relay(9 + lax.div(h, 2))

        @pl.when(h == 4)
        def _():
            scatter.pass_on(1)

    @functools.partial(loop, rows // 64)
    def _(i):
        at = pl.ds(pl.multiple_of((1 - core) * rows + i * 64, 64), 64)
        give_near[rows_of(i, 64)] = acc[at].astype(BF16)

    to_near.start()
    scatter.keep(1)
    scatter.between()
    relay(13)
    to_near.wait_recv()

    @functools.partial(loop, rows // 64)
    def _(i):
        at = pl.ds(pl.multiple_of(core * rows + i * 64, 64), 64)
        near_at = rows_of(i, 64)
        total_at = acc[at] + got_near[near_at].astype(F32)
        g_qkv_v[near_at, width : 2 * width] = (total_at[:, :width] * scale).astype(BF16)
        g_qkv_v[near_at, 2 * width :] = total_at[:, width:].astype(BF16)

    @pl.when(has_before)
    def _():
        for item in to_after:
            item.wait_recv()

    @functools.partial(loop, rows // CHUNK)
    def _(i):
        at = rows_of(i, CHUNK)
        both = att_t[:, at] + got_q[:, at].astype(F32)
        g_qkv_v[at, :width] = (both.T * scale).astype(BF16)

    loop(count + 2 - 14, lambda i: relay(14 + i))
    stores = [
        pltpu.make_async_copy(g_qkv_v, g_qkv_hbm, store_sem.at[0]),
        pltpu.make_async_copy(total, ffn_sum_hbm, store_sem.at[1]),
    ]
    stores[0].start()
    loop(count, line.get)
    stores[1].start()

    def write(tile, value):
        up_out[:, tile * 512 : (tile + 1) * 512] = value

    scatter.finish(write)
    scatter.drain()
    line.drain_all()
    to_near.wait_send()

    @pl.when(has_before)
    def _():
        for item in to_before:
            item.wait_send()

    @pl.when(has_after)
    def _():
        for item in to_after:
            item.wait_send()

    for item in stores:
        item.wait()


def grad_attend(g_attn, wout, q, q_next, kv, att_t, lse, lengths, until, ffn_low, norm2, g_pre):
    rows, depth = g_attn.shape
    width = q.shape[1]
    heads = width // HD
    hidden = g_pre.shape[1]
    chunk = depth // lax.axis_size("cp")
    shape = jax.ShapeDtypeStruct
    return pl.pallas_call(
        grad_attend_kernel,
        out_shape=(
            shape((rows, 3 * width), BF16),
            shape((rows, depth), BF16),
            shape((chunk, hidden), F32),
        ),
        in_specs=[ANY] * 6 + [IN_VMEM, IN_SMEM, IN_SMEM, ANY, ANY, ANY],
        out_specs=(ANY, ANY, IN_VMEM),
        scratch_shapes=[
            pltpu.VMEM((rows, depth), BF16),
            pltpu.VMEM((width, depth), BF16),
            pltpu.VMEM((rows, width), BF16),
            pltpu.VMEM((rows, width), BF16),
            pltpu.VMEM((2 * rows, 2 * width), BF16),
            pltpu.VMEM((width, 2 * rows), BF16),
            pltpu.VMEM((width, rows), F32),
            pltpu.VMEM((heads, 2 * HD, rows), BF16),
            pltpu.VMEM((rows, width), BF16),
            pltpu.VMEM((rows, width), BF16),
            pltpu.VMEM((heads, 2 * HD, rows), BF16),
            pltpu.VMEM((2 * heads, rows), F32),
            pltpu.VMEM((2 * heads, rows), F32),
            pltpu.VMEM((2 * rows, 2 * width), F32),
            pltpu.VMEM((rows, 3 * width), BF16),
            pltpu.VMEM((width, rows), F32),
            pltpu.VMEM((width, rows), BF16),
            pltpu.VMEM((width, rows), BF16),
            pltpu.VMEM((rows, 2 * width), BF16),
            pltpu.VMEM((rows, 2 * width), BF16),
            pltpu.SemaphoreType.DMA((3 + heads // 2,)),
            pltpu.SemaphoreType.DMA((3 + heads // 2,)),
            pltpu.VMEM((rows, depth), BF16),
            pltpu.VMEM((rows, hidden), BF16),
            pltpu.VMEM((depth, hidden), BF16),
            *scatter_scratch(depth, hidden, SPLIT_UP),
            *line_scratch(rows, depth),
            pltpu.SemaphoreType.DMA((9,)),
            pltpu.SemaphoreType.DMA((2,)),
        ],
        compiler_params=pltpu.CompilerParams(collective_id=2, has_side_effects=True, vmem_limit_bytes=63 * 2**20),
        name="grad_attend",
    )(g_attn, wout, q, q_next, kv, att_t, lse, lengths, until, ffn_low, norm2, g_pre)


def last_kernel(
    g_qkv_hbm, wqkv_hbm, x_hbm, g_hidden_hbm, norm_hbm, g_attn_hbm, att_hbm, attn_sum_hbm, ffn_sum_hbm,
    up_hbm, down_hbm, lengths_ref, until_ref, gains, b_outs, sums_in,
    g_x, out, up_out, down_out, qkv_out, w_out_out, gains_out, shifts_out, bqv_out, bouts_out, bup_out,
    g_qkv_v, w_v, x_v, norm_v, g_attn_v, att_v, attn_sum, ffn_sum, acc, small, small_got, late, late_got,
    terms, near, far, rs_send, rs_recv,
    part, slot_a, slot_b, total, ar_send, ar_recv, small_send, small_recv, load_sem,
):
    cp, tp, core, chip = place()
    rows, depth = x_v.shape
    width = att_v.shape[1]
    count = rows // SUB
    loads = [
        pltpu.make_async_copy(source, target, load_sem.at[i])
        for i, (source, target) in enumerate(
            (
                (g_qkv_hbm, g_qkv_v),
                (wqkv_hbm, w_v),
                (norm_hbm, norm_v),
                (g_attn_hbm, g_attn_v),
                (att_hbm, att_v),
                (x_hbm, x_v),
                (g_hidden_hbm, g_x),
                (attn_sum_hbm, attn_sum),
                (ffn_sum_hbm, ffn_sum),
                (up_hbm, up_out),
                (down_hbm, down_out),
            )
        )
    ]
    for item in loads[:2]:
        item.start()
    line = LineSum(part, slot_a, slot_b, total, ar_send, ar_recv)
    scatter = Scatter(terms, near, far, rs_send, rs_recv, SPLIT_LAST)
    bands = lax.axis_size("cp")
    greet(cp, tp, [(lax.rem(cp + k, bands), tp) for k in range(1, bands)])
    _, live = band_info(lengths_ref, until_ref, cp * rows)
    acc[...] = jnp.zeros_like(acc)
    loads[0].wait()
    loads[1].wait()

    for c in range(rows // CHUNK):
        chunk = slice(c * CHUNK, (c + 1) * CHUNK)

        @functools.partial(loop, depth // 512)
        def _(t, chunk=chunk):
            lanes = rows_of(t, 512)
            value = dot_nt(g_qkv_v[chunk, :width], w_v[0, lanes])
            value = value + dot_nt(g_qkv_v[chunk, width : 2 * width], w_v[1, lanes])
            value = value + dot_nt(g_qkv_v[chunk, 2 * width :], w_v[2, lanes])
            part[chunk, lanes] = value.astype(BF16)

        loop(CHUNK // SUB, lambda s, c=c: line.push(s + c * (CHUNK // SUB)))
        if c == 0:
            for item in loads[2:]:
                item.start()

    def small_copy(which, sender, receiver):
        source, target = ((small, small_got), (late, late_got))[which]
        return pltpu.make_async_remote_copy(
            src_ref=source, dst_ref=target.at[sender], send_sem=small_send.at[which, receiver],
            recv_sem=small_recv.at[which, sender], device_id=(receiver, tp), device_id_type=MESH,
        )

    def give_small(which):
        loop(bands - 1, lambda k: small_copy(which, cp, lax.rem(cp + 1 + k, bands)).start())

    def take_small(which):
        source, target = ((small, small_got), (late, late_got))[which]
        target[cp] = source[...]

        @functools.partial(loop, bands - 1)
        def _(k):
            sender = lax.rem(cp + 1 + k, bands)
            small_copy(which, sender, sender).wait_recv()

        value = target[0]
        for k in range(1, bands):
            value = value + target[k]
        return value

    small[0:5] = sums_in[0:5]
    small[6:8] = jnp.zeros((2, depth), F32)
    small[5:6, 2 * width :] = jnp.zeros((1, depth - 2 * width), F32)
    for j in range(2):
        bias = jnp.sum(g_qkv_v[:, 2 * j * width : (2 * j + 1) * width].astype(F32), axis=0, keepdims=True)
        small[5:6, j * width : (j + 1) * width] = bias
    give_small(0)
    for item in loads[2:]:
        item.wait()

    def back(s):
        line.get(s)
        at = rows_of(s, SUB)
        e = total[at].astype(F32)
        v = x_v[at].astype(F32)
        centred = v - jnp.mean(v, axis=-1, keepdims=True)
        scale = lax.rsqrt(jnp.mean(centred * centred, axis=-1, keepdims=True) + EPS)
        hat = centred * scale
        t = e * gains[0:1]
        along = t - jnp.mean(t, axis=-1, keepdims=True) - hat * jnp.mean(t * hat, axis=-1, keepdims=True)
        g_x[at] = g_x[at] + along * scale
        row = lax.broadcasted_iota(jnp.int32, (SUB, 1), 0) + s * SUB
        branches = attn_sum[at].astype(F32) + b_outs[0:1] + (ffn_sum[at].astype(F32) + b_outs[1:2])
        out[at] = v + jnp.where(row < live, branches, 0.0)
        acc[0] += fold(e * hat)
        acc[1] += fold(e)

    behind = 4

    def ahead(s):
        line.tick(s)

        @pl.when(s >= behind)
        def _():
            back(s - behind)

    def pick(tile, at):
        if tile < 3:
            return norm_v[:, at], g_qkv_v[:, tile * width : (tile + 1) * width]
        return g_attn_v[:, at], att_v[...]

    scatter.fill_near(pick)
    ahead(0)
    ahead(1)
    scatter.fill_own(pick)
    ahead(2)
    scatter.add_near()
    loop(9 - 3, lambda i: ahead(3 + i))
    scatter.pass_on(1)
    loop(13 - 9, lambda i: ahead(9 + i))
    scatter.keep(1)
    scatter.between()
    loop(count + 2 - 13, lambda i: ahead(13 + i))
    loop(behind - 2, lambda i: back(count + 2 - behind + i))

    for k in range(2):
        late[k : k + 1] = jnp.sum(acc[k], axis=0, keepdims=True)
    give_small(1)
    early = take_small(0)
    bouts_out[...] = early[2:4]
    bup_out[...] = early[4:5]
    for j in range(2):
        bqv_out[j : j + 1] = early[5:6, j * width : (j + 1) * width]

    def write(tile, value):
        if tile < 3:
            qkv_out[tile] = value
        else:
            w_out_out[...] = value.T

    scatter.finish(write)
    final = take_small(1)
    gains_out[0:1] = final[0:1]
    gains_out[1:2] = early[0:1]
    shifts_out[0:1] = final[1:2]
    shifts_out[1:2] = early[1:2]
    scatter.drain()
    line.drain_all()

    @functools.partial(loop, bands - 1)
    def _(k):
        other = lax.rem(cp + 1 + k, bands)
        small_copy(0, cp, other).wait_send()
        small_copy(1, cp, other).wait_send()


def last(g_qkv, wqkv, x, g_hidden, norm1, g_attn, att, attn_sum, ffn_sum, g_up, g_down, lengths, until, gains, b_outs, sums):
    rows, depth = x.shape
    width = att.shape[1]
    bands = lax.axis_size("cp")
    chunk = depth // bands
    pinned = bands <= 8
    result = pltpu.VMEM if pinned else jax.ShapeDtypeStruct
    return pl.pallas_call(
        last_kernel,
        out_shape=(
            result((rows, depth), F32),
            result((rows, depth), F32),
            result(g_up.shape, F32),
            result(g_down.shape, F32),
            result((3, chunk, width), F32),
            result((width, chunk), F32),
            result((2, depth), F32),
            result((2, depth), F32),
            result((2, width), F32),
            result((2, depth), F32),
            result((1, depth), F32),
        ),
        in_specs=[ANY] * 11 + [IN_SMEM] * 2 + [IN_VMEM] * 3,
        out_specs=(IN_VMEM,) * 11,
        scratch_shapes=[
            pltpu.VMEM((rows, 3 * width), BF16),
            pltpu.VMEM((3, depth, width), BF16),
            pltpu.VMEM((rows, depth), BF16),
            pltpu.VMEM((rows, depth), BF16),
            pltpu.VMEM((rows, depth), BF16),
            pltpu.VMEM((rows, width), BF16),
            pltpu.VMEM((rows, depth), BF16),
            pltpu.VMEM((rows, depth), BF16),
            pltpu.VMEM((2, 8, depth), F32),
            pltpu.VMEM((8, depth), F32),
            pltpu.VMEM((bands, 8, depth), F32),
            pltpu.VMEM((2, depth), F32),
            pltpu.VMEM((bands, 2, depth), F32),
            pltpu.VMEM((depth, depth), BF16),
            *scatter_scratch(depth, depth, SPLIT_LAST),
            *line_scratch(rows, depth),
            pltpu.SemaphoreType.DMA((2, bands)),
            pltpu.SemaphoreType.DMA((2, bands)),
            pltpu.SemaphoreType.DMA((11,)),
        ],
        compiler_params=pltpu.CompilerParams(collective_id=3, has_side_effects=True, vmem_limit_bytes=(45 if pinned else 62) * 2**20),
        name="last",
    )(g_qkv, wqkv, x, g_hidden, norm1, g_attn, att, attn_sum, ffn_sum, g_up, g_down, lengths, until, gains, b_outs, sums)


def shards(
    layer_input,
    seq_lengths,
    active_until,
    ln_gains,
    ln_shifts,
    query_key_value_weight,
    b_qv,
    w_out,
    b_outs,
    w_up,
    b_up,
    w_down,
    d_out,
):
    wqkv = jnp.transpose(query_key_value_weight, (1, 0, 2))
    (attn_sum, norm1, q, q_next, kv, att, att_t, norm2, g_pre, ffn_low, g_hidden, g_attn, lse, sums, g_down) = front(
        layer_input, d_out, seq_lengths, active_until, ln_gains, ln_shifts, wqkv, b_qv, w_out, b_outs, b_up[None],
        w_up, w_down,
    )
    g_qkv_rows, ffn_sum, g_up = grad_attend(
        g_attn, w_out, q, q_next, kv, att_t, lse, seq_lengths, active_until, ffn_low, norm2, g_pre
    )
    g_x, out, g_up, g_down, g_qkv, g_out, g_ln_gains, g_ln_shifts, g_bqv, g_bouts, g_bup = last(
        g_qkv_rows, wqkv, layer_input, g_hidden, norm1, g_attn, att, attn_sum, ffn_sum, g_up, g_down,
        seq_lengths, active_until, ln_gains, b_outs, sums,
    )
    g_qkv = jnp.transpose(g_qkv, (1, 0, 2))
    return (out, g_x, g_ln_gains, g_ln_shifts, g_qkv, g_bqv, g_out, g_bouts, g_up, g_bup[0], g_down)


def solution(mesh):
    return jax.shard_map(
        shards,
        mesh=mesh,
        in_specs=(
            P("cp", None),
            P(),
            P(),
            P(),
            P(),
            P(None, None, "tp"),
            P(None, "tp"),
            P("tp", None),
            P(),
            P(None, "tp"),
            P("tp"),
            P("tp", None),
            P("cp", None),
        ),
        out_specs=(
            P("cp", None),
            P("cp", None),
            P(),
            P(),
            P("cp", None, "tp"),
            P(None, "tp"),
            P("tp", "cp"),
            P(),
            P("cp", "tp"),
            P("tp"),
            P("tp", "cp"),
        ),
        check_vma=False,
    )
```

```python
import functools
import math

import jax
import jax.numpy as jnp
from jax import lax
from jax.experimental import pallas as pl
from jax.experimental.pallas import tpu as pltpu
from jax.sharding import PartitionSpec as P

HD = 64
LONG = 2048
EPS = 1e-05
NEG = -1e30
MESH = pl.DeviceIdType.MESH
F32 = jnp.float32
BF16 = jnp.bfloat16
ANY = pl.BlockSpec(memory_space=pl.ANY)
IN_VMEM = pl.BlockSpec(memory_space=pltpu.VMEM)
IN_SMEM = pl.BlockSpec(memory_space=pltpu.SMEM)
SUB = 32
PIECE = 16
CHUNK = 256


def dot(a, b):
    return jnp.dot(a, b, preferred_element_type=F32)


def dot_nt(a, b):
    return lax.dot_general(a, b, (((1,), (1,)), ((), ())), preferred_element_type=F32)


def dot_tn(a, b):
    return lax.dot_general(a, b, (((0,), (0,)), ((), ())), preferred_element_type=F32)


def rows_of(index, size):
    return pl.ds(pl.multiple_of(index * size, size), size)


def place():
    cp = lax.axis_index("cp")
    tp = lax.axis_index("tp")
    return cp, tp, lax.rem(cp, 2), lax.div(cp, 2)


def greet(cp, tp, others):
    barrier = pltpu.get_barrier_semaphore()
    edge = (tp == 0) | (tp == 3)
    for other in [*others, (cp, line_near(tp))]:
        pl.semaphore_signal(barrier, inc=1, device_id=other, device_id_type=MESH)

    @pl.when(jnp.logical_not(edge))
    def _():
        pl.semaphore_signal(barrier, inc=1, device_id=(cp, 3 - tp), device_id_type=MESH)

    pl.semaphore_wait(barrier, len(others) + jnp.where(edge, 1, 2))


def line_near(tp):
    return jnp.where(tp == 0, 1, jnp.where(tp == 1, 0, jnp.where(tp == 2, 3, 2)))


class LineSum:
    def __init__(self, part, slot_a, slot_b, total, send, recv):
        self.cp, self.tp, _, _ = place()
        self.edge = (self.tp == 0) | (self.tp == 3)
        self.refs = (part, slot_a, slot_b, total)
        self.send, self.recv = send, recv
        self.count = part.shape[0] // SUB

    def copy(self, kind, piece):
        part, slot_a, slot_b, total = self.refs
        src, dst = ((part, slot_a), (part, slot_b), (total, total))[kind]
        other = (self.cp, 3 - self.tp if kind == 1 else line_near(self.tp))
        rows = rows_of(piece, PIECE)
        return pltpu.make_async_remote_copy(
            src_ref=src.at[rows],
            dst_ref=dst.at[rows],
            send_sem=self.send.at[kind, piece],
            recv_sem=self.recv.at[kind, piece],
            device_id=other,
            device_id_type=MESH,
        )

    def pieces(self, s):
        return [s * (SUB // PIECE) + j for j in range(SUB // PIECE)]

    def push(self, s):
        @pl.when(self.edge)
        def _():
            for piece in self.pieces(s):
                self.copy(0, piece).start()

    def relay_in(self, s):
        part, slot_a, _, _ = self.refs

        @pl.when(jnp.logical_not(self.edge))
        def _():
            for piece in self.pieces(s):
                rows = rows_of(piece, PIECE)
                self.copy(0, piece).wait_recv()
                part[rows] = (part[rows].astype(F32) + slot_a[rows].astype(F32)).astype(BF16)
                self.copy(1, piece).start()

    def relay_out(self, s):
        part, _, slot_b, total = self.refs

        @pl.when(jnp.logical_not(self.edge))
        def _():
            for piece in self.pieces(s):
                rows = rows_of(piece, PIECE)
                self.copy(1, piece).wait_recv()
                total[rows] = (part[rows].astype(F32) + slot_b[rows].astype(F32)).astype(BF16)
                self.copy(2, piece).start()

    def get(self, s):
        @pl.when(self.edge)
        def _():
            for piece in self.pieces(s):
                self.copy(2, piece).wait_recv()

    def tick(self, s):
        @pl.when(s < self.count)
        def _():
            self.relay_in(s)

        @pl.when(s >= 2)
        def _():
            self.relay_out(s - 2)

    def drain_all(self):
        @pl.when(self.edge)
        def _():
            loop(self.refs[0].shape[0] // PIECE, lambda piece: self.copy(0, piece).wait_send())

        @pl.when(jnp.logical_not(self.edge))
        def _():
            @functools.partial(loop, self.refs[0].shape[0] // PIECE)
            def _(piece):
                self.copy(1, piece).wait_send()
                self.copy(2, piece).wait_send()


def line_scratch(rows, width):
    return [pltpu.VMEM((rows, width), BF16)] * 4 + [pltpu.SemaphoreType.DMA((3, rows // PIECE))] * 2


def band_info(lengths_ref, until_ref, first):
    start = jnp.int32(0)
    begin = jnp.int32(0)
    until = jnp.int32(0)
    for i in range(lengths_ref.shape[0]):
        length = lengths_ref[i]
        inside = (first >= start) & (first < start + length)
        begin = jnp.where(inside, start, begin)
        until = jnp.where(inside, until_ref[i], until)
        start = start + length
    return begin, until + begin - first


def loop(count, body):
    def step(i, carry):
        body(i)
        return carry

    lax.fori_loop(0, count, step, 0)


class Scatter:
    def __init__(self, terms, near, far, send, recv, split):
        self.cp, self.tp, self.core, self.chip = place()
        self.count = lax.axis_size("cp")
        self.half = self.count // 2
        self.depth = self.half.bit_length() - 1
        self.terms, self.near, self.far = terms, near, far
        self.send, self.recv = send, recv
        self.chunk = terms.shape[0] // self.count
        self.width = terms.shape[1]
        self.lanes = {p: c for p, c in ((0, slice(0, split)), (1, slice(split, self.width))) if c.stop > c.start}
        self.order = list(range(self.half))[::-1]
        self.whole_blocks = self.chunk >= 128

    def partners(self):
        others = [(self.cp + 1 - 2 * self.core, self.tp)]
        for bit in range(self.depth):
            others.append((self.cp + 2 * self.flip(1 << bit), self.tp))
        return others

    def flip(self, e):
        change = 0
        for bit in range(self.depth):
            if e >> bit & 1:
                change = change + (1 - 2 * lax.rem(lax.div(self.chip, 1 << bit), 2)) * (1 << bit)
        return change

    def row(self, e, core):
        if isinstance(e, int):
            other = self.chip + self.flip(e)
        else:
            other = 0
            for bit in range(self.depth):
                mine = lax.rem(lax.div(self.chip, 1 << bit), 2)
                change = lax.rem(lax.div(e, 1 << bit), 2)
                other = other + (mine + change - 2 * mine * change) * (1 << bit)
        return (2 * other + core) * self.chunk

    def fill_block(self, first, size, pick):
        rows = pl.ds(pl.multiple_of(first, size), size)

        for tile in range(self.width // 512):
            left, right = pick(tile, rows)
            self.terms[rows, tile * 512 : (tile + 1) * 512] = dot_tn(left, right).astype(BF16)

    def fill_near(self, pick):
        if not self.whole_blocks:
            loop(self.terms.shape[0] // 128, lambda k: self.fill_block(k * 128, 128, pick))

        @functools.partial(loop, self.half)
        def _(k):
            e = self.half - 1 - k
            if self.whole_blocks:
                self.fill_block(self.row(e, 1 - self.core), self.chunk, pick)
            self.near_copy(e).start()

    def fill_own(self, pick):
        if self.whole_blocks:
            loop(self.half, lambda k: self.fill_block(self.row(self.half - 1 - k, self.core), self.chunk, pick))

    def near_copy(self, e):
        return pltpu.make_async_remote_copy(
            src_ref=self.terms.at[pl.ds(pl.multiple_of(self.row(e, 1 - self.core), self.chunk), self.chunk)],
            dst_ref=self.near.at[rows_of(e, self.chunk)],
            send_sem=self.send.at[e],
            recv_sem=self.recv.at[e],
            device_id=(self.cp + 1 - 2 * self.core, self.tp),
            device_id_type=MESH,
        )

    def add(self, e, source, first, lanes):
        base = self.row(e, self.core)

        @functools.partial(loop, self.chunk // 32)
        def _(i):
            mine = pl.ds(pl.multiple_of(base + i * 32, 32), 32)
            other = pl.ds(pl.multiple_of(first + i * 32, 32), 32)
            self.terms[mine, lanes] = (
                self.terms[mine, lanes].astype(F32) + source[other, lanes].astype(F32)
            ).astype(BF16)

    def add_near(self):
        for e in self.order:
            self.near_copy(e).wait_recv()
            self.add(e, self.near, e * self.chunk, slice(0, self.width))
            for part in self.lanes:
                if self.sent(1, part, e):
                    self.far_copy(1, part, e).start()

    def bit(self, level, part):
        return level - 1 if part == 0 else self.depth - level

    def sent(self, level, part, e):
        bit = self.bit(level, part)
        return e >> bit & 1 and (e & ((1 << bit) - 1) if part == 0 else e >> (bit + 1)) == 0

    def slot(self, level, part, e):
        bit = self.bit(level, part)
        return e >> (bit + 1) if part == 0 else e & ((1 << bit) - 1)

    def place(self, level):
        return sum(self.terms.shape[0] >> (earlier + 1) for earlier in range(1, level))

    def far_copy(self, level, part, e):
        bit = self.bit(level, part)
        sem = self.half + sum(len(self.lanes) * (self.half >> earlier) for earlier in range(1, level))
        sem += list(self.lanes).index(part) * (self.half >> level) + self.slot(level, part, e)
        first = self.place(level) + self.slot(level, part, e) * self.chunk
        return pltpu.make_async_remote_copy(
            src_ref=self.terms.at[
                pl.ds(pl.multiple_of(self.row(e, self.core), self.chunk), self.chunk), self.lanes[part]
            ],
            dst_ref=self.far.at[first : first + self.chunk, self.lanes[part]],
            send_sem=self.send.at[sem],
            recv_sem=self.recv.at[sem],
            device_id=(self.cp + 2 * self.flip(1 << bit), self.tp),
            device_id_type=MESH,
        )

    def coming(self, level, passed_on):
        for e in self.order:
            for part in self.lanes:
                if self.sent(level, part, e):
                    kept = e ^ (1 << self.bit(level, part))
                    if (level < self.depth and bool(self.sent(level + 1, part, kept))) == passed_on:
                        yield part, e, kept

    def arrive(self, level, part, e, kept):
        self.far_copy(level, part, e).wait_recv()
        self.add(kept, self.far, self.place(level) + self.slot(level, part, e) * self.chunk, self.lanes[part])

    def pass_on(self, level):
        for part, e, kept in self.coming(level, True):
            self.arrive(level, part, e, kept)
            self.far_copy(level + 1, part, kept).start()

    def keep(self, level):
        for part, e, kept in self.coming(level, False):
            self.arrive(level, part, e, kept)

    def between(self):
        for level in range(2, self.depth):
            self.pass_on(level)
            self.keep(level)

    def finish(self, write):
        level = self.depth
        mine = pl.ds(pl.multiple_of(self.row(0, self.core), self.chunk), self.chunk)
        for part, e, _ in self.coming(level, False):
            self.far_copy(level, part, e).wait_recv()
            lanes = self.lanes[part]
            for tile in range(lanes.start // 512, lanes.stop // 512):
                cut = slice(tile * 512, (tile + 1) * 512)
                other = pl.ds(self.place(level), self.chunk)
                write(tile, self.terms[mine, cut].astype(F32) + self.far[other, cut].astype(F32))

    def drain(self):
        for e in self.order:
            self.near_copy(e).wait_send()
            for part in self.lanes:
                for level in range(1, self.depth + 1):
                    if self.sent(level, part, e):
                        self.far_copy(level, part, e).wait_send()


def scatter_scratch(depth, width, split):
    count = lax.axis_size("cp")
    parts = (split > 0) + (split < width)
    sems = count // 2 + parts * (count // 2 - 1)
    return [
        pltpu.VMEM((depth // 2, width), BF16),
        pltpu.VMEM((depth // 2 - depth // count, width), BF16),
        pltpu.SemaphoreType.DMA((sems,)),
        pltpu.SemaphoreType.DMA((sems,)),
    ]


def fold(v):
    return jnp.sum(v.reshape(v.shape[0] // 8, 8, v.shape[1]), axis=0)


def gelu_parts(u):
    root = math.sqrt(2.0 / math.pi)
    square = u * u
    th = jnp.tanh(root * (u + 0.044715 * u * square))
    half = 0.5 * (1.0 + th)
    return u * half, half + 0.5 * u * (1.0 - th * th) * (root * (1.0 + 3 * 0.044715 * square))


LAG = 5
SPLIT_DOWN = 1024


def front_kernel(
    x_hbm, d_hbm, lengths_ref, until_ref, gains, shifts, wqkv_hbm, bqv, wout_hbm, b_outs, b_up, up_hbm, down_hbm,
    attn_sum_hbm, norm1_hbm, q_hbm, q_next_hbm, kv_hbm, att_hbm, att_t_hbm, norm2_hbm, g_pre_hbm, ffn_hbm, g_hidden_hbm,
    g_attn_hbm, lse_out, sums_out, down_out,
    x_v, d_v, norm_v, up_v, down_v, q_v, q_next, kv, q_t, q_t_next, v_t, att_t, att_v, cross, cross_in, lse_cross, lse_in, xhat, rstd, act_v, g_pre_v, acc,
    part, slot_a, total, slot_b1, slot_b2, ar_send, ar_recv, near, far, rs_send, rs_recv,
    x_send, x_recv, load_sem, store_sem,
):
    cp, tp, core, chip = place()
    bands = lax.axis_size("cp")
    chips = bands // 2
    rows, depth = x_v.shape
    width = q_v.shape[1]
    heads = width // HD
    hidden = act_v.shape[1]
    count = rows // SUB
    per_chunk = CHUNK // SUB
    sibling = (cp + 1 - 2 * core, tp)
    after = (lax.rem(cp + 2, bands), tp)
    before = (lax.rem(cp + bands - 2, bands), tp)
    wout_v, scores, g_hidden, g_attn, part2, ffn_v = act_v, xhat, xhat, x_v, v_t, part
    loads = [
        pltpu.make_async_copy(x_hbm, x_v, load_sem.at[0]),
        *[
            pltpu.make_async_copy(
                wqkv_hbm.at[j], up_v.at[:, j * width : (j + 1) * width], load_sem.at[i]
            )
            for i, j in ((1, 0), (2, 1), (3, 2))
        ],
        pltpu.make_async_copy(wout_hbm, wout_v, load_sem.at[4]),
        pltpu.make_async_copy(down_hbm, down_v, load_sem.at[5]),
        pltpu.make_async_copy(d_hbm, d_v, load_sem.at[6]),
        pltpu.make_async_copy(up_hbm, up_v, load_sem.at[7]),
    ]
    for item in loads[:4]:
        item.start()
    stores = {
        name: pltpu.make_async_copy(source, target, store_sem.at[i])
        for i, (name, source, target) in enumerate(
            (
                ("norm1", norm_v, norm1_hbm),
                ("q", q_v, q_hbm),
                ("kv", kv, kv_hbm),
                ("q_next", q_next, q_next_hbm),
                ("att", att_v, att_hbm),
                ("att_t", att_t, att_t_hbm),
                ("sum0", total.at[:CHUNK], attn_sum_hbm.at[:CHUNK]),
                ("sum1", total.at[CHUNK:], attn_sum_hbm.at[CHUNK:]),
                ("norm2", norm_v, norm2_hbm),
                ("g_pre", g_pre_v, g_pre_hbm),
                ("ffn", ffn_v, ffn_hbm),
                ("g_hidden", g_hidden, g_hidden_hbm),
                ("g_attn", g_attn, g_attn_hbm),
            )
        )
    }
    line1 = LineSum(part, slot_a, slot_b1, total, ar_send.at[0], ar_recv.at[0])
    line2 = LineSum(part2, slot_a, slot_b2, total, ar_send.at[1], ar_recv.at[1])
    scatter = Scatter(up_v, near, far, rs_send, rs_recv, SPLIT_DOWN)
    greet(cp, tp, [*scatter.partners(), after, before])
    _, live = band_info(lengths_ref, until_ref, cp * rows)
    begin, _ = band_info(lengths_ref, until_ref, (chip + 1) * 2 * rows)
    bias = jnp.where(begin < (chip + 1) * 2 * rows, 0.0, NEG)
    loads[0].wait()

    @functools.partial(loop, rows // 64)
    def _(i):
        at = rows_of(i, 64)
        v = x_v[at].astype(F32)
        mean = jnp.mean(v, axis=-1, keepdims=True)
        centred = v - mean
        var = jnp.mean(centred * centred, axis=-1, keepdims=True)
        norm_v[at] = (centred * lax.rsqrt(var + EPS) * gains[0:1] + shifts[0:1]).astype(BF16)

    stores["norm1"].start()
    chunks = rows // CHUNK

    def exchange(kind, c=0):
        cut = slice(c * CHUNK, (c + 1) * CHUNK)
        source, target, device = (
            (q_v.at[cut], q_next.at[cut], before),
            (cross.at[c], cross_in.at[c], after),
            (lse_cross.at[c], lse_in.at[c], after),
            (kv.at[rows_of(core, rows)], kv.at[rows_of(core, rows)], sibling),
        )[kind]
        sem = kind * chunks + c
        return pltpu.make_async_remote_copy(
            src_ref=source, dst_ref=target, send_sem=x_send.at[sem], recv_sem=x_recv.at[sem],
            device_id=device, device_id_type=MESH,
        )

    queries = [exchange(0, c) for c in range(chunks)]
    gathered = [[exchange(1, c), exchange(2, c)] for c in range(chunks)]
    to_near = exchange(3)
    has_before, has_after = chip > 0, chip < chips - 1
    loads[1].wait()

    for c in range(chunks):
        at = slice(c * CHUNK, (c + 1) * CHUNK)
        q_v[at] = (dot(norm_v[at], up_v[:, :width]) + bqv[0:1]).astype(BF16)

        @pl.when(has_before)
        def _(c=c):
            queries[c].start()

    @pl.when(jnp.logical_not(has_after))
    def _():
        q_next[...] = jnp.zeros_like(q_next)

    @pl.when(jnp.logical_not(has_before))
    def _():
        cross_in[...] = jnp.zeros_like(cross_in)
        lse_in[...] = jnp.full_like(lse_in, NEG)

    for load, column in ((2, 0), (3, 1)):
        loads[load].wait()

        @functools.partial(loop, rows // CHUNK)
        def _(i):
            value = dot(norm_v[rows_of(i, CHUNK)], up_v[:, (column + 1) * width : (column + 2) * width])
            if column:
                value = value + bqv[1:2]
            target = pl.ds(pl.multiple_of(core * rows + i * CHUNK, CHUNK), CHUNK)
            kv[target, column * width : (column + 1) * width] = value.astype(BF16)

    to_near.start()
    for item in loads[4:]:
        item.start()
    stores["q"].start()

    def turned(value, h):
        upper = lax.broadcasted_iota(jnp.int32, value.shape, 0) < HD
        return jnp.where(upper == (h % 2 == 0), value, 0.0).astype(BF16)

    @functools.partial(loop, rows // CHUNK)
    def _(i):
        at = rows_of(i, CHUNK)
        value = q_v[at].astype(F32).T * (HD ** -0.5)
        for h in range(heads):
            q_t[h, :, at] = turned(value[(h // 2) * 2 * HD : (h // 2 + 1) * 2 * HD], h)

    def turn_values(slot):
        v_t[:, rows_of(slot, rows)] = kv[rows_of(slot, rows), width:].astype(F32).T.astype(BF16)

    turn_values(core)
    to_near.wait_recv()
    stores["kv"].start()
    turn_values(1 - core)

    def attend(query, lanes, feature, mask):
        top = jnp.full((1, CHUNK), NEG, F32)
        for b in range(2):
            s = mask(b, dot(kv[b * rows : (b + 1) * rows, lanes], query))
            scores[:, b * CHUNK : (b + 1) * CHUNK] = s
            top = jnp.maximum(top, jnp.max(s, axis=0, keepdims=True))
        mass = jnp.zeros((1, CHUNK), F32)
        mixed = jnp.zeros((HD, CHUNK), F32)
        for b in range(2):
            p = jnp.exp(scores[:, b * CHUNK : (b + 1) * CHUNK] - top)
            mass = mass + jnp.sum(p, axis=0, keepdims=True)
            mixed = mixed + dot(v_t[feature, b * rows : (b + 1) * rows], p.astype(BF16))
        return mixed / mass, top + jnp.log(mass)

    def cross_chunk(c):
        columns = slice(c * CHUNK, (c + 1) * CHUNK)
        queries[c].wait_recv()
        value = q_next[columns].astype(F32).T * (HD ** -0.5)
        for h in range(heads):
            q_t_next[h] = turned(value[(h // 2) * 2 * HD : (h // 2 + 1) * 2 * HD], h)

        @functools.partial(loop, heads)
        def _(h):
            lanes = pl.ds(pl.multiple_of(lax.div(h, 2) * 2 * HD, 2 * HD), 2 * HD)
            feature = pl.ds(pl.multiple_of(h * HD, HD), HD)
            mixed, lse_row = attend(q_t_next[h], lanes, feature, lambda b, s: s + bias)
            cross[c, feature] = mixed.astype(BF16)
            lse_cross[c, pl.ds(h, 1)] = lse_row
            if c > 0:
                @pl.when(lax.rem(h, 4) == 3)
                def _():
                    line1.tick(lax.div(h, 4))

        for item in gathered[c]:
            item.start()

    loads[4].wait()

    for c in range(rows // CHUNK):
        columns = slice(c * CHUNK, (c + 1) * CHUNK)

        @pl.when(has_after)
        def _(c=c):
            cross_chunk(c)

        if c > 0:
            @pl.when(jnp.logical_not(has_after))
            def _():
                loop(2, line1.tick)

        def causal(b, s, c=c):
            key = lax.broadcasted_iota(jnp.int32, (rows, CHUNK), 0) + b * rows
            row = lax.broadcasted_iota(jnp.int32, (rows, CHUNK), 1) + c * CHUNK
            return jnp.where(key <= row + core * rows, s, NEG)

        def head(h, c=c, columns=columns, causal=causal):
            lanes = pl.ds(pl.multiple_of(lax.div(h, 2) * 2 * HD, 2 * HD), 2 * HD)
            feature = pl.ds(pl.multiple_of(h * HD, HD), HD)
            mixed, lse_row = attend(q_t[h, :, columns], lanes, feature, causal)
            att_t[feature, columns] = mixed
            lse_out[pl.ds(h, 1), columns] = lse_row
            if c > 0:
                @pl.when(lax.rem(h, 4) == 3)
                def _():
                    line1.tick(2 + lax.div(h, 4))

        loop(heads, head)

        @pl.when(has_before)
        def _(c=c):
            for item in gathered[c]:
                item.wait_recv()

        mine, other = lse_out[:, columns], lse_in[c]
        top = jnp.maximum(mine, other)
        both = top + jnp.log(jnp.exp(mine - top) + jnp.exp(other - top))
        share, share_in = jnp.exp(mine - both), jnp.exp(other - both)
        lse_out[:, columns] = both
        for h in range(heads):
            feature = slice(h * HD, (h + 1) * HD)
            att_t[feature, columns] = (
                att_t[feature, columns] * share[h : h + 1]
                + cross_in[c, feature].astype(F32) * share_in[h : h + 1]
            )
        att_v[columns] = att_t[:, columns].T.astype(BF16)

        @functools.partial(loop, depth // 512)
        def _(t, columns=columns):
            lanes = rows_of(t, 512)
            part[columns, lanes] = dot(att_v[columns], wout_v[:, lanes]).astype(BF16)

        loop(per_chunk, lambda s, c=c: line1.push(s + c * per_chunk))

    stores["q_next"].start()
    stores["att"].start()
    stores["att_t"].start()
    acc[...] = jnp.zeros_like(acc)
    stores["norm1"].wait()
    loads[6].wait()

    def second_norm(s):
        line1.get(s)
        at = rows_of(s, SUB)
        row = lax.broadcasted_iota(jnp.int32, (SUB, 1), 0) + s * SUB
        on = row < live
        v = x_v[at].astype(F32) + jnp.where(on, total[at].astype(F32) + b_outs[0:1], 0.0)
        mean = jnp.mean(v, axis=-1, keepdims=True)
        centred = v - mean
        scale = lax.rsqrt(jnp.mean(centred * centred, axis=-1, keepdims=True) + EPS)
        hat = centred * scale
        xhat[at] = hat
        rstd[at] = jnp.broadcast_to(scale, (SUB, 128))
        norm_v[at] = (hat * gains[1:2] + shifts[1:2]).astype(BF16)
        acc[3] += fold(jnp.where(on, d_v[at].astype(F32), 0.0))

    def feed_forward(c, ticks):
        chunk = slice(c * CHUNK, (c + 1) * CHUNK)
        on = lax.broadcasted_iota(jnp.int32, (CHUNK, 1), 0) + c * CHUNK < live

        @functools.partial(loop, hidden // 512)
        def _(t):
            lanes = rows_of(t, 512)
            pre = dot(norm_v[chunk], up_v[:, lanes]) + b_up[0:1, lanes]
            g_act = dot_nt(d_v[chunk], down_v[lanes])
            act, slope = gelu_parts(pre)
            act_v[chunk, lanes] = jnp.where(on, act, 0.0).astype(BF16)
            g_pre = jnp.where(on, g_act * slope, 0.0).astype(BF16)
            g_pre_v[chunk, lanes] = g_pre
            acc[4, :, lanes] += fold(g_pre.astype(F32))

            @pl.when(lax.rem(t, 2) == 1)
            def _():
                ticks(lax.div(t, 2))

        @functools.partial(loop, depth // 512)
        def _(t):
            lanes = rows_of(t, 512)
            part2[chunk, lanes] = dot_nt(g_pre_v[chunk], up_v[lanes]).astype(BF16)

            @pl.when(lax.rem(t, 2) == 1)
            def _():
                ticks(2 + lax.div(t, 2))

    @functools.partial(loop, per_chunk)
    def _(i):
        line1.tick(4 + i)
        second_norm(i)

    stores["sum0"].start()
    loads[5].wait()
    loads[7].wait()
    feed_forward(0, lambda i: line1.tick(4 + per_chunk + i))
    stores["sum0"].wait()
    loop(per_chunk, line2.push)
    loop(4, lambda i: second_norm(per_chunk + i))
    for i in range(2):
        line1.tick(count + i)
        line2.relay_in(i)
        second_norm(per_chunk + 4 + 2 * i)
        second_norm(per_chunk + 5 + 2 * i)
    stores["sum1"].start()
    stores["norm2"].start()
    line1.drain_all()
    feed_forward(1, lambda i: line2.tick(2 + i))
    stores["g_pre"].start()
    stores["sum1"].wait()
    loop(per_chunk, lambda s: line2.push(per_chunk + s))

    def back(s):
        line2.get(s)
        at = rows_of(s, SUB)
        e = total[at].astype(F32)
        hat = xhat[at]
        t = e * gains[1:2]
        along = t - jnp.mean(t, axis=-1, keepdims=True) - hat * jnp.mean(t * hat, axis=-1, keepdims=True)
        value = d_v[at].astype(F32) + along * rstd[at, 0:1]
        g_hidden[at] = value
        row = lax.broadcasted_iota(jnp.int32, (SUB, 1), 0) + s * SUB
        low = jnp.where(row < live, value, 0.0).astype(BF16)
        g_attn[at] = low
        acc[0] += fold(e * hat)
        acc[1] += fold(e)
        acc[2] += fold(low.astype(F32))

    def ahead(s):
        line2.tick(s)
        back(s - LAG)

    def pick(tile, at):
        return d_v[:, at], act_v[:, tile * 512 : (tile + 1) * 512]

    def project(k):
        chunk = rows_of(lax.div(k, depth // 512), CHUNK)
        lanes = rows_of(lax.rem(k, depth // 512), 512)
        ffn_v[chunk, lanes] = dot(act_v[chunk], down_v[:, lanes]).astype(BF16)

    scatter.fill_near(pick)
    line2.tick(6)
    scatter.fill_own(pick)
    line2.tick(7)
    scatter.add_near()
    line2.tick(8)
    loop(4, back)

    @functools.partial(loop, 4)
    def _(i):
        project(2 * i)
        project(2 * i + 1)
        ahead(9 + i)

    scatter.pass_on(1)
    stores["ffn"].start()
    loop(3, lambda i: ahead(13 + i))
    scatter.keep(1)
    scatter.between()
    loop(count + 2 - 16, lambda i: ahead(16 + i))
    loop(LAG - 2, lambda i: back(count - LAG + 2 + i))
    stores["g_hidden"].start()
    stores["g_attn"].start()
    for k in range(5):
        sums_out[k : k + 1] = jnp.sum(acc[k], axis=0, keepdims=True)

    sums_out[5:8] = jnp.zeros((3, sums_out.shape[1]), F32)

    def write(tile, value):
        down_out[tile * 512 : (tile + 1) * 512] = value.T

    scatter.finish(write)
    scatter.drain()
    line2.drain_all()

    to_near.wait_send()

    @pl.when(has_before)
    def _():
        for item in queries:
            item.wait_send()

    @pl.when(has_after)
    def _():
        for items in gathered:
            for item in items:
                item.wait_send()

    for name in ("q", "q_next", "kv", "att", "att_t", "norm2", "g_pre", "ffn", "g_hidden", "g_attn"):
        stores[name].wait()


def front(x, d_out, lengths, until, gains, shifts, wqkv, bqv, wout, b_outs, b_up, w_up, w_down):
    rows, depth = x.shape
    width = wqkv.shape[2]
    heads = width // HD
    hidden = w_up.shape[1]
    chunk = depth // lax.axis_size("cp")
    shape = jax.ShapeDtypeStruct
    return pl.pallas_call(
        front_kernel,
        out_shape=(
            shape((rows, depth), BF16),
            shape((rows, depth), BF16),
            shape((rows, width), BF16),
            shape((rows, width), BF16),
            shape((2 * rows, 2 * width), BF16),
            shape((rows, width), BF16),
            shape((width, rows), F32),
            shape((rows, depth), BF16),
            shape((rows, hidden), BF16),
            shape((rows, depth), BF16),
            shape((rows, depth), F32),
            shape((rows, depth), BF16),
            shape((heads, rows), F32),
            shape((8, depth), F32),
            shape((hidden, chunk), F32),
        ),
        in_specs=[ANY, ANY, IN_SMEM, IN_SMEM, IN_VMEM, IN_VMEM, ANY, IN_VMEM, ANY, IN_VMEM, IN_VMEM, ANY, ANY],
        out_specs=(ANY,) * 12 + (IN_VMEM,) * 3,
        scratch_shapes=[
            pltpu.VMEM((rows, depth), BF16),
            pltpu.VMEM((rows, depth), BF16),
            pltpu.VMEM((rows, depth), BF16),
            pltpu.VMEM((depth, hidden), BF16),
            pltpu.VMEM((hidden, depth), BF16),
            pltpu.VMEM((rows, width), BF16),
            pltpu.VMEM((rows, width), BF16),
            pltpu.VMEM((2 * rows, 2 * width), BF16),
            pltpu.VMEM((heads, 2 * HD, rows), BF16),
            pltpu.VMEM((heads, 2 * HD, CHUNK), BF16),
            pltpu.VMEM((width, depth), BF16),
            pltpu.VMEM((width, rows), F32),
            pltpu.VMEM((rows, width), BF16),
            pltpu.VMEM((rows // CHUNK, width, CHUNK), BF16),
            pltpu.VMEM((rows // CHUNK, width, CHUNK), BF16),
            pltpu.VMEM((rows // CHUNK, heads, CHUNK), F32),
            pltpu.VMEM((rows // CHUNK, heads, CHUNK), F32),
            pltpu.VMEM((rows, depth), F32),
            pltpu.VMEM((rows, 128), F32),
            pltpu.VMEM((rows, hidden), BF16),
            pltpu.VMEM((rows, hidden), BF16),
            pltpu.VMEM((5, 8, depth), F32),
            *[pltpu.VMEM((rows, depth), BF16)] * 5,
            *[pltpu.SemaphoreType.DMA((2, 3, rows // PIECE))] * 2,
            *scatter_scratch(depth, hidden, SPLIT_DOWN),
            pltpu.SemaphoreType.DMA((3 * (rows // CHUNK) + 1,)),
            pltpu.SemaphoreType.DMA((3 * (rows // CHUNK) + 1,)),
            pltpu.SemaphoreType.DMA((8,)),
            pltpu.SemaphoreType.DMA((13,)),
        ],
        compiler_params=pltpu.CompilerParams(collective_id=1, has_side_effects=True, vmem_limit_bytes=63 * 2**20),
        name="front",
    )(x, d_out, lengths, until, gains, shifts, wqkv, bqv, wout, b_outs, b_up, w_up, w_down)


SPLIT_UP = 1024
SPLIT_LAST = 1024


def grad_attend_kernel(
    g_attn_hbm, wout_hbm, q_hbm, q_next_hbm, kv_hbm, att_t_hbm, lse, lengths_ref, until_ref, ffn_hbm, norm_hbm, g_pre_hbm,
    g_qkv_hbm, ffn_sum_hbm, up_out,
    g_attn_v, wout_v, q_v, q_next, kv, k_t, att_t, q_t, g_v, g_next, g_t, stats, stats_next, acc, g_qkv_v,
    g_q_next, give_q, got_q, give_near, got_near, x_send, x_recv,
    norm_v, g_pre_v, terms, near, far, rs_send, rs_recv,
    part, slot_a, slot_b, total, ar_send, ar_recv, load_sem, store_sem,
):
    cp, tp, core, chip = place()
    bands = lax.axis_size("cp")
    chips = bands // 2
    rows, width = q_v.shape
    heads = width // HD
    count = rows // SUB
    sibling = (cp + 1 - 2 * core, tp)
    after = (lax.rem(cp + 2, bands), tp)
    before = (lax.rem(cp + bands - 2, bands), tp)
    loads = [
        pltpu.make_async_copy(source, target, load_sem.at[i])
        for i, (source, target) in enumerate(
            (
                (norm_hbm, norm_v),
                (g_pre_hbm, g_pre_v),
                (ffn_hbm, part),
                (g_attn_hbm, g_attn_v),
                (wout_hbm, wout_v),
                (q_hbm, q_v),
                (q_next_hbm, q_next),
                (kv_hbm, kv),
                (att_t_hbm, att_t),
            )
        )
    ]
    for item in loads[:5]:
        item.start()
    line = LineSum(part, slot_a, slot_b, total, ar_send, ar_recv)
    scatter = Scatter(terms, near, far, rs_send, rs_recv, SPLIT_UP)
    greet(cp, tp, [*scatter.partners(), after, before])
    begin, _ = band_info(lengths_ref, until_ref, (chip + 1) * 2 * rows)
    has_before, has_after = chip > 0, chip < chips - 1
    bias = jnp.where((begin < (chip + 1) * 2 * rows) & has_after, 0.0, NEG)
    loads[0].wait()
    loads[1].wait()
    loads[2].wait()
    loop(count, line.push)

    def pick(tile, at):
        return norm_v[:, at], g_pre_v[:, tile * 512 : (tile + 1) * 512]

    for item in loads[5:]:
        item.start()
    scatter.fill_near(pick)
    relay = line.tick
    relay(0)
    for item in loads[3:]:
        item.wait()
    scale = HD ** -0.5

    pairs = heads // 2

    def exchange(kind, p=0):
        lanes = slice(p * 2 * HD, (p + 1) * 2 * HD)
        source, target, device = (
            (g_v, g_next, before),
            (stats, stats_next, before),
            (give_near, got_near, sibling),
            (give_q.at[lanes], got_q.at[lanes], after),
        )[kind]
        return pltpu.make_async_remote_copy(
            src_ref=source, dst_ref=target, send_sem=x_send.at[kind + p], recv_sem=x_recv.at[kind + p],
            device_id=device, device_id_type=MESH,
        )

    to_before = [exchange(0), exchange(1)]
    to_near = exchange(2)
    to_after = [exchange(3, p) for p in range(pairs)]

    def turn(source, target, factor):
        @functools.partial(loop, rows // CHUNK)
        def _(i):
            at = rows_of(i, CHUNK)
            value = source[at].astype(F32).T * factor
            upper = lax.broadcasted_iota(jnp.int32, (2 * HD, CHUNK), 0) < HD
            for h in range(heads):
                both = slice((h // 2) * 2 * HD, (h // 2 + 1) * 2 * HD)
                target[h, :, at] = jnp.where(upper == (h % 2 == 0), value[both], 0.0).astype(BF16)

    stats[:heads] = lse[...]

    @functools.partial(loop, rows // CHUNK)
    def _(i):
        at = rows_of(i, CHUNK)
        low = dot_nt(g_attn_v[at], wout_v[...]).astype(BF16)
        g_v[at] = low
        value = low.astype(F32).T
        for h in range(heads):
            mine = slice(h * HD, (h + 1) * HD)
            stats[heads + h : heads + h + 1, at] = jnp.sum(value[mine] * att_t[mine, at], axis=0, keepdims=True)

    @pl.when(has_before)
    def _():
        for item in to_before:
            item.start()

    relay(1)
    scatter.fill_own(pick)
    scatter.add_near()

    @pl.when(jnp.logical_not(has_after))
    def _():
        g_next[...] = jnp.zeros_like(g_next)
        stats_next[...] = jnp.zeros_like(stats_next)

    @pl.when(jnp.logical_not(has_before))
    def _():
        got_q[...] = jnp.zeros_like(got_q)

    @functools.partial(loop, 2)
    def _(i):
        at = rows_of(i, rows)
        k_t[:, at] = kv[at, :width].astype(F32).T.astype(BF16)

    @functools.partial(loop, rows // 64)
    def _(i):
        att_t[rows_of(i, 64)] = jnp.zeros((64, rows), F32)
        g_q_next[rows_of(i, 64)] = jnp.zeros((64, rows), F32)

    @functools.partial(loop, 2 * rows // 64)
    def _(i):
        acc[rows_of(i, 64)] = jnp.zeros((64, 2 * width), F32)

    relay(2)

    def head(h, q_rows, g_rows, numbers, g_q_t, mask):
        offset = lax.div(h, 2) * 2 * HD
        lanes = pl.ds(pl.multiple_of(offset, 2 * HD), 2 * HD)
        lanes_v = pl.ds(pl.multiple_of(offset + width, 2 * HD), 2 * HD)
        feature = pl.ds(pl.multiple_of(h * HD, HD), HD)
        low_lanes = lax.broadcasted_iota(jnp.int32, (CHUNK, 2 * HD), 1) < HD
        mine = low_lanes == (lax.rem(h, 2) == 0)
        for c in range(rows // CHUNK):
            cols = slice(c * CHUNK, (c + 1) * CHUNK)
            q_n = jnp.where(mine, q_rows[cols, lanes].astype(F32), 0.0).astype(BF16)
            g_n = jnp.where(mine, g_rows[cols, lanes].astype(F32), 0.0).astype(BF16)
            lse_row = numbers[pl.ds(h, 1), cols]
            delta_row = numbers[pl.ds(heads + h, 1), cols]
            for b in range(2):
                keys = slice(b * rows, (b + 1) * rows)
                s = dot(kv[keys, lanes], q_t[h, :, cols])
                p = jnp.exp(mask(b, c, s, lse_row))
                g_s = (p * (dot(kv[keys, lanes_v], g_t[h, :, cols]) - delta_row)).astype(BF16)
                acc[keys, lanes] += dot(g_s, q_n)
                acc[keys, lanes_v] += dot(p.astype(BF16), g_n)
                g_q_t[feature, cols] += dot(k_t[feature, keys], g_s)

    def causal(b, c, s, lse_row):
        key = lax.broadcasted_iota(jnp.int32, (rows, CHUNK), 0) + b * rows
        row = lax.broadcasted_iota(jnp.int32, (rows, CHUNK), 1) + c * CHUNK
        return jnp.where(key <= row + core * rows, s - lse_row, NEG)

    @pl.when(has_after)
    def _():
        for item in to_before:
            item.wait_recv()

    turn(g_next, g_t, 1.0)
    turn(q_next, q_t, scale)
    relay(3)
    for p in range(pairs):

        @functools.partial(loop, 2)
        def _(parity, p=p):
            head(2 * p + parity, q_next, g_next, stats_next, g_q_next, lambda b, c, s, row: s + (bias - row))

        pair = slice(p * 2 * HD, (p + 1) * 2 * HD)
        give_q[pair] = g_q_next[pair].astype(BF16)

        @pl.when(has_after)
        def _(p=p):
            to_after[p].start()

        relay(4 + p)

    turn(g_v, g_t, 1.0)
    turn(q_v, q_t, scale)
    relay(8)

    @functools.partial(loop, heads)
    def _(h):
        head(h, q_v, g_v, stats, att_t, causal)

        @pl.when(lax.rem(h, 2) == 1)
        def _():
            relay(9 + lax.div(h, 2))

        @pl.when(h == 4)
        def _():
            scatter.pass_on(1)

    @functools.partial(loop, rows // 64)
    def _(i):
        at = pl.ds(pl.multiple_of((1 - core) * rows + i * 64, 64), 64)
        give_near[rows_of(i, 64)] = acc[at].astype(BF16)

    to_near.start()
    scatter.keep(1)
    scatter.between()
    relay(13)
    to_near.wait_recv()

    @functools.partial(loop, rows // 64)
    def _(i):
        at = pl.ds(pl.multiple_of(core * rows + i * 64, 64), 64)
        near_at = rows_of(i, 64)
        total_at = acc[at] + got_near[near_at].astype(F32)
        g_qkv_v[near_at, width : 2 * width] = (total_at[:, :width] * scale).astype(BF16)
        g_qkv_v[near_at, 2 * width :] = total_at[:, width:].astype(BF16)

    @pl.when(has_before)
    def _():
        for item in to_after:
            item.wait_recv()

    @functools.partial(loop, rows // CHUNK)
    def _(i):
        at = rows_of(i, CHUNK)
        both = att_t[:, at] + got_q[:, at].astype(F32)
        g_qkv_v[at, :width] = (both.T * scale).astype(BF16)

    loop(count + 2 - 14, lambda i: relay(14 + i))
    stores = [
        pltpu.make_async_copy(g_qkv_v, g_qkv_hbm, store_sem.at[0]),
        pltpu.make_async_copy(total, ffn_sum_hbm, store_sem.at[1]),
    ]
    stores[0].start()
    loop(count, line.get)
    stores[1].start()

    def write(tile, value):
        up_out[:, tile * 512 : (tile + 1) * 512] = value

    scatter.finish(write)
    scatter.drain()
    line.drain_all()
    to_near.wait_send()

    @pl.when(has_before)
    def _():
        for item in to_before:
            item.wait_send()

    @pl.when(has_after)
    def _():
        for item in to_after:
            item.wait_send()

    for item in stores:
        item.wait()


def grad_attend(g_attn, wout, q, q_next, kv, att_t, lse, lengths, until, ffn_low, norm2, g_pre):
    rows, depth = g_attn.shape
    width = q.shape[1]
    heads = width // HD
    hidden = g_pre.shape[1]
    chunk = depth // lax.axis_size("cp")
    shape = jax.ShapeDtypeStruct
    return pl.pallas_call(
        grad_attend_kernel,
        out_shape=(
            shape((rows, 3 * width), BF16),
            shape((rows, depth), BF16),
            shape((chunk, hidden), F32),
        ),
        in_specs=[ANY] * 6 + [IN_VMEM, IN_SMEM, IN_SMEM, ANY, ANY, ANY],
        out_specs=(ANY, ANY, IN_VMEM),
        scratch_shapes=[
            pltpu.VMEM((rows, depth), BF16),
            pltpu.VMEM((width, depth), BF16),
            pltpu.VMEM((rows, width), BF16),
            pltpu.VMEM((rows, width), BF16),
            pltpu.VMEM((2 * rows, 2 * width), BF16),
            pltpu.VMEM((width, 2 * rows), BF16),
            pltpu.VMEM((width, rows), F32),
            pltpu.VMEM((heads, 2 * HD, rows), BF16),
            pltpu.VMEM((rows, width), BF16),
            pltpu.VMEM((rows, width), BF16),
            pltpu.VMEM((heads, 2 * HD, rows), BF16),
            pltpu.VMEM((2 * heads, rows), F32),
            pltpu.VMEM((2 * heads, rows), F32),
            pltpu.VMEM((2 * rows, 2 * width), F32),
            pltpu.VMEM((rows, 3 * width), BF16),
            pltpu.VMEM((width, rows), F32),
            pltpu.VMEM((width, rows), BF16),
            pltpu.VMEM((width, rows), BF16),
            pltpu.VMEM((rows, 2 * width), BF16),
            pltpu.VMEM((rows, 2 * width), BF16),
            pltpu.SemaphoreType.DMA((3 + heads // 2,)),
            pltpu.SemaphoreType.DMA((3 + heads // 2,)),
            pltpu.VMEM((rows, depth), BF16),
            pltpu.VMEM((rows, hidden), BF16),
            pltpu.VMEM((depth, hidden), BF16),
            *scatter_scratch(depth, hidden, SPLIT_UP),
            *line_scratch(rows, depth),
            pltpu.SemaphoreType.DMA((9,)),
            pltpu.SemaphoreType.DMA((2,)),
        ],
        compiler_params=pltpu.CompilerParams(collective_id=2, has_side_effects=True, vmem_limit_bytes=63 * 2**20),
        name="grad_attend",
    )(g_attn, wout, q, q_next, kv, att_t, lse, lengths, until, ffn_low, norm2, g_pre)


def last_kernel(
    g_qkv_hbm, wqkv_hbm, x_hbm, g_hidden_hbm, norm_hbm, g_attn_hbm, att_hbm, attn_sum_hbm, ffn_sum_hbm,
    up_hbm, down_hbm, lengths_ref, until_ref, gains, b_outs, sums_in,
    g_x, out, up_out, down_out, qkv_out, w_out_out, gains_out, shifts_out, bqv_out, bouts_out, bup_out,
    g_qkv_v, w_v, x_v, norm_v, g_attn_v, att_v, attn_sum, ffn_sum, acc, small, small_got, late, late_got,
    terms, near, far, rs_send, rs_recv,
    part, slot_a, slot_b, total, ar_send, ar_recv, small_send, small_recv, load_sem,
):
    cp, tp, core, chip = place()
    rows, depth = x_v.shape
    width = att_v.shape[1]
    count = rows // SUB
    loads = [
        pltpu.make_async_copy(source, target, load_sem.at[i])
        for i, (source, target) in enumerate(
            (
                (g_qkv_hbm, g_qkv_v),
                (wqkv_hbm, w_v),
                (norm_hbm, norm_v),
                (g_attn_hbm, g_attn_v),
                (att_hbm, att_v),
                (x_hbm, x_v),
                (g_hidden_hbm, g_x),
                (attn_sum_hbm, attn_sum),
                (ffn_sum_hbm, ffn_sum),
                (up_hbm, up_out),
                (down_hbm, down_out),
            )
        )
    ]
    for item in loads[:2]:
        item.start()
    line = LineSum(part, slot_a, slot_b, total, ar_send, ar_recv)
    scatter = Scatter(terms, near, far, rs_send, rs_recv, SPLIT_LAST)
    bands = lax.axis_size("cp")
    greet(cp, tp, [(lax.rem(cp + k, bands), tp) for k in range(1, bands)])
    _, live = band_info(lengths_ref, until_ref, cp * rows)
    acc[...] = jnp.zeros_like(acc)
    loads[0].wait()
    loads[1].wait()

    for c in range(rows // CHUNK):
        chunk = slice(c * CHUNK, (c + 1) * CHUNK)

        @functools.partial(loop, depth // 512)
        def _(t, chunk=chunk):
            lanes = rows_of(t, 512)
            value = dot_nt(g_qkv_v[chunk, :width], w_v[0, lanes])
            value = value + dot_nt(g_qkv_v[chunk, width : 2 * width], w_v[1, lanes])
            value = value + dot_nt(g_qkv_v[chunk, 2 * width :], w_v[2, lanes])
            part[chunk, lanes] = value.astype(BF16)

        loop(CHUNK // SUB, lambda s, c=c: line.push(s + c * (CHUNK // SUB)))
        if c == 0:
            for item in loads[2:]:
                item.start()

    def small_copy(which, sender, receiver):
        source, target = ((small, small_got), (late, late_got))[which]
        return pltpu.make_async_remote_copy(
            src_ref=source, dst_ref=target.at[sender], send_sem=small_send.at[which, receiver],
            recv_sem=small_recv.at[which, sender], device_id=(receiver, tp), device_id_type=MESH,
        )

    def give_small(which):
        loop(bands - 1, lambda k: small_copy(which, cp, lax.rem(cp + 1 + k, bands)).start())

    def take_small(which):
        source, target = ((small, small_got), (late, late_got))[which]
        target[cp] = source[...]

        @functools.partial(loop, bands - 1)
        def _(k):
            sender = lax.rem(cp + 1 + k, bands)
            small_copy(which, sender, sender).wait_recv()

        value = target[0]
        for k in range(1, bands):
            value = value + target[k]
        return value

    small[0:5] = sums_in[0:5]
    small[6:8] = jnp.zeros((2, depth), F32)
    small[5:6, 2 * width :] = jnp.zeros((1, depth - 2 * width), F32)
    for j in range(2):
        bias = jnp.sum(g_qkv_v[:, 2 * j * width : (2 * j + 1) * width].astype(F32), axis=0, keepdims=True)
        small[5:6, j * width : (j + 1) * width] = bias
    give_small(0)
    for item in loads[2:9]:
        item.wait()

    def back(s):
        line.get(s)
        at = rows_of(s, SUB)
        e = total[at].astype(F32)
        v = x_v[at].astype(F32)
        centred = v - jnp.mean(v, axis=-1, keepdims=True)
        scale = lax.rsqrt(jnp.mean(centred * centred, axis=-1, keepdims=True) + EPS)
        hat = centred * scale
        t = e * gains[0:1]
        along = t - jnp.mean(t, axis=-1, keepdims=True) - hat * jnp.mean(t * hat, axis=-1, keepdims=True)
        g_x[at] = g_x[at] + along * scale
        row = lax.broadcasted_iota(jnp.int32, (SUB, 1), 0) + s * SUB
        branches = attn_sum[at].astype(F32) + b_outs[0:1] + (ffn_sum[at].astype(F32) + b_outs[1:2])
        out[at] = v + jnp.where(row < live, branches, 0.0)
        acc[0] += fold(e * hat)
        acc[1] += fold(e)

    behind = 3

    def ahead(s):
        line.tick(s)

        @pl.when(s >= behind)
        def _():
            back(s - behind)

    def pick(tile, at):
        if tile < 3:
            return norm_v[:, at], g_qkv_v[:, tile * width : (tile + 1) * width]
        return g_attn_v[:, at], att_v[...]

    scatter.fill_near(pick)
    ahead(0)
    ahead(1)
    scatter.fill_own(pick)
    ahead(2)
    scatter.add_near()
    loop(9 - 3, lambda i: ahead(3 + i))
    scatter.pass_on(1)
    loop(13 - 9, lambda i: ahead(9 + i))
    scatter.keep(1)
    scatter.between()
    loop(count + 2 - 13, lambda i: ahead(13 + i))
    loop(behind - 2, lambda i: back(count + 2 - behind + i))

    for k in range(2):
        late[k : k + 1] = jnp.sum(acc[k], axis=0, keepdims=True)
    give_small(1)
    early = take_small(0)
    bouts_out[...] = early[2:4]
    bup_out[...] = early[4:5]
    for j in range(2):
        bqv_out[j : j + 1] = early[5:6, j * width : (j + 1) * width]

    def write(tile, value):
        if tile < 3:
            qkv_out[tile] = value
        else:
            w_out_out[...] = value.T

    scatter.finish(write)
    for item in loads[9:]:
        item.wait()
    final = take_small(1)
    gains_out[0:1] = final[0:1]
    gains_out[1:2] = early[0:1]
    shifts_out[0:1] = final[1:2]
    shifts_out[1:2] = early[1:2]
    scatter.drain()
    line.drain_all()

    @functools.partial(loop, bands - 1)
    def _(k):
        other = lax.rem(cp + 1 + k, bands)
        small_copy(0, cp, other).wait_send()
        small_copy(1, cp, other).wait_send()


def last(g_qkv, wqkv, x, g_hidden, norm1, g_attn, att, attn_sum, ffn_sum, g_up, g_down, lengths, until, gains, b_outs, sums):
    rows, depth = x.shape
    width = att.shape[1]
    bands = lax.axis_size("cp")
    chunk = depth // bands
    pinned = bands <= 8
    result = pltpu.VMEM if pinned else jax.ShapeDtypeStruct
    return pl.pallas_call(
        last_kernel,
        out_shape=(
            result((rows, depth), F32),
            result((rows, depth), F32),
            result(g_up.shape, F32),
            result(g_down.shape, F32),
            result((3, chunk, width), F32),
            result((width, chunk), F32),
            result((2, depth), F32),
            result((2, depth), F32),
            result((2, width), F32),
            result((2, depth), F32),
            result((1, depth), F32),
        ),
        in_specs=[ANY] * 11 + [IN_SMEM] * 2 + [IN_VMEM] * 3,
        out_specs=(IN_VMEM,) * 11,
        scratch_shapes=[
            pltpu.VMEM((rows, 3 * width), BF16),
            pltpu.VMEM((3, depth, width), BF16),
            pltpu.VMEM((rows, depth), BF16),
            pltpu.VMEM((rows, depth), BF16),
            pltpu.VMEM((rows, depth), BF16),
            pltpu.VMEM((rows, width), BF16),
            pltpu.VMEM((rows, depth), BF16),
            pltpu.VMEM((rows, depth), BF16),
            pltpu.VMEM((2, 8, depth), F32),
            pltpu.VMEM((8, depth), F32),
            pltpu.VMEM((bands, 8, depth), F32),
            pltpu.VMEM((2, depth), F32),
            pltpu.VMEM((bands, 2, depth), F32),
            pltpu.VMEM((depth, depth), BF16),
            *scatter_scratch(depth, depth, SPLIT_LAST),
            *line_scratch(rows, depth),
            pltpu.SemaphoreType.DMA((2, bands)),
            pltpu.SemaphoreType.DMA((2, bands)),
            pltpu.SemaphoreType.DMA((11,)),
        ],
        compiler_params=pltpu.CompilerParams(collective_id=3, has_side_effects=True, vmem_limit_bytes=(45 if pinned else 62) * 2**20),
        name="last",
    )(g_qkv, wqkv, x, g_hidden, norm1, g_attn, att, attn_sum, ffn_sum, g_up, g_down, lengths, until, gains, b_outs, sums)


def shards(
    layer_input,
    seq_lengths,
    active_until,
    ln_gains,
    ln_shifts,
    query_key_value_weight,
    b_qv,
    w_out,
    b_outs,
    w_up,
    b_up,
    w_down,
    d_out,
):
    wqkv = jnp.transpose(query_key_value_weight, (1, 0, 2))
    (attn_sum, norm1, q, q_next, kv, att, att_t, norm2, g_pre, ffn_low, g_hidden, g_attn, lse, sums, g_down) = front(
        layer_input, d_out, seq_lengths, active_until, ln_gains, ln_shifts, wqkv, b_qv, w_out, b_outs, b_up[None],
        w_up, w_down,
    )
    g_qkv_rows, ffn_sum, g_up = grad_attend(
        g_attn, w_out, q, q_next, kv, att_t, lse, seq_lengths, active_until, ffn_low, norm2, g_pre
    )
    g_x, out, g_up, g_down, g_qkv, g_out, g_ln_gains, g_ln_shifts, g_bqv, g_bouts, g_bup = last(
        g_qkv_rows, wqkv, layer_input, g_hidden, norm1, g_attn, att, attn_sum, ffn_sum, g_up, g_down,
        seq_lengths, active_until, ln_gains, b_outs, sums,
    )
    g_qkv = jnp.transpose(g_qkv, (1, 0, 2))
    return (out, g_x, g_ln_gains, g_ln_shifts, g_qkv, g_bqv, g_out, g_bouts, g_up, g_bup[0], g_down)


def solution(mesh):
    return jax.shard_map(
        shards,
        mesh=mesh,
        in_specs=(
            P("cp", None),
            P(),
            P(),
            P(),
            P(),
            P(None, None, "tp"),
            P(None, "tp"),
            P("tp", None),
            P(),
            P(None, "tp"),
            P("tp"),
            P("tp", None),
            P("cp", None),
        ),
        out_specs=(
            P("cp", None),
            P("cp", None),
            P(),
            P(),
            P("cp", None, "tp"),
            P(None, "tp"),
            P("tp", "cp"),
            P(),
            P("cp", "tp"),
            P("tp"),
            P("tp", "cp"),
        ),
        check_vma=False,
    )
```
